32 devices in a mesh: dp: 16 (over z, x, core), seq: 2 (over y).
Axes of the slice: x: 2, y: 2, z: 4, core: 2. Of those that a mesh axis runs over, the one named last changes fastest.
Arguments:
- block_input: bfloat16 [16, 1024, 1024], P('dp', 'seq'), may hold values from -6 to 6
- doc_starts: int32 [16, 6], P('dp'), may hold values from 1 to 1023, as said below
- norm_in: bfloat16 [1024], P(('dp', 'seq')), may hold values from 0.5 to 1.5
- w_mix: bfloat16 [1024, 6144], P(('dp', 'seq')), may hold values from -0.1875 to 0.1875
- w_small: bfloat16 [1024, 24], P(('dp', 'seq')), may hold values from -0.1875 to 0.1875
- conv_w: bfloat16 [4, 5120], P(None, ('dp', 'seq')), may hold values from -3 to 3
- decay_log: bfloat16 [8], replicated, may hold values from -8 to -2.5
- norm_out: bfloat16 [128], replicated, may hold values from 0.5 to 1.5
- w_out: bfloat16 [1024, 1024], P(('dp', 'seq')), may hold values from -0.25 to 0.25
- norm_mlp: bfloat16 [1024], P(('dp', 'seq')), may hold values from 0.5 to 1.5
- w_gu: bfloat16 [1024, 5632], P(('dp', 'seq')), may hold values from -0.1875 to 0.1875
- w_down: bfloat16 [2816, 1024], P(('dp', 'seq')), may hold values from -0.15625 to 0.15625
- cotangent: bfloat16 [16, 1024, 1024], P('dp', 'seq'), may hold values from -6 to 6
Outputs:
- block_output: bfloat16 [16, 1024, 1024], P('dp', 'seq')
- input_grad: bfloat16 [16, 1024, 1024], P('dp', 'seq')
- grad_norm_in: float32 [1024], P(('dp', 'seq'))
- grad_mix: float32 [1024, 6144], P(('dp', 'seq'))
- grad_small: float32 [1024, 24], P(('dp', 'seq'))
- grad_conv: float32 [4, 5120], P(None, ('dp', 'seq'))
- grad_decay: float32 [8], replicated
- grad_norm_out: float32 [128], replicated
- grad_out: float32 [1024, 1024], P(('dp', 'seq'))
- grad_norm_mlp: float32 [1024], P(('dp', 'seq'))
- grad_gu: float32 [1024, 5632], P(('dp', 'seq'))
- grad_down: float32 [2816, 1024], P(('dp', 'seq'))
The draws below stay inside these ranges and needn't reach their ends.
Inputs may be any that keep to these rules, and one draw needn't show every extreme that they name: `doc_starts`: each row's starts are strictly increasing; three lie among the row's first 512 positions and three among its last 512, so that one document covers the middle of every row.
All inputs are finite; a program needn't handle non-finite values.
Results may differ from the reference program's by a relative error of at most 0.012.
Values may be sent and summed in bfloat16 or wider, within the bound.
A program may use at most 320 MiB of HBM per device.

```python
import jax
import jax.numpy as jnp
from jax import lax

D = 1024
H = 8
DK = 128
DV = 128
FF = 2816
NH = 2
CONV = 4
GROUP = 64
NB = 6
SEG = 512
LENGTH = 1024
ROWS = 16


def draw_doc_starts(key, part):
    key = jax.random.fold_in(key, 7)
    row_keys = jax.random.split(key, ROWS)

    def one_row(row_key):
        head_key, tail_key = jax.random.split(row_key)
        head_part = jax.random.permutation(head_key, SEG - 1)[:NB // 2] + 1
        tail_part = jax.random.permutation(tail_key, SEG)[:NB - NB // 2] + (LENGTH - SEG)
        return jnp.sort(jnp.concatenate([head_part, tail_part])).astype(jnp.int32)
    return jax.vmap(one_row)(row_keys)


def block_levels(own_key, shape, cuts, smallest, top_value):
    level = 1.0
    for dim, blocks in cuts:
        steps = jax.random.uniform(jax.random.fold_in(jax.random.fold_in(own_key, 6), dim), (blocks,), jnp.float32, smallest / len(cuts), top_value / len(cuts))
        level = level * jnp.repeat(jnp.exp(steps), shape[dim] // blocks).reshape((-1,) + (1,) * (len(shape) - 1 - dim))
    return level


def noise(rng, dims, spread, reach, pieces=(), held_as=jnp.bfloat16):
    entries = jax.random.normal(rng, dims, jnp.float32) * spread
    if len(pieces) > 0:
        entries = block_levels(rng, dims, pieces, -0.22, 0.18) * entries
    return jnp.clip(entries, min=-reach, max=reach).astype(held_as)


def setup_inputs(seed: int = 0) -> dict:
    seeds = jax.random.split(jax.random.key(seed), 14)
    return {
        "block_input": noise(seeds[0], (ROWS, LENGTH, D), 1.0, 6.0, ((0, 16), (1, 2))),
        "doc_starts": draw_doc_starts(jax.random.fold_in(seeds[13], 71), 0),
        "norm_in": jnp.clip(1.0 + 0.1 * jax.random.normal(seeds[2], (D,), jnp.float32), 0.5, 1.5).astype(jnp.bfloat16),
        "w_mix": noise(seeds[3], (D, 6 * H * DK), D ** -0.5, 0.1875, ((0, 32),)),
        "w_small": noise(seeds[4], (D, NH * H + H), D ** -0.5, 0.1875, ((0, 32),)),
        "conv_w": noise(seeds[5], (CONV, 5 * H * DK), CONV ** -0.5, 3.0, ((1, 32),)),
        "decay_log": jnp.clip(jax.random.uniform(seeds[6], (H,), jnp.float32, -8.0, -2.5), -8.0, -2.5).astype(jnp.bfloat16),
        "norm_out": jnp.clip(1.0 + 0.1 * jax.random.normal(seeds[7], (DV,), jnp.float32), 0.5, 1.5).astype(jnp.bfloat16),
        "w_out": noise(seeds[8], (H * DV, D), (H * DV // 2) ** -0.5, 0.25, ((0, 32),)),
        "norm_mlp": jnp.clip(1.0 + 0.1 * jax.random.normal(seeds[9], (D,), jnp.float32), 0.5, 1.5).astype(jnp.bfloat16),
        "w_gu": noise(seeds[10], (D, 2 * FF), D ** -0.5, 0.1875, ((0, 32),)),
        "w_down": noise(seeds[11], (FF, D), (FF // 2) ** -0.5, 0.15625, ((0, 32),)),
        "cotangent": noise(seeds[12], (ROWS, LENGTH, D), 1.0, 6.0, ((0, 16), (1, 2))),
    }


EPSILON = 1e-06
HIGHEST = lax.Precision.HIGHEST

@jax.custom_vjp
def low(v):
    return lax.optimization_barrier(v.astype(jnp.bfloat16)).astype(jnp.float32)

@jax.custom_vjp
def low_back(v):
    return v

def low_keep(v):
    return (low(v), None)

def low_pass(kept, grad):
    return (grad,)

def back_keep(v):
    return (v, None)

def back_low(kept, grad):
    return (low(grad),)
low.defvjp(low_keep, low_pass)
low_back.defvjp(back_keep, back_low)

def rms_scale(values, scale_gain):
    return values * lax.rsqrt(lax.optimization_barrier(jnp.mean(values * values, axis=-1, keepdims=True)) + EPSILON) * scale_gain

def segment_ids(row_starts):
    positions = jnp.arange(LENGTH, dtype=jnp.int32)
    return lax.optimization_barrier(jnp.sum((positions[:, None] >= row_starts[None, :]).astype(jnp.int32), axis=1))

def short_conv(channels, row_segments, conv_taps):
    length = channels.shape[0]
    summed = channels * conv_taps[0]
    for tap_index in range(1, CONV):
        shifted = jnp.concatenate([jnp.zeros((tap_index, channels.shape[1]), jnp.float32), channels[:length - tap_index]], 0)
        shifted_seg = jnp.concatenate([jnp.full((tap_index,), -1, jnp.int32), row_segments[:length - tap_index]], 0)
        summed = summed + shifted * conv_taps[tap_index] * (shifted_seg == row_segments).astype(jnp.float32)[:, None]
    return jax.nn.silu(summed)

def token_step(memory_state, token_item):
    query_vec, key_pair, value_pair, beta_pair, log_rate, keep_flag = token_item
    memory_state = memory_state * (jnp.exp(log_rate) * keep_flag)[:, None, None]
    for house_index in range(NH):
        predicted = jnp.einsum('hvk,hk->hv', memory_state, key_pair[house_index], precision=HIGHEST)
        update = (beta_pair[house_index][:, None] * (predicted - value_pair[house_index]))[:, :, None]
        memory_state = memory_state - update * key_pair[house_index][:, None, :]
    return (memory_state, jnp.einsum('hvk,hk->hv', memory_state, query_vec, precision=HIGHEST))

@jax.checkpoint
def block_step(memory_state, block_items):
    return lax.scan(token_step, memory_state, block_items)

def delta_product(queries, key_rows, value_rows, beta_rows, decay_rows, keep_rows):
    length = queries.shape[0]
    blocks = length // GROUP

    def as_blocks(array_in):
        return array_in.reshape((blocks, GROUP) + array_in.shape[1:])
    zero_state = jnp.zeros((H, DV, DK), jnp.float32)
    items = tuple((as_blocks(array_in) for array_in in (queries, key_rows, value_rows, beta_rows, decay_rows, keep_rows)))
    final_state, readouts = lax.scan(block_step, zero_state, items)
    return readouts.reshape(length, H, DV)

def row_forward(params, row_input, row_segments):
    norm_in, w_mix, w_small, conv_w, decay_log, norm_out, w_out, norm_mlp, w_gu, w_down = params
    key_width = H * DK
    normed = low(rms_scale(row_input, norm_in))
    projected = low_back(jnp.dot(normed, w_mix, precision=HIGHEST))
    gates_raw = low_back(jnp.dot(normed, w_small, precision=HIGHEST))
    convolved = short_conv(projected[:, :5 * key_width], row_segments, conv_w)
    queries = convolved[:, :key_width].reshape(-1, H, DK)
    queries = queries * lax.rsqrt(lax.optimization_barrier(jnp.sum(queries * queries, axis=-1, keepdims=True)) + EPSILON) * DK ** (-0.5)
    key_rows = convolved[:, key_width:3 * key_width].reshape(-1, NH, H, DK)
    key_rows = key_rows * lax.rsqrt(lax.optimization_barrier(jnp.sum(key_rows * key_rows, axis=-1, keepdims=True)) + EPSILON)
    value_rows = convolved[:, 3 * key_width:].reshape(-1, NH, H, DV)
    beta_rows = jax.nn.sigmoid(gates_raw[:, :NH * H]).reshape(-1, NH, H)
    decay_rows = -jnp.exp(decay_log) * jax.nn.softplus(gates_raw[:, NH * H:])
    keep_rows = jnp.concatenate([jnp.zeros((1,), jnp.float32), (row_segments[1:] == row_segments[:-1]).astype(jnp.float32)])
    readouts = delta_product(queries, key_rows, value_rows, beta_rows, decay_rows, keep_rows)
    gated_out = rms_scale(readouts, norm_out) * jax.nn.silu(projected[:, 5 * key_width:].reshape(-1, H, DV))
    mixer_out = low_back(jnp.dot(low(gated_out.reshape(-1, H * DV)), w_out, precision=HIGHEST))
    hidden = row_input + mixer_out
    mlp_in = low(rms_scale(hidden, norm_mlp))
    gate_up = low_back(jnp.dot(mlp_in, w_gu, precision=HIGHEST))
    activated = low(jax.nn.silu(gate_up[:, :FF]) * gate_up[:, FF:])
    return hidden + low_back(jnp.dot(activated, w_down, precision=HIGHEST))

def reference(block_input, doc_starts, norm_in, w_mix, w_small, conv_w, decay_log, norm_out, w_out, norm_mlp, w_gu, w_down, cotangent):
    row_segments = jax.vmap(segment_ids)(doc_starts)
    weights = tuple((weight.astype(jnp.float32) for weight in (norm_in, w_mix, w_small, conv_w, decay_log, norm_out, w_out, norm_mlp, w_gu, w_down)))

    def forward(all_input, *params):

        def one_row(row_pair):
            return row_forward(params, row_pair[0], row_pair[1])
        return lax.map(jax.checkpoint(one_row), (all_input, row_segments))
    result, pullback = jax.vjp(forward, block_input.astype(jnp.float32), *weights)
    grads = pullback(cotangent.astype(jnp.float32))
    return (result.astype(jnp.bfloat16), grads[0].astype(jnp.bfloat16), grads[1], grads[2], grads[3], grads[4], grads[5], grads[6], grads[7], grads[8], grads[9], grads[10])
```

```python
from functools import partial

import jax
import jax.numpy as jnp
from jax import lax
from jax.experimental import pallas as pl
from jax.experimental.pallas import tpu as pltpu
from jax.sharding import PartitionSpec as P

H = 8
DK = 128
DV = 128
NH = 2
GROUP = 64
SPAN = NH * GROUP
LEVELS = 6
EPSILON = 1e-06
HIGHEST = lax.Precision.HIGHEST
LIMIT = 50 * 1024 * 1024


def mm(left, right, left_dim=1, right_dim=0):
    return lax.dot_general(
        left.astype(jnp.bfloat16),
        right.astype(jnp.bfloat16),
        (((left_dim,), (right_dim,)), ((), ())),
        preferred_element_type=jnp.float32,
    )


def iotas(rows, columns):
    return (
        lax.broadcasted_iota(jnp.int32, (rows, columns), 0),
        lax.broadcasted_iota(jnp.int32, (rows, columns), 1),
    )


def order_masks():
    row, column = iotas(SPAN, SPAN)
    row_tok, column_tok = row % GROUP, column % GROUP
    row_step, column_step = row // GROUP, column // GROUP
    pair = (row_tok == column_tok) & (row_step > column_step)
    strict = (row_tok > column_tok) | pair
    levels = []
    for level in range(LEVELS):
        row_half, column_half = row_tok >> level, column_tok >> level
        levels.append((row_half == column_half + 1) & (row_half % 2 == 1))
    eye = jnp.where(row == column, 1.0, 0.0)
    return strict, pair, levels, eye


def unit_inverses(lowers, pair, levels, eye):
    inverses = [eye - jnp.where(pair, lower, 0.0) for lower in lowers]
    for level in levels:
        parts = [mm(jnp.where(level, lower, 0.0), inv) for lower, inv in zip(lowers, inverses)]
        inverses = [inv - mm(inv, part) for part, inv in zip(parts, inverses)]
    return inverses


def silu_pair(values):
    sig = jax.nn.sigmoid(values)
    return values * sig, sig


def conv_block(channel_ref, border_ref, tap_ref, mask_ref, ext_ref):
    length = channel_ref.shape[0]
    ext_ref[0:8, :] = border_ref[...]
    ext_ref[8 : 8 + length, :] = channel_ref[...]
    summed = channel_ref[...] * tap_ref[0:1, :]
    for tap in range(1, 4):
        summed = summed + ext_ref[8 - tap : 8 - tap + length, :] * tap_ref[tap : tap + 1, :] * mask_ref[tap - 1]
    return summed


def unit_rows(values):
    inv = lax.rsqrt(jnp.sum(values * values, axis=1, keepdims=True) + EPSILON)
    return values * inv, inv


def chunk_vectors(vec_ref, chunk):
    rows = vec_ref[0, chunk]
    columns = jnp.transpose(rows)
    return rows, columns


def link_matrix(rows, columns):
    row, column = iotas(GROUP, SPAN)
    linked = (columns[:GROUP, 2:3] == rows[2:3, :]) & (row >= column % GROUP)
    return jnp.exp(jnp.where(linked, columns[:GROUP, 0:1] - rows[0:1, :], -1e30))


def twice(values):
    return jnp.concatenate([values, values], axis=0)


def forward_kernel(
    q_in, k0_in, k1_in, v0_in, v1_in,
    bq, bk0, bk1, bv0, bv1,
    tq, tk0, tk1, tv0, tv1,
    mask_ref, vec_ref, start_ref,
    x_out, w_out, u_out, t_out, i_out, ok_out, o_out, state_out,
    ext_ref, q_ref, k_ref, v_ref,
):
    length = q_in.shape[0]
    chunks = length // GROUP
    conv = []
    for channel, border, tap in (
        (q_in, bq, tq), (k0_in, bk0, tk0), (k1_in, bk1, tk1), (v0_in, bv0, tv0), (v1_in, bv1, tv1),
    ):
        conv.append(silu_pair(conv_block(channel, border, tap, mask_ref, ext_ref))[0])
    q_ref[...] = unit_rows(conv[0])[0] * DK ** (-0.5)
    for step in range(NH):
        k_ref[step] = unit_rows(conv[1 + step])[0]
        v_ref[step] = conv[1 + NH + step]
    strict, pair, levels, eye = order_masks()
    items = []
    lowers = []
    for chunk in range(chunks):
        here = slice(chunk * GROUP, (chunk + 1) * GROUP)
        rows, columns = chunk_vectors(vec_ref, chunk)
        keys = k_ref[:, here, :].reshape(SPAN, DK)
        values = v_ref[:, here, :].reshape(SPAN, DV)
        queries = q_ref[here, :]
        link = link_matrix(rows, columns)
        lower = jnp.where(strict, columns[:, 1:2] * twice(link) * mm(keys, keys, 1, 1), 0.0)
        reading = link * mm(queries, keys, 1, 1)
        lowers.append(lower)
        items.append((rows, columns, keys, values, queries, reading))
    inverses = unit_inverses(lowers, pair, levels, eye)
    state = start_ref[0]
    for chunk in range(chunks):
        rows, columns, keys, values, queries, reading = items[chunk]
        inverse = inverses[chunk]
        here = slice(chunk * GROUP, (chunk + 1) * GROUP)
        beta, scale, tail = columns[:, 1:2], columns[:, 3:4], columns[:, 4:5]
        key_part = mm(inverse, beta * scale * keys)
        value_part = mm(inverse, beta * values)
        tail_keys = tail * keys
        transfer = mm(key_part, tail_keys, 0, 0)
        inject = mm(value_part, tail_keys, 0, 0)
        x_out[0, chunk] = inverse.astype(x_out.dtype)
        w_out[0, chunk] = key_part.astype(w_out.dtype)
        u_out[0, chunk] = value_part.astype(u_out.dtype)
        t_out[0, chunk] = transfer.astype(t_out.dtype)
        i_out[0, chunk] = inject
        ok_out[0, chunk] = (columns[:GROUP, 3:4] * queries - mm(reading, key_part)).astype(ok_out.dtype)
        o_out[0, chunk] = mm(reading, value_part)
        state = rows[3:4, GROUP - 1 : GROUP] * state - mm(state, transfer) + inject
    state_out[0] = state


def chain_kernel(vec_ref, t_in, start_ref, state_out):
    chunks = t_in.shape[1]
    state = start_ref[0]
    for chunk in range(chunks):
        state = vec_ref[0, chunk, 3:4, GROUP - 1 : GROUP] * state - mm(state, t_in[0, chunk])
    state_out[0] = state


def readout_kernel(vec_ref, w_in, u_in, t_in, i_in, ok_in, o_in, entry_ref, gate_ref, gain_ref, gated_out, mixed_out, u_out, s_out):
    chunks = w_in.shape[1]
    state = entry_ref[0]
    states = []
    for chunk in range(chunks):
        states.append(state)
        state = vec_ref[0, chunk, 3:4, GROUP - 1 : GROUP] * state - mm(state, t_in[0, chunk]) + i_in[0, chunk]
    for chunk in range(chunks):
        here = slice(chunk * GROUP, (chunk + 1) * GROUP)
        state = states[chunk].astype(jnp.bfloat16)
        s_out[0, chunk] = state
        u_out[0, chunk] = (u_in[0, chunk].astype(jnp.float32) - mm(w_in[0, chunk], state, 1, 1)).astype(u_out.dtype)
        mixed = o_in[0, chunk] + mm(ok_in[0, chunk], state, 1, 1)
        mixed_out[here, :] = mixed
        inv = lax.rsqrt(jnp.mean(mixed * mixed, axis=1, keepdims=True) + EPSILON)
        gate = silu_pair(gate_ref[here, :])[0]
        gated_out[here, :] = (mixed * inv * gain_ref[0:1, :] * gate).astype(gated_out.dtype)


def readout_back_kernel(vec_ref, t_in, ok_in, mixed_in, gate_ref, gain_ref, d_ref, start_ref, d_mixed_out, d_gate_out, local_out, state_out, gain_out):
    chunks = t_in.shape[1]
    gain = gain_ref[0:1, :]
    gain_grad = jnp.zeros((1, DV), jnp.float32)
    locals_ = []
    for chunk in range(chunks):
        here = slice(chunk * GROUP, (chunk + 1) * GROUP)
        mixed = mixed_in[here, :]
        inv = lax.rsqrt(jnp.mean(mixed * mixed, axis=1, keepdims=True) + EPSILON)
        unit = mixed * inv
        gate = gate_ref[here, :]
        open_, sig = silu_pair(gate)
        d_gated = d_ref[here, :]
        d_scaled = d_gated * open_
        d_gate_out[here, :] = (d_gated * unit * gain * sig * (1.0 + gate * (1.0 - sig))).astype(d_gate_out.dtype)
        gain_grad = gain_grad + jnp.sum(d_scaled * unit, axis=0, keepdims=True)
        d_unit = d_scaled * gain
        d_mixed = inv * (d_unit - unit * jnp.mean(d_unit * unit, axis=1, keepdims=True))
        d_mixed_low = d_mixed.astype(jnp.bfloat16)
        d_mixed_out[here, :] = d_mixed_low
        local = mm(d_mixed_low, ok_in[0, chunk], 0, 0)
        local_out[0, chunk] = local
        locals_.append(local)
    gain_out[0] = jnp.broadcast_to(gain_grad, (8, DV))
    state = start_ref[0]
    for chunk in reversed(range(chunks)):
        state = vec_ref[0, chunk, 3:4, GROUP - 1 : GROUP] * state - mm(state, t_in[0, chunk], 1, 1) + locals_[chunk]
    state_out[0] = state


def backward_kernel(
    q_in, k0_in, k1_in, v0_in, v1_in,
    bq, bk0, bk1, bv0, bv1,
    tq, tk0, tk1, tv0, tv1,
    mask_ref, vec_ref, t_in, x_in, u_in, s_in, d_mixed_in, local_in, exit_ref,
    dq_out, dk0_out, dk1_out, dv0_out, dv1_out,
    eq_out, ek0_out, ek1_out, ev0_out, ev1_out,
    gq_out, gk0_out, gk1_out, gv0_out, gv1_out,
    d_vec_out,
    ext_ref, pre_ref, q_ref, k_ref, v_ref, inv_ref, d_ref, z_ref,
):
    length = q_in.shape[0]
    chunks = length // GROUP
    channels = (q_in, k0_in, k1_in, v0_in, v1_in)
    taps = (tq, tk0, tk1, tv0, tv1)
    for part, (channel, border, tap) in enumerate(zip(channels, (bq, bk0, bk1, bv0, bv1), taps)):
        pre = conv_block(channel, border, tap, mask_ref, ext_ref.at[part])
        pre_ref[part] = pre
        value = silu_pair(pre)[0]
        if part == 0:
            unit, inv = unit_rows(value)
            q_ref[...] = unit * DK ** (-0.5)
            inv_ref[0] = jnp.broadcast_to(inv, (length, DK))
        elif part <= NH:
            unit, inv = unit_rows(value)
            k_ref[part - 1] = unit
            inv_ref[part] = jnp.broadcast_to(inv, (length, DK))
        else:
            v_ref[part - 1 - NH] = value
    strict, pair, levels, eye = order_masks()
    column_index = iotas(SPAN, 8)[1]
    exit_grads = [None] * chunks
    grad = exit_ref[0]
    for chunk in reversed(range(chunks)):
        exit_grads[chunk] = grad
        grad = vec_ref[0, chunk, 3:4, GROUP - 1 : GROUP] * grad - mm(grad, t_in[0, chunk], 1, 1) + local_in[0, chunk]
    for chunk in reversed(range(chunks)):
        here = slice(chunk * GROUP, (chunk + 1) * GROUP)
        rows, columns = chunk_vectors(vec_ref, chunk)
        beta, scale, tail = columns[:, 1:2], columns[:, 3:4], columns[:, 4:5]
        keys = k_ref[:, here, :].reshape(SPAN, DK)
        values = v_ref[:, here, :].reshape(SPAN, DV)
        queries = q_ref[here, :]
        link = link_matrix(rows, columns)
        link_gram = jnp.where(strict, twice(link) * mm(keys, keys, 1, 1), 0.0)
        reading = link * mm(queries, keys, 1, 1)
        d_exit = exit_grads[chunk]
        solved = u_in[0, chunk]
        entry = s_in[0, chunk]
        d_mixed = d_mixed_in[here, :]
        tail_keys = tail * keys
        d_solved = mm(reading, d_mixed, 0, 0) + mm(tail_keys, d_exit, 1, 1)
        d_right = mm(x_in[0, chunk], d_solved, 0, 0)
        d_lower = jnp.where(strict, -mm(d_right, solved, 1, 1), 0.0)
        d_tail_keys = mm(solved, d_exit)
        d_right_entry = mm(d_right, entry)
        d_reading = mm(d_mixed, solved, 1, 1)
        d_query_entry = mm(d_mixed, entry)
        both_scale = -jnp.sum(d_right_entry * keys, axis=1, keepdims=True)
        lower_weight = d_lower * link_gram
        d_beta = (
            jnp.sum(d_right * values, axis=1, keepdims=True)
            + scale * both_scale
            + jnp.sum(lower_weight, axis=1, keepdims=True)
        )
        lower_moment = lower_weight * beta
        reading_moment = d_reading * reading
        d_gram = beta * twice(link) * d_lower
        d_gram = d_gram + jnp.transpose(d_gram)
        d_query_gram = link * d_reading
        d_keys = (
            tail * d_tail_keys
            - beta * scale * d_right_entry
            + mm(d_gram, keys)
            + mm(d_query_gram, queries, 0, 0)
        )
        d_queries = mm(d_query_gram, keys) + scale[:GROUP] * d_query_entry
        d_values = beta * d_right
        none = jnp.zeros((GROUP, 1), jnp.float32)
        d_gap = jnp.sum(lower_moment, axis=1, keepdims=True) + jnp.concatenate(
            [jnp.sum(reading_moment, axis=1, keepdims=True), none], axis=0
        )
        last = jnp.sum(jnp.sum(d_exit * entry.astype(jnp.float32), axis=1, keepdims=True), axis=0, keepdims=True)
        own_scale = jnp.sum(d_query_entry * queries, axis=1, keepdims=True)
        own_scale = own_scale + jnp.where(iotas(GROUP, 1)[0] == GROUP - 1, last, 0.0)
        d_scale = beta * both_scale + jnp.concatenate([own_scale, none], axis=0)
        d_tail = jnp.sum(d_tail_keys * keys, axis=1, keepdims=True)
        grads = jnp.where(
            column_index == 0,
            d_gap,
            jnp.where(
                column_index == 1,
                d_beta,
                jnp.where(column_index == 3, d_scale, jnp.where(column_index == 4, d_tail, 0.0)),
            ),
        )
        grads = jnp.transpose(grads)
        sums = jnp.sum(lower_moment, axis=0, keepdims=True) + jnp.sum(reading_moment, axis=0, keepdims=True)
        grads = grads - jnp.where(iotas(8, SPAN)[0] == 0, sums, 0.0)
        d_vec_out[0, chunk] = grads
        d_ref[0, here, :] = d_queries
        for step in range(NH):
            mine = slice(step * GROUP, (step + 1) * GROUP)
            d_ref[1 + step, here, :] = d_keys[mine]
            d_ref[1 + NH + step, here, :] = d_values[mine]
    outs = (dq_out, dk0_out, dk1_out, dv0_out, dv1_out)
    edges = (eq_out, ek0_out, ek1_out, ev0_out, ev1_out)
    tap_grads = (gq_out, gk0_out, gk1_out, gv0_out, gv1_out)
    z_ref[0:8, :] = jnp.zeros((8, DK), jnp.float32)
    z_ref[8 + length : 16 + length, :] = jnp.zeros((8, DK), jnp.float32)
    for part in range(1 + 2 * NH):
        grad = d_ref[part]
        if part <= NH:
            unit = q_ref[...] * DK ** 0.5 if part == 0 else k_ref[part - 1]
            if part == 0:
                grad = grad * DK ** (-0.5)
            grad = inv_ref[part] * (grad - unit * jnp.sum(grad * unit, axis=1, keepdims=True))
        pre = pre_ref[part]
        sig = jax.nn.sigmoid(pre)
        grad = grad * sig * (1.0 + pre * (1.0 - sig))
        tap = taps[part]
        total = grad * tap[0:1, :]
        edge = jnp.zeros((8, DK), jnp.float32)
        tap_rows = [jnp.sum(grad * channels[part][...], axis=0, keepdims=True)]
        for index in range(1, 4):
            shifted = grad * mask_ref[index - 1]
            tap_rows.append(
                jnp.sum(shifted * ext_ref[part, 8 - index : 8 - index + length, :], axis=0, keepdims=True)
            )
            z_ref[8 : 8 + length, :] = shifted * tap[index : index + 1, :]
            total = total + z_ref[8 + index : 8 + index + length, :]
            edge = edge + z_ref[index : index + 8, :]
        outs[part][...] = total.astype(outs[part].dtype)
        edges[part][0:8, :] = edge
        edges[part][8:16, :] = total[length - 8 :, :]
        tap_grads[part][...] = jnp.concatenate(tap_rows + [jnp.zeros((4, DK), jnp.float32)], axis=0)


MESH = pl.DeviceIdType.MESH
ZS = 4
STACK = (ZS, 2, 2, 2)
STAGES = 6


def place():
    dp, seq = lax.axis_index("dp"), lax.axis_index("seq")
    return dp // 4, (dp // 2) % 2, dp % 2, seq


def device_at(z, x, core, y):
    return (z * 4 + x * 2 + core, y)


def peers():
    z, x, core, y = place()
    ring = [device_at((z + step) % ZS, x, core, y) for step in range(1, ZS)]
    return ring + [device_at(z, 1 - x, core, y), device_at(z, x, core, 1 - y), device_at(z, x, 1 - core, y)]


def meet(devices):
    barrier = pltpu.get_barrier_semaphore()
    for device in devices:
        pl.semaphore_signal(barrier, inc=1, device_id=device, device_id_type=MESH)
    pl.semaphore_wait(barrier, len(devices))


class Gather:
    def __init__(self, source, target, x_first, sems, index):
        self.source, self.target, self.x_first = source, target, x_first
        self.send, self.recv, self.local = sems
        self.index = index
        self.copies = []

    def remote(self, source, target, slot):
        copy = pltpu.make_async_remote_copy(
            src_ref=source, dst_ref=target,
            send_sem=self.send.at[self.index, slot], recv_sem=self.recv.at[self.index, slot],
            device_id=peers()[slot], device_id_type=MESH,
        )
        copy.start()
        self.copies.append(copy)
        return copy

    def begin(self):
        z, x, core, y = place()
        mine = self.target(z, x, core, y)
        self.own = pltpu.make_async_copy(self.source, mine, self.local.at[self.index])
        self.own.start()
        self.waiting = [self.remote(self.source, mine, slot) for slot in range(ZS - 1)]

    def second(self):
        z, x, core, y = place()
        self.own.wait()
        for copy in self.waiting:
            copy.wait_recv()
        block = self.target(slice(None), x, core, y)
        self.waiting = [self.remote(block, block, ZS - 1 if self.x_first else ZS)]

    def third(self):
        z, x, core, y = place()
        self.waiting[0].wait_recv()
        every = slice(None)
        block = self.target(every, every, core, y) if self.x_first else self.target(every, x, core, every)
        self.waiting = [self.remote(block, block, ZS if self.x_first else ZS - 1)]

    def fourth(self):
        z, x, core, y = place()
        self.waiting[0].wait_recv()
        every = slice(None)
        block = self.target(every, every, core, every)
        self.waiting = [self.remote(block, block, ZS + 1)]

    def finish(self):
        self.waiting[0].wait_recv()
        for copy in self.copies:
            copy.wait_send()


def columns_of(ref, first, width):
    return lambda z, x, core, y: ref.at[z, x, core, y, :, pl.ds(first, width)]


def gather_project_kernel(
    x_ref, small_in, mix_in, out_in,
    mix_out, out_out, small_out, normed_ref, projected_out, gates_ref,
    mix_ref, small_ref, slab_ref,
    send, recv, local, store_mix, store_slab, store_small,
):
    sems = (send, recv, local)
    chunk = 1024
    half = chunk // 2
    items = []

    def add(source, first, width, ref, x_first):
        items.append(
            Gather(source.at[:, pl.ds(first, width)], columns_of(ref, first, width), x_first, sems, len(items))
        )
        return items[-1]

    ticks = []
    chunks = mix_in.shape[1] // chunk
    small = add(small_in, 0, small_in.shape[1], small_ref, True)
    for index in range(chunks):
        ticks.append([add(mix_in, index * chunk + part * half, half, mix_ref, part == 0) for part in range(2)])
    ticks.append([add(out_in, part * half, half, out_out, part == 0) for part in range(2)])
    ticks[0].insert(0, small)
    meet(peers())
    steps = (Gather.begin, Gather.second, Gather.third, Gather.fourth, Gather.finish)
    values = x_ref[...].astype(jnp.float32)
    scaled = values * lax.rsqrt(jnp.mean(values * values, axis=1, keepdims=True) + EPSILON)
    stores = []
    for tick in range(len(ticks) + len(steps) - 1):
        for step, action in reversed(list(enumerate(steps))):
            if 0 <= tick - step < len(ticks):
                for item in ticks[tick - step]:
                    action(item)
        done = tick - len(steps) + 1
        if done == 0:
            smalls = small_ref[...].reshape(-1, small_in.shape[1])
            gain = jnp.transpose(smalls.astype(jnp.float32))[24:25, :]
            normed_ref[...] = (scaled * gain).astype(jnp.bfloat16)
            gates_ref[...] = mm(normed_ref[...], smalls)
            stores.append(pltpu.make_async_copy(small_ref, small_out, store_small))
            stores[-1].start()
        if 0 <= done < chunks:
            here = pl.ds(done * chunk, chunk)
            keep = pltpu.make_async_copy(
                mix_ref.at[:, :, :, :, :, here], mix_out.at[:, :, :, :, :, here], store_mix.at[done]
            )
            keep.start()
            stores.append(keep)
            weights = mix_ref[:, :, :, :, :, done * chunk : (done + 1) * chunk].reshape(-1, chunk)
            slab = done % 2
            if done >= 2:
                slab_stores[done - 2].wait()
            else:
                slab_stores = [] if done == 0 else slab_stores
            slab_ref[slab] = mm(normed_ref[...], weights)
            slab_stores.append(
                pltpu.make_async_copy(slab_ref.at[slab], projected_out.at[:, here], store_slab.at[slab])
            )
            slab_stores[-1].start()
    for store in stores + slab_stores[-2:]:
        store.wait()


def gather_project_call(x, small, mix, out):
    length = x.shape[0]
    rows, width = mix.shape
    everywhere = pl.BlockSpec(memory_space=pl.ANY)
    held = pl.BlockSpec(memory_space=pltpu.VMEM)
    items = 3 + 2 * (width // 1024)
    full = STACK + (rows,)
    outs = pl.pallas_call(
        gather_project_kernel,
        out_shape=[
            jax.ShapeDtypeStruct(full + (width,), jnp.bfloat16),
            jax.ShapeDtypeStruct(full + (out.shape[1],), jnp.bfloat16),
            jax.ShapeDtypeStruct(full + (small.shape[1],), jnp.bfloat16),
            jax.ShapeDtypeStruct(x.shape, jnp.bfloat16),
            jax.ShapeDtypeStruct((length, width), jnp.float32),
            jax.ShapeDtypeStruct((length, small.shape[1]), jnp.float32),
        ],
        in_specs=[held, everywhere, everywhere, everywhere],
        out_specs=[everywhere, everywhere, everywhere, held, everywhere, held],
        scratch_shapes=[
            pltpu.VMEM(full + (width,), jnp.bfloat16),
            pltpu.VMEM(full + (small.shape[1],), jnp.bfloat16),
            pltpu.VMEM((2, length, 1024), jnp.float32),
            pltpu.SemaphoreType.DMA((items, STAGES)),
            pltpu.SemaphoreType.DMA((items, STAGES)),
            pltpu.SemaphoreType.DMA((items,)),
            pltpu.SemaphoreType.DMA((width // 1024,)),
            pltpu.SemaphoreType.DMA((2,)),
            pltpu.SemaphoreType.DMA,
        ],
        compiler_params=pltpu.CompilerParams(collective_id=1, has_side_effects=True, vmem_limit_bytes=LIMIT),
        cost_estimate=pl.CostEstimate(flops=2 * length * width * 1024, bytes_accessed=60_000_000, transcendentals=0),
    )(x, small, mix, out)
    return [part.reshape((-1,) + part.shape[5:]) if part.ndim == 6 else part for part in outs]


def from_behind(block, axis, distance):
    devices = range(lax.axis_size(axis))
    route = [(i - distance, i) for i in devices if i - distance in devices]
    return lax.ppermute(block, axis, route)


def rms_scale(values, scale_gain):
    return (
        values * lax.rsqrt(jnp.mean(values * values, axis=-1, keepdims=True) + EPSILON) * scale_gain
    )


def swiglu(gate_up):
    half_width = gate_up.shape[-1] // 2
    return jax.nn.silu(gate_up[:, :half_width]) * gate_up[:, half_width:]


def exchange(block, axis, bit):
    route = [(i, i ^ (1 << bit)) for i in range(lax.axis_size(axis))]
    return lax.ppermute(block, axis, route)


def axis_bits(axis):
    return lax.axis_size(axis).bit_length() - 1


def bit_orders():
    dp_bits = [("dp", bit) for bit in range(axis_bits("dp"))]
    seq_bits = [("seq", bit) for bit in range(axis_bits("seq"))]
    first, rest = dp_bits[:1], dp_bits[1:]
    inner = rest[:1] + seq_bits[:1]
    outer = rest[1:] + seq_bits[1:]
    return first + inner + outer, first + inner[::-1] + outer


def scatter_sum(part, order):
    dp_bits, seq_bits = axis_bits("dp"), axis_bits("seq")
    dims = [("dp", bit) for bit in reversed(range(dp_bits))] + [("seq", bit) for bit in reversed(range(seq_bits))]
    rows = part.shape[0] >> len(dims)
    part = part.reshape((2,) * len(dims) + (rows, part.shape[1]))
    for axis, bit in order:
        place = dims.index((axis, bit))
        dims.pop(place)
        mine = (lax.axis_index(axis) >> bit) & 1
        sent = lax.dynamic_index_in_dim(part, 1 - mine, place, keepdims=False)
        kept = lax.dynamic_index_in_dim(part, mine, place, keepdims=False)
        got = exchange(sent.astype(jnp.bfloat16), axis, bit)
        part = kept.astype(jnp.float32) + got.astype(jnp.float32)
    return part


def scatter_halves(part):
    half = part.shape[1] // 2
    orders = bit_orders()
    return jnp.concatenate(
        [scatter_sum(part[:, :half], orders[0]), scatter_sum(part[:, half:], orders[1])], axis=1
    )


def total_sum(block):
    for axis in ("dp", "seq"):
        for bit in range(axis_bits(axis)):
            block = block + exchange(block, axis, bit)
    return block


def gate_vectors(seg_now, seg_prev, gates_raw, decay_log):
    length = gates_raw.shape[0]
    chunks = length // GROUP
    beta = jax.nn.sigmoid(gates_raw[:, : NH * H]).reshape(chunks, GROUP, NH, H)
    rate = -jnp.exp(decay_log) * jax.nn.softplus(gates_raw[:, NH * H :])
    lower = jnp.tril(jnp.ones((GROUP, GROUP), jnp.float32))
    total = jnp.einsum("ts,csh->cth", lower, rate.reshape(chunks, GROUP, H), precision=HIGHEST)
    seg = seg_now.reshape(chunks, GROUP)
    before = jnp.concatenate([seg_prev.reshape(1), seg[:-1, -1]])
    scale = jnp.exp(total) * (seg == before[:, None]).astype(jnp.float32)[:, :, None]
    tail = jnp.exp(total[:, -1:, :] - total) * (seg == seg[:, -1:]).astype(jnp.float32)[:, :, None]

    def both(values):
        moved = jnp.moveaxis(values, 2, 0)
        return jnp.concatenate([moved, moved], axis=-1)

    beta_rows = beta.transpose(3, 0, 2, 1).reshape(H, chunks, SPAN)
    seg_rows = jnp.broadcast_to(jnp.concatenate([seg, seg], axis=1).astype(jnp.float32), (H, chunks, SPAN))
    none = jnp.zeros((H, chunks, SPAN), jnp.float32)
    return jnp.stack([both(total), beta_rows, seg_rows, both(scale), both(tail), none, none, none], axis=2)


def head_spec(shape):
    rank = len(shape)
    return pl.BlockSpec((1,) + shape, lambda head: (head,) + (0,) * rank)


def column_spec(rows, first):
    return pl.BlockSpec((rows, DK), lambda head: (0, first + head))


def whole_spec(shape):
    rank = len(shape)
    return pl.BlockSpec(shape, lambda head: (0,) * rank)


def per_head(shape, dtype=jnp.float32):
    return jax.ShapeDtypeStruct((H,) + shape, dtype)


def call(kernel, out_shape, in_specs, out_specs, scratch, flops, bytes_accessed):
    return pl.pallas_call(
        kernel,
        grid=(H,),
        out_shape=out_shape,
        in_specs=in_specs,
        out_specs=out_specs,
        scratch_shapes=scratch,
        compiler_params=pltpu.CompilerParams(
            dimension_semantics=("arbitrary",), vmem_limit_bytes=LIMIT
        ),
        cost_estimate=pl.CostEstimate(flops=flops, bytes_accessed=bytes_accessed, transcendentals=0),
    )


def conv_specs(length):
    return (
        [column_spec(length, H * part) for part in range(1 + 2 * NH)]
        + [column_spec(8, H * part) for part in range(1 + 2 * NH)] * 2
        + [whole_spec((3, length, DK))]
    )


def forward_call(projected, border, taps, masks, vec, start):
    length = projected.shape[0]
    chunks = length // GROUP
    square = (chunks, SPAN, DK)
    outs = [
        (square, jnp.bfloat16),
        (square, jnp.bfloat16),
        (square, jnp.float32),
        (square, jnp.bfloat16),
        (square, jnp.float32),
        ((chunks, GROUP, DK), jnp.bfloat16),
        ((chunks, GROUP, DV), jnp.float32),
        ((DV, DK), jnp.float32),
    ]
    parts = 1 + 2 * NH
    return call(
        forward_kernel,
        [per_head(*out) for out in outs],
        conv_specs(length) + [head_spec((chunks, 8, SPAN)), head_spec((DV, DK))],
        [head_spec(out[0]) for out in outs],
        [
            pltpu.VMEM((length + 8, DK), jnp.float32),
            pltpu.VMEM((length, DK), jnp.float32),
            pltpu.VMEM((NH, length, DK), jnp.float32),
            pltpu.VMEM((NH, length, DK), jnp.float32),
        ],
        H * chunks * 20 * 2 * SPAN**3 * 4,
        H * chunks * 8 * SPAN * DK * 4,
    )(*[projected] * parts, *[border] * parts, *[taps] * parts, masks, vec, start)


def chain_call(vec, transfer, start):
    chunks = transfer.shape[1]
    return call(
        chain_kernel,
        per_head((DV, DK)),
        [head_spec((chunks, 8, SPAN)), head_spec((chunks, SPAN, DK)), head_spec((DV, DK))],
        head_spec((DV, DK)),
        [],
        H * chunks * 2 * SPAN**3,
        H * chunks * SPAN * DK * 4,
    )(vec, transfer, start)


def readout_call(vec, key_part, value_part, transfer, inject, out_keys, out_values, entry, projected, gain):
    length = projected.shape[0]
    chunks = length // GROUP
    square = head_spec((chunks, SPAN, DK))
    half = head_spec((chunks, GROUP, DK))
    return call(
        readout_kernel,
        [
            jax.ShapeDtypeStruct((length, H * DV), jnp.bfloat16),
            jax.ShapeDtypeStruct((length, H * DV), jnp.float32),
            per_head((chunks, SPAN, DK), jnp.bfloat16),
            per_head((chunks, SPAN, DK), jnp.bfloat16),
        ],
        [
            head_spec((chunks, 8, SPAN)), square, square, square, square, half, half,
            head_spec((DV, DK)), column_spec(length, (1 + 2 * NH) * H), whole_spec((8, DV)),
        ],
        [column_spec(length, 0), column_spec(length, 0), square, square],
        [],
        H * chunks * 4 * 2 * SPAN**3 * 4,
        H * chunks * 8 * SPAN * DK * 4,
    )(vec, key_part, value_part, transfer, inject, out_keys, out_values, entry, projected, gain)


def readout_back_call(vec, transfer, out_keys, mixed, projected, gain, d_gated, start):
    length = projected.shape[0]
    chunks = length // GROUP
    square = head_spec((chunks, SPAN, DK))
    return call(
        readout_back_kernel,
        [
            jax.ShapeDtypeStruct((length, H * DV), jnp.bfloat16),
            jax.ShapeDtypeStruct((length, H * DV), jnp.bfloat16),
            per_head((chunks, SPAN, DK)),
            per_head((DV, DK)),
            per_head((8, DV)),
        ],
        [
            head_spec((chunks, 8, SPAN)), square, head_spec((chunks, GROUP, DK)),
            column_spec(length, 0), column_spec(length, (1 + 2 * NH) * H), whole_spec((8, DV)),
            column_spec(length, 0), head_spec((DV, DK)),
        ],
        [column_spec(length, 0), column_spec(length, 0), square, head_spec((DV, DK)), head_spec((8, DV))],
        [],
        H * chunks * 4 * 2 * SPAN**3 * 4,
        H * chunks * 8 * SPAN * DK * 4,
    )(vec, transfer, out_keys, mixed, projected, gain, d_gated, start)


def backward_call(projected, border, taps, masks, vec, transfer, inverse, solved, entries, d_mixed, local, exit_grad):
    length = projected.shape[0]
    chunks = length // GROUP
    parts = 1 + 2 * NH
    square = head_spec((chunks, SPAN, DK))
    outs = (
        [jax.ShapeDtypeStruct((length, H * DK), jnp.bfloat16)] * parts
        + [jax.ShapeDtypeStruct((16, H * DK), jnp.float32)] * parts
        + [jax.ShapeDtypeStruct((8, H * DK), jnp.float32)] * parts
        + [per_head((chunks, 8, SPAN))]
    )
    out_specs = (
        [column_spec(length, 0)] * parts
        + [column_spec(16, 0)] * parts
        + [column_spec(8, 0)] * parts
        + [head_spec((chunks, 8, SPAN))]
    )
    tall = pltpu.VMEM((parts, length, DK), jnp.float32)
    return call(
        backward_kernel,
        outs,
        conv_specs(length)
        + [head_spec((chunks, 8, SPAN)), square, square, square, square, column_spec(length, 0), square, head_spec((DV, DK))],
        out_specs,
        [
            pltpu.VMEM((parts, length + 8, DK), jnp.float32),
            tall,
            pltpu.VMEM((length, DK), jnp.float32),
            pltpu.VMEM((NH, length, DK), jnp.float32),
            pltpu.VMEM((NH, length, DK), jnp.float32),
            pltpu.VMEM((1 + NH, length, DK), jnp.float32),
            tall,
            pltpu.VMEM((length + 16, DK), jnp.float32),
        ],
        H * chunks * 14 * 2 * SPAN**3 * 4,
        H * chunks * 16 * SPAN * DK * 4,
    )(*[projected] * parts, *[border] * parts, *[taps] * parts, masks, vec, transfer, inverse, solved, entries, d_mixed, local, exit_grad)


def gather(block, dim=0):
    return lax.all_gather(block, ("dp", "seq"), axis=dim, tiled=True)


def on_device(
    block_input, doc_starts, norm_in, w_mix, w_small, conv_w, decay_log, norm_out,
    w_out, norm_mlp, w_gu, w_down, cotangent,
):
    row_count, seg_len, width = block_input.shape
    tap_count = conv_w.shape[0]
    key_width = H * DK
    parts = 1 + 2 * NH
    seqs = lax.axis_size("seq")
    residual_in = block_input.astype(jnp.float32).reshape(seg_len, width)
    smalls, rows = w_small.shape[1], w_mix.shape[0]
    fast = lax.axis_size("dp") == 4 * ZS and seqs == 2 and rows % 16 == 0
    if fast:
        small = jnp.concatenate(
            [w_small, norm_in[:, None], norm_mlp[:, None], conv_w.reshape(tap_count, rows, -1).transpose(1, 2, 0).reshape(rows, -1)], axis=1
        )
        small = jnp.concatenate([small, jnp.zeros((rows, DK - small.shape[1]), small.dtype)], axis=1)
        mix_all, out_all, small_pack, normed_low, projected, gates_raw = gather_project_call(
            block_input.reshape(seg_len, width), small, w_mix, w_out
        )
        small_all = small_pack[:, :smalls]
        gates_raw = gates_raw[:, :smalls]
        norm_in_all = small_pack[:, smalls].astype(jnp.float32)
        norm_mlp_all = small_pack[:, smalls + 1].astype(jnp.float32)
        per_row = conv_w.shape[1] // rows
        conv_all = small_pack[:, smalls + 2 : smalls + 2 + per_row * tap_count]
        conv_all = conv_all.reshape(-1, tap_count).transpose(1, 0)
        normed, norm_in_back = jax.vjp(rms_scale, residual_in, norm_in_all)
    else:
        mix_all, small_all, conv_all, out_all = gather(w_mix), gather(w_small), gather(conv_w, 1), gather(w_out)
        norm_in_all = gather(norm_in).astype(jnp.float32)
        norm_mlp_all = gather(norm_mlp).astype(jnp.float32)
        normed, norm_in_back = jax.vjp(rms_scale, residual_in, norm_in_all)
        normed_low = normed.astype(jnp.bfloat16)
        projected = jnp.dot(normed_low, mix_all, preferred_element_type=jnp.float32)
        gates_raw = jnp.dot(normed_low, small_all, preferred_element_type=jnp.float32)
    gu_all, down_all = gather(w_gu), gather(w_down)
    border = from_behind(projected[seg_len - tap_count + 1 :, : parts * key_width], "seq", 1)
    border = jnp.concatenate([jnp.zeros((9 - tap_count, parts * key_width), jnp.float32), border], axis=0)
    positions = lax.axis_index("seq") * seg_len + jnp.arange(1 - tap_count, seg_len, dtype=jnp.int32)
    seg_ext = jnp.sum((positions[:, None] >= doc_starts[0][None, :]).astype(jnp.int32), axis=1)
    seg_ext = jnp.where(positions < 0, -1, seg_ext)
    seg_now = seg_ext[tap_count - 1 :]
    masks = jnp.stack(
        [seg_ext[tap_count - 1 - tap : tap_count - 1 - tap + seg_len] == seg_now for tap in range(1, tap_count)]
    ).astype(jnp.float32)
    masks = jnp.broadcast_to(masks[:, :, None], (tap_count - 1, seg_len, DK))
    taps = jnp.concatenate([conv_all.astype(jnp.float32), jnp.zeros((8 - tap_count, parts * key_width), jnp.float32)], axis=0)
    vec, vec_back = jax.vjp(
        partial(gate_vectors, seg_now, seg_ext[tap_count - 2]), gates_raw, decay_log.astype(jnp.float32)
    )
    zero_state = jnp.zeros((H, DV, DK), jnp.float32)
    inverse, key_part, value_part, transfer, inject, out_keys, out_values, final_state = forward_call(
        projected, border, taps, masks, vec, zero_state
    )
    entry = zero_state
    device_transfer = None
    if seqs > 2:
        eye = jnp.broadcast_to(jnp.eye(DK, dtype=jnp.float32), (H, DK, DK))
        device_transfer = chain_call(vec, transfer, eye)
    for turn in range(seqs - 1):
        leaving = final_state
        if turn > 0:
            leaving = leaving + jnp.einsum("hvk,hkl->hvl", entry, device_transfer, precision=HIGHEST)
        entry = from_behind(leaving.astype(jnp.bfloat16), "seq", 1).astype(jnp.float32)
    gain = jnp.broadcast_to(norm_out.astype(jnp.float32)[None, :], (8, DV))
    normed_out_low, mixed, solved, entries = readout_call(
        vec, key_part, value_part, transfer, inject, out_keys, out_values, entry, projected, gain
    )
    hidden = residual_in + jnp.dot(normed_out_low, out_all, preferred_element_type=jnp.float32)
    mlp_in, norm_mlp_back = jax.vjp(rms_scale, hidden, norm_mlp_all)
    mlp_in_low = mlp_in.astype(jnp.bfloat16)
    gate_up = jnp.dot(mlp_in_low, gu_all, preferred_element_type=jnp.float32)
    activated, act_back = jax.vjp(swiglu, gate_up)
    activated_low = activated.astype(jnp.bfloat16)
    result = hidden + jnp.dot(activated_low, down_all, preferred_element_type=jnp.float32)
    block_output = result.astype(jnp.bfloat16).reshape(block_input.shape)

    d_result_low = cotangent.reshape(seg_len, width)
    d_result = d_result_low.astype(jnp.float32)
    grad_down = jnp.einsum("nf,nd->fd", activated_low, d_result_low, preferred_element_type=jnp.float32)
    d_activated = jnp.einsum("nd,fd->nf", d_result_low, down_all, preferred_element_type=jnp.float32)
    (d_gate_up,) = act_back(d_activated)
    d_gate_low = d_gate_up.astype(jnp.bfloat16)
    grad_gu = jnp.einsum("nd,nf->df", mlp_in_low, d_gate_low, preferred_element_type=jnp.float32)
    d_mlp_in = jnp.einsum("nf,df->nd", d_gate_low, gu_all, preferred_element_type=jnp.float32)
    d_hidden_norm, grad_norm_mlp = norm_mlp_back(d_mlp_in)
    d_hidden = d_result + d_hidden_norm
    grad_gu = scatter_halves(grad_gu.astype(jnp.bfloat16))
    grad_down = scatter_halves(grad_down.astype(jnp.bfloat16))

    d_mixer_low = d_hidden.astype(jnp.bfloat16)
    grad_out = jnp.einsum("nh,nd->hd", normed_out_low, d_mixer_low, preferred_element_type=jnp.float32)
    grad_out = scatter_halves(grad_out.astype(jnp.bfloat16))
    d_normed_out = jnp.einsum("nd,hd->nh", d_mixer_low, out_all, preferred_element_type=jnp.float32)
    d_mixed, d_out_gate, local, own_entry, gain_parts = readout_back_call(
        vec, transfer, out_keys, mixed, projected, gain, d_normed_out, zero_state
    )
    grad_norm_out = jnp.sum(gain_parts[:, 0, :], axis=0)
    exit_grad = zero_state
    for turn in range(seqs - 1):
        leaving = own_entry
        if turn > 0:
            leaving = leaving + jnp.einsum("hvl,hkl->hvk", exit_grad, device_transfer, precision=HIGHEST)
        exit_grad = from_behind(leaving.astype(jnp.bfloat16), "seq", -1).astype(jnp.float32)
    backs = backward_call(
        projected, border, taps, masks, vec, transfer, inverse, solved, entries, d_mixed, local, exit_grad
    )
    d_columns, edges, tap_grads, d_vec = backs[:parts], backs[parts : 2 * parts], backs[2 * parts : 3 * parts], backs[-1]
    edge = jnp.concatenate(edges, axis=1)
    returned = from_behind(edge[9 - tap_count : 8].astype(jnp.bfloat16), "seq", -1).astype(jnp.float32)
    fixed = (edge[17 - tap_count :] + returned).astype(jnp.bfloat16)
    d_projected = jnp.concatenate(list(d_columns) + [d_out_gate], axis=1)
    d_projected = lax.dynamic_update_slice(d_projected, fixed, (seg_len - tap_count + 1, 0))
    d_gates_raw, grad_decay = vec_back(d_vec)
    d_gates_low = d_gates_raw.astype(jnp.bfloat16)
    grad_mix = jnp.einsum("nd,nc->dc", normed_low, d_projected, preferred_element_type=jnp.float32)
    grad_mix = scatter_halves(grad_mix.astype(jnp.bfloat16))
    grad_small = jnp.einsum("nd,nc->dc", normed_low, d_gates_low, preferred_element_type=jnp.float32)
    d_normed = jnp.einsum("nc,dc->nd", d_projected, mix_all, preferred_element_type=jnp.float32)
    d_normed = d_normed + jnp.einsum("nc,dc->nd", d_gates_low, small_all, preferred_element_type=jnp.float32)
    d_input_norm, grad_norm_in = norm_in_back(d_normed)
    input_grad = (d_hidden + d_input_norm).astype(jnp.bfloat16).reshape(block_input.shape)

    grad_conv = jnp.concatenate(tap_grads, axis=1)[:tap_count]
    devices = lax.axis_size("dp") * seqs
    conv_rows = grad_conv.reshape(tap_count, devices, -1).transpose(1, 0, 2).reshape(width, -1)
    packed = jnp.concatenate([grad_small, grad_norm_in[:, None], grad_norm_mlp[:, None], conv_rows], axis=1)
    packed = jnp.concatenate([packed, jnp.zeros((width, 128 - packed.shape[1]), jnp.float32)], axis=1)
    packed = scatter_sum(packed, bit_orders()[0])
    smalls = grad_small.shape[1]
    grad_small = packed[:, :smalls]
    grad_norm_in, grad_norm_mlp = packed[:, smalls], packed[:, smalls + 1]
    grad_conv = packed[:, smalls + 2 : smalls + 2 + conv_rows.shape[1]].reshape(tap_count, -1)
    sums = total_sum(jnp.concatenate([grad_norm_out, grad_decay]))
    grad_norm_out, grad_decay = sums[:DV], sums[DV:]
    return (
        block_output, input_grad, grad_norm_in, grad_mix, grad_small, grad_conv, grad_decay,
        grad_norm_out, grad_out, grad_norm_mlp, grad_gu, grad_down,
    )


def solution(mesh):
    sharded = ("dp", "seq")
    in_specs = (
        P("dp", "seq", None), P("dp", None), P(sharded), P(sharded, None), P(sharded, None),
        P(None, sharded), P(), P(), P(sharded, None), P(sharded), P(sharded, None),
        P(sharded, None), P("dp", "seq", None),
    )
    out_specs = (
        P("dp", "seq", None), P("dp", "seq", None), P(sharded), P(sharded, None), P(sharded, None),
        P(None, sharded), P(), P(), P(sharded, None), P(sharded), P(sharded, None), P(sharded, None),
    )
    return jax.shard_map(
        on_device, mesh=mesh, in_specs=in_specs, out_specs=out_specs, check_vma=False
    )
```

```python
from functools import partial

import jax
import jax.numpy as jnp
from jax import lax
from jax.experimental import pallas as pl
from jax.experimental.pallas import tpu as pltpu
from jax.sharding import PartitionSpec as P

H = 8
DK = 128
DV = 128
NH = 2
GROUP = 64
SPAN = NH * GROUP
LEVELS = 6
EPSILON = 1e-06
HIGHEST = lax.Precision.HIGHEST
LIMIT = 50 * 1024 * 1024


def mm(left, right, left_dim=1, right_dim=0):
    return lax.dot_general(
        left.astype(jnp.bfloat16),
        right.astype(jnp.bfloat16),
        (((left_dim,), (right_dim,)), ((), ())),
        preferred_element_type=jnp.float32,
    )


def halves_of(values):
    high = values.astype(jnp.bfloat16)
    return high, (values - high.astype(jnp.float32)).astype(jnp.bfloat16)


def mm3(left, right, left_dim=1, right_dim=0):
    left_high, left_low = halves_of(left)
    right_high, right_low = halves_of(right)
    wide = right.shape[1 - right_dim]
    lefts = jnp.concatenate([left_high, left_low], axis=left_dim)
    rights = jnp.concatenate(
        [
            jnp.concatenate([right_high, right_high], axis=right_dim),
            jnp.concatenate([right_low, jnp.zeros_like(right_low)], axis=right_dim),
        ],
        axis=1 - right_dim,
    )
    both = mm(lefts, rights, left_dim, right_dim)
    return both[:, :wide] + both[:, wide:]


def iotas(rows, columns):
    return (
        lax.broadcasted_iota(jnp.int32, (rows, columns), 0),
        lax.broadcasted_iota(jnp.int32, (rows, columns), 1),
    )


def order_masks():
    row, column = iotas(SPAN, SPAN)
    row_tok, column_tok = row % GROUP, column % GROUP
    row_step, column_step = row // GROUP, column // GROUP
    pair = (row_tok == column_tok) & (row_step > column_step)
    strict = (row_tok > column_tok) | pair
    levels = []
    for level in range(LEVELS):
        row_half, column_half = row_tok >> level, column_tok >> level
        levels.append((row_half == column_half + 1) & (row_half % 2 == 1))
    eye = jnp.where(row == column, 1.0, 0.0)
    return strict, pair, levels, eye


def unit_inverses(lowers, pair, levels, eye):
    inverses = [eye - jnp.where(pair, lower, 0.0) for lower in lowers]
    for level in levels:
        parts = [mm3(jnp.where(level, lower, 0.0), inv) for lower, inv in zip(lowers, inverses)]
        inverses = [inv - mm3(inv, part) for part, inv in zip(parts, inverses)]
    return inverses


def silu_pair(values):
    sig = jax.nn.sigmoid(values)
    return values * sig, sig


def conv_block(channel_ref, border_ref, tap_ref, mask_ref, ext_ref):
    length = channel_ref.shape[0]
    ext_ref[0:8, :] = border_ref[...]
    ext_ref[8 : 8 + length, :] = channel_ref[...]
    summed = channel_ref[...] * tap_ref[0:1, :]
    for tap in range(1, 4):
        summed = summed + ext_ref[8 - tap : 8 - tap + length, :] * tap_ref[tap : tap + 1, :] * mask_ref[tap - 1]
    return summed


def unit_rows(values):
    inv = lax.rsqrt(jnp.sum(values * values, axis=1, keepdims=True) + EPSILON)
    return values * inv, inv


def chunk_vectors(vec_ref, chunk):
    rows = vec_ref[0, chunk]
    columns = jnp.transpose(rows)
    return rows, columns


def link_matrix(rows, columns):
    row, column = iotas(GROUP, SPAN)
    linked = (columns[:GROUP, 2:3] == rows[2:3, :]) & (row >= column % GROUP)
    return jnp.exp(jnp.where(linked, columns[:GROUP, 0:1] - rows[0:1, :], -1e30))


def twice(values):
    return jnp.concatenate([values, values], axis=0)


def forward_kernel(
    q_in, k0_in, k1_in, v0_in, v1_in,
    bq, bk0, bk1, bv0, bv1,
    tq, tk0, tk1, tv0, tv1,
    mask_ref, vec_ref, start_ref,
    x_out, w_out, u_out, t_out, i_out, ok_out, o_out, state_out,
    ext_ref, q_ref, k_ref, v_ref,
):
    length = q_in.shape[0]
    chunks = length // GROUP
    conv = []
    for channel, border, tap in (
        (q_in, bq, tq), (k0_in, bk0, tk0), (k1_in, bk1, tk1), (v0_in, bv0, tv0), (v1_in, bv1, tv1),
    ):
        conv.append(silu_pair(conv_block(channel, border, tap, mask_ref, ext_ref))[0])
    q_ref[...] = unit_rows(conv[0])[0] * DK ** (-0.5)
    for step in range(NH):
        k_ref[step] = unit_rows(conv[1 + step])[0]
        v_ref[step] = conv[1 + NH + step]
    strict, pair, levels, eye = order_masks()
    items = []
    lowers = []
    for chunk in range(chunks):
        here = slice(chunk * GROUP, (chunk + 1) * GROUP)
        rows, columns = chunk_vectors(vec_ref, chunk)
        keys = k_ref[:, here, :].reshape(SPAN, DK)
        values = v_ref[:, here, :].reshape(SPAN, DV)
        queries = q_ref[here, :]
        link = link_matrix(rows, columns)
        lower = jnp.where(strict, columns[:, 1:2] * twice(link) * mm3(keys, keys, 1, 1), 0.0)
        reading = link * mm3(queries, keys, 1, 1)
        lowers.append(lower)
        items.append((rows, columns, keys, values, queries, reading))
    inverses = unit_inverses(lowers, pair, levels, eye)
    state = start_ref[0]
    for chunk in range(chunks):
        rows, columns, keys, values, queries, reading = items[chunk]
        inverse = inverses[chunk]
        here = slice(chunk * GROUP, (chunk + 1) * GROUP)
        beta, scale, tail = columns[:, 1:2], columns[:, 3:4], columns[:, 4:5]
        key_part = mm3(inverse, beta * scale * keys)
        value_part = mm3(inverse, beta * values)
        tail_keys = tail * keys
        transfer = mm3(key_part, tail_keys, 0, 0)
        inject = mm3(value_part, tail_keys, 0, 0)
        x_out[0, chunk] = inverse.astype(x_out.dtype)
        w_out[0, chunk] = key_part.astype(w_out.dtype)
        u_out[0, chunk] = value_part.astype(u_out.dtype)
        t_out[0, chunk] = transfer.astype(t_out.dtype)
        i_out[0, chunk] = inject
        ok_out[0, chunk] = (columns[:GROUP, 3:4] * queries - mm3(reading, key_part)).astype(ok_out.dtype)
        o_out[0, chunk] = mm3(reading, value_part)
        state = rows[3:4, GROUP - 1 : GROUP] * state - mm3(state, transfer) + inject
    state_out[0] = state


def chain_kernel(vec_ref, t_in, start_ref, state_out):
    chunks = t_in.shape[1]
    state = start_ref[0]
    for chunk in range(chunks):
        state = vec_ref[0, chunk, 3:4, GROUP - 1 : GROUP] * state - mm3(state, t_in[0, chunk])
    state_out[0] = state


def readout_kernel(vec_ref, w_in, u_in, t_in, i_in, ok_in, o_in, entry_ref, gate_ref, gain_ref, gated_out, mixed_out, u_out, s_out):
    chunks = w_in.shape[1]
    state = entry_ref[0]
    states = []
    for chunk in range(chunks):
        states.append(state)
        state = vec_ref[0, chunk, 3:4, GROUP - 1 : GROUP] * state - mm3(state, t_in[0, chunk]) + i_in[0, chunk]
    for chunk in range(chunks):
        here = slice(chunk * GROUP, (chunk + 1) * GROUP)
        state = states[chunk]
        s_out[0, chunk] = state
        u_out[0, chunk] = (u_in[0, chunk].astype(jnp.float32) - mm3(w_in[0, chunk], state, 1, 1)).astype(u_out.dtype)
        mixed = o_in[0, chunk] + mm3(ok_in[0, chunk], state, 1, 1)
        mixed_out[here, :] = mixed
        inv = lax.rsqrt(jnp.mean(mixed * mixed, axis=1, keepdims=True) + EPSILON)
        gate = silu_pair(gate_ref[here, :])[0]
        gated_out[here, :] = (mixed * inv * gain_ref[0:1, :] * gate).astype(gated_out.dtype)


def readout_back_kernel(vec_ref, t_in, ok_in, mixed_in, gate_ref, gain_ref, d_ref, start_ref, d_mixed_out, d_gate_out, local_out, state_out, gain_out):
    chunks = t_in.shape[1]
    gain = gain_ref[0:1, :]
    gain_grad = jnp.zeros((1, DV), jnp.float32)
    locals_ = []
    for chunk in range(chunks):
        here = slice(chunk * GROUP, (chunk + 1) * GROUP)
        mixed = mixed_in[here, :]
        inv = lax.rsqrt(jnp.mean(mixed * mixed, axis=1, keepdims=True) + EPSILON)
        unit = mixed * inv
        gate = gate_ref[here, :]
        open_, sig = silu_pair(gate)
        d_gated = d_ref[here, :]
        d_scaled = d_gated * open_
        d_gate_out[here, :] = (d_gated * unit * gain * sig * (1.0 + gate * (1.0 - sig))).astype(d_gate_out.dtype)
        gain_grad = gain_grad + jnp.sum(d_scaled * unit, axis=0, keepdims=True)
        d_unit = d_scaled * gain
        d_mixed = inv * (d_unit - unit * jnp.mean(d_unit * unit, axis=1, keepdims=True))
        d_mixed_low = d_mixed
        d_mixed_out[here, :] = d_mixed_low
        local = mm3(d_mixed_low, ok_in[0, chunk], 0, 0)
        local_out[0, chunk] = local
        locals_.append(local)
    gain_out[0] = jnp.broadcast_to(gain_grad, (8, DV))
    state = start_ref[0]
    for chunk in reversed(range(chunks)):
        state = vec_ref[0, chunk, 3:4, GROUP - 1 : GROUP] * state - mm3(state, t_in[0, chunk], 1, 1) + locals_[chunk]
    state_out[0] = state


def backward_kernel(
    q_in, k0_in, k1_in, v0_in, v1_in,
    bq, bk0, bk1, bv0, bv1,
    tq, tk0, tk1, tv0, tv1,
    mask_ref, vec_ref, t_in, x_in, u_in, s_in, d_mixed_in, local_in, exit_ref,
    dq_out, dk0_out, dk1_out, dv0_out, dv1_out,
    eq_out, ek0_out, ek1_out, ev0_out, ev1_out,
    gq_out, gk0_out, gk1_out, gv0_out, gv1_out,
    d_vec_out,
    ext_ref, pre_ref, q_ref, k_ref, v_ref, inv_ref, d_ref, z_ref,
):
    length = q_in.shape[0]
    chunks = length // GROUP
    channels = (q_in, k0_in, k1_in, v0_in, v1_in)
    taps = (tq, tk0, tk1, tv0, tv1)
    for part, (channel, border, tap) in enumerate(zip(channels, (bq, bk0, bk1, bv0, bv1), taps)):
        pre = conv_block(channel, border, tap, mask_ref, ext_ref.at[part])
        pre_ref[part] = pre
        value = silu_pair(pre)[0]
        if part == 0:
            unit, inv = unit_rows(value)
            q_ref[...] = unit * DK ** (-0.5)
            inv_ref[0] = jnp.broadcast_to(inv, (length, DK))
        elif part <= NH:
            unit, inv = unit_rows(value)
            k_ref[part - 1] = unit
            inv_ref[part] = jnp.broadcast_to(inv, (length, DK))
        else:
            v_ref[part - 1 - NH] = value
    strict, pair, levels, eye = order_masks()
    column_index = iotas(SPAN, 8)[1]
    exit_grads = [None] * chunks
    grad = exit_ref[0]
    for chunk in reversed(range(chunks)):
        exit_grads[chunk] = grad
        grad = vec_ref[0, chunk, 3:4, GROUP - 1 : GROUP] * grad - mm3(grad, t_in[0, chunk], 1, 1) + local_in[0, chunk]
    for chunk in reversed(range(chunks)):
        here = slice(chunk * GROUP, (chunk + 1) * GROUP)
        rows, columns = chunk_vectors(vec_ref, chunk)
        beta, scale, tail = columns[:, 1:2], columns[:, 3:4], columns[:, 4:5]
        keys = k_ref[:, here, :].reshape(SPAN, DK)
        values = v_ref[:, here, :].reshape(SPAN, DV)
        queries = q_ref[here, :]
        link = link_matrix(rows, columns)
        link_gram = jnp.where(strict, twice(link) * mm3(keys, keys, 1, 1), 0.0)
        reading = link * mm3(queries, keys, 1, 1)
        d_exit = exit_grads[chunk]
        solved = u_in[0, chunk]
        entry = s_in[0, chunk]
        d_mixed = d_mixed_in[here, :]
        tail_keys = tail * keys
        d_solved = mm3(reading, d_mixed, 0, 0) + mm3(tail_keys, d_exit, 1, 1)
        d_right = mm3(x_in[0, chunk], d_solved, 0, 0)
        d_lower = jnp.where(strict, -mm3(d_right, solved, 1, 1), 0.0)
        d_tail_keys = mm3(solved, d_exit)
        d_right_entry = mm3(d_right, entry)
        d_reading = mm3(d_mixed, solved, 1, 1)
        d_query_entry = mm3(d_mixed, entry)
        both_scale = -jnp.sum(d_right_entry * keys, axis=1, keepdims=True)
        lower_weight = d_lower * link_gram
        d_beta = (
            jnp.sum(d_right * values, axis=1, keepdims=True)
            + scale * both_scale
            + jnp.sum(lower_weight, axis=1, keepdims=True)
        )
        lower_moment = lower_weight * beta
        reading_moment = d_reading * reading
        d_gram = beta * twice(link) * d_lower
        d_gram = d_gram + jnp.transpose(d_gram)
        d_query_gram = link * d_reading
        d_keys = (
            tail * d_tail_keys
            - beta * scale * d_right_entry
            + mm3(d_gram, keys)
            + mm3(d_query_gram, queries, 0, 0)
        )
        d_queries = mm3(d_query_gram, keys) + scale[:GROUP] * d_query_entry
        d_values = beta * d_right
        none = jnp.zeros((GROUP, 1), jnp.float32)
        d_gap = jnp.sum(lower_moment, axis=1, keepdims=True) + jnp.concatenate(
            [jnp.sum(reading_moment, axis=1, keepdims=True), none], axis=0
        )
        last = jnp.sum(jnp.sum(d_exit * entry.astype(jnp.float32), axis=1, keepdims=True), axis=0, keepdims=True)
        own_scale = jnp.sum(d_query_entry * queries, axis=1, keepdims=True)
        own_scale = own_scale + jnp.where(iotas(GROUP, 1)[0] == GROUP - 1, last, 0.0)
        d_scale = beta * both_scale + jnp.concatenate([own_scale, none], axis=0)
        d_tail = jnp.sum(d_tail_keys * keys, axis=1, keepdims=True)
        grads = jnp.where(
            column_index == 0,
            d_gap,
            jnp.where(
                column_index == 1,
                d_beta,
                jnp.where(column_index == 3, d_scale, jnp.where(column_index == 4, d_tail, 0.0)),
            ),
        )
        grads = jnp.transpose(grads)
        sums = jnp.sum(lower_moment, axis=0, keepdims=True) + jnp.sum(reading_moment, axis=0, keepdims=True)
        grads = grads - jnp.where(iotas(8, SPAN)[0] == 0, sums, 0.0)
        d_vec_out[0, chunk] = grads
        d_ref[0, here, :] = d_queries
        for step in range(NH):
            mine = slice(step * GROUP, (step + 1) * GROUP)
            d_ref[1 + step, here, :] = d_keys[mine]
            d_ref[1 + NH + step, here, :] = d_values[mine]
    outs = (dq_out, dk0_out, dk1_out, dv0_out, dv1_out)
    edges = (eq_out, ek0_out, ek1_out, ev0_out, ev1_out)
    tap_grads = (gq_out, gk0_out, gk1_out, gv0_out, gv1_out)
    z_ref[0:8, :] = jnp.zeros((8, DK), jnp.float32)
    z_ref[8 + length : 16 + length, :] = jnp.zeros((8, DK), jnp.float32)
    for part in range(1 + 2 * NH):
        grad = d_ref[part]
        if part <= NH:
            unit = q_ref[...] * DK ** 0.5 if part == 0 else k_ref[part - 1]
            if part == 0:
                grad = grad * DK ** (-0.5)
            grad = inv_ref[part] * (grad - unit * jnp.sum(grad * unit, axis=1, keepdims=True))
        pre = pre_ref[part]
        sig = jax.nn.sigmoid(pre)
        grad = grad * sig * (1.0 + pre * (1.0 - sig))
        tap = taps[part]
        total = grad * tap[0:1, :]
        edge = jnp.zeros((8, DK), jnp.float32)
        tap_rows = [jnp.sum(grad * channels[part][...], axis=0, keepdims=True)]
        for index in range(1, 4):
            shifted = grad * mask_ref[index - 1]
            tap_rows.append(
                jnp.sum(shifted * ext_ref[part, 8 - index : 8 - index + length, :], axis=0, keepdims=True)
            )
            z_ref[8 : 8 + length, :] = shifted * tap[index : index + 1, :]
            total = total + z_ref[8 + index : 8 + index + length, :]
            edge = edge + z_ref[index : index + 8, :]
        outs[part][...] = total.astype(outs[part].dtype)
        edges[part][0:8, :] = edge
        edges[part][8:16, :] = total[length - 8 :, :]
        tap_grads[part][...] = jnp.concatenate(tap_rows + [jnp.zeros((4, DK), jnp.float32)], axis=0)


MESH = pl.DeviceIdType.MESH
ZS = 4
STACK = (ZS, 2, 2, 2)
STAGES = 6


def place():
    dp, seq = lax.axis_index("dp"), lax.axis_index("seq")
    return dp // 4, (dp // 2) % 2, dp % 2, seq


def device_at(z, x, core, y):
    return (z * 4 + x * 2 + core, y)


def peers():
    z, x, core, y = place()
    ring = [device_at((z + step) % ZS, x, core, y) for step in range(1, ZS)]
    return ring + [device_at(z, 1 - x, core, y), device_at(z, x, core, 1 - y), device_at(z, x, 1 - core, y)]


def meet(devices):
    barrier = pltpu.get_barrier_semaphore()
    for device in devices:
        pl.semaphore_signal(barrier, inc=1, device_id=device, device_id_type=MESH)
    pl.semaphore_wait(barrier, len(devices))


class Gather:
    def __init__(self, source, target, x_first, sems, index):
        self.source, self.target, self.x_first = source, target, x_first
        self.send, self.recv, self.local = sems
        self.index = index
        self.copies = []

    def remote(self, source, target, slot):
        copy = pltpu.make_async_remote_copy(
            src_ref=source, dst_ref=target,
            send_sem=self.send.at[self.index, slot], recv_sem=self.recv.at[self.index, slot],
            device_id=peers()[slot], device_id_type=MESH,
        )
        copy.start()
        self.copies.append(copy)
        return copy

    def begin(self):
        z, x, core, y = place()
        mine = self.target(z, x, core, y)
        self.own = pltpu.make_async_copy(self.source, mine, self.local.at[self.index])
        self.own.start()
        self.waiting = [self.remote(self.source, mine, slot) for slot in range(ZS - 1)]

    def second(self):
        z, x, core, y = place()
        self.own.wait()
        for copy in self.waiting:
            copy.wait_recv()
        block = self.target(slice(None), x, core, y)
        self.waiting = [self.remote(block, block, ZS - 1 if self.x_first else ZS)]

    def third(self):
        z, x, core, y = place()
        self.waiting[0].wait_recv()
        every = slice(None)
        block = self.target(every, every, core, y) if self.x_first else self.target(every, x, core, every)
        self.waiting = [self.remote(block, block, ZS if self.x_first else ZS - 1)]

    def fourth(self):
        z, x, core, y = place()
        self.waiting[0].wait_recv()
        every = slice(None)
        block = self.target(every, every, core, every)
        self.waiting = [self.remote(block, block, ZS + 1)]

    def finish(self):
        self.waiting[0].wait_recv()
        for copy in self.copies:
            copy.wait_send()


def columns_of(ref, first, width):
    return lambda z, x, core, y: ref.at[z, x, core, y, :, pl.ds(first, width)]


def gather_project_kernel(
    x_ref, small_in, mix_in, out_in,
    mix_out, out_out, small_out, normed_ref, projected_out, gates_ref,
    mix_ref, small_ref, slab_ref,
    send, recv, local, store_mix, store_slab, store_small,
):
    sems = (send, recv, local)
    chunk = 1024
    half = chunk // 2
    items = []

    def add(source, first, width, ref, x_first):
        items.append(
            Gather(source.at[:, pl.ds(first, width)], columns_of(ref, first, width), x_first, sems, len(items))
        )
        return items[-1]

    ticks = []
    chunks = mix_in.shape[1] // chunk
    small = add(small_in, 0, small_in.shape[1], small_ref, True)
    for index in range(chunks):
        ticks.append([add(mix_in, index * chunk + part * half, half, mix_ref, part == 0) for part in range(2)])
    ticks.append([add(out_in, part * half, half, out_out, part == 0) for part in range(2)])
    ticks[0].insert(0, small)
    meet(peers())
    steps = (Gather.begin, Gather.second, Gather.third, Gather.fourth, Gather.finish)
    values = x_ref[...].astype(jnp.float32)
    scaled = values * lax.rsqrt(jnp.mean(values * values, axis=1, keepdims=True) + EPSILON)
    stores = []
    for tick in range(len(ticks) + len(steps) - 1):
        for step, action in reversed(list(enumerate(steps))):
            if 0 <= tick - step < len(ticks):
                for item in ticks[tick - step]:
                    action(item)
        done = tick - len(steps) + 1
        if done == 0:
            smalls = small_ref[...].reshape(-1, small_in.shape[1])
            gain = jnp.transpose(smalls.astype(jnp.float32))[24:25, :]
            normed_ref[...] = (scaled * gain).astype(jnp.bfloat16)
            gates_ref[...] = mm(normed_ref[...], smalls)
            stores.append(pltpu.make_async_copy(small_ref, small_out, store_small))
            stores[-1].start()
        if 0 <= done < chunks:
            here = pl.ds(done * chunk, chunk)
            keep = pltpu.make_async_copy(
                mix_ref.at[:, :, :, :, :, here], mix_out.at[:, :, :, :, :, here], store_mix.at[done]
            )
            keep.start()
            stores.append(keep)
            weights = mix_ref[:, :, :, :, :, done * chunk : (done + 1) * chunk].reshape(-1, chunk)
            slab = done % 2
            if done >= 2:
                slab_stores[done - 2].wait()
            else:
                slab_stores = [] if done == 0 else slab_stores
            slab_ref[slab] = mm(normed_ref[...], weights)
            slab_stores.append(
                pltpu.make_async_copy(slab_ref.at[slab], projected_out.at[:, here], store_slab.at[slab])
            )
            slab_stores[-1].start()
    for store in stores + slab_stores[-2:]:
        store.wait()


def gather_project_call(x, small, mix, out):
    length = x.shape[0]
    rows, width = mix.shape
    everywhere = pl.BlockSpec(memory_space=pl.ANY)
    held = pl.BlockSpec(memory_space=pltpu.VMEM)
    items = 3 + 2 * (width // 1024)
    full = STACK + (rows,)
    outs = pl.pallas_call(
        gather_project_kernel,
        out_shape=[
            jax.ShapeDtypeStruct(full + (width,), jnp.bfloat16),
            jax.ShapeDtypeStruct(full + (out.shape[1],), jnp.bfloat16),
            jax.ShapeDtypeStruct(full + (small.shape[1],), jnp.bfloat16),
            jax.ShapeDtypeStruct(x.shape, jnp.bfloat16),
            jax.ShapeDtypeStruct((length, width), jnp.float32),
            jax.ShapeDtypeStruct((length, small.shape[1]), jnp.float32),
        ],
        in_specs=[held, everywhere, everywhere, everywhere],
        out_specs=[everywhere, everywhere, everywhere, held, everywhere, held],
        scratch_shapes=[
            pltpu.VMEM(full + (width,), jnp.bfloat16),
            pltpu.VMEM(full + (small.shape[1],), jnp.bfloat16),
            pltpu.VMEM((2, length, 1024), jnp.float32),
            pltpu.SemaphoreType.DMA((items, STAGES)),
            pltpu.SemaphoreType.DMA((items, STAGES)),
            pltpu.SemaphoreType.DMA((items,)),
            pltpu.SemaphoreType.DMA((width // 1024,)),
            pltpu.SemaphoreType.DMA((2,)),
            pltpu.SemaphoreType.DMA,
        ],
        compiler_params=pltpu.CompilerParams(collective_id=1, has_side_effects=True, vmem_limit_bytes=LIMIT),
        cost_estimate=pl.CostEstimate(flops=2 * length * width * 1024, bytes_accessed=60_000_000, transcendentals=0),
    )(x, small, mix, out)
    return [part.reshape((-1,) + part.shape[5:]) if part.ndim == 6 else part for part in outs]


WIDE = 256
RING = 4
SPAN_TICKS = 2
REDUCE_STAGES = 5
CORE, NEAR, FAR, RINGS = 0, 1, 2, 3


class Reduce:
    def __init__(self, refs, lane, count):
        (
            self.own, self.first_send, self.first, self.near_kept, self.near_send, self.near,
            self.far_kept, self.far_send, self.far, self.last_kept, self.last_send, self.last,
            self.load_sem, self.send_sem, self.recv_sem,
        ) = refs
        self.lane, self.count = lane, count
        self.z, self.x, self.core, self.y = place()
        self.peers = peers()
        self.x_first = lane == 0

    def copy(self, source, target, slot_of, stage, index, device):
        lane = self.lane
        return pltpu.make_async_remote_copy(
            src_ref=source, dst_ref=target,
            send_sem=self.send_sem.at[lane, stage, lax.rem(index, 2)],
            recv_sem=self.recv_sem.at[lane, stage, lax.rem(index, RING)],
            device_id=device, device_id_type=MESH,
        )

    def core_copy(self, source, index):
        return self.copy(source, self.first.at[self.lane, lax.rem(index, RING)], None, CORE, index, self.peers[ZS + 1])

    def near_copy(self, index):
        lane = self.lane
        return self.copy(
            self.near_send.at[lane, lax.rem(index, 2)], self.near.at[lane, lax.rem(index, RING)], None, NEAR, index,
            self.peers[ZS - 1 if self.x_first else ZS],
        )

    def far_copy(self, index):
        lane = self.lane
        return self.copy(
            self.far_send.at[lane, lax.rem(index, 2)], self.far.at[lane, lax.rem(index, RING)], None, FAR, index,
            self.peers[ZS if self.x_first else ZS - 1],
        )

    def ring_copies(self, index):
        lane = self.lane
        return [
            self.copy(
                self.last_send.at[lane, lax.rem(index, 2), step], self.last.at[lane, lax.rem(index, RING), step],
                None, RINGS + step, index, self.peers[step],
            )
            for step in range(ZS - 1)
        ]

    def load_copy(self, source, index):
        slot = lax.rem(index, 2)
        return pltpu.make_async_copy(source, self.own.at[self.lane, slot], self.load_sem.at[self.lane, slot])

    def from_core(self, index, loaded):
        lane, slot, ring = self.lane, lax.rem(index, 2), lax.rem(index, RING)
        arrived = self.core_copy(self.first_send.at[lane, slot], index)
        arrived.wait_recv()
        arrived.wait_send()

        @pl.when(loaded)
        def _():
            self.load_copy(self.first_send.at[lane, slot], index).wait()

        def one(z, carry):
            if self.x_first:
                pick = lambda ref, half: ref[lane, slot, z, half]
                pick_got = lambda half: self.first[lane, ring, z, half]
                mine = self.x
            else:
                pick = lambda ref, half: ref[lane, slot, z, :, half]
                pick_got = lambda half: self.first[lane, ring, z, :, half]
                mine = self.y
            kept = pick(self.own, mine).astype(jnp.float32) + pick_got(mine).astype(jnp.float32)
            sent = pick(self.own, 1 - mine).astype(jnp.float32) + pick_got(1 - mine).astype(jnp.float32)
            self.near_kept[lane, slot, z] = kept
            self.near_send[lane, slot, z] = sent.astype(jnp.bfloat16)
            return carry

        lax.fori_loop(0, ZS, one, 0)
        self.near_copy(index).start()

    def from_near(self, index):
        lane, slot, ring = self.lane, lax.rem(index, 2), lax.rem(index, RING)
        arrived = self.near_copy(index)
        arrived.wait_recv()
        arrived.wait_send()
        mine = self.y if self.x_first else self.x

        def one(z, carry):
            kept = self.near_kept[lane, slot, z, mine] + self.near[lane, ring, z, mine].astype(jnp.float32)
            sent = self.near_kept[lane, slot, z, 1 - mine] + self.near[lane, ring, z, 1 - mine].astype(jnp.float32)
            self.far_kept[lane, slot, z] = kept
            self.far_send[lane, slot, z] = sent.astype(jnp.bfloat16)
            return carry

        lax.fori_loop(0, ZS, one, 0)
        self.far_copy(index).start()

    def from_far(self, index):
        lane, slot, ring = self.lane, lax.rem(index, 2), lax.rem(index, RING)
        arrived = self.far_copy(index)
        arrived.wait_recv()
        arrived.wait_send()

        def total(z):
            return self.far_kept[lane, slot, z] + self.far[lane, ring, z].astype(jnp.float32)

        self.last_kept[lane, slot] = total(self.z)
        for step, copy in enumerate(self.ring_copies(index)):
            self.last_send[lane, slot, step] = total(lax.rem(self.z + 1 + step, ZS)).astype(jnp.bfloat16)
            copy.start()

    def from_ring(self, index):
        lane, slot, ring = self.lane, lax.rem(index, 2), lax.rem(index, RING)
        total = self.last_kept[lane, slot]
        for step, copy in enumerate(self.ring_copies(index)):
            copy.wait_recv()
            copy.wait_send()
            total = total + self.last[lane, ring, step].astype(jnp.float32)
        return total


def reduce_scratch(rows):
    half = (2, 2, rows, WIDE)
    lanes = 2
    return [
        pltpu.VMEM((lanes, 2, ZS) + half, jnp.bfloat16),
        pltpu.VMEM((lanes, 2, ZS) + half, jnp.bfloat16),
        pltpu.VMEM((lanes, RING, ZS) + half, jnp.bfloat16),
        pltpu.VMEM((lanes, 2, ZS, 2, rows, WIDE), jnp.float32),
        pltpu.VMEM((lanes, 2, ZS, 2, rows, WIDE), jnp.bfloat16),
        pltpu.VMEM((lanes, RING, ZS, 2, rows, WIDE), jnp.bfloat16),
        pltpu.VMEM((lanes, 2, ZS, rows, WIDE), jnp.float32),
        pltpu.VMEM((lanes, 2, ZS, rows, WIDE), jnp.bfloat16),
        pltpu.VMEM((lanes, RING, ZS, rows, WIDE), jnp.bfloat16),
        pltpu.VMEM((lanes, 2, rows, WIDE), jnp.float32),
        pltpu.VMEM((lanes, 2, ZS - 1, rows, WIDE), jnp.bfloat16),
        pltpu.VMEM((lanes, RING, ZS - 1, rows, WIDE), jnp.bfloat16),
        pltpu.SemaphoreType.DMA((lanes, 2)),
        pltpu.SemaphoreType.DMA((lanes, RINGS + ZS - 1, 2)),
        pltpu.SemaphoreType.DMA((lanes, RINGS + ZS - 1, RING)),
    ]


def at_columns(ref, core, first, row=0, rows=32):
    return ref.at[:, :, core, :, pl.ds(row, rows), pl.ds(pl.multiple_of(first, WIDE), WIDE)]


def make_mixer_back_kernel(length, gu_count, down_count, out_count, down_blocks):
    chunks = length // GROUP
    parts = 1 + 2 * NH
    pairs = H // 2
    gate_count = H * DV // WIDE
    down_first = gu_count
    out_first = down_first + down_count
    gate_first = out_first + out_count
    head_first = gate_first + gate_count
    items = head_first + parts * pairs
    count = items // 2
    early_ticks = H // 2
    ticks = count + (REDUCE_STAGES - 1) * SPAN_TICKS
    head_ticks = 3
    rows = 32

    def kernel(
        vec_ref, t_in, ok_in, mixed_in, gate_ref, gain_ref, d_gated_ref,
        q_in, k0_in, k1_in, v0_in, v1_in, bq, bk0, bk1, bv0, bv1, tq, tk0, tk1, tv0, tv1, mask_ref,
        x_in, u_in, s_in, normed_ref, gu_in, down_in, out_in,
        gain_out, d_vec_out, gq_out, gk0_out, gk1_out, gv0_out, gv1_out, d_projected_out,
        gu_out, down_out, out_out, mix_out,
        d_mixed_ref, local_ref, all_ref, relay_send, relay_recv, edge_send, edge_recv, tail_ref,
        ext_ref, pre_ref, q_ref, k_ref, v_ref, inv_ref, d_ref, z_ref,
        relay_sems, edge_send_sem, edge_recv_sem, store_sem, *engine_refs,
    ):
        step = pl.program_id(0)
        z, x, core, y = place()
        y_peer = device_at(z, x, core, 1 - y)
        lanes = [Reduce(engine_refs, lane, count) for lane in range(2)]
        first_device = jnp.where(y == 0, 1.0, 0.0)

        def source_of(item):
            within = item - head_first
            is_gate = item < head_first
            part = jnp.where(is_gate, parts, lax.rem(within, parts))
            column = jnp.where(is_gate, item - gate_first, within // parts) * WIDE
            return part, column

        def begin(lane, index):
            engine = lanes[lane]
            item = 2 * index + lane
            slot = lax.rem(index, 2)

            def from_hbm(ref, first, row):
                engine.core_copy(at_columns(ref, 1 - core, first, row), index).start()
                engine.load_copy(at_columns(ref, core, first, row), index).start()

            @pl.when(item < down_first)
            def _():
                from_hbm(gu_in, item * WIDE, 0)

            @pl.when((item >= down_first) & (item < out_first))
            def _():
                within = item - down_first
                from_hbm(down_in, lax.rem(within, 4) * WIDE, pl.multiple_of((within // 4) * rows, rows))

            @pl.when((item >= out_first) & (item < gate_first))
            def _():
                from_hbm(out_in, (item - out_first) * WIDE, 0)

            @pl.when(item >= gate_first)
            def _():
                part, column = source_of(item)
                right = all_ref[part, :, pl.ds(pl.multiple_of(column, WIDE), WIDE)]
                for half, target in ((1 - core, engine.first_send), (core, engine.own)):
                    left = normed_ref[:, :, half].reshape(-1, length)
                    target[lane, slot] = mm(left, right).astype(jnp.bfloat16).reshape(ZS, 2, 2, rows, WIDE)
                engine.core_copy(engine.first_send.at[lane, slot], index).start()

        def end(lane, index):
            item = 2 * index + lane
            total = lanes[lane].from_ring(index)

            def here(first):
                return pl.ds(pl.multiple_of(first, WIDE), WIDE)

            @pl.when(item < down_first)
            def _():
                gu_out[:, here(item * WIDE)] = total

            @pl.when((item >= down_first) & (item < out_first))
            def _():
                within = item - down_first
                down_out[within // 4, :, here(lax.rem(within, 4) * WIDE)] = total

            @pl.when((item >= out_first) & (item < gate_first))
            def _():
                out_out[:, here((item - out_first) * WIDE)] = total

            @pl.when(item >= gate_first)
            def _():
                part, column = source_of(item)
                mix_out[:, here(part * (H * DK) + column)] = total

        def tick(number):
            for stage in reversed(range(REDUCE_STAGES)):
                index = number - stage * SPAN_TICKS

                @pl.when((index >= 0) & (index < count))
                def _():
                    for lane in range(2):
                        engine = lanes[lane]
                        if stage == 0:
                            begin(lane, index)
                        elif stage == 1:
                            engine.from_core(index, 2 * index + lane < gate_first)
                        elif stage == 2:
                            engine.from_near(index)
                        elif stage == 3:
                            engine.from_far(index)
                        else:
                            end(lane, index)

        def readout_back(head):
            gain = gain_ref[0:1, :]
            gain_grad = jnp.zeros((1, DV), jnp.float32)
            column = pl.ds(pl.multiple_of(head * DV, DV), DV)
            locals_ = []
            for chunk in range(chunks):
                here = slice(chunk * GROUP, (chunk + 1) * GROUP)
                mixed = mixed_in[here, :]
                inv = lax.rsqrt(jnp.mean(mixed * mixed, axis=1, keepdims=True) + EPSILON)
                unit = mixed * inv
                gate = gate_ref[here, :]
                open_, sig = silu_pair(gate)
                d_gated = d_gated_ref[here, :]
                d_scaled = d_gated * open_
                d_gate = d_gated * unit * gain * sig * (1.0 + gate * (1.0 - sig))
                all_ref[parts, here, column] = d_gate.astype(jnp.bfloat16)
                gain_grad = gain_grad + jnp.sum(d_scaled * unit, axis=0, keepdims=True)
                d_unit = d_scaled * gain
                d_mixed = inv * (d_unit - unit * jnp.mean(d_unit * unit, axis=1, keepdims=True))
                d_mixed_ref[head, here] = d_mixed
                local = mm3(d_mixed, ok_in[0, chunk], 0, 0)
                local_ref[head, chunk] = local
                locals_.append(local)
            gain_out[0] = jnp.broadcast_to(gain_grad, (8, DV))
            state = jnp.zeros((DV, DK), jnp.float32)
            for chunk in reversed(range(chunks)):
                state = (
                    vec_ref[0, chunk, 3:4, GROUP - 1 : GROUP] * state
                    - mm3(state, t_in[0, chunk], 1, 1)
                    + locals_[chunk]
                )
            relay_send[head] = state.astype(jnp.bfloat16)

        channels = (q_in, k0_in, k1_in, v0_in, v1_in)
        taps = (tq, tk0, tk1, tv0, tv1)

        def prepare(head):
            for part, (channel, border, tap) in enumerate(zip(channels, (bq, bk0, bk1, bv0, bv1), taps)):
                pre = conv_block(channel, border, tap, mask_ref, ext_ref.at[part])
                pre_ref[part] = pre
                value = silu_pair(pre)[0]
                if part == 0:
                    unit, inv = unit_rows(value)
                    q_ref[...] = unit * DK ** (-0.5)
                    inv_ref[0] = jnp.broadcast_to(inv, (length, DK))
                elif part <= NH:
                    unit, inv = unit_rows(value)
                    k_ref[part - 1] = unit
                    inv_ref[part] = jnp.broadcast_to(inv, (length, DK))
                else:
                    v_ref[part - 1 - NH] = value

        def chain(head):
            exit_grads = [None] * chunks
            grad = first_device * relay_recv[head].astype(jnp.float32)
            for chunk in reversed(range(chunks)):
                exit_grads[chunk] = grad
                grad = (
                    vec_ref[0, chunk, 3:4, GROUP - 1 : GROUP] * grad
                    - mm3(grad, t_in[0, chunk], 1, 1)
                    + local_ref[head, chunk]
                )
            return exit_grads

        def one_chunk(chunk, head, d_exit):
            strict = order_masks()[0]
            column_index = iotas(SPAN, 8)[1]
            here = slice(chunk * GROUP, (chunk + 1) * GROUP)
            rows_, columns = chunk_vectors(vec_ref, chunk)
            beta, scale, tail = columns[:, 1:2], columns[:, 3:4], columns[:, 4:5]
            keys = k_ref[:, here, :].reshape(SPAN, DK)
            values = v_ref[:, here, :].reshape(SPAN, DV)
            queries = q_ref[here, :]
            link = link_matrix(rows_, columns)
            link_gram = jnp.where(strict, twice(link) * mm3(keys, keys, 1, 1), 0.0)
            reading = link * mm3(queries, keys, 1, 1)
            solved = u_in[0, chunk]
            entry = s_in[0, chunk]
            d_mixed = d_mixed_ref[head, here]
            tail_keys = tail * keys
            d_solved = mm3(reading, d_mixed, 0, 0) + mm3(tail_keys, d_exit, 1, 1)
            d_right = mm3(x_in[0, chunk], d_solved, 0, 0)
            d_lower = jnp.where(strict, -mm3(d_right, solved, 1, 1), 0.0)
            d_tail_keys = mm3(solved, d_exit)
            d_right_entry = mm3(d_right, entry)
            d_reading = mm3(d_mixed, solved, 1, 1)
            d_query_entry = mm3(d_mixed, entry)
            both_scale = -jnp.sum(d_right_entry * keys, axis=1, keepdims=True)
            lower_weight = d_lower * link_gram
            d_beta = (
                jnp.sum(d_right * values, axis=1, keepdims=True)
                + scale * both_scale
                + jnp.sum(lower_weight, axis=1, keepdims=True)
            )
            lower_moment = lower_weight * beta
            reading_moment = d_reading * reading
            d_gram = beta * twice(link) * d_lower
            d_gram = d_gram + jnp.transpose(d_gram)
            d_query_gram = link * d_reading
            d_keys = (
                tail * d_tail_keys
                - beta * scale * d_right_entry
                + mm3(d_gram, keys)
                + mm3(d_query_gram, queries, 0, 0)
            )
            d_queries = mm3(d_query_gram, keys) + scale[:GROUP] * d_query_entry
            d_values = beta * d_right
            none = jnp.zeros((GROUP, 1), jnp.float32)
            d_gap = jnp.sum(lower_moment, axis=1, keepdims=True) + jnp.concatenate(
                [jnp.sum(reading_moment, axis=1, keepdims=True), none], axis=0
            )
            last = jnp.sum(jnp.sum(d_exit * entry, axis=1, keepdims=True), axis=0, keepdims=True)
            own_scale = jnp.sum(d_query_entry * queries, axis=1, keepdims=True)
            own_scale = own_scale + jnp.where(iotas(GROUP, 1)[0] == GROUP - 1, last, 0.0)
            d_scale = beta * both_scale + jnp.concatenate([own_scale, none], axis=0)
            d_tail = jnp.sum(d_tail_keys * keys, axis=1, keepdims=True)
            grads = jnp.where(
                column_index == 0,
                d_gap,
                jnp.where(
                    column_index == 1,
                    d_beta,
                    jnp.where(column_index == 3, d_scale, jnp.where(column_index == 4, d_tail, 0.0)),
                ),
            )
            grads = jnp.transpose(grads)
            sums = jnp.sum(lower_moment, axis=0, keepdims=True) + jnp.sum(reading_moment, axis=0, keepdims=True)
            d_vec_out[0, chunk] = grads - jnp.where(iotas(8, SPAN)[0] == 0, sums, 0.0)
            d_ref[0, here, :] = d_queries
            for house in range(NH):
                mine = slice(house * GROUP, (house + 1) * GROUP)
                d_ref[1 + house, here, :] = d_keys[mine]
                d_ref[1 + NH + house, here, :] = d_values[mine]

        def finish_head(head):
            tap_grads = (gq_out, gk0_out, gk1_out, gv0_out, gv1_out)
            column = pl.ds(pl.multiple_of(head * DK, DK), DK)
            z_ref[0:8, :] = jnp.zeros((8, DK), jnp.float32)
            z_ref[8 + length : 16 + length, :] = jnp.zeros((8, DK), jnp.float32)
            for part in range(parts):
                grad = d_ref[part]
                if part <= NH:
                    unit = q_ref[...] * DK ** 0.5 if part == 0 else k_ref[part - 1]
                    if part == 0:
                        grad = grad * DK ** (-0.5)
                    grad = inv_ref[part] * (grad - unit * jnp.sum(grad * unit, axis=1, keepdims=True))
                pre = pre_ref[part]
                sig = jax.nn.sigmoid(pre)
                grad = grad * sig * (1.0 + pre * (1.0 - sig))
                tap = taps[part]
                total = grad * tap[0:1, :]
                edge = jnp.zeros((8, DK), jnp.float32)
                tap_rows = [jnp.sum(grad * channels[part][...], axis=0, keepdims=True)]
                for index in range(1, 4):
                    shifted = grad * mask_ref[index - 1]
                    tap_rows.append(
                        jnp.sum(shifted * ext_ref[part, 8 - index : 8 - index + length, :], axis=0, keepdims=True)
                    )
                    z_ref[8 : 8 + length, :] = shifted * tap[index : index + 1, :]
                    total = total + z_ref[8 + index : 8 + index + length, :]
                    edge = edge + z_ref[index : index + 8, :]
                all_ref[part, :, column] = total.astype(jnp.bfloat16)
                edge_send[lax.rem(head, 2), part] = edge
                tail_ref[part] = total[length - 16 :, :]
                tap_grads[part][...] = jnp.concatenate(tap_rows + [jnp.zeros((4, DK), jnp.float32)], axis=0)

        @pl.when(step == 0)
        def _():
            meet(peers())

        @pl.when((step < H) & (lax.rem(step, 2) == 0))
        def _():
            tick(step // 2)

        @pl.when(step < H)
        def _():
            readout_back(step)

        relay = pltpu.make_async_remote_copy(
            src_ref=relay_send, dst_ref=relay_recv, send_sem=relay_sems.at[0], recv_sem=relay_sems.at[1],
            device_id=y_peer, device_id_type=MESH,
        )

        @pl.when(step == H - 1)
        def _():
            relay.start()

        @pl.when(step == H)
        def _():
            relay.wait()

        def edge_copy(head):
            slot = lax.rem(head, 2)
            return pltpu.make_async_remote_copy(
                src_ref=edge_send.at[slot], dst_ref=edge_recv.at[slot], send_sem=edge_send_sem.at[slot],
                recv_sem=edge_recv_sem.at[slot], device_id=y_peer, device_id_type=MESH,
            )

        @pl.when(step > H)
        def _():
            head = step - H - 1
            edge = edge_copy(head)
            edge.wait()
            here = pl.ds(pl.multiple_of(head * DK, DK), DK)
            for part in range(parts):
                fixed = tail_ref[part, 8:16] + first_device * edge_recv[lax.rem(head, 2), part]
                both = jnp.concatenate([tail_ref[part, 0:8], fixed], axis=0)
                all_ref[part, length - 16 : length, here] = both.astype(jnp.bfloat16)

        head_tick = early_ticks + (step - H) * head_ticks

        @pl.when((step >= H) & (step < 2 * H))
        def _():
            head = step - H
            tick(head_tick)
            prepare(head)
            exit_grads = chain(head)
            for chunk in reversed(range(chunks // 2, chunks)):
                one_chunk(chunk, head, exit_grads[chunk])
            tick(head_tick + 1)
            for chunk in reversed(range(chunks // 2)):
                one_chunk(chunk, head, exit_grads[chunk])
            tick(head_tick + 2)
            finish_head(head)
            edge_copy(head).start()

        @pl.when(step == 2 * H)
        def _():
            stores = [
                pltpu.make_async_copy(
                    all_ref.at[part], d_projected_out.at[:, pl.ds(part * H * DK, H * DK)], store_sem.at[part]
                )
                for part in range(parts + 1)
            ]
            for store in stores:
                store.start()

            def drain(number, carry):
                tick(number)
                return carry

            lax.fori_loop(early_ticks + H * head_ticks, ticks, drain, 0)
            for store in stores:
                store.wait()

    return kernel, ticks


def mixer_back_call(
    vec, transfer, out_keys, mixed, projected, gain, d_gated, border, taps, masks, inverse, solved, entries,
    normed_t, grad_gu, grad_down, grad_out,
):
    length = projected.shape[0]
    chunks = length // GROUP
    parts = 1 + 2 * NH
    rows = grad_gu.shape[4]
    down_blocks = grad_down.shape[4] // rows
    kernel, ticks = make_mixer_back_kernel(
        length, grad_gu.shape[5] // WIDE, down_blocks * (grad_down.shape[5] // WIDE), grad_out.shape[5] // WIDE, down_blocks
    )

    def either(step):
        return lax.rem(step, H)

    def early(step):
        return jnp.minimum(step, H - 1)

    def late(step):
        return jnp.clip(step - H, 0, H - 1)

    def heads(shape, which):
        rank = len(shape)
        return pl.BlockSpec((1,) + shape, lambda step: (which(step),) + (0,) * rank)

    def cols(count, first, which):
        return pl.BlockSpec((count, DK), lambda step: (0, first + which(step)))

    def whole(shape):
        rank = len(shape)
        return pl.BlockSpec(shape, lambda step: (0,) * rank)

    square = (chunks, SPAN, DK)
    anywhere = pl.BlockSpec(memory_space=pl.ANY)
    in_specs = (
        [
            heads((chunks, 8, SPAN), either), heads(square, either), heads((chunks, GROUP, DK), early),
            cols(length, 0, early), cols(length, parts * H, early), whole((8, DV)), cols(length, 0, early),
        ]
        + [cols(length, H * part, late) for part in range(parts)]
        + [cols(8, H * part, late) for part in range(parts)] * 2
        + [whole((3, length, DK))]
        + [heads(square, late)] * 3
        + [whole(normed_t.shape)]
        + [anywhere] * 3
    )
    shard = (rows,)
    out_shape = (
        [per_head((8, DV)), per_head((chunks, 8, SPAN))]
        + [jax.ShapeDtypeStruct((8, H * DK), jnp.float32)] * parts
        + [
            jax.ShapeDtypeStruct((length, (parts + 1) * H * DK), jnp.bfloat16),
            jax.ShapeDtypeStruct((rows, grad_gu.shape[5]), jnp.float32),
            jax.ShapeDtypeStruct((down_blocks, rows, grad_down.shape[5]), jnp.float32),
            jax.ShapeDtypeStruct((rows, grad_out.shape[5]), jnp.float32),
            jax.ShapeDtypeStruct((rows, (parts + 1) * H * DK), jnp.float32),
        ]
    )
    out_specs = (
        [heads((8, DV), early), heads((chunks, 8, SPAN), late)]
        + [cols(8, 0, late)] * parts
        + [anywhere]
        + [whole(out.shape) for out in out_shape[-4:]]
    )
    tall = pltpu.VMEM((parts, length, DK), jnp.float32)
    scratch = [
        pltpu.VMEM((H, length, DV), jnp.float32),
        pltpu.VMEM((H,) + square, jnp.float32),
        pltpu.VMEM((parts + 1, length, H * DK), jnp.bfloat16),
        pltpu.VMEM((H, DV, DK), jnp.bfloat16),
        pltpu.VMEM((H, DV, DK), jnp.bfloat16),
        pltpu.VMEM((2, parts, 8, DK), jnp.float32),
        pltpu.VMEM((2, parts, 8, DK), jnp.float32),
        pltpu.VMEM((parts, 16, DK), jnp.float32),
        pltpu.VMEM((parts, length + 8, DK), jnp.float32),
        tall,
        pltpu.VMEM((length, DK), jnp.float32),
        pltpu.VMEM((NH, length, DK), jnp.float32),
        pltpu.VMEM((NH, length, DK), jnp.float32),
        pltpu.VMEM((1 + NH, length, DK), jnp.float32),
        tall,
        pltpu.VMEM((length + 16, DK), jnp.float32),
        pltpu.SemaphoreType.DMA((2,)),
        pltpu.SemaphoreType.DMA((2,)),
        pltpu.SemaphoreType.DMA((2,)),
        pltpu.SemaphoreType.DMA((parts + 1,)),
    ] + reduce_scratch(rows)
    return pl.pallas_call(
        kernel,
        grid=(2 * H + 1,),
        out_shape=out_shape,
        in_specs=in_specs,
        out_specs=out_specs,
        scratch_shapes=scratch,
        compiler_params=pltpu.CompilerParams(
            dimension_semantics=("arbitrary",), collective_id=2, has_side_effects=True, vmem_limit_bytes=58 * 1024 * 1024
        ),
        cost_estimate=pl.CostEstimate(
            flops=H * chunks * 14 * 2 * SPAN**3 * 4, bytes_accessed=100_000_000, transcendentals=0
        ),
    )(
        vec, transfer, out_keys, mixed, projected, gain, d_gated,
        *[projected] * parts, *[border] * parts, *[taps] * parts, masks,
        inverse, solved, entries, normed_t, grad_gu, grad_down, grad_out,
    )


def total_kernel(packed_ref, sums_ref, packed_out, sums_out, first, near, far, last, kept, pair, ring, send, recv):
    z, x, core, y = place()
    targets = peers()
    meet(targets)

    def copy(source, target, slot, device):
        made = pltpu.make_async_remote_copy(
            src_ref=source, dst_ref=target, send_sem=send.at[slot], recv_sem=recv.at[slot],
            device_id=device, device_id_type=MESH,
        )
        made.start()
        return made

    def swap(source, target, index, device):
        pair[2 * index] = sums_out[...]
        copies = [
            copy(source, target, 2 * index, device),
            copy(pair.at[2 * index], pair.at[2 * index + 1], 2 * index + 1, device),
        ]
        for made in copies:
            made.wait()
        sums_out[...] = sums_out[...] + pair[2 * index + 1]

    sums_out[...] = sums_ref[...]
    swap(packed_ref.at[:, :, 1 - core], first, 0, targets[ZS + 1])
    kept[...] = packed_ref[:, :, core] + first[...]
    swap(kept.at[:, 1 - x], near, 1, targets[ZS - 1])
    kept[:, 0] = kept[:, x] + near[...]
    swap(kept.at[:, 0, 1 - y], far, 2, targets[ZS])
    kept[:, 0, 0] = kept[:, 0, y] + far[...]
    ring[z] = sums_out[...]
    copies = []
    for step in range(ZS - 1):
        other = lax.rem(z + 1 + step, ZS)
        copies.append(copy(kept.at[other, 0, 0], last.at[step], 6 + 2 * step, targets[step]))
        copies.append(copy(ring.at[z], ring.at[z], 7 + 2 * step, targets[step]))
    for made in copies:
        made.wait()
    packed_out[...] = kept[z, 0, 0] + last[0] + last[1] + last[2]
    sums_out[...] = ring[0] + ring[1] + ring[2] + ring[3]


def total_call(packed, sums):
    rows, wide = packed.shape[4], packed.shape[5]
    held = pl.BlockSpec(memory_space=pltpu.VMEM)
    return pl.pallas_call(
        total_kernel,
        out_shape=[jax.ShapeDtypeStruct((rows, wide), jnp.float32), jax.ShapeDtypeStruct(sums.shape, jnp.float32)],
        in_specs=[held, held],
        out_specs=[held, held],
        scratch_shapes=[
            pltpu.VMEM((ZS, 2, 2, rows, wide), jnp.float32),
            pltpu.VMEM((ZS, 2, rows, wide), jnp.float32),
            pltpu.VMEM((ZS, rows, wide), jnp.float32),
            pltpu.VMEM((ZS - 1, rows, wide), jnp.float32),
            pltpu.VMEM((ZS, 2, 2, rows, wide), jnp.float32),
            pltpu.VMEM((6,) + sums.shape, jnp.float32),
            pltpu.VMEM((ZS,) + sums.shape, jnp.float32),
            pltpu.SemaphoreType.DMA((12,)),
            pltpu.SemaphoreType.DMA((12,)),
        ],
        compiler_params=pltpu.CompilerParams(collective_id=3, has_side_effects=True, vmem_limit_bytes=LIMIT),
        cost_estimate=pl.CostEstimate(flops=1000000, bytes_accessed=2_000_000, transcendentals=0),
    )(packed, sums)


def from_behind(block, axis, distance):
    devices = range(lax.axis_size(axis))
    route = [(i - distance, i) for i in devices if i - distance in devices]
    return lax.ppermute(block, axis, route)


def rms_scale(values, scale_gain):
    return (
        values * lax.rsqrt(jnp.mean(values * values, axis=-1, keepdims=True) + EPSILON) * scale_gain
    )


def swiglu(gate_up):
    half_width = gate_up.shape[-1] // 2
    return jax.nn.silu(gate_up[:, :half_width]) * gate_up[:, half_width:]


def exchange(block, axis, bit):
    route = [(i, i ^ (1 << bit)) for i in range(lax.axis_size(axis))]
    return lax.ppermute(block, axis, route)


def axis_bits(axis):
    return lax.axis_size(axis).bit_length() - 1


def bit_orders():
    dp_bits = [("dp", bit) for bit in range(axis_bits("dp"))]
    seq_bits = [("seq", bit) for bit in range(axis_bits("seq"))]
    first, rest = dp_bits[:1], dp_bits[1:]
    inner = rest[:1] + seq_bits[:1]
    outer = rest[1:] + seq_bits[1:]
    return first + inner + outer, first + inner[::-1] + outer


def scatter_sum(part, order):
    dp_bits, seq_bits = axis_bits("dp"), axis_bits("seq")
    dims = [("dp", bit) for bit in reversed(range(dp_bits))] + [("seq", bit) for bit in reversed(range(seq_bits))]
    rows = part.shape[0] >> len(dims)
    part = part.reshape((2,) * len(dims) + (rows, part.shape[1]))
    for axis, bit in order:
        place = dims.index((axis, bit))
        dims.pop(place)
        mine = (lax.axis_index(axis) >> bit) & 1
        sent = lax.dynamic_index_in_dim(part, 1 - mine, place, keepdims=False)
        kept = lax.dynamic_index_in_dim(part, mine, place, keepdims=False)
        got = exchange(sent.astype(jnp.bfloat16), axis, bit)
        part = kept.astype(jnp.float32) + got.astype(jnp.float32)
    return part


def scatter_halves(part):
    half = part.shape[1] // 2
    orders = bit_orders()
    return jnp.concatenate(
        [scatter_sum(part[:, :half], orders[0]), scatter_sum(part[:, half:], orders[1])], axis=1
    )


def total_sum(block):
    for axis in ("dp", "seq"):
        for bit in range(axis_bits(axis)):
            block = block + exchange(block, axis, bit)
    return block


def gate_vectors(seg_now, seg_prev, gates_raw, decay_log):
    length = gates_raw.shape[0]
    chunks = length // GROUP
    beta = jax.nn.sigmoid(gates_raw[:, : NH * H]).reshape(chunks, GROUP, NH, H)
    rate = -jnp.exp(decay_log) * jax.nn.softplus(gates_raw[:, NH * H :])
    lower = jnp.tril(jnp.ones((GROUP, GROUP), jnp.float32))
    total = jnp.einsum("ts,csh->cth", lower, rate.reshape(chunks, GROUP, H), precision=HIGHEST)
    seg = seg_now.reshape(chunks, GROUP)
    before = jnp.concatenate([seg_prev.reshape(1), seg[:-1, -1]])
    scale = jnp.exp(total) * (seg == before[:, None]).astype(jnp.float32)[:, :, None]
    tail = jnp.exp(total[:, -1:, :] - total) * (seg == seg[:, -1:]).astype(jnp.float32)[:, :, None]

    def both(values):
        moved = jnp.moveaxis(values, 2, 0)
        return jnp.concatenate([moved, moved], axis=-1)

    beta_rows = beta.transpose(3, 0, 2, 1).reshape(H, chunks, SPAN)
    seg_rows = jnp.broadcast_to(jnp.concatenate([seg, seg], axis=1).astype(jnp.float32), (H, chunks, SPAN))
    none = jnp.zeros((H, chunks, SPAN), jnp.float32)
    return jnp.stack([both(total), beta_rows, seg_rows, both(scale), both(tail), none, none, none], axis=2)


def head_spec(shape):
    rank = len(shape)
    return pl.BlockSpec((1,) + shape, lambda head: (head,) + (0,) * rank)


def column_spec(rows, first):
    return pl.BlockSpec((rows, DK), lambda head: (0, first + head))


def whole_spec(shape):
    rank = len(shape)
    return pl.BlockSpec(shape, lambda head: (0,) * rank)


def per_head(shape, dtype=jnp.float32):
    return jax.ShapeDtypeStruct((H,) + shape, dtype)


def call(kernel, out_shape, in_specs, out_specs, scratch, flops, bytes_accessed):
    return pl.pallas_call(
        kernel,
        grid=(H,),
        out_shape=out_shape,
        in_specs=in_specs,
        out_specs=out_specs,
        scratch_shapes=scratch,
        compiler_params=pltpu.CompilerParams(
            dimension_semantics=("arbitrary",), vmem_limit_bytes=LIMIT
        ),
        cost_estimate=pl.CostEstimate(flops=flops, bytes_accessed=bytes_accessed, transcendentals=0),
    )


def conv_specs(length):
    return (
        [column_spec(length, H * part) for part in range(1 + 2 * NH)]
        + [column_spec(8, H * part) for part in range(1 + 2 * NH)] * 2
        + [whole_spec((3, length, DK))]
    )


def forward_call(projected, border, taps, masks, vec, start):
    length = projected.shape[0]
    chunks = length // GROUP
    square = (chunks, SPAN, DK)
    outs = [
        (square, jnp.float32),
        (square, jnp.float32),
        (square, jnp.float32),
        (square, jnp.float32),
        (square, jnp.float32),
        ((chunks, GROUP, DK), jnp.float32),
        ((chunks, GROUP, DV), jnp.float32),
        ((DV, DK), jnp.float32),
    ]
    parts = 1 + 2 * NH
    return call(
        forward_kernel,
        [per_head(*out) for out in outs],
        conv_specs(length) + [head_spec((chunks, 8, SPAN)), head_spec((DV, DK))],
        [head_spec(out[0]) for out in outs],
        [
            pltpu.VMEM((length + 8, DK), jnp.float32),
            pltpu.VMEM((length, DK), jnp.float32),
            pltpu.VMEM((NH, length, DK), jnp.float32),
            pltpu.VMEM((NH, length, DK), jnp.float32),
        ],
        H * chunks * 20 * 2 * SPAN**3 * 4,
        H * chunks * 8 * SPAN * DK * 4,
    )(*[projected] * parts, *[border] * parts, *[taps] * parts, masks, vec, start)


def chain_call(vec, transfer, start):
    chunks = transfer.shape[1]
    return call(
        chain_kernel,
        per_head((DV, DK)),
        [head_spec((chunks, 8, SPAN)), head_spec((chunks, SPAN, DK)), head_spec((DV, DK))],
        head_spec((DV, DK)),
        [],
        H * chunks * 2 * SPAN**3,
        H * chunks * SPAN * DK * 4,
    )(vec, transfer, start)


def readout_call(vec, key_part, value_part, transfer, inject, out_keys, out_values, entry, projected, gain):
    length = projected.shape[0]
    chunks = length // GROUP
    square = head_spec((chunks, SPAN, DK))
    half = head_spec((chunks, GROUP, DK))
    return call(
        readout_kernel,
        [
            jax.ShapeDtypeStruct((length, H * DV), jnp.bfloat16),
            jax.ShapeDtypeStruct((length, H * DV), jnp.float32),
            per_head((chunks, SPAN, DK)),
            per_head((chunks, SPAN, DK)),
        ],
        [
            head_spec((chunks, 8, SPAN)), square, square, square, square, half, half,
            head_spec((DV, DK)), column_spec(length, (1 + 2 * NH) * H), whole_spec((8, DV)),
        ],
        [column_spec(length, 0), column_spec(length, 0), square, square],
        [],
        H * chunks * 4 * 2 * SPAN**3 * 4,
        H * chunks * 8 * SPAN * DK * 4,
    )(vec, key_part, value_part, transfer, inject, out_keys, out_values, entry, projected, gain)


def readout_back_call(vec, transfer, out_keys, mixed, projected, gain, d_gated, start):
    length = projected.shape[0]
    chunks = length // GROUP
    square = head_spec((chunks, SPAN, DK))
    return call(
        readout_back_kernel,
        [
            jax.ShapeDtypeStruct((length, H * DV), jnp.float32),
            jax.ShapeDtypeStruct((length, H * DV), jnp.bfloat16),
            per_head((chunks, SPAN, DK)),
            per_head((DV, DK)),
            per_head((8, DV)),
        ],
        [
            head_spec((chunks, 8, SPAN)), square, head_spec((chunks, GROUP, DK)),
            column_spec(length, 0), column_spec(length, (1 + 2 * NH) * H), whole_spec((8, DV)),
            column_spec(length, 0), head_spec((DV, DK)),
        ],
        [column_spec(length, 0), column_spec(length, 0), square, head_spec((DV, DK)), head_spec((8, DV))],
        [],
        H * chunks * 4 * 2 * SPAN**3 * 4,
        H * chunks * 8 * SPAN * DK * 4,
    )(vec, transfer, out_keys, mixed, projected, gain, d_gated, start)


def backward_call(projected, border, taps, masks, vec, transfer, inverse, solved, entries, d_mixed, local, exit_grad):
    length = projected.shape[0]
    chunks = length // GROUP
    parts = 1 + 2 * NH
    square = head_spec((chunks, SPAN, DK))
    outs = (
        [jax.ShapeDtypeStruct((length, H * DK), jnp.bfloat16)] * parts
        + [jax.ShapeDtypeStruct((16, H * DK), jnp.float32)] * parts
        + [jax.ShapeDtypeStruct((8, H * DK), jnp.float32)] * parts
        + [per_head((chunks, 8, SPAN))]
    )
    out_specs = (
        [column_spec(length, 0)] * parts
        + [column_spec(16, 0)] * parts
        + [column_spec(8, 0)] * parts
        + [head_spec((chunks, 8, SPAN))]
    )
    tall = pltpu.VMEM((parts, length, DK), jnp.float32)
    return call(
        backward_kernel,
        outs,
        conv_specs(length)
        + [head_spec((chunks, 8, SPAN)), square, square, square, square, column_spec(length, 0), square, head_spec((DV, DK))],
        out_specs,
        [
            pltpu.VMEM((parts, length + 8, DK), jnp.float32),
            tall,
            pltpu.VMEM((length, DK), jnp.float32),
            pltpu.VMEM((NH, length, DK), jnp.float32),
            pltpu.VMEM((NH, length, DK), jnp.float32),
            pltpu.VMEM((1 + NH, length, DK), jnp.float32),
            tall,
            pltpu.VMEM((length + 16, DK), jnp.float32),
        ],
        H * chunks * 14 * 2 * SPAN**3 * 4,
        H * chunks * 16 * SPAN * DK * 4,
    )(*[projected] * parts, *[border] * parts, *[taps] * parts, masks, vec, transfer, inverse, solved, entries, d_mixed, local, exit_grad)


def gather(block, dim=0):
    return lax.all_gather(block, ("dp", "seq"), axis=dim, tiled=True)


def on_device(
    block_input, doc_starts, norm_in, w_mix, w_small, conv_w, decay_log, norm_out,
    w_out, norm_mlp, w_gu, w_down, cotangent,
):
    row_count, seg_len, width = block_input.shape
    tap_count = conv_w.shape[0]
    key_width = H * DK
    parts = 1 + 2 * NH
    seqs = lax.axis_size("seq")
    residual_in = block_input.astype(jnp.float32).reshape(seg_len, width)
    smalls, rows = w_small.shape[1], w_mix.shape[0]
    fast = lax.axis_size("dp") == 4 * ZS and seqs == 2 and rows % 16 == 0
    if fast:
        small = jnp.concatenate(
            [w_small, norm_in[:, None], norm_mlp[:, None], conv_w.reshape(tap_count, rows, -1).transpose(1, 2, 0).reshape(rows, -1)], axis=1
        )
        small = jnp.concatenate([small, jnp.zeros((rows, DK - small.shape[1]), small.dtype)], axis=1)
        mix_all, out_all, small_pack, normed_low, projected, gates_raw = gather_project_call(
            block_input.reshape(seg_len, width), small, w_mix, w_out
        )
        small_all = small_pack[:, :smalls]
        gates_raw = gates_raw[:, :smalls]
        norm_in_all = small_pack[:, smalls].astype(jnp.float32)
        norm_mlp_all = small_pack[:, smalls + 1].astype(jnp.float32)
        per_row = conv_w.shape[1] // rows
        conv_all = small_pack[:, smalls + 2 : smalls + 2 + per_row * tap_count]
        conv_all = conv_all.reshape(-1, tap_count).transpose(1, 0)
        normed, norm_in_back = jax.vjp(rms_scale, residual_in, norm_in_all)
    else:
        mix_all, small_all, conv_all, out_all = gather(w_mix), gather(w_small), gather(conv_w, 1), gather(w_out)
        norm_in_all = gather(norm_in).astype(jnp.float32)
        norm_mlp_all = gather(norm_mlp).astype(jnp.float32)
        normed, norm_in_back = jax.vjp(rms_scale, residual_in, norm_in_all)
        normed_low = normed.astype(jnp.bfloat16)
        projected = jnp.dot(normed_low, mix_all, preferred_element_type=jnp.float32)
        gates_raw = jnp.dot(normed_low, small_all, preferred_element_type=jnp.float32)
    gu_all, down_all = gather(w_gu), gather(w_down)
    border = from_behind(projected[seg_len - tap_count + 1 :, : parts * key_width], "seq", 1)
    border = jnp.concatenate([jnp.zeros((9 - tap_count, parts * key_width), jnp.float32), border], axis=0)
    positions = lax.axis_index("seq") * seg_len + jnp.arange(1 - tap_count, seg_len, dtype=jnp.int32)
    seg_ext = jnp.sum((positions[:, None] >= doc_starts[0][None, :]).astype(jnp.int32), axis=1)
    seg_ext = jnp.where(positions < 0, -1, seg_ext)
    seg_now = seg_ext[tap_count - 1 :]
    masks = jnp.stack(
        [seg_ext[tap_count - 1 - tap : tap_count - 1 - tap + seg_len] == seg_now for tap in range(1, tap_count)]
    ).astype(jnp.float32)
    masks = jnp.broadcast_to(masks[:, :, None], (tap_count - 1, seg_len, DK))
    taps = jnp.concatenate([conv_all.astype(jnp.float32), jnp.zeros((8 - tap_count, parts * key_width), jnp.float32)], axis=0)
    vec, vec_back = jax.vjp(
        partial(gate_vectors, seg_now, seg_ext[tap_count - 2]), gates_raw, decay_log.astype(jnp.float32)
    )
    zero_state = jnp.zeros((H, DV, DK), jnp.float32)
    inverse, key_part, value_part, transfer, inject, out_keys, out_values, final_state = forward_call(
        projected, border, taps, masks, vec, zero_state
    )
    entry = zero_state
    device_transfer = None
    if seqs > 2:
        eye = jnp.broadcast_to(jnp.eye(DK, dtype=jnp.float32), (H, DK, DK))
        device_transfer = chain_call(vec, transfer, eye)
    for turn in range(seqs - 1):
        leaving = final_state
        if turn > 0:
            leaving = leaving + jnp.einsum("hvk,hkl->hvl", entry, device_transfer, precision=HIGHEST)
        entry = from_behind(leaving.astype(jnp.bfloat16), "seq", 1).astype(jnp.float32)
    gain = jnp.broadcast_to(norm_out.astype(jnp.float32)[None, :], (8, DV))
    normed_out_low, mixed, solved, entries = readout_call(
        vec, key_part, value_part, transfer, inject, out_keys, out_values, entry, projected, gain
    )
    hidden = residual_in + jnp.dot(normed_out_low, out_all, preferred_element_type=jnp.float32)
    mlp_in, norm_mlp_back = jax.vjp(rms_scale, hidden, norm_mlp_all)
    mlp_in_low = mlp_in.astype(jnp.bfloat16)
    gate_up = jnp.dot(mlp_in_low, gu_all, preferred_element_type=jnp.float32)
    activated, act_back = jax.vjp(swiglu, gate_up)
    activated_low = activated.astype(jnp.bfloat16)
    result = hidden + jnp.dot(activated_low, down_all, preferred_element_type=jnp.float32)
    block_output = result.astype(jnp.bfloat16).reshape(block_input.shape)

    d_result_low = cotangent.reshape(seg_len, width)
    d_result = d_result_low.astype(jnp.float32)
    grad_down = jnp.einsum("nf,nd->fd", activated_low, d_result_low, preferred_element_type=jnp.float32)
    d_activated = jnp.einsum("nd,fd->nf", d_result_low, down_all, preferred_element_type=jnp.float32)
    (d_gate_up,) = act_back(d_activated)
    d_gate_low = d_gate_up.astype(jnp.bfloat16)
    grad_gu = jnp.einsum("nd,nf->df", mlp_in_low, d_gate_low, preferred_element_type=jnp.float32)
    d_mlp_in = jnp.einsum("nf,df->nd", d_gate_low, gu_all, preferred_element_type=jnp.float32)
    d_hidden_norm, grad_norm_mlp = norm_mlp_back(d_mlp_in)
    d_hidden = d_result + d_hidden_norm
    d_mixer_low = d_hidden.astype(jnp.bfloat16)
    grad_out = jnp.einsum("nh,nd->hd", normed_out_low, d_mixer_low, preferred_element_type=jnp.float32)
    d_normed_out = jnp.einsum("nd,hd->nh", d_mixer_low, out_all, preferred_element_type=jnp.float32)
    if fast:
        blocks = grad_down.astype(jnp.bfloat16).reshape(lax.axis_size("dp") * seqs, -1, width)
        down_rows = blocks.shape[1]
        blocks = jnp.pad(blocks, ((0, 0), (0, -down_rows % rows), (0, 0)))
        backs = mixer_back_call(
            vec, transfer, out_keys, mixed, projected, gain, d_normed_out, border, taps, masks, inverse, solved, entries,
            normed_low.T.reshape(STACK + (rows, seg_len)),
            grad_gu.astype(jnp.bfloat16).reshape(STACK + (rows, -1)),
            blocks.reshape(STACK + (-1, width)),
            grad_out.astype(jnp.bfloat16).reshape(STACK + (rows, -1)),
        )
        gain_parts, d_vec, tap_grads, d_projected = backs[0], backs[1], backs[2 : 2 + parts], backs[2 + parts]
        grad_gu, grad_down, grad_out, grad_mix = backs[3 + parts :]
        grad_down = grad_down.reshape(-1, width)[:down_rows]
    else:
        grad_gu = scatter_halves(grad_gu.astype(jnp.bfloat16))
        grad_down = scatter_halves(grad_down.astype(jnp.bfloat16))
        grad_out = scatter_halves(grad_out.astype(jnp.bfloat16))
        d_mixed, d_out_gate, local, own_entry, gain_parts = readout_back_call(
            vec, transfer, out_keys, mixed, projected, gain, d_normed_out, zero_state
        )
        exit_grad = zero_state
        for turn in range(seqs - 1):
            leaving = own_entry
            if turn > 0:
                leaving = leaving + jnp.einsum("hvl,hkl->hvk", exit_grad, device_transfer, precision=HIGHEST)
            exit_grad = from_behind(leaving.astype(jnp.bfloat16), "seq", -1).astype(jnp.float32)
        backs = backward_call(
            projected, border, taps, masks, vec, transfer, inverse, solved, entries, d_mixed, local, exit_grad
        )
        d_columns, edges, tap_grads, d_vec = backs[:parts], backs[parts : 2 * parts], backs[2 * parts : 3 * parts], backs[-1]
        edge = jnp.concatenate(edges, axis=1)
        returned = from_behind(edge[9 - tap_count : 8].astype(jnp.bfloat16), "seq", -1).astype(jnp.float32)
        fixed = (edge[17 - tap_count :] + returned).astype(jnp.bfloat16)
        d_projected = jnp.concatenate(list(d_columns) + [d_out_gate], axis=1)
        d_projected = lax.dynamic_update_slice(d_projected, fixed, (seg_len - tap_count + 1, 0))
        grad_mix = jnp.einsum("nd,nc->dc", normed_low, d_projected, preferred_element_type=jnp.float32)
        grad_mix = scatter_halves(grad_mix.astype(jnp.bfloat16))
    grad_norm_out = jnp.sum(gain_parts[:, 0, :], axis=0)
    d_gates_raw, grad_decay = vec_back(d_vec)
    d_gates_low = d_gates_raw.astype(jnp.bfloat16)
    grad_small = jnp.einsum("nd,nc->dc", normed_low, d_gates_low, preferred_element_type=jnp.float32)
    d_normed = jnp.einsum("nc,dc->nd", d_projected, mix_all, preferred_element_type=jnp.float32)
    d_normed = d_normed + jnp.einsum("nc,dc->nd", d_gates_low, small_all, preferred_element_type=jnp.float32)
    d_input_norm, grad_norm_in = norm_in_back(d_normed)
    input_grad = (d_hidden + d_input_norm).astype(jnp.bfloat16).reshape(block_input.shape)

    grad_conv = jnp.concatenate(tap_grads, axis=1)[:tap_count]
    devices = lax.axis_size("dp") * seqs
    conv_rows = grad_conv.reshape(tap_count, devices, -1).transpose(1, 0, 2).reshape(width, -1)
    packed = jnp.concatenate([grad_small, grad_norm_in[:, None], grad_norm_mlp[:, None], conv_rows], axis=1)
    packed = jnp.concatenate([packed, jnp.zeros((width, 128 - packed.shape[1]), jnp.float32)], axis=1)
    if fast:
        sums = jnp.stack([grad_norm_out, jnp.pad(grad_decay, (0, DV - H))] + [jnp.zeros((DV,), jnp.float32)] * 6)
        packed, sums = total_call(packed.reshape(STACK + (rows, -1)), sums)
        grad_norm_out, grad_decay = sums[0], sums[1, :H]
    else:
        packed = scatter_sum(packed, bit_orders()[0])
        sums = total_sum(jnp.concatenate([grad_norm_out, grad_decay]))
        grad_norm_out, grad_decay = sums[:DV], sums[DV:]
    smalls = grad_small.shape[1]
    grad_small = packed[:, :smalls]
    grad_norm_in, grad_norm_mlp = packed[:, smalls], packed[:, smalls + 1]
    grad_conv = packed[:, smalls + 2 : smalls + 2 + conv_rows.shape[1]].reshape(tap_count, -1)
    return (
        block_output, input_grad, grad_norm_in, grad_mix, grad_small, grad_conv, grad_decay,
        grad_norm_out, grad_out, grad_norm_mlp, grad_gu, grad_down,
    )


def solution(mesh):
    sharded = ("dp", "seq")
    in_specs = (
        P("dp", "seq", None), P("dp", None), P(sharded), P(sharded, None), P(sharded, None),
        P(None, sharded), P(), P(), P(sharded, None), P(sharded), P(sharded, None),
        P(sharded, None), P("dp", "seq", None),
    )
    out_specs = (
        P("dp", "seq", None), P("dp", "seq", None), P(sharded), P(sharded, None), P(sharded, None),
        P(None, sharded), P(), P(), P(sharded, None), P(sharded), P(sharded, None), P(sharded, None),
    )
    return jax.shard_map(
        on_device, mesh=mesh, in_specs=in_specs, out_specs=out_specs, check_vma=False
    )
```

```python
from functools import partial

import jax
import jax.numpy as jnp
from jax import lax
from jax.experimental import pallas as pl
from jax.experimental.pallas import tpu as pltpu
from jax.sharding import PartitionSpec as P

H = 8
DK = 128
DV = 128
NH = 2
GROUP = 64
SPAN = NH * GROUP
LEVELS = 6
EPSILON = 1e-06
HIGHEST = lax.Precision.HIGHEST
LIMIT = 50 * 1024 * 1024


def mm(left, right, left_dim=1, right_dim=0):
    return lax.dot_general(
        left.astype(jnp.bfloat16),
        right.astype(jnp.bfloat16),
        (((left_dim,), (right_dim,)), ((), ())),
        preferred_element_type=jnp.float32,
    )


def halves_of(values):
    high = values.astype(jnp.bfloat16)
    return high, (values - high.astype(jnp.float32)).astype(jnp.bfloat16)


def mm3(left, right, left_dim=1, right_dim=0):
    left_high, left_low = halves_of(left)
    right_high, right_low = halves_of(right)
    wide = right.shape[1 - right_dim]
    lefts = jnp.concatenate([left_high, left_low], axis=left_dim)
    rights = jnp.concatenate(
        [
            jnp.concatenate([right_high, right_high], axis=right_dim),
            jnp.concatenate([right_low, jnp.zeros_like(right_low)], axis=right_dim),
        ],
        axis=1 - right_dim,
    )
    both = mm(lefts, rights, left_dim, right_dim)
    return both[:, :wide] + both[:, wide:]


def iotas(rows, columns):
    return (
        lax.broadcasted_iota(jnp.int32, (rows, columns), 0),
        lax.broadcasted_iota(jnp.int32, (rows, columns), 1),
    )


def order_masks():
    row, column = iotas(SPAN, SPAN)
    row_tok, column_tok = row % GROUP, column % GROUP
    row_step, column_step = row // GROUP, column // GROUP
    pair = (row_tok == column_tok) & (row_step > column_step)
    strict = (row_tok > column_tok) | pair
    levels = []
    for level in range(LEVELS):
        row_half, column_half = row_tok >> level, column_tok >> level
        levels.append((row_half == column_half + 1) & (row_half % 2 == 1))
    eye = jnp.where(row == column, 1.0, 0.0)
    return strict, pair, levels, eye


TOGETHER = 16


def together(runs):
    for first in range(0, len(runs), TOGETHER):
        group = runs[first : first + TOGETHER]
        while group:
            group = [run for run in group if next(run, "done") != "done"]


def unit_inverses(lowers, pair, levels, eye):
    inverses = [eye - jnp.where(pair, lower, 0.0) for lower in lowers]
    for level in levels:
        parts = [mm3(jnp.where(level, lower, 0.0), inv) for lower, inv in zip(lowers, inverses)]
        inverses = [inv - mm3(inv, part) for part, inv in zip(parts, inverses)]
    return inverses


def silu_pair(values):
    sig = jax.nn.sigmoid(values)
    return values * sig, sig


def conv_block(channels, border, taps, mask_ref, ext_ref):
    length = channels.shape[0]
    ext_ref[0:8, :] = border
    ext_ref[8 : 8 + length, :] = channels
    summed = channels * taps[0:1, :]
    for tap in range(1, 4):
        summed = summed + ext_ref[8 - tap : 8 - tap + length, :] * taps[tap : tap + 1, :] * mask_ref[tap - 1].astype(jnp.float32)
    return summed


def unit_rows(values):
    inv = lax.rsqrt(jnp.sum(values * values, axis=1, keepdims=True) + EPSILON)
    return values * inv, inv


def chunk_vectors(vec_ref, chunk):
    rows = vec_ref[0, chunk]
    columns = jnp.transpose(rows)
    return rows, columns


def link_matrix(rows, columns):
    row, column = iotas(GROUP, SPAN)
    linked = (columns[:GROUP, 2:3] == rows[2:3, :]) & (row >= column % GROUP)
    return jnp.exp(jnp.where(linked, columns[:GROUP, 0:1] - rows[0:1, :], -1e30))


def twice(values):
    return jnp.concatenate([values, values], axis=0)


def forward_kernel(
    q_in, k0_in, k1_in, v0_in, v1_in,
    bq, bk0, bk1, bv0, bv1,
    tq, tk0, tk1, tv0, tv1,
    mask_ref, vec_ref, start_ref,
    x_out, w_out, u_out, t_out, i_out, ok_out, o_out, state_out,
    ext_ref, q_ref, k_ref, v_ref,
):
    length = q_in.shape[0]
    chunks = length // GROUP
    conv = []
    for channel, border, tap in (
        (q_in, bq, tq), (k0_in, bk0, tk0), (k1_in, bk1, tk1), (v0_in, bv0, tv0), (v1_in, bv1, tv1),
    ):
        conv.append(silu_pair(conv_block(channel[...], border[...], tap[...], mask_ref, ext_ref))[0])
    q_ref[...] = unit_rows(conv[0])[0] * DK ** (-0.5)
    for step in range(NH):
        k_ref[step] = unit_rows(conv[1 + step])[0]
        v_ref[step] = conv[1 + NH + step]
    strict, pair, levels, eye = order_masks()
    items = []
    lowers = []
    for chunk in range(chunks):
        here = slice(chunk * GROUP, (chunk + 1) * GROUP)
        rows, columns = chunk_vectors(vec_ref, chunk)
        keys = k_ref[:, here, :].reshape(SPAN, DK)
        values = v_ref[:, here, :].reshape(SPAN, DV)
        queries = q_ref[here, :]
        link = link_matrix(rows, columns)
        lower = jnp.where(strict, columns[:, 1:2] * twice(link) * mm3(keys, keys, 1, 1), 0.0)
        reading = link * mm3(queries, keys, 1, 1)
        lowers.append(lower)
        items.append((rows, columns, keys, values, queries, reading))
    inverses = unit_inverses(lowers, pair, levels, eye)
    state = start_ref[0]
    for chunk in range(chunks):
        rows, columns, keys, values, queries, reading = items[chunk]
        inverse = inverses[chunk]
        here = slice(chunk * GROUP, (chunk + 1) * GROUP)
        beta, scale, tail = columns[:, 1:2], columns[:, 3:4], columns[:, 4:5]
        key_part = mm3(inverse, beta * scale * keys)
        value_part = mm3(inverse, beta * values)
        tail_keys = tail * keys
        transfer = mm3(key_part, tail_keys, 0, 0)
        inject = mm3(value_part, tail_keys, 0, 0)
        x_out[0, chunk] = inverse.astype(x_out.dtype)
        w_out[0, chunk] = key_part.astype(w_out.dtype)
        u_out[0, chunk] = value_part.astype(u_out.dtype)
        t_out[0, chunk] = transfer.astype(t_out.dtype)
        i_out[0, chunk] = inject
        ok_out[0, chunk] = (columns[:GROUP, 3:4] * queries - mm3(reading, key_part)).astype(ok_out.dtype)
        o_out[0, chunk] = mm3(reading, value_part)
        state = rows[3:4, GROUP - 1 : GROUP] * state - mm3(state, transfer) + inject
    state_out[0] = state


def chain_kernel(vec_ref, t_in, start_ref, state_out):
    chunks = t_in.shape[1]
    state = start_ref[0]
    for chunk in range(chunks):
        state = vec_ref[0, chunk, 3:4, GROUP - 1 : GROUP] * state - mm3(state, t_in[0, chunk])
    state_out[0] = state


def readout_kernel(vec_ref, w_in, u_in, t_in, i_in, ok_in, o_in, entry_ref, gate_ref, gain_ref, gated_out, mixed_out, u_out, s_out):
    chunks = w_in.shape[1]
    state = entry_ref[0]
    states = []
    for chunk in range(chunks):
        states.append(state)
        state = vec_ref[0, chunk, 3:4, GROUP - 1 : GROUP] * state - mm3(state, t_in[0, chunk]) + i_in[0, chunk]
    for chunk in range(chunks):
        here = slice(chunk * GROUP, (chunk + 1) * GROUP)
        state = states[chunk]
        s_out[0, chunk] = state
        u_out[0, chunk] = (u_in[0, chunk].astype(jnp.float32) - mm3(w_in[0, chunk], state, 1, 1)).astype(u_out.dtype)
        mixed = o_in[0, chunk] + mm3(ok_in[0, chunk], state, 1, 1)
        mixed_out[here, :] = mixed
        inv = lax.rsqrt(jnp.mean(mixed * mixed, axis=1, keepdims=True) + EPSILON)
        gate = silu_pair(gate_ref[here, :])[0]
        gated_out[here, :] = (mixed * inv * gain_ref[0:1, :] * gate).astype(gated_out.dtype)


def readout_back_kernel(vec_ref, t_in, ok_in, mixed_in, gate_ref, gain_ref, d_ref, start_ref, d_mixed_out, d_gate_out, local_out, state_out, gain_out):
    chunks = t_in.shape[1]
    gain = gain_ref[0:1, :]
    gain_grad = jnp.zeros((1, DV), jnp.float32)
    locals_ = []
    for chunk in range(chunks):
        here = slice(chunk * GROUP, (chunk + 1) * GROUP)
        mixed = mixed_in[here, :]
        inv = lax.rsqrt(jnp.mean(mixed * mixed, axis=1, keepdims=True) + EPSILON)
        unit = mixed * inv
        gate = gate_ref[here, :]
        open_, sig = silu_pair(gate)
        d_gated = d_ref[here, :]
        d_scaled = d_gated * open_
        d_gate_out[here, :] = (d_gated * unit * gain * sig * (1.0 + gate * (1.0 - sig))).astype(d_gate_out.dtype)
        gain_grad = gain_grad + jnp.sum(d_scaled * unit, axis=0, keepdims=True)
        d_unit = d_scaled * gain
        d_mixed = inv * (d_unit - unit * jnp.mean(d_unit * unit, axis=1, keepdims=True))
        d_mixed_low = d_mixed
        d_mixed_out[here, :] = d_mixed_low
        local = mm3(d_mixed_low, ok_in[0, chunk], 0, 0)
        local_out[0, chunk] = local
        locals_.append(local)
    gain_out[0] = jnp.broadcast_to(gain_grad, (8, DV))
    state = start_ref[0]
    for chunk in reversed(range(chunks)):
        state = vec_ref[0, chunk, 3:4, GROUP - 1 : GROUP] * state - mm3(state, t_in[0, chunk], 1, 1) + locals_[chunk]
    state_out[0] = state


def backward_kernel(
    q_in, k0_in, k1_in, v0_in, v1_in,
    bq, bk0, bk1, bv0, bv1,
    tq, tk0, tk1, tv0, tv1,
    mask_ref, vec_ref, t_in, x_in, u_in, s_in, d_mixed_in, local_in, exit_ref,
    dq_out, dk0_out, dk1_out, dv0_out, dv1_out,
    eq_out, ek0_out, ek1_out, ev0_out, ev1_out,
    gq_out, gk0_out, gk1_out, gv0_out, gv1_out,
    d_vec_out,
    ext_ref, pre_ref, q_ref, k_ref, v_ref, inv_ref, d_ref, z_ref,
):
    length = q_in.shape[0]
    chunks = length // GROUP
    channels = (q_in, k0_in, k1_in, v0_in, v1_in)
    taps = (tq, tk0, tk1, tv0, tv1)
    for part, (channel, border, tap) in enumerate(zip(channels, (bq, bk0, bk1, bv0, bv1), taps)):
        pre = conv_block(channel[...], border[...], tap[...], mask_ref, ext_ref.at[part])
        pre_ref[part] = pre
        value = silu_pair(pre)[0]
        if part == 0:
            unit, inv = unit_rows(value)
            q_ref[...] = unit * DK ** (-0.5)
            inv_ref[0] = jnp.broadcast_to(inv, (length, DK))
        elif part <= NH:
            unit, inv = unit_rows(value)
            k_ref[part - 1] = unit
            inv_ref[part] = jnp.broadcast_to(inv, (length, DK))
        else:
            v_ref[part - 1 - NH] = value
    strict, pair, levels, eye = order_masks()
    column_index = iotas(SPAN, 8)[1]
    exit_grads = [None] * chunks
    grad = exit_ref[0]
    for chunk in reversed(range(chunks)):
        exit_grads[chunk] = grad
        grad = vec_ref[0, chunk, 3:4, GROUP - 1 : GROUP] * grad - mm3(grad, t_in[0, chunk], 1, 1) + local_in[0, chunk]
    for chunk in reversed(range(chunks)):
        here = slice(chunk * GROUP, (chunk + 1) * GROUP)
        rows, columns = chunk_vectors(vec_ref, chunk)
        beta, scale, tail = columns[:, 1:2], columns[:, 3:4], columns[:, 4:5]
        keys = k_ref[:, here, :].reshape(SPAN, DK)
        values = v_ref[:, here, :].reshape(SPAN, DV)
        queries = q_ref[here, :]
        link = link_matrix(rows, columns)
        link_gram = jnp.where(strict, twice(link) * mm3(keys, keys, 1, 1), 0.0)
        reading = link * mm3(queries, keys, 1, 1)
        d_exit = exit_grads[chunk]
        solved = u_in[0, chunk]
        entry = s_in[0, chunk]
        d_mixed = d_mixed_in[here, :]
        tail_keys = tail * keys
        d_solved = mm3(reading, d_mixed, 0, 0) + mm3(tail_keys, d_exit, 1, 1)
        d_right = mm3(x_in[0, chunk], d_solved, 0, 0)
        d_lower = jnp.where(strict, -mm3(d_right, solved, 1, 1), 0.0)
        d_tail_keys = mm3(solved, d_exit)
        d_right_entry = mm3(d_right, entry)
        d_reading = mm3(d_mixed, solved, 1, 1)
        d_query_entry = mm3(d_mixed, entry)
        both_scale = -jnp.sum(d_right_entry * keys, axis=1, keepdims=True)
        lower_weight = d_lower * link_gram
        d_beta = (
            jnp.sum(d_right * values, axis=1, keepdims=True)
            + scale * both_scale
            + jnp.sum(lower_weight, axis=1, keepdims=True)
        )
        lower_moment = lower_weight * beta
        reading_moment = d_reading * reading
        d_gram = beta * twice(link) * d_lower
        d_gram = d_gram + jnp.transpose(d_gram)
        d_query_gram = link * d_reading
        d_keys = (
            tail * d_tail_keys
            - beta * scale * d_right_entry
            + mm3(d_gram, keys)
            + mm3(d_query_gram, queries, 0, 0)
        )
        d_queries = mm3(d_query_gram, keys) + scale[:GROUP] * d_query_entry
        d_values = beta * d_right
        none = jnp.zeros((GROUP, 1), jnp.float32)
        d_gap = jnp.sum(lower_moment, axis=1, keepdims=True) + jnp.concatenate(
            [jnp.sum(reading_moment, axis=1, keepdims=True), none], axis=0
        )
        last = jnp.sum(jnp.sum(d_exit * entry.astype(jnp.float32), axis=1, keepdims=True), axis=0, keepdims=True)
        own_scale = jnp.sum(d_query_entry * queries, axis=1, keepdims=True)
        own_scale = own_scale + jnp.where(iotas(GROUP, 1)[0] == GROUP - 1, last, 0.0)
        d_scale = beta * both_scale + jnp.concatenate([own_scale, none], axis=0)
        d_tail = jnp.sum(d_tail_keys * keys, axis=1, keepdims=True)
        grads = jnp.where(
            column_index == 0,
            d_gap,
            jnp.where(
                column_index == 1,
                d_beta,
                jnp.where(column_index == 3, d_scale, jnp.where(column_index == 4, d_tail, 0.0)),
            ),
        )
        grads = jnp.transpose(grads)
        sums = jnp.sum(lower_moment, axis=0, keepdims=True) + jnp.sum(reading_moment, axis=0, keepdims=True)
        grads = grads - jnp.where(iotas(8, SPAN)[0] == 0, sums, 0.0)
        d_vec_out[0, chunk] = grads
        d_ref[0, here, :] = d_queries
        for step in range(NH):
            mine = slice(step * GROUP, (step + 1) * GROUP)
            d_ref[1 + step, here, :] = d_keys[mine]
            d_ref[1 + NH + step, here, :] = d_values[mine]
    outs = (dq_out, dk0_out, dk1_out, dv0_out, dv1_out)
    edges = (eq_out, ek0_out, ek1_out, ev0_out, ev1_out)
    tap_grads = (gq_out, gk0_out, gk1_out, gv0_out, gv1_out)
    z_ref[0:8, :] = jnp.zeros((8, DK), jnp.float32)
    z_ref[8 + length : 16 + length, :] = jnp.zeros((8, DK), jnp.float32)
    for part in range(1 + 2 * NH):
        grad = d_ref[part]
        if part <= NH:
            unit = q_ref[...] * DK ** 0.5 if part == 0 else k_ref[part - 1]
            if part == 0:
                grad = grad * DK ** (-0.5)
            grad = inv_ref[part] * (grad - unit * jnp.sum(grad * unit, axis=1, keepdims=True))
        pre = pre_ref[part]
        sig = jax.nn.sigmoid(pre)
        grad = grad * sig * (1.0 + pre * (1.0 - sig))
        tap = taps[part]
        total = grad * tap[0:1, :]
        edge = jnp.zeros((8, DK), jnp.float32)
        tap_rows = [jnp.sum(grad * channels[part][...], axis=0, keepdims=True)]
        for index in range(1, 4):
            shifted = grad * mask_ref[index - 1]
            tap_rows.append(
                jnp.sum(shifted * ext_ref[part, 8 - index : 8 - index + length, :], axis=0, keepdims=True)
            )
            z_ref[8 : 8 + length, :] = shifted * tap[index : index + 1, :]
            total = total + z_ref[8 + index : 8 + index + length, :]
            edge = edge + z_ref[index : index + 8, :]
        outs[part][...] = total.astype(outs[part].dtype)
        edges[part][0:8, :] = edge
        edges[part][8:16, :] = total[length - 8 :, :]
        tap_grads[part][...] = jnp.concatenate(tap_rows + [jnp.zeros((4, DK), jnp.float32)], axis=0)


MESH = pl.DeviceIdType.MESH
ZS = 4
STACK = (ZS, 2, 2, 2)
STAGES = 6


def place():
    dp, seq = lax.axis_index("dp"), lax.axis_index("seq")
    return dp // 4, (dp // 2) % 2, dp % 2, seq


def device_at(z, x, core, y):
    return (z * 4 + x * 2 + core, y)


def peers():
    z, x, core, y = place()
    ring = [device_at((z + step) % ZS, x, core, y) for step in range(1, ZS)]
    return ring + [device_at(z, 1 - x, core, y), device_at(z, x, core, 1 - y), device_at(z, x, 1 - core, y)]


def meet(devices):
    barrier = pltpu.get_barrier_semaphore()
    for device in devices:
        pl.semaphore_signal(barrier, inc=1, device_id=device, device_id_type=MESH)
    pl.semaphore_wait(barrier, len(devices))


class Gather:
    def __init__(self, source, target, x_first, sems, index):
        self.source, self.target, self.x_first = source, target, x_first
        self.send, self.recv, self.local = sems
        self.index = index
        self.copies = []

    def remote(self, source, target, slot):
        copy = pltpu.make_async_remote_copy(
            src_ref=source, dst_ref=target,
            send_sem=self.send.at[self.index, slot], recv_sem=self.recv.at[self.index, slot],
            device_id=peers()[slot], device_id_type=MESH,
        )
        copy.start()
        self.copies.append(copy)
        return copy

    def begin(self):
        z, x, core, y = place()
        mine = self.target(z, x, core, y)
        self.own = pltpu.make_async_copy(self.source, mine, self.local.at[self.index])
        self.own.start()
        self.waiting = [self.remote(self.source, mine, slot) for slot in range(ZS - 1)]

    def second(self):
        z, x, core, y = place()
        self.own.wait()
        for copy in self.waiting:
            copy.wait_recv()
        block = self.target(slice(None), x, core, y)
        self.waiting = [self.remote(block, block, ZS - 1 if self.x_first else ZS)]

    def third(self):
        z, x, core, y = place()
        self.waiting[0].wait_recv()
        every = slice(None)
        block = self.target(every, every, core, y) if self.x_first else self.target(every, x, core, every)
        self.waiting = [self.remote(block, block, ZS if self.x_first else ZS - 1)]

    def fourth(self):
        z, x, core, y = place()
        self.waiting[0].wait_recv()
        every = slice(None)
        block = self.target(every, every, core, every)
        self.waiting = [self.remote(block, block, ZS + 1)]

    def finish(self):
        self.waiting[0].wait_recv()
        for copy in self.copies:
            copy.wait_send()


def columns_of(ref, first, width):
    return lambda z, x, core, y: ref.at[z, x, core, y, :, pl.ds(first, width)]


class Spread:
    def __init__(self, source, target, lane, width, sems, first=0):
        self.first = first
        self.source, self.target, self.lane, self.width = source, target, lane, width
        self.send_sem, self.recv_sem, self.local_sem = sems
        self.place, self.peers = place(), peers()

    def here(self, index):
        return pl.ds(pl.multiple_of((2 * (index - self.first) + self.lane) * self.width, self.width), self.width)

    def block(self, index, stage):
        z, x, core, y = self.place
        every = slice(None)
        here = self.here(index)
        if stage == 0:
            return self.target.at[z, x, core, y, :, here]
        if stage == 1:
            return self.target.at[:, x, core, y, :, here]
        if stage == 2:
            if self.lane == 0:
                return self.target.at[:, :, core, y, :, here]
            return self.target.at[:, x, core, :, :, here]
        return self.target.at[:, :, core, :, :, here]

    def copies(self, index, stage):
        near, far = (ZS - 1, ZS) if self.lane == 0 else (ZS, ZS - 1)
        slots = (0, 1, 2) if stage == 0 else ((near,), (far,), (ZS + 1,))[stage - 1]
        target = self.block(index, stage)
        source = self.source.at[:, self.here(index)] if stage == 0 else target
        ring = lax.rem(index, RING)
        return [
            pltpu.make_async_remote_copy(
                src_ref=source, dst_ref=target,
                send_sem=self.send_sem.at[self.lane, slot, ring], recv_sem=self.recv_sem.at[self.lane, slot, ring],
                device_id=self.peers[slot], device_id_type=MESH,
            )
            for slot in slots
        ]

    def own(self, index):
        return pltpu.make_async_copy(
            self.source.at[:, self.here(index)], self.block(index, 0), self.local_sem.at[self.lane, lax.rem(index, RING)]
        )

    def step(self, index, stage):
        if stage > 0:
            for copy in self.copies(index, stage - 1):
                copy.wait_recv()
                copy.wait_send()
        if stage == 1:
            self.own(index).wait()
        if stage == 0:
            self.own(index).start()
        if stage < SPREAD_STAGES - 1:
            for copy in self.copies(index, stage):
                copy.start()


SPREAD_STAGES = 5
SPREAD_TICKS = 2
SPREAD_FILL = (SPREAD_STAGES - 1) * SPREAD_TICKS
FINE = 256


def gather_project_kernel(
    x_ref, small_in, mix_in, out_in,
    mix_out, out_out, small_out, normed_ref, normed_t_ref, channels_out, gate_out, gates_ref, border_ref,
    mix_ref, small_ref, slab_ref,
    small_send, small_recv, small_local, send, recv, local, store_mix, store_slab, store_small, edge_send, edge_recv,
):
    parts, heads = channels_out.shape[0], channels_out.shape[1]
    length = x_ref.shape[0]
    block = 2 * FINE
    count = mix_in.shape[1] // block
    more = out_in.shape[1] // block
    per_part, across = heads * DK // block, block // DK
    z, x, core, y = place()
    sems = (send, recv, local)
    small = Gather(small_in, lambda z, x, core, y: small_ref.at[z, x, core, y], True, (small_send, small_recv, small_local), 0)
    mix_lanes = [Spread(mix_in, mix_ref, lane, FINE, sems) for lane in range(2)]
    out_lanes = [Spread(out_in, out_out, lane, FINE, sems, count) for lane in range(2)]

    def here(index):
        return pl.ds(pl.multiple_of(index * block, block), block)

    def slab_copies(index):
        slot, first = lax.rem(index, 2), lax.rem(index, per_part) * across
        return [
            [
                pltpu.make_async_copy(
                    slab_ref.at[slot, :, half * DK : (half + 1) * DK], target.at[first + half], store_slab.at[slot, half]
                )
                for half in range(across)
            ]
            for target in (channels_out.at[jnp.minimum(index // per_part, parts - 1)], gate_out)
        ]

    def edge(index):
        return pltpu.make_async_remote_copy(
            src_ref=slab_ref.at[lax.rem(index, 2), length - 8 :, :], dst_ref=border_ref.at[:, here(index)],
            send_sem=edge_send.at[lax.rem(index, 2)], recv_sem=edge_recv.at[index],
            device_id=device_at(z, x, core, 1 - y), device_id_type=MESH,
        )

    def kept(index):
        return pltpu.make_async_copy(
            mix_ref.at[:, :, :, :, :, here(index)], mix_out.at[:, :, :, :, :, here(index)], store_mix.at[lax.rem(index, 2)]
        )

    def release(index):
        for copy in slab_copies(index)[0]:
            copy.wait()
        kept(index).wait()

        @pl.when(index < parts * per_part)
        def _():
            edge(index).wait_send()

    def project(index):
        @pl.when(index >= 2)
        def _():
            release(index - 2)

        kept(index).start()
        weights = mix_ref[:, :, :, :, :, here(index)].reshape(-1, block)
        slab_ref[lax.rem(index, 2)] = mm(normed_ref[...], weights)
        channels, gates = slab_copies(index)

        @pl.when(index < parts * per_part)
        def _():
            for copy in channels:
                copy.start()
            edge(index).start()

        @pl.when(index >= parts * per_part)
        def _():
            for copy in gates:
                copy.start()

    def tick(number):
        for stage in reversed(range(SPREAD_STAGES)):
            index = number - stage * SPREAD_TICKS

            @pl.when((index >= 0) & (index < count))
            def _():
                for lane in mix_lanes:
                    lane.step(index, stage)

            @pl.when((index >= count) & (index < count + more))
            def _():
                for lane in out_lanes:
                    lane.step(index, stage)

        @pl.when((number >= SPREAD_FILL) & (number < count + SPREAD_FILL))
        def _():
            project(number - SPREAD_FILL)

    meet(peers())
    small.begin()
    for number in range(SPREAD_FILL):
        tick(number)
        if number == 0:
            values = x_ref[...].astype(jnp.float32)
            scaled = values * lax.rsqrt(jnp.mean(values * values, axis=1, keepdims=True) + EPSILON)
        if number % SPREAD_TICKS == SPREAD_TICKS - 1:
            (small.second, small.third, small.fourth, small.finish)[number // SPREAD_TICKS]()
    smalls = small_ref[...].reshape(-1, small_in.shape[1])
    gain = jnp.transpose(smalls.astype(jnp.float32))[24:25, :]
    normed = (scaled * gain).astype(jnp.bfloat16)
    normed_ref[...] = normed
    keep_small = pltpu.make_async_copy(small_ref, small_out, store_small)
    keep_small.start()

    def loop(number, carry):
        tick(number)
        return carry

    lax.fori_loop(SPREAD_FILL, 2 * SPREAD_FILL, loop, 0)
    gates_ref[...] = mm(normed_ref[...], smalls)
    flipped = jnp.transpose(normed_ref[...].astype(jnp.float32)).astype(jnp.bfloat16)
    normed_t_ref[...] = flipped.reshape(normed_t_ref.shape)
    lax.fori_loop(2 * SPREAD_FILL, count + more + SPREAD_FILL, loop, 0)
    release(count - 2)
    release(count - 1)
    keep_small.wait()

    def last(index, carry):
        edge(index).wait_recv()
        return carry

    lax.fori_loop(0, parts * per_part, last, 0)


def gather_project_call(x, small, mix, out):
    length = x.shape[0]
    rows, width = mix.shape
    everywhere = pl.BlockSpec(memory_space=pl.ANY)
    held = pl.BlockSpec(memory_space=pltpu.VMEM)
    full = STACK + (rows,)
    block = 2 * FINE
    parts = width // (H * DK) - 1
    outs = pl.pallas_call(
        gather_project_kernel,
        out_shape=[
            jax.ShapeDtypeStruct(full + (width,), jnp.bfloat16),
            jax.ShapeDtypeStruct(full + (out.shape[1],), jnp.bfloat16),
            jax.ShapeDtypeStruct(full + (small.shape[1],), jnp.bfloat16),
            jax.ShapeDtypeStruct(x.shape, jnp.bfloat16),
            jax.ShapeDtypeStruct(full + (length,), jnp.bfloat16),
            jax.ShapeDtypeStruct((parts, H, length, DK), jnp.float32),
            jax.ShapeDtypeStruct((H, length, DK), jnp.float32),
            jax.ShapeDtypeStruct((length, small.shape[1]), jnp.float32),
            jax.ShapeDtypeStruct((8, parts * H * DK), jnp.float32),
        ],
        in_specs=[held, everywhere, everywhere, everywhere],
        out_specs=[everywhere, everywhere, everywhere, held, held, everywhere, everywhere, held, held],
        scratch_shapes=[
            pltpu.VMEM(full + (width,), jnp.bfloat16),
            pltpu.VMEM(full + (small.shape[1],), jnp.bfloat16),
            pltpu.VMEM((2, length, block), jnp.float32),
            pltpu.SemaphoreType.DMA((1, STAGES)),
            pltpu.SemaphoreType.DMA((1, STAGES)),
            pltpu.SemaphoreType.DMA((1,)),
            pltpu.SemaphoreType.DMA((2, STAGES, RING)),
            pltpu.SemaphoreType.DMA((2, STAGES, RING)),
            pltpu.SemaphoreType.DMA((2, RING)),
            pltpu.SemaphoreType.DMA((2,)),
            pltpu.SemaphoreType.DMA((2, block // DK)),
            pltpu.SemaphoreType.DMA,
            pltpu.SemaphoreType.DMA((2,)),
            pltpu.SemaphoreType.DMA((parts * H * DK // block,)),
        ],
        compiler_params=pltpu.CompilerParams(collective_id=1, has_side_effects=True, vmem_limit_bytes=LIMIT),
        cost_estimate=pl.CostEstimate(flops=2 * length * width * 1024, bytes_accessed=60_000_000, transcendentals=0),
    )(x, small, mix, out)
    return [part.reshape((-1,) + part.shape[5:]) if index < 3 else part for index, part in enumerate(outs)]


PAIR = 2


def mixer_kernel(
    channel_ref, gate_ref, vec_ref, mask_ref, tap_ref, border_ref, gain_ref, shard_in,
    xt_out, ok_out, us_out, gated_out, mixed_out, gathered_out,
    w_ref, u_ref, t_ref, i_ref, k_read_ref, v_read_ref, relay_send, relay_recv,
    ext_ref, q_ref, k_ref, v_ref,
    relay_sems, send_sem, recv_sem, local_sem,
):
    step = pl.program_id(0)
    steps = H // PAIR
    parts = channel_ref.shape[0]
    length = channel_ref.shape[2]
    chunks = length // GROUP
    z, x, core, y = place()
    count = shard_in.shape[1] // (2 * WIDE)
    lanes = [Spread(shard_in, gathered_out, lane, WIDE, (send_sem, recv_sem, local_sem)) for lane in range(2)]

    def tick(number):
        for stage in reversed(range(SPREAD_STAGES)):
            index = number - stage * SPREAD_TICKS

            @pl.when((index >= 0) & (index < count))
            def _():
                for lane in lanes:
                    lane.step(index, stage)

    def convolve(pair):
        head = step * PAIR + pair
        column = lambda part: pl.ds(pl.multiple_of((part * H + head) * DK, DK), DK)
        for part in range(parts):
            value = silu_pair(
                conv_block(
                    channel_ref[part, pair], border_ref[:, column(part)], tap_ref[:, column(part)], mask_ref,
                    ext_ref.at[pair],
                )
            )[0]
            if part == 0:
                q_ref[pair] = unit_rows(value)[0] * DK ** (-0.5)
            elif part <= NH:
                k_ref[pair, part - 1] = unit_rows(value)[0]
            else:
                v_ref[pair, part - 1 - NH] = value
            yield

    def chunk_terms(pair, chunk, masks):
        strict, same, levels, eye = masks
        head = step * PAIR + pair
        here = slice(chunk * GROUP, (chunk + 1) * GROUP)
        rows = vec_ref[head, chunk]
        columns = jnp.transpose(rows)
        keys = k_ref[pair, :, here, :].reshape(SPAN, DK)
        beta, scale, tail = columns[:, 1:2], columns[:, 3:4], columns[:, 4:5]
        link = link_matrix(rows, columns)
        lower = jnp.where(strict, beta * twice(link) * mm3(keys, keys, 1, 1), 0.0)
        yield
        inverse = eye - jnp.where(same, lower, 0.0)
        for level in levels:
            part = mm3(jnp.where(level, lower, 0.0), inverse)
            yield
            inverse = inverse - mm3(inverse, part)
            yield
        xt_out[pair, 0, chunk] = inverse

    def chunk_rest(pair, chunk):
        head = step * PAIR + pair
        here = slice(chunk * GROUP, (chunk + 1) * GROUP)
        rows = vec_ref[head, chunk]
        columns = jnp.transpose(rows)
        keys = k_ref[pair, :, here, :].reshape(SPAN, DK)
        values = v_ref[pair, :, here, :].reshape(SPAN, DV)
        queries = q_ref[pair, here, :]
        beta, scale, tail = columns[:, 1:2], columns[:, 3:4], columns[:, 4:5]
        inverse = xt_out[pair, 0, chunk]
        reading = link_matrix(rows, columns) * mm3(queries, keys, 1, 1)
        key_part = mm3(inverse, beta * scale * keys)
        value_part = mm3(inverse, beta * values)
        w_ref[head, chunk] = key_part
        u_ref[head, chunk] = value_part
        yield
        tail_keys = tail * keys
        transfer = mm3(key_part, tail_keys, 0, 0)
        inject = mm3(value_part, tail_keys, 0, 0)
        t_ref[head, chunk] = transfer
        xt_out[pair, 1, chunk] = transfer
        i_ref[head, chunk] = inject
        yield
        read_keys = scale[:GROUP] * queries - mm3(reading, key_part)
        k_read_ref[head, chunk] = read_keys
        ok_out[pair, chunk] = read_keys
        v_read_ref[head, chunk] = mm3(reading, value_part)

    def final_state(pair):
        head = step * PAIR + pair
        state = jnp.zeros((DV, DK), jnp.float32)
        for chunk in range(chunks):
            state = (
                vec_ref[head, chunk, 3:4, GROUP - 1 : GROUP] * state - mm3(state, t_ref[head, chunk]) + i_ref[head, chunk]
            )
            yield
        relay_send[head] = state.astype(jnp.bfloat16)

    def readout(pair):
        head = (step - steps) * PAIR + pair
        state = jnp.where(y == 0, 0.0, 1.0) * relay_recv[head].astype(jnp.float32)
        for chunk in range(chunks):
            here = slice(chunk * GROUP, (chunk + 1) * GROUP)
            us_out[pair, 1, chunk] = state
            later = (
                vec_ref[head, chunk, 3:4, GROUP - 1 : GROUP] * state - mm3(state, t_ref[head, chunk]) + i_ref[head, chunk]
            )
            us_out[pair, 0, chunk] = u_ref[head, chunk] - mm3(w_ref[head, chunk], state, 1, 1)
            mixed = v_read_ref[head, chunk] + mm3(k_read_ref[head, chunk], state, 1, 1)
            yield
            mixed_out[pair, here, :] = mixed
            inv = lax.rsqrt(jnp.mean(mixed * mixed, axis=1, keepdims=True) + EPSILON)
            gate = silu_pair(gate_ref[pair, here, :])[0]
            gated = mixed * inv * gain_ref[0:1, :] * gate
            gated_out[here, pair * DV : (pair + 1) * DV] = gated.astype(gated_out.dtype)
            state = later

    relay = pltpu.make_async_remote_copy(
        src_ref=relay_send, dst_ref=relay_recv, send_sem=relay_sems.at[0], recv_sem=relay_sems.at[1],
        device_id=device_at(z, x, core, 1 - y), device_id_type=MESH,
    )

    @pl.when(step == 0)
    def _():
        meet(peers())

    @pl.when(step < steps)
    def _():
        tick(step * 3)
        together([convolve(pair) for pair in range(PAIR)])
        masks = order_masks()
        together([chunk_terms(pair, chunk, masks) for pair in range(PAIR) for chunk in range(chunks)])
        tick(step * 3 + 1)
        together([chunk_rest(pair, chunk) for pair in range(PAIR) for chunk in range(chunks)])
        together([final_state(pair) for pair in range(PAIR)])
        tick(step * 3 + 2)

    @pl.when(step == steps - 1)
    def _():
        relay.start()

    @pl.when(step == steps)
    def _():
        relay.wait()

    @pl.when(step >= steps)
    def _():
        tick(steps * 3 + step - steps)
        together([readout(pair) for pair in range(PAIR)])

    @pl.when(step == 2 * steps - 1)
    def _():
        def drain(number, carry):
            tick(number)
            return carry

        lax.fori_loop(steps * 4, max(count + SPREAD_FILL, steps * 4), drain, 0)


def held_specs(count):
    return [pl.BlockSpec(memory_space=pltpu.VMEM)] * count


def mixer_call(channels, gate, vec, masks, taps, border, gain, shard):
    parts, heads, length, width = channels.shape
    chunks = length // GROUP
    steps = H // PAIR

    def early(step):
        return jnp.minimum(step, steps - 1)

    def late(step):
        return jnp.maximum(step - steps, 0)

    def heads_spec(shape, which):
        rank = len(shape)
        return pl.BlockSpec((PAIR,) + shape, lambda step: (which(step),) + (0,) * rank)

    square = (chunks, SPAN, DK)
    anywhere = pl.BlockSpec(memory_space=pl.ANY)
    return pl.pallas_call(
        mixer_kernel,
        grid=(2 * steps,),
        out_shape=[
            per_head((2,) + square),
            per_head((chunks, GROUP, DK)),
            per_head((2,) + square),
            jax.ShapeDtypeStruct((length, H * DV), jnp.bfloat16),
            per_head((length, DV)),
            jax.ShapeDtypeStruct(STACK + shard.shape, jnp.bfloat16),
        ],
        in_specs=[
            pl.BlockSpec((parts, PAIR, length, DK), lambda step: (0, early(step), 0, 0)),
            heads_spec((length, DV), late),
        ]
        + held_specs(5)
        + [anywhere],
        out_specs=[
            heads_spec((2,) + square, early),
            heads_spec((chunks, GROUP, DK), early),
            heads_spec((2,) + square, late),
            pl.BlockSpec((length, PAIR * DV), lambda step: (0, late(step))),
            heads_spec((length, DV), late),
            anywhere,
        ],
        scratch_shapes=[pltpu.VMEM((H,) + square, jnp.float32)] * 4
        + [pltpu.VMEM((H, chunks, GROUP, DK), jnp.float32)] * 2
        + [pltpu.VMEM((H, DV, DK), jnp.bfloat16)] * 2
        + [
            pltpu.VMEM((PAIR, length + 8, DK), jnp.float32),
            pltpu.VMEM((PAIR, length, DK), jnp.float32),
            pltpu.VMEM((PAIR, NH, length, DK), jnp.float32),
            pltpu.VMEM((PAIR, NH, length, DK), jnp.float32),
            pltpu.SemaphoreType.DMA((2,)),
            pltpu.SemaphoreType.DMA((2, STAGES, RING)),
            pltpu.SemaphoreType.DMA((2, STAGES, RING)),
            pltpu.SemaphoreType.DMA((2, RING)),
        ],
        compiler_params=pltpu.CompilerParams(
            dimension_semantics=("arbitrary",), collective_id=4, has_side_effects=True, vmem_limit_bytes=58 * 1024 * 1024
        ),
        cost_estimate=pl.CostEstimate(
            flops=H * chunks * 24 * 2 * SPAN**3 * 4, bytes_accessed=80_000_000, transcendentals=0
        ),
    )(channels, gate, vec, masks, taps, border, gain, shard)


WIDE = 256
RING = 4
SPAN_TICKS = 2
REDUCE_STAGES = 5
CORE, NEAR, FAR, RINGS = 0, 1, 2, 3


class Reduce:
    def __init__(self, refs, lane, count):
        (
            self.both, self.first, self.near_kept, self.near_send, self.near,
            self.far_kept, self.far_send, self.far, self.last_kept, self.last_send, self.last,
            self.send_sem, self.recv_sem,
        ) = refs
        self.lane, self.count = lane, count
        self.z, self.x, self.core, self.y = place()
        self.peers = peers()
        self.x_first = lane == 0
        self.columns = slice(lane * WIDE, (lane + 1) * WIDE)

    def copy(self, source, target, slot_of, stage, index, device):
        lane = self.lane
        return pltpu.make_async_remote_copy(
            src_ref=source, dst_ref=target,
            send_sem=self.send_sem.at[lane, stage, lax.rem(index, 2)],
            recv_sem=self.recv_sem.at[lane, stage, lax.rem(index, RING)],
            device_id=device, device_id_type=MESH,
        )

    def core_copy(self, index):
        source = self.both.at[lax.rem(index, 2), :, :, 1 - self.core, :, :, self.columns]
        return self.copy(source, self.first.at[self.lane, lax.rem(index, RING)], None, CORE, index, self.peers[ZS + 1])

    def near_copy(self, index):
        lane = self.lane
        return self.copy(
            self.near_send.at[lane, lax.rem(index, 2)], self.near.at[lane, lax.rem(index, RING)], None, NEAR, index,
            self.peers[ZS - 1 if self.x_first else ZS],
        )

    def far_copy(self, index):
        lane = self.lane
        return self.copy(
            self.far_send.at[lane, lax.rem(index, 2)], self.far.at[lane, lax.rem(index, RING)], None, FAR, index,
            self.peers[ZS if self.x_first else ZS - 1],
        )

    def ring_copies(self, index):
        lane = self.lane
        return [
            self.copy(
                self.last_send.at[lane, lax.rem(index, 2), step], self.last.at[lane, lax.rem(index, RING), step],
                None, RINGS + step, index, self.peers[step],
            )
            for step in range(ZS - 1)
        ]

    def from_core(self, index):
        lane, slot, ring = self.lane, lax.rem(index, 2), lax.rem(index, RING)
        arrived = self.core_copy(index)
        arrived.wait_recv()
        arrived.wait_send()

        def one(z, carry):
            if self.x_first:
                pick = lambda half: self.both[slot, z, half, self.core, :, :, self.columns]
                pick_got = lambda half: self.first[lane, ring, z, half]
                mine = self.x
            else:
                pick = lambda half: self.both[slot, z, :, self.core, half, :, self.columns]
                pick_got = lambda half: self.first[lane, ring, z, :, half]
                mine = self.y
            kept = pick(mine).astype(jnp.float32) + pick_got(mine).astype(jnp.float32)
            sent = pick(1 - mine).astype(jnp.float32) + pick_got(1 - mine).astype(jnp.float32)
            self.near_kept[lane, slot, z] = kept
            self.near_send[lane, slot, z] = sent.astype(jnp.bfloat16)
            return carry

        lax.fori_loop(0, ZS, one, 0)
        self.near_copy(index).start()

    def from_near(self, index):
        lane, slot, ring = self.lane, lax.rem(index, 2), lax.rem(index, RING)
        arrived = self.near_copy(index)
        arrived.wait_recv()
        arrived.wait_send()
        mine = self.y if self.x_first else self.x

        def one(z, carry):
            kept = self.near_kept[lane, slot, z, mine] + self.near[lane, ring, z, mine].astype(jnp.float32)
            sent = self.near_kept[lane, slot, z, 1 - mine] + self.near[lane, ring, z, 1 - mine].astype(jnp.float32)
            self.far_kept[lane, slot, z] = kept
            self.far_send[lane, slot, z] = sent.astype(jnp.bfloat16)
            return carry

        lax.fori_loop(0, ZS, one, 0)
        self.far_copy(index).start()

    def from_far(self, index):
        lane, slot, ring = self.lane, lax.rem(index, 2), lax.rem(index, RING)
        arrived = self.far_copy(index)
        arrived.wait_recv()
        arrived.wait_send()

        def total(z):
            return self.far_kept[lane, slot, z] + self.far[lane, ring, z].astype(jnp.float32)

        self.last_kept[lane, slot] = total(self.z)
        for step, copy in enumerate(self.ring_copies(index)):
            self.last_send[lane, slot, step] = total(lax.rem(self.z + 1 + step, ZS)).astype(jnp.bfloat16)
            copy.start()

    def from_ring(self, index):
        lane, slot, ring = self.lane, lax.rem(index, 2), lax.rem(index, RING)
        total = self.last_kept[lane, slot]
        for step, copy in enumerate(self.ring_copies(index)):
            copy.wait_recv()
            copy.wait_send()
            total = total + self.last[lane, ring, step].astype(jnp.float32)
        return total


def reduce_scratch(rows):
    half = (2, 2, rows, WIDE)
    lanes = 2
    return [
        pltpu.VMEM((2,) + STACK + (rows, lanes * WIDE), jnp.bfloat16),
        pltpu.VMEM((lanes, RING, ZS) + half, jnp.bfloat16),
        pltpu.VMEM((lanes, 2, ZS, 2, rows, WIDE), jnp.float32),
        pltpu.VMEM((lanes, 2, ZS, 2, rows, WIDE), jnp.bfloat16),
        pltpu.VMEM((lanes, RING, ZS, 2, rows, WIDE), jnp.bfloat16),
        pltpu.VMEM((lanes, 2, ZS, rows, WIDE), jnp.float32),
        pltpu.VMEM((lanes, 2, ZS, rows, WIDE), jnp.bfloat16),
        pltpu.VMEM((lanes, RING, ZS, rows, WIDE), jnp.bfloat16),
        pltpu.VMEM((lanes, 2, rows, WIDE), jnp.float32),
        pltpu.VMEM((lanes, 2, ZS - 1, rows, WIDE), jnp.bfloat16),
        pltpu.VMEM((lanes, RING, ZS - 1, rows, WIDE), jnp.bfloat16),
        pltpu.SemaphoreType.DMA((lanes, RINGS + ZS - 1, 2)),
        pltpu.SemaphoreType.DMA((lanes, RINGS + ZS - 1, RING)),
    ]


def make_back_kernel(length, width, hidden):
    chunks = length // GROUP
    parts = 1 + 2 * NH
    blocks = hidden // WIDE
    halves = width // WIDE // 2
    down_first = blocks
    out_first = down_first + 3 * halves
    gate_first = out_first + halves
    head_first = gate_first + halves
    count = head_first + parts * (H // 2) // 2
    ticks = count + (REDUCE_STAGES - 1) * SPAN_TICKS
    rows = 32
    shard = hidden // 32
    early = blocks + 2
    late = early + H
    last = late + H
    early_tick = blocks
    late_tick = early_tick + H // 2

    def kernel(
        xt_in, ok_in, mixed_in, gate_ref, channel_ref, us_in, wg_ref, wu_ref, wd_ref,
        vec_ref, mask_ref, tap_ref, border_ref, gain_ref, out_ref, mlp_gain_ref,
        x_in, gated_in, cot_in, mix_in, normed_in,
        d_projected_out, y_out, d_hidden_out, d_normed_out,
        gain_out, d_vec_out, tap_out, mlp_gain_out, gu_out, down_out, out_out, mix_out,
        d_mixed_ref, local_ref, all_ref, relay_send, relay_recv, edge_send, edge_recv, tail_ref,
        ext_ref, pre_ref, q_ref, k_ref, inv_ref, d_ref, z_ref,
        cot_ref, left_ref, act_t_ref, right_ref, d_mixer_ref,
        relay_sems, edge_send_sem, edge_recv_sem, store_sem, load_sem, out_sem, mix_sem, *engine_refs,
    ):
        step = pl.program_id(0)
        z, x, core, y = place()
        y_peer = device_at(z, x, core, 1 - y)
        lanes = [Reduce(engine_refs, lane, count) for lane in range(2)]
        first_device = jnp.where(y == 0, 1.0, 0.0)
        halves_of_width = width // 2 // WIDE

        def wide(first):
            return pl.ds(pl.multiple_of(first, WIDE), WIDE)

        def down_item(lane, index):
            within = index - down_first
            return lane * halves_of_width + within // 3, lax.rem(within, 3)

        def mix_item(lane, index):
            within = 2 * (index - head_first) + lane
            is_gate = index < head_first
            part = jnp.where(is_gate, parts, lax.rem(within, parts))
            column = jnp.where(is_gate, 2 * (index - gate_first) + lane, within // parts) * WIDE
            return part, column

        def begin(index):
            slot = lax.rem(index, 2)
            is_down = (index >= down_first) & (index < out_first)

            def product(left):
                made = mm(left.reshape(-1, length), right_ref[...]).astype(jnp.bfloat16)
                lanes[0].both[slot] = made.reshape(STACK + (rows, 2 * WIDE))

            def pair(column):
                return pl.ds(pl.multiple_of(column * 2 * WIDE, 2 * WIDE), 2 * WIDE)

            @pl.when(is_down)
            def _():
                for lane in range(2):
                    right_ref[:, lane * WIDE : (lane + 1) * WIDE] = cot_ref[:, wide(down_item(lane, index)[0] * WIDE)]
                here = pl.ds(pl.multiple_of(down_item(0, index)[1] * rows, rows), rows)
                product(act_t_ref[:, :, :, :, here, :])

            @pl.when((index >= out_first) & (index < gate_first))
            def _():
                right_ref[...] = d_mixer_ref[:, pair(index - out_first)]

            @pl.when((index >= gate_first) & (index < head_first))
            def _():
                right_ref[...] = all_ref[parts, :, pair(index - gate_first)]

            @pl.when(index >= head_first)
            def _():
                for lane in range(2):
                    part, column = mix_item(lane, index)
                    right_ref[:, lane * WIDE : (lane + 1) * WIDE] = all_ref[part, :, wide(column)]

            @pl.when(jnp.logical_not(is_down))
            def _():
                product(left_ref[jnp.where(index < down_first, 0, jnp.where(index < gate_first, 1, 2))])

            for engine in lanes:
                engine.core_copy(index).start()

        def end(lane, index):
            total = lanes[lane].from_ring(index)

            @pl.when(index < down_first)
            def _():
                gu_out[:, wide(lane * hidden + index * WIDE)] = total

            @pl.when((index >= down_first) & (index < out_first))
            def _():
                column, block = down_item(lane, index)
                down_out[block, :, wide(column * WIDE)] = total

            @pl.when((index >= out_first) & (index < gate_first))
            def _():
                out_out[:, wide((2 * (index - out_first) + lane) * WIDE)] = total

            @pl.when(index >= gate_first)
            def _():
                part, column = mix_item(lane, index)
                mix_out[:, wide(part * (H * DK) + column)] = total

        def tick(number):
            for stage in reversed(range(REDUCE_STAGES)):
                index = number - stage * SPAN_TICKS

                @pl.when((index >= 0) & (index < count))
                def _():
                    if stage == 0:
                        begin(index)
                    for lane, engine in enumerate(lanes):
                        if stage == 1:
                            engine.from_core(index)
                        elif stage == 2:
                            engine.from_near(index)
                        elif stage == 3:
                            engine.from_far(index)
                        elif stage == 4:
                            end(lane, index)

        def transposed(values):
            flipped = jnp.transpose(values.astype(jnp.float32)).astype(jnp.bfloat16)
            return flipped.reshape(STACK + (rows, length))

        def head_slices():
            return [slice(head * DV, (head + 1) * DV) for head in range(H)]

        def joined(ref, first):
            quarter = length // SPAN
            return jnp.concatenate(
                [ref[head, first * quarter : (first + 1) * quarter].reshape(length, DV) for head in range(H)], axis=1
            )

        def split(ref, first, values):
            quarter = length // SPAN
            for head, here in enumerate(head_slices()):
                ref[head, first * quarter : (first + 1) * quarter] = values[:, here].reshape(quarter, SPAN, DV)

        def enter_mlp():
            loads = [
                pltpu.make_async_copy(source, target, load_sem.at[index])
                for index, (source, target) in enumerate(
                    ((gated_in, all_ref.at[1]), (x_in, all_ref.at[0]), (cot_in, cot_ref), (normed_in, left_ref.at[2]))
                )
            ]
            for load in loads:
                load.start()
            for load in loads:
                load.wait()
            split(local_ref, 1, mm(all_ref[1], out_ref[...]))
            quarter = length // SPAN

            def one(index, carry):
                here = pl.ds(pl.multiple_of(index * SPAN, SPAN), SPAN)
                mixed_rows = jnp.concatenate([local_ref[head, quarter + index] for head in range(H)], axis=1)
                hidden_rows = all_ref[0, here].astype(jnp.float32) + mixed_rows
                inv = lax.rsqrt(jnp.mean(hidden_rows * hidden_rows, axis=1, keepdims=True) + EPSILON)
                all_ref[3, here] = (hidden_rows * inv * mlp_gain_ref[0:1, :]).astype(jnp.bfloat16)
                for head, columns in enumerate(head_slices()):
                    local_ref[head, index] = hidden_rows[:, columns]
                    local_ref[head, quarter + index] = hidden_rows[:, columns]
                return carry

            lax.fori_loop(0, quarter, one, 0)
            d_mixed_ref[...] = jnp.zeros_like(d_mixed_ref)
            left_ref[0] = transposed(all_ref[3])
            left_ref[1] = transposed(all_ref[1])
            act_t_ref[:, :, :, :, shard:, :] = jnp.zeros(STACK + (act_t_ref.shape[4] - shard, length), jnp.float32)

        def mlp_block(block):
            mlp_in = all_ref[3]
            gate = mm(mlp_in, wg_ref[...])
            up = mm(mlp_in, wu_ref[...])
            open_, sig = silu_pair(gate)
            act = (open_ * up).astype(jnp.bfloat16)
            d_act = mm(cot_ref[...], wd_ref[...], 1, 1)
            d_gate = (d_act * up * sig * (1.0 + gate * (1.0 - sig))).astype(jnp.bfloat16)
            d_up = (d_act * open_).astype(jnp.bfloat16)
            right_ref[:, :WIDE] = d_gate
            right_ref[:, WIDE:] = d_up
            split(local_ref, 0, joined(local_ref, 0) + mm(act, wd_ref[...]))
            d_in = mm(d_gate, wg_ref[...], 1, 1) + mm(d_up, wu_ref[...], 1, 1)
            for head, here in enumerate(head_slices()):
                d_mixed_ref[head] = d_mixed_ref[head] + d_in[:, here]
            act_t = jnp.transpose(act.astype(jnp.float32))
            for group in range(WIDE // 8):
                place_ = block * (WIDE // 8) + group
                owner, row = place_ // (shard // 8), lax.rem(place_, shard // 8) * 8
                act_t_ref[
                    owner // 8, lax.rem(owner // 4, 2), lax.rem(owner // 2, 2), lax.rem(owner, 2),
                    pl.ds(pl.multiple_of(row, 8), 8), :,
                ] = act_t[group * 8 : (group + 1) * 8]

        y_store = pltpu.make_async_copy(all_ref.at[0], y_out, out_sem.at[0])

        def leave_mlp():
            quarter = length // SPAN

            def tile(ref, first, index):
                return jnp.concatenate([ref[head, first * quarter + index] for head in range(H)], axis=1)

            def one(index, gain_grad):
                here = pl.ds(pl.multiple_of(index * SPAN, SPAN), SPAN)
                all_ref[0, here] = tile(local_ref, 0, index).astype(jnp.bfloat16)
                hidden_rows = tile(local_ref, 1, index)
                d_in = jnp.concatenate([d_mixed_ref[head, here] for head in range(H)], axis=1)
                inv = lax.rsqrt(jnp.mean(hidden_rows * hidden_rows, axis=1, keepdims=True) + EPSILON)
                unit = hidden_rows * inv
                d_unit = d_in * mlp_gain_ref[0:1, :]
                d_norm = inv * (d_unit - unit * jnp.mean(d_unit * unit, axis=1, keepdims=True))
                d_hidden = cot_ref[here].astype(jnp.float32) + d_norm
                for head, columns in enumerate(head_slices()):
                    local_ref[head, quarter + index] = d_hidden[:, columns]
                d_mixer_ref[here] = d_hidden.astype(jnp.bfloat16)
                return gain_grad + jnp.sum(d_in * unit, axis=0, keepdims=True)

            gain_grad = lax.fori_loop(0, quarter, one, jnp.zeros((1, width), jnp.float32))
            mlp_gain_out[...] = jnp.broadcast_to(gain_grad, (8, width))
            y_store.start()
            stores = [
                pltpu.make_async_copy(
                    local_ref.at[head, quarter : 2 * quarter], d_hidden_out.at[:, :, here], out_sem.at[1 + head]
                )
                for head, here in enumerate(head_slices())
            ]
            for store in stores:
                store.start()
            d_normed_rows = mm(d_mixer_ref[...], out_ref[...], 1, 1)
            for head, here in enumerate(head_slices()):
                d_mixed_ref[head] = d_normed_rows[:, here]
            for store in stores:
                store.wait()

        def readout_back(head):
            gain = gain_ref[0:1, :]
            gain_grad = jnp.zeros((1, DV), jnp.float32)
            column = pl.ds(pl.multiple_of(head * DV, DV), DV)
            state = jnp.zeros((DV, DK), jnp.float32)
            for chunk in reversed(range(chunks)):
                here = slice(chunk * GROUP, (chunk + 1) * GROUP)
                mixed = mixed_in[0, here, :]
                inv = lax.rsqrt(jnp.mean(mixed * mixed, axis=1, keepdims=True) + EPSILON)
                unit = mixed * inv
                gate = gate_ref[0, here, :]
                open_, sig = silu_pair(gate)
                d_gated = d_mixed_ref[head, here]
                d_scaled = d_gated * open_
                d_gate = d_gated * unit * gain * sig * (1.0 + gate * (1.0 - sig))
                all_ref[parts, here, column] = d_gate.astype(jnp.bfloat16)
                gain_grad = gain_grad + jnp.sum(d_scaled * unit, axis=0, keepdims=True)
                d_unit = d_scaled * gain
                d_mixed = inv * (d_unit - unit * jnp.mean(d_unit * unit, axis=1, keepdims=True))
                d_mixed_ref[head, here] = d_mixed
                local = mm3(d_mixed, ok_in[0, chunk], 0, 0)
                local_ref[head, chunk] = local
                state = (
                    vec_ref[head, chunk, 3:4, GROUP - 1 : GROUP] * state
                    - mm3(state, xt_in[0, 1, chunk], 1, 1)
                    + local
                )
            gain_out[head] = jnp.broadcast_to(gain_grad, (8, DV))
            relay_send[head] = state.astype(jnp.bfloat16)

        def head_columns(part, head):
            return pl.ds(pl.multiple_of((part * H + head) * DK, DK), DK)

        def prepare(head):
            for part in range(parts):
                here = head_columns(part, head)
                pre = conv_block(channel_ref[part], border_ref[:, here], tap_ref[:, here], mask_ref, ext_ref.at[part])
                yield
                pre_ref[part] = pre
                if part > NH:
                    continue
                value = silu_pair(pre)[0]
                if part == 0:
                    unit, inv = unit_rows(value)
                    q_ref[...] = unit * DK ** (-0.5)
                    inv_ref[:, 0:1] = inv
                else:
                    unit, inv = unit_rows(value)
                    k_ref[part - 1] = unit
                    inv_ref[:, part : part + 1] = inv

        def chain(head, exit_grads):
            grad = first_device * relay_recv[head].astype(jnp.float32)
            for chunk in reversed(range(chunks)):
                exit_grads[chunk] = grad
                grad = (
                    vec_ref[head, chunk, 3:4, GROUP - 1 : GROUP] * grad
                    - mm3(grad, xt_in[0, 1, chunk], 1, 1)
                    + local_ref[head, chunk]
                )
                yield

        def one_chunk(chunk, head, d_exit):
            strict = order_masks()[0]
            column_index = iotas(SPAN, 8)[1]
            here = slice(chunk * GROUP, (chunk + 1) * GROUP)
            rows_ = vec_ref[head, chunk]
            columns = jnp.transpose(rows_)
            beta, scale, tail = columns[:, 1:2], columns[:, 3:4], columns[:, 4:5]
            keys = k_ref[:, here, :].reshape(SPAN, DK)
            values = silu_pair(pre_ref[1 + NH :, here, :].reshape(SPAN, DV))[0]
            queries = q_ref[here, :]
            link = link_matrix(rows_, columns)
            link_gram = jnp.where(strict, twice(link) * mm3(keys, keys, 1, 1), 0.0)
            reading = link * mm3(queries, keys, 1, 1)
            yield
            solved = us_in[0, 0, chunk]
            entry = us_in[0, 1, chunk]
            d_mixed = d_mixed_ref[head, here]
            tail_keys = tail * keys
            d_solved = mm3(reading, d_mixed, 0, 0) + mm3(tail_keys, d_exit, 1, 1)
            yield
            d_right = mm3(xt_in[0, 0, chunk], d_solved, 0, 0)
            yield
            d_lower = jnp.where(strict, -mm3(d_right, solved, 1, 1), 0.0)
            yield
            d_tail_keys = mm3(solved, d_exit)
            d_right_entry = mm3(d_right, entry)
            d_reading = mm3(d_mixed, solved, 1, 1)
            d_query_entry = mm3(d_mixed, entry)
            yield
            both_scale = -jnp.sum(d_right_entry * keys, axis=1, keepdims=True)
            lower_weight = d_lower * link_gram
            d_beta = (
                jnp.sum(d_right * values, axis=1, keepdims=True)
                + scale * both_scale
                + jnp.sum(lower_weight, axis=1, keepdims=True)
            )
            lower_moment = lower_weight * beta
            reading_moment = d_reading * reading
            d_gram = beta * twice(link) * d_lower
            d_gram = d_gram + jnp.transpose(d_gram)
            yield
            d_query_gram = link * d_reading
            d_keys = (
                tail * d_tail_keys
                - beta * scale * d_right_entry
                + mm3(d_gram, keys)
                + mm3(d_query_gram, queries, 0, 0)
            )
            d_queries = mm3(d_query_gram, keys) + scale[:GROUP] * d_query_entry
            d_values = beta * d_right
            yield
            none = jnp.zeros((GROUP, 1), jnp.float32)
            d_gap = jnp.sum(lower_moment, axis=1, keepdims=True) + jnp.concatenate(
                [jnp.sum(reading_moment, axis=1, keepdims=True), none], axis=0
            )
            last = jnp.sum(jnp.sum(d_exit * entry, axis=1, keepdims=True), axis=0, keepdims=True)
            own_scale = jnp.sum(d_query_entry * queries, axis=1, keepdims=True)
            own_scale = own_scale + jnp.where(iotas(GROUP, 1)[0] == GROUP - 1, last, 0.0)
            d_scale = beta * both_scale + jnp.concatenate([own_scale, none], axis=0)
            d_tail = jnp.sum(d_tail_keys * keys, axis=1, keepdims=True)
            grads = jnp.where(
                column_index == 0,
                d_gap,
                jnp.where(
                    column_index == 1,
                    d_beta,
                    jnp.where(column_index == 3, d_scale, jnp.where(column_index == 4, d_tail, 0.0)),
                ),
            )
            grads = jnp.transpose(grads)
            sums = jnp.sum(lower_moment, axis=0, keepdims=True) + jnp.sum(reading_moment, axis=0, keepdims=True)
            d_vec_out[head, chunk] = grads - jnp.where(iotas(8, SPAN)[0] == 0, sums, 0.0)
            d_ref[0, here, :] = d_queries
            for house in range(NH):
                mine = slice(house * GROUP, (house + 1) * GROUP)
                d_ref[1 + house, here, :] = d_keys[mine]
                d_ref[1 + NH + house, here, :] = d_values[mine]

        def finish_head(head):
            column = pl.ds(pl.multiple_of(head * DK, DK), DK)
            z_ref[0:8, :] = jnp.zeros((8, DK), jnp.float32)
            z_ref[8 + length : 16 + length, :] = jnp.zeros((8, DK), jnp.float32)
            for part in range(parts):
                grad = d_ref[part]
                if part <= NH:
                    unit = q_ref[...] * DK ** 0.5 if part == 0 else k_ref[part - 1]
                    if part == 0:
                        grad = grad * DK ** (-0.5)
                    grad = inv_ref[:, part : part + 1] * (grad - unit * jnp.sum(grad * unit, axis=1, keepdims=True))
                pre = pre_ref[part]
                sig = jax.nn.sigmoid(pre)
                grad = grad * sig * (1.0 + pre * (1.0 - sig))
                here = head_columns(part, head)
                tap = tap_ref[:, here]
                total = grad * tap[0:1, :]
                edge = jnp.zeros((8, DK), jnp.float32)
                tap_rows = [jnp.sum(grad * channel_ref[part], axis=0, keepdims=True)]
                for index in range(1, 4):
                    shifted = grad * mask_ref[index - 1].astype(jnp.float32)
                    tap_rows.append(
                        jnp.sum(shifted * ext_ref[part, 8 - index : 8 - index + length, :], axis=0, keepdims=True)
                    )
                    z_ref[8 : 8 + length, :] = shifted * tap[index : index + 1, :]
                    total = total + z_ref[8 + index : 8 + index + length, :]
                    edge = edge + z_ref[index : index + 8, :]
                all_ref[part, :, column] = total.astype(jnp.bfloat16)
                edge_send[lax.rem(head, 2), part] = edge
                tail_ref[part] = total[length - 16 :, :]
                tap_out[:, here] = jnp.concatenate(tap_rows + [jnp.zeros((4, DK), jnp.float32)], axis=0)

        @pl.when(step == 0)
        def _():
            meet(peers())
            enter_mlp()

        @pl.when((step >= 1) & (step <= blocks))
        def _():
            mlp_block(step - 1)

        @pl.when(step == blocks + 1)
        def _():
            leave_mlp()

        early_head = step - early

        @pl.when((step >= early) & (step < late))
        def _():
            readout_back(early_head)

        relay = pltpu.make_async_remote_copy(
            src_ref=relay_send, dst_ref=relay_recv, send_sem=relay_sems.at[0], recv_sem=relay_sems.at[1],
            device_id=y_peer, device_id_type=MESH,
        )

        @pl.when(step == late - 1)
        def _():
            relay.start()

        @pl.when(step == late)
        def _():
            relay.wait()
            y_store.wait()

        def edge_copy(head):
            slot = lax.rem(head, 2)
            return pltpu.make_async_remote_copy(
                src_ref=edge_send.at[slot], dst_ref=edge_recv.at[slot], send_sem=edge_send_sem.at[slot],
                recv_sem=edge_recv_sem.at[slot], device_id=y_peer, device_id_type=MESH,
            )

        def fix_edges(head):
            edge_copy(head).wait()
            here = pl.ds(pl.multiple_of(head * DK, DK), DK)
            for part in range(parts):
                fixed = tail_ref[part, 8:16] + first_device * edge_recv[lax.rem(head, 2), part]
                both = jnp.concatenate([tail_ref[part, 0:8], fixed], axis=0)
                all_ref[part, length - 16 : length, here] = both.astype(jnp.bfloat16)

        @pl.when((step >= late) & (step < last))
        def _():
            head = step - late
            exit_grads = [None] * chunks
            together([chain(head, exit_grads), prepare(head)])

            @pl.when(head > 0)
            def _():
                fix_edges(head - 1)

            tick(late_tick + jnp.minimum(2 * head, head + 5))
            together([one_chunk(chunk, head, exit_grads[chunk]) for chunk in reversed(range(chunks))])

            finish_head(head)
            edge_copy(head).start()

        late_head = step - late
        in_mlp = (step >= 1) & (step <= blocks)
        in_early = (step >= early) & (step < late) & (lax.rem(early_head, 2) == 0)
        in_late = (late_head >= 0) & (late_head < 5)
        number = jnp.where(
            in_mlp, step - 1, jnp.where(in_early, early_tick + early_head // 2, late_tick + 2 * late_head + 1)
        )

        @pl.when(in_mlp | in_early | in_late)
        def _():
            tick(number)

        @pl.when(step == last)
        def _():
            fix_edges(H - 1)
            stores = [
                pltpu.make_async_copy(
                    all_ref.at[part], d_projected_out.at[:, pl.ds(part * H * DK, H * DK)], store_sem.at[part]
                )
                for part in range(parts + 1)
            ]
            for store in stores:
                store.start()
            loads = mix_in.shape[5] // length

            def load(index):
                here = pl.ds(pl.multiple_of(index * length, length), length)
                slot = lax.rem(index, 2)
                return pltpu.make_async_copy(mix_in.at[:, :, :, :, :, here], left_ref.at[slot], mix_sem.at[slot])

            load(0).start()
            load(1).start()
            d_mixed_ref[...] = jnp.zeros_like(d_mixed_ref)
            per_part = H * DK // length

            def drain(index, carry):
                tick(late_tick + H + 5 + index)
                load(index).wait()
                here = pl.ds(pl.multiple_of(lax.rem(index, per_part) * length, length), length)
                left = all_ref[index // per_part, :, here]
                added = mm(left, left_ref[lax.rem(index, 2)].reshape(-1, length), 1, 1)
                for head, place_ in enumerate(head_slices()):
                    d_mixed_ref[head] = d_mixed_ref[head] + added[:, place_]

                @pl.when(index + 2 < loads)
                def _():
                    load(index + 2).start()

                return carry

            lax.fori_loop(0, loads, drain, 0)
            assert late_tick + H + 5 + loads >= ticks
            for head, here in enumerate(head_slices()):
                stores.append(
                    pltpu.make_async_copy(d_mixed_ref.at[head], d_normed_out.at[:, here], out_sem.at[head])
                )
                stores[-1].start()
            for store in stores:
                store.wait()

    return kernel, ticks


def back_call(
    xt, out_keys, mixed, gate, channels, us, gu, down, vec, masks, taps, border, gain, out, mlp_gain,
    x, gated, cot, mix, normed_t,
):
    parts, heads, length, width = channels.shape
    chunks = length // GROUP
    model, hidden = gu.shape[0], down.shape[0]
    rows, blocks = 32, hidden // WIDE
    padded = -(-(hidden // 32) // rows) * rows
    kernel, ticks = make_back_kernel(length, model, hidden)
    first = blocks + 2

    def either(step):
        return lax.rem(jnp.maximum(step - first, 0), H)

    def early(step):
        return jnp.clip(step - first, 0, H - 1)

    def late(step):
        return jnp.clip(step - first - H, 0, H - 1)

    def block(step):
        return jnp.clip(step - 1, 0, blocks - 1)

    def heads_spec(shape, which):
        rank = len(shape)
        return pl.BlockSpec((1,) + shape, lambda step: (which(step),) + (0,) * rank)

    square = (chunks, SPAN, DK)
    anywhere = pl.BlockSpec(memory_space=pl.ANY)
    in_specs = (
        [
            heads_spec((2,) + square, either), heads_spec((chunks, GROUP, DK), early), heads_spec((length, DV), early),
            heads_spec((length, DV), early),
            pl.BlockSpec((parts, None, length, DK), lambda step: (0, late(step), 0, 0)), heads_spec((2,) + square, late),
            pl.BlockSpec((model, WIDE), lambda step: (0, block(step))),
            pl.BlockSpec((model, WIDE), lambda step: (0, blocks + block(step))),
            pl.BlockSpec((WIDE, model), lambda step: (block(step), 0)),
        ]
        + held_specs(7)
        + [anywhere] * 5
    )
    out_shape = [
        jax.ShapeDtypeStruct((length, (parts + 1) * H * DK), jnp.bfloat16),
        jax.ShapeDtypeStruct((length, model), jnp.bfloat16),
        jax.ShapeDtypeStruct((length // SPAN, SPAN, model), jnp.float32),
        jax.ShapeDtypeStruct((length, model), jnp.float32),
        per_head((8, DV)),
        per_head((chunks, 8, SPAN)),
        jax.ShapeDtypeStruct((8, parts * H * DK), jnp.float32),
        jax.ShapeDtypeStruct((8, model), jnp.float32),
        jax.ShapeDtypeStruct((rows, gu.shape[1]), jnp.float32),
        jax.ShapeDtypeStruct((padded // rows, rows, model), jnp.float32),
        jax.ShapeDtypeStruct((rows, model), jnp.float32),
        jax.ShapeDtypeStruct((rows, (parts + 1) * H * DK), jnp.float32),
    ]
    tall = pltpu.VMEM((parts, length, DK), jnp.float32)
    scratch = [
        pltpu.VMEM((H, length, DV), jnp.float32),
        pltpu.VMEM((H,) + square, jnp.float32),
        pltpu.VMEM((parts + 1, length, H * DK), jnp.bfloat16),
        pltpu.VMEM((H, DV, DK), jnp.bfloat16),
        pltpu.VMEM((H, DV, DK), jnp.bfloat16),
        pltpu.VMEM((2, parts, 8, DK), jnp.float32),
        pltpu.VMEM((2, parts, 8, DK), jnp.float32),
        pltpu.VMEM((parts, 16, DK), jnp.float32),
        pltpu.VMEM((parts, length + 8, DK), jnp.float32),
        tall,
        pltpu.VMEM((length, DK), jnp.float32),
        pltpu.VMEM((NH, length, DK), jnp.float32),
        pltpu.VMEM((length, DK), jnp.float32),
        tall,
        pltpu.VMEM((length + 16, DK), jnp.float32),
        pltpu.VMEM((length, model), jnp.bfloat16),
        pltpu.VMEM((3,) + STACK + (rows, length), jnp.bfloat16),
        pltpu.VMEM(STACK + (padded, length), jnp.float32),
        pltpu.VMEM((length, 2 * WIDE), jnp.bfloat16),
        pltpu.VMEM((length, model), jnp.bfloat16),
        pltpu.SemaphoreType.DMA((2,)),
        pltpu.SemaphoreType.DMA((2,)),
        pltpu.SemaphoreType.DMA((2,)),
        pltpu.SemaphoreType.DMA((parts + 1,)),
        pltpu.SemaphoreType.DMA((4,)),
        pltpu.SemaphoreType.DMA((1 + H,)),
        pltpu.SemaphoreType.DMA((2,)),
    ] + reduce_scratch(rows)
    return pl.pallas_call(
        kernel,
        grid=(first + 2 * H + 1,),
        out_shape=out_shape,
        in_specs=in_specs,
        out_specs=[anywhere] * 4 + held_specs(len(out_shape) - 4),
        scratch_shapes=scratch,
        compiler_params=pltpu.CompilerParams(
            dimension_semantics=("arbitrary",), collective_id=2, has_side_effects=True, vmem_limit_bytes=255 * 256 * 1024
        ),
        cost_estimate=pl.CostEstimate(
            flops=H * chunks * 14 * 2 * SPAN**3 * 4, bytes_accessed=100_000_000, transcendentals=0
        ),
    )(
        xt, out_keys, mixed, gate, channels, us, gu, gu, down, vec, masks, taps, border, gain, out, mlp_gain,
        x, gated, cot, mix, normed_t,
    )


def total_kernel(packed_ref, sums_ref, packed_out, sums_out, first, near, far, last, kept, pair, ring, send, recv):
    z, x, core, y = place()
    targets = peers()
    meet(targets)

    def copy(source, target, slot, device):
        made = pltpu.make_async_remote_copy(
            src_ref=source, dst_ref=target, send_sem=send.at[slot], recv_sem=recv.at[slot],
            device_id=device, device_id_type=MESH,
        )
        made.start()
        return made

    def swap(source, target, index, device):
        pair[2 * index] = sums_out[...]
        copies = [
            copy(source, target, 2 * index, device),
            copy(pair.at[2 * index], pair.at[2 * index + 1], 2 * index + 1, device),
        ]
        for made in copies:
            made.wait()
        sums_out[...] = sums_out[...] + pair[2 * index + 1]

    sums_out[...] = sums_ref[...]
    swap(packed_ref.at[:, :, 1 - core], first, 0, targets[ZS + 1])
    kept[...] = packed_ref[:, :, core] + first[...]
    swap(kept.at[:, 1 - x], near, 1, targets[ZS - 1])
    kept[:, 0] = kept[:, x] + near[...]
    swap(kept.at[:, 0, 1 - y], far, 2, targets[ZS])
    kept[:, 0, 0] = kept[:, 0, y] + far[...]
    ring[z] = sums_out[...]
    copies = []
    for step in range(ZS - 1):
        other = lax.rem(z + 1 + step, ZS)
        copies.append(copy(kept.at[other, 0, 0], last.at[step], 6 + 2 * step, targets[step]))
        copies.append(copy(ring.at[z], ring.at[z], 7 + 2 * step, targets[step]))
    for made in copies:
        made.wait()
    packed_out[...] = kept[z, 0, 0] + last[0] + last[1] + last[2]
    sums_out[...] = ring[0] + ring[1] + ring[2] + ring[3]


def total_call(packed, sums):
    rows, wide = packed.shape[4], packed.shape[5]
    held = pl.BlockSpec(memory_space=pltpu.VMEM)
    return pl.pallas_call(
        total_kernel,
        out_shape=[jax.ShapeDtypeStruct((rows, wide), jnp.float32), jax.ShapeDtypeStruct(sums.shape, jnp.float32)],
        in_specs=[held, held],
        out_specs=[held, held],
        scratch_shapes=[
            pltpu.VMEM((ZS, 2, 2, rows, wide), jnp.float32),
            pltpu.VMEM((ZS, 2, rows, wide), jnp.float32),
            pltpu.VMEM((ZS, rows, wide), jnp.float32),
            pltpu.VMEM((ZS - 1, rows, wide), jnp.float32),
            pltpu.VMEM((ZS, 2, 2, rows, wide), jnp.float32),
            pltpu.VMEM((6,) + sums.shape, jnp.float32),
            pltpu.VMEM((ZS,) + sums.shape, jnp.float32),
            pltpu.SemaphoreType.DMA((12,)),
            pltpu.SemaphoreType.DMA((12,)),
        ],
        compiler_params=pltpu.CompilerParams(collective_id=3, has_side_effects=True, vmem_limit_bytes=LIMIT),
        cost_estimate=pl.CostEstimate(flops=1000000, bytes_accessed=2_000_000, transcendentals=0),
    )(packed, sums)


def from_behind(block, axis, distance):
    devices = range(lax.axis_size(axis))
    route = [(i - distance, i) for i in devices if i - distance in devices]
    return lax.ppermute(block, axis, route)


def rms_scale(values, scale_gain):
    return (
        values * lax.rsqrt(jnp.mean(values * values, axis=-1, keepdims=True) + EPSILON) * scale_gain
    )


def swiglu(gate_up):
    half_width = gate_up.shape[-1] // 2
    return jax.nn.silu(gate_up[:, :half_width]) * gate_up[:, half_width:]


def exchange(block, axis, bit):
    route = [(i, i ^ (1 << bit)) for i in range(lax.axis_size(axis))]
    return lax.ppermute(block, axis, route)


def axis_bits(axis):
    return lax.axis_size(axis).bit_length() - 1


def bit_orders():
    dp_bits = [("dp", bit) for bit in range(axis_bits("dp"))]
    seq_bits = [("seq", bit) for bit in range(axis_bits("seq"))]
    first, rest = dp_bits[:1], dp_bits[1:]
    inner = rest[:1] + seq_bits[:1]
    outer = rest[1:] + seq_bits[1:]
    return first + inner + outer, first + inner[::-1] + outer


def scatter_sum(part, order):
    dp_bits, seq_bits = axis_bits("dp"), axis_bits("seq")
    dims = [("dp", bit) for bit in reversed(range(dp_bits))] + [("seq", bit) for bit in reversed(range(seq_bits))]
    rows = part.shape[0] >> len(dims)
    part = part.reshape((2,) * len(dims) + (rows, part.shape[1]))
    for axis, bit in order:
        place = dims.index((axis, bit))
        dims.pop(place)
        mine = (lax.axis_index(axis) >> bit) & 1
        sent = lax.dynamic_index_in_dim(part, 1 - mine, place, keepdims=False)
        kept = lax.dynamic_index_in_dim(part, mine, place, keepdims=False)
        got = exchange(sent.astype(jnp.bfloat16), axis, bit)
        part = kept.astype(jnp.float32) + got.astype(jnp.float32)
    return part


def scatter_halves(part):
    half = part.shape[1] // 2
    orders = bit_orders()
    return jnp.concatenate(
        [scatter_sum(part[:, :half], orders[0]), scatter_sum(part[:, half:], orders[1])], axis=1
    )


def total_sum(block):
    for axis in ("dp", "seq"):
        for bit in range(axis_bits(axis)):
            block = block + exchange(block, axis, bit)
    return block


def gate_vectors(seg_now, seg_prev, gates_raw, decay_log):
    length = gates_raw.shape[0]
    chunks = length // GROUP
    beta = jax.nn.sigmoid(gates_raw[:, : NH * H]).reshape(chunks, GROUP, NH, H)
    rate = -jnp.exp(decay_log) * jax.nn.softplus(gates_raw[:, NH * H :])
    lower = jnp.tril(jnp.ones((GROUP, GROUP), jnp.float32))
    total = jnp.einsum("ts,csh->cth", lower, rate.reshape(chunks, GROUP, H), precision=HIGHEST)
    seg = seg_now.reshape(chunks, GROUP)
    before = jnp.concatenate([seg_prev.reshape(1), seg[:-1, -1]])
    scale = jnp.exp(total) * (seg == before[:, None]).astype(jnp.float32)[:, :, None]
    tail = jnp.exp(total[:, -1:, :] - total) * (seg == seg[:, -1:]).astype(jnp.float32)[:, :, None]

    def both(values):
        moved = jnp.moveaxis(values, 2, 0)
        return jnp.concatenate([moved, moved], axis=-1)

    beta_rows = beta.transpose(3, 0, 2, 1).reshape(H, chunks, SPAN)
    seg_rows = jnp.broadcast_to(jnp.concatenate([seg, seg], axis=1).astype(jnp.float32), (H, chunks, SPAN))
    none = jnp.zeros((H, chunks, SPAN), jnp.float32)
    return jnp.stack([both(total), beta_rows, seg_rows, both(scale), both(tail), none, none, none], axis=2)


def head_spec(shape):
    rank = len(shape)
    return pl.BlockSpec((1,) + shape, lambda head: (head,) + (0,) * rank)


def column_spec(rows, first):
    return pl.BlockSpec((rows, DK), lambda head: (0, first + head))


def whole_spec(shape):
    rank = len(shape)
    return pl.BlockSpec(shape, lambda head: (0,) * rank)


def per_head(shape, dtype=jnp.float32):
    return jax.ShapeDtypeStruct((H,) + shape, dtype)


def call(kernel, out_shape, in_specs, out_specs, scratch, flops, bytes_accessed):
    return pl.pallas_call(
        kernel,
        grid=(H,),
        out_shape=out_shape,
        in_specs=in_specs,
        out_specs=out_specs,
        scratch_shapes=scratch,
        compiler_params=pltpu.CompilerParams(
            dimension_semantics=("arbitrary",), vmem_limit_bytes=LIMIT
        ),
        cost_estimate=pl.CostEstimate(flops=flops, bytes_accessed=bytes_accessed, transcendentals=0),
    )


def conv_specs(length):
    return (
        [column_spec(length, H * part) for part in range(1 + 2 * NH)]
        + [column_spec(8, H * part) for part in range(1 + 2 * NH)] * 2
        + [whole_spec((3, length, DK))]
    )


def forward_call(projected, border, taps, masks, vec, start):
    length = projected.shape[0]
    chunks = length // GROUP
    square = (chunks, SPAN, DK)
    outs = [
        (square, jnp.float32),
        (square, jnp.float32),
        (square, jnp.float32),
        (square, jnp.float32),
        (square, jnp.float32),
        ((chunks, GROUP, DK), jnp.float32),
        ((chunks, GROUP, DV), jnp.float32),
        ((DV, DK), jnp.float32),
    ]
    parts = 1 + 2 * NH
    return call(
        forward_kernel,
        [per_head(*out) for out in outs],
        conv_specs(length) + [head_spec((chunks, 8, SPAN)), head_spec((DV, DK))],
        [head_spec(out[0]) for out in outs],
        [
            pltpu.VMEM((length + 8, DK), jnp.float32),
            pltpu.VMEM((length, DK), jnp.float32),
            pltpu.VMEM((NH, length, DK), jnp.float32),
            pltpu.VMEM((NH, length, DK), jnp.float32),
        ],
        H * chunks * 20 * 2 * SPAN**3 * 4,
        H * chunks * 8 * SPAN * DK * 4,
    )(*[projected] * parts, *[border] * parts, *[taps] * parts, masks, vec, start)


def chain_call(vec, transfer, start):
    chunks = transfer.shape[1]
    return call(
        chain_kernel,
        per_head((DV, DK)),
        [head_spec((chunks, 8, SPAN)), head_spec((chunks, SPAN, DK)), head_spec((DV, DK))],
        head_spec((DV, DK)),
        [],
        H * chunks * 2 * SPAN**3,
        H * chunks * SPAN * DK * 4,
    )(vec, transfer, start)


def readout_call(vec, key_part, value_part, transfer, inject, out_keys, out_values, entry, projected, gain):
    length = projected.shape[0]
    chunks = length // GROUP
    square = head_spec((chunks, SPAN, DK))
    half = head_spec((chunks, GROUP, DK))
    return call(
        readout_kernel,
        [
            jax.ShapeDtypeStruct((length, H * DV), jnp.bfloat16),
            jax.ShapeDtypeStruct((length, H * DV), jnp.float32),
            per_head((chunks, SPAN, DK)),
            per_head((chunks, SPAN, DK)),
        ],
        [
            head_spec((chunks, 8, SPAN)), square, square, square, square, half, half,
            head_spec((DV, DK)), column_spec(length, (1 + 2 * NH) * H), whole_spec((8, DV)),
        ],
        [column_spec(length, 0), column_spec(length, 0), square, square],
        [],
        H * chunks * 4 * 2 * SPAN**3 * 4,
        H * chunks * 8 * SPAN * DK * 4,
    )(vec, key_part, value_part, transfer, inject, out_keys, out_values, entry, projected, gain)


def readout_back_call(vec, transfer, out_keys, mixed, projected, gain, d_gated, start):
    length = projected.shape[0]
    chunks = length // GROUP
    square = head_spec((chunks, SPAN, DK))
    return call(
        readout_back_kernel,
        [
            jax.ShapeDtypeStruct((length, H * DV), jnp.float32),
            jax.ShapeDtypeStruct((length, H * DV), jnp.bfloat16),
            per_head((chunks, SPAN, DK)),
            per_head((DV, DK)),
            per_head((8, DV)),
        ],
        [
            head_spec((chunks, 8, SPAN)), square, head_spec((chunks, GROUP, DK)),
            column_spec(length, 0), column_spec(length, (1 + 2 * NH) * H), whole_spec((8, DV)),
            column_spec(length, 0), head_spec((DV, DK)),
        ],
        [column_spec(length, 0), column_spec(length, 0), square, head_spec((DV, DK)), head_spec((8, DV))],
        [],
        H * chunks * 4 * 2 * SPAN**3 * 4,
        H * chunks * 8 * SPAN * DK * 4,
    )(vec, transfer, out_keys, mixed, projected, gain, d_gated, start)


def backward_call(projected, border, taps, masks, vec, transfer, inverse, solved, entries, d_mixed, local, exit_grad):
    length = projected.shape[0]
    chunks = length // GROUP
    parts = 1 + 2 * NH
    square = head_spec((chunks, SPAN, DK))
    outs = (
        [jax.ShapeDtypeStruct((length, H * DK), jnp.bfloat16)] * parts
        + [jax.ShapeDtypeStruct((16, H * DK), jnp.float32)] * parts
        + [jax.ShapeDtypeStruct((8, H * DK), jnp.float32)] * parts
        + [per_head((chunks, 8, SPAN))]
    )
    out_specs = (
        [column_spec(length, 0)] * parts
        + [column_spec(16, 0)] * parts
        + [column_spec(8, 0)] * parts
        + [head_spec((chunks, 8, SPAN))]
    )
    tall = pltpu.VMEM((parts, length, DK), jnp.float32)
    return call(
        backward_kernel,
        outs,
        conv_specs(length)
        + [head_spec((chunks, 8, SPAN)), square, square, square, square, column_spec(length, 0), square, head_spec((DV, DK))],
        out_specs,
        [
            pltpu.VMEM((parts, length + 8, DK), jnp.float32),
            tall,
            pltpu.VMEM((length, DK), jnp.float32),
            pltpu.VMEM((NH, length, DK), jnp.float32),
            pltpu.VMEM((NH, length, DK), jnp.float32),
            pltpu.VMEM((1 + NH, length, DK), jnp.float32),
            tall,
            pltpu.VMEM((length + 16, DK), jnp.float32),
        ],
        H * chunks * 14 * 2 * SPAN**3 * 4,
        H * chunks * 16 * SPAN * DK * 4,
    )(*[projected] * parts, *[border] * parts, *[taps] * parts, masks, vec, transfer, inverse, solved, entries, d_mixed, local, exit_grad)


def gather(block, dim=0):
    return lax.all_gather(block, ("dp", "seq"), axis=dim, tiled=True)


def on_device(
    block_input, doc_starts, norm_in, w_mix, w_small, conv_w, decay_log, norm_out,
    w_out, norm_mlp, w_gu, w_down, cotangent,
):
    row_count, seg_len, width = block_input.shape
    tap_count = conv_w.shape[0]
    key_width = H * DK
    parts = 1 + 2 * NH
    seqs = lax.axis_size("seq")
    residual_in = block_input.astype(jnp.float32).reshape(seg_len, width)
    smalls, rows = w_small.shape[1], w_mix.shape[0]
    fast = lax.axis_size("dp") == 4 * ZS and seqs == 2 and rows % 16 == 0
    if fast:
        small = jnp.concatenate(
            [w_small, norm_in[:, None], norm_mlp[:, None], conv_w.reshape(tap_count, rows, -1).transpose(1, 2, 0).reshape(rows, -1)], axis=1
        )
        small = jnp.concatenate([small, jnp.zeros((rows, DK - small.shape[1]), small.dtype)], axis=1)
        mix_all, out_all, small_pack, normed_low, normed_t, channels, gate, gates_raw, border = gather_project_call(
            block_input.reshape(seg_len, width), small, w_mix, w_out
        )
        small_all = small_pack[:, :smalls]
        gates_raw = gates_raw[:, :smalls]
        norm_in_all = small_pack[:, smalls].astype(jnp.float32)
        norm_mlp_all = small_pack[:, smalls + 1].astype(jnp.float32)
        per_row = conv_w.shape[1] // rows
        conv_all = small_pack[:, smalls + 2 : smalls + 2 + per_row * tap_count]
        conv_all = conv_all.reshape(-1, tap_count).transpose(1, 0)
        normed, norm_in_back = jax.vjp(rms_scale, residual_in, norm_in_all)
    else:
        mix_all, small_all, conv_all, out_all = gather(w_mix), gather(w_small), gather(conv_w, 1), gather(w_out)
        norm_in_all = gather(norm_in).astype(jnp.float32)
        norm_mlp_all = gather(norm_mlp).astype(jnp.float32)
        normed, norm_in_back = jax.vjp(rms_scale, residual_in, norm_in_all)
        normed_low = normed.astype(jnp.bfloat16)
        projected = jnp.dot(normed_low, mix_all, preferred_element_type=jnp.float32)
        gates_raw = jnp.dot(normed_low, small_all, preferred_element_type=jnp.float32)
    if fast:
        down_own = w_down + (gates_raw[0, 0] * 0.0).astype(w_down.dtype)
        down_all = gather(down_own)
    else:
        gu_all, down_all = gather(w_gu), gather(w_down)
        border = from_behind(projected[seg_len - tap_count + 1 :, : parts * key_width], "seq", 1)
        border = jnp.concatenate([jnp.zeros((9 - tap_count, parts * key_width), jnp.float32), border], axis=0)
    positions = lax.axis_index("seq") * seg_len + jnp.arange(1 - tap_count, seg_len, dtype=jnp.int32)
    seg_ext = jnp.sum((positions[:, None] >= doc_starts[0][None, :]).astype(jnp.int32), axis=1)
    seg_ext = jnp.where(positions < 0, -1, seg_ext)
    seg_now = seg_ext[tap_count - 1 :]
    masks = jnp.stack(
        [seg_ext[tap_count - 1 - tap : tap_count - 1 - tap + seg_len] == seg_now for tap in range(1, tap_count)]
    ).astype(jnp.float32)
    masks = jnp.broadcast_to(masks[:, :, None], (tap_count - 1, seg_len, DK))
    if fast:
        masks = masks.astype(jnp.bfloat16)
    taps = jnp.concatenate([conv_all.astype(jnp.float32), jnp.zeros((8 - tap_count, parts * key_width), jnp.float32)], axis=0)
    vec, vec_back = jax.vjp(
        partial(gate_vectors, seg_now, seg_ext[tap_count - 2]), gates_raw, decay_log.astype(jnp.float32)
    )
    gain = jnp.broadcast_to(norm_out.astype(jnp.float32)[None, :], (8, DV))
    if fast:
        xt, out_keys, us, normed_out_low, mixed, gu_all = mixer_call(channels, gate, vec, masks, taps, border, gain, w_gu)
        gu_all = gu_all.reshape(width, -1)
    else:
        zero_state = jnp.zeros((H, DV, DK), jnp.float32)
        inverse, key_part, value_part, transfer, inject, out_keys, out_values, final_state = forward_call(
            projected, border, taps, masks, vec, zero_state
        )
        entry = zero_state
        device_transfer = None
        if seqs > 2:
            eye = jnp.broadcast_to(jnp.eye(DK, dtype=jnp.float32), (H, DK, DK))
            device_transfer = chain_call(vec, transfer, eye)
        for turn in range(seqs - 1):
            leaving = final_state
            if turn > 0:
                leaving = leaving + jnp.einsum("hvk,hkl->hvl", entry, device_transfer, precision=HIGHEST)
            entry = from_behind(leaving.astype(jnp.bfloat16), "seq", 1).astype(jnp.float32)
        normed_out_low, mixed, solved, entries = readout_call(
            vec, key_part, value_part, transfer, inject, out_keys, out_values, entry, projected, gain
        )
    if fast:
        mlp_gain = jnp.broadcast_to(norm_mlp_all[None, :], (8, width))
        backs = back_call(
            xt, out_keys, mixed, gate, channels, us, gu_all, down_all, vec, masks, taps, border, gain,
            out_all, mlp_gain,
            block_input.reshape(seg_len, width), normed_out_low, cotangent.reshape(seg_len, width), mix_all.reshape(STACK + (rows, -1)), normed_t,
        )
        d_projected, block_output, d_hidden, d_normed, gain_parts, d_vec, grad_conv, mlp_gain_parts = backs[:8]
        grad_gu, grad_down, grad_out, grad_mix = backs[8:]
        block_output = block_output.reshape(block_input.shape)
        d_hidden = d_hidden.reshape(seg_len, width)
        grad_norm_mlp = mlp_gain_parts[0]
        grad_down = grad_down.reshape(-1, width)[: w_down.shape[0]]
    else:
        hidden = residual_in + jnp.dot(normed_out_low, out_all, preferred_element_type=jnp.float32)
        mlp_in, norm_mlp_back = jax.vjp(rms_scale, hidden, norm_mlp_all)
        mlp_in_low = mlp_in.astype(jnp.bfloat16)
        gate_up = jnp.dot(mlp_in_low, gu_all, preferred_element_type=jnp.float32)
        activated, act_back = jax.vjp(swiglu, gate_up)
        activated_low = activated.astype(jnp.bfloat16)
        result = hidden + jnp.dot(activated_low, down_all, preferred_element_type=jnp.float32)
        block_output = result.astype(jnp.bfloat16).reshape(block_input.shape)

        d_result_low = cotangent.reshape(seg_len, width)
        d_result = d_result_low.astype(jnp.float32)
        grad_down = jnp.einsum("nf,nd->fd", activated_low, d_result_low, preferred_element_type=jnp.float32)
        d_activated = jnp.einsum("nd,fd->nf", d_result_low, down_all, preferred_element_type=jnp.float32)
        (d_gate_up,) = act_back(d_activated)
        d_gate_low = d_gate_up.astype(jnp.bfloat16)
        grad_gu = jnp.einsum("nd,nf->df", mlp_in_low, d_gate_low, preferred_element_type=jnp.float32)
        d_mlp_in = jnp.einsum("nf,df->nd", d_gate_low, gu_all, preferred_element_type=jnp.float32)
        d_hidden_norm, grad_norm_mlp = norm_mlp_back(d_mlp_in)
        d_hidden = d_result + d_hidden_norm
        d_mixer_low = d_hidden.astype(jnp.bfloat16)
        grad_out = jnp.einsum("nh,nd->hd", normed_out_low, d_mixer_low, preferred_element_type=jnp.float32)
        d_normed_out = jnp.einsum("nd,hd->nh", d_mixer_low, out_all, preferred_element_type=jnp.float32)
        grad_gu = scatter_halves(grad_gu.astype(jnp.bfloat16))
        grad_down = scatter_halves(grad_down.astype(jnp.bfloat16))
        grad_out = scatter_halves(grad_out.astype(jnp.bfloat16))
        d_mixed, d_out_gate, local, own_entry, gain_parts = readout_back_call(
            vec, transfer, out_keys, mixed, projected, gain, d_normed_out, zero_state
        )
        exit_grad = zero_state
        for turn in range(seqs - 1):
            leaving = own_entry
            if turn > 0:
                leaving = leaving + jnp.einsum("hvl,hkl->hvk", exit_grad, device_transfer, precision=HIGHEST)
            exit_grad = from_behind(leaving.astype(jnp.bfloat16), "seq", -1).astype(jnp.float32)
        backs = backward_call(
            projected, border, taps, masks, vec, transfer, inverse, solved, entries, d_mixed, local, exit_grad
        )
        d_columns, edges, tap_grads, d_vec = backs[:parts], backs[parts : 2 * parts], backs[2 * parts : 3 * parts], backs[-1]
        edge = jnp.concatenate(edges, axis=1)
        returned = from_behind(edge[9 - tap_count : 8].astype(jnp.bfloat16), "seq", -1).astype(jnp.float32)
        fixed = (edge[17 - tap_count :] + returned).astype(jnp.bfloat16)
        d_projected = jnp.concatenate(list(d_columns) + [d_out_gate], axis=1)
        d_projected = lax.dynamic_update_slice(d_projected, fixed, (seg_len - tap_count + 1, 0))
        grad_mix = jnp.einsum("nd,nc->dc", normed_low, d_projected, preferred_element_type=jnp.float32)
        grad_mix = scatter_halves(grad_mix.astype(jnp.bfloat16))
        grad_conv = jnp.concatenate(tap_grads, axis=1)
    grad_norm_out = jnp.sum(gain_parts[:, 0, :], axis=0)
    d_gates_raw, grad_decay = vec_back(d_vec)
    d_gates_low = d_gates_raw.astype(jnp.bfloat16)
    grad_small = jnp.einsum("nd,nc->dc", normed_low, d_gates_low, preferred_element_type=jnp.float32)
    if not fast:
        d_normed = jnp.einsum("nc,dc->nd", d_projected, mix_all, preferred_element_type=jnp.float32)
    d_normed = d_normed + jnp.einsum("nc,dc->nd", d_gates_low, small_all, preferred_element_type=jnp.float32)
    d_input_norm, grad_norm_in = norm_in_back(d_normed)
    input_grad = (d_hidden + d_input_norm).astype(jnp.bfloat16).reshape(block_input.shape)

    grad_conv = grad_conv[:tap_count]
    devices = lax.axis_size("dp") * seqs
    conv_rows = grad_conv.reshape(tap_count, devices, -1).transpose(1, 0, 2).reshape(width, -1)
    packed = jnp.concatenate([grad_small, grad_norm_in[:, None], grad_norm_mlp[:, None], conv_rows], axis=1)
    packed = jnp.concatenate([packed, jnp.zeros((width, 128 - packed.shape[1]), jnp.float32)], axis=1)
    if fast:
        sums = jnp.stack([grad_norm_out, jnp.pad(grad_decay, (0, DV - H))] + [jnp.zeros((DV,), jnp.float32)] * 6)
        packed, sums = total_call(packed.reshape(STACK + (rows, -1)), sums)
        grad_norm_out, grad_decay = sums[0], sums[1, :H]
    else:
        packed = scatter_sum(packed, bit_orders()[0])
        sums = total_sum(jnp.concatenate([grad_norm_out, grad_decay]))
        grad_norm_out, grad_decay = sums[:DV], sums[DV:]
    smalls = grad_small.shape[1]
    grad_small = packed[:, :smalls]
    grad_norm_in, grad_norm_mlp = packed[:, smalls], packed[:, smalls + 1]
    grad_conv = packed[:, smalls + 2 : smalls + 2 + conv_rows.shape[1]].reshape(tap_count, -1)
    return (
        block_output, input_grad, grad_norm_in, grad_mix, grad_small, grad_conv, grad_decay,
        grad_norm_out, grad_out, grad_norm_mlp, grad_gu, grad_down,
    )


def solution(mesh):
    sharded = ("dp", "seq")
    in_specs = (
        P("dp", "seq", None), P("dp", None), P(sharded), P(sharded, None), P(sharded, None),
        P(None, sharded), P(), P(), P(sharded, None), P(sharded), P(sharded, None),
        P(sharded, None), P("dp", "seq", None),
    )
    out_specs = (
        P("dp", "seq", None), P("dp", "seq", None), P(sharded), P(sharded, None), P(sharded, None),
        P(None, sharded), P(), P(), P(sharded, None), P(sharded), P(sharded, None), P(sharded, None),
    )
    return jax.shard_map(
        on_device, mesh=mesh, in_specs=in_specs, out_specs=out_specs, check_vma=False
    )
```

```python
from functools import partial

import jax
import jax.numpy as jnp
from jax import lax
from jax.experimental import pallas as pl
from jax.experimental.pallas import tpu as pltpu
from jax.sharding import PartitionSpec as P

H = 8
DK = 128
DV = 128
NH = 2
GROUP = 64
SPAN = NH * GROUP
LEVELS = 6
EPSILON = 1e-06
HIGHEST = lax.Precision.HIGHEST
LIMIT = 50 * 1024 * 1024


def mm(left, right, left_dim=1, right_dim=0):
    return lax.dot_general(
        left.astype(jnp.bfloat16),
        right.astype(jnp.bfloat16),
        (((left_dim,), (right_dim,)), ((), ())),
        preferred_element_type=jnp.float32,
    )


def halves_of(values):
    high = values.astype(jnp.bfloat16)
    return high, (values - high.astype(jnp.float32)).astype(jnp.bfloat16)


def mm3(left, right, left_dim=1, right_dim=0):
    left_high, left_low = halves_of(left)
    right_high, right_low = halves_of(right)
    wide = right.shape[1 - right_dim]
    lefts = jnp.concatenate([left_high, left_low], axis=left_dim)
    rights = jnp.concatenate(
        [
            jnp.concatenate([right_high, right_high], axis=right_dim),
            jnp.concatenate([right_low, jnp.zeros_like(right_low)], axis=right_dim),
        ],
        axis=1 - right_dim,
    )
    both = mm(lefts, rights, left_dim, right_dim)
    return both[:, :wide] + both[:, wide:]


def iotas(rows, columns):
    return (
        lax.broadcasted_iota(jnp.int32, (rows, columns), 0),
        lax.broadcasted_iota(jnp.int32, (rows, columns), 1),
    )


def order_masks():
    row, column = iotas(SPAN, SPAN)
    row_tok, column_tok = row % GROUP, column % GROUP
    row_step, column_step = row // GROUP, column // GROUP
    pair = (row_tok == column_tok) & (row_step > column_step)
    strict = (row_tok > column_tok) | pair
    levels = []
    for level in range(LEVELS):
        row_half, column_half = row_tok >> level, column_tok >> level
        levels.append((row_half == column_half + 1) & (row_half % 2 == 1))
    eye = jnp.where(row == column, 1.0, 0.0)
    return strict, pair, levels, eye


TOGETHER = 16


def together(runs):
    for first in range(0, len(runs), TOGETHER):
        group = runs[first : first + TOGETHER]
        while group:
            group = [run for run in group if next(run, "done") != "done"]


def unit_inverses(lowers, pair, levels, eye):
    inverses = [eye - jnp.where(pair, lower, 0.0) for lower in lowers]
    for level in levels:
        parts = [mm3(jnp.where(level, lower, 0.0), inv) for lower, inv in zip(lowers, inverses)]
        inverses = [inv - mm3(inv, part) for part, inv in zip(parts, inverses)]
    return inverses


def silu_pair(values):
    sig = jax.nn.sigmoid(values)
    return values * sig, sig


def conv_block(channels, border, taps, mask_ref, ext_ref):
    length = channels.shape[0]
    ext_ref[0:8, :] = border
    ext_ref[8 : 8 + length, :] = channels
    summed = channels * taps[0:1, :]
    for tap in range(1, 4):
        summed = summed + ext_ref[8 - tap : 8 - tap + length, :] * taps[tap : tap + 1, :] * mask_ref[tap - 1].astype(jnp.float32)
    return summed


def unit_rows(values):
    inv = lax.rsqrt(jnp.sum(values * values, axis=1, keepdims=True) + EPSILON)
    return values * inv, inv


def chunk_vectors(vec_ref, chunk):
    rows = vec_ref[0, chunk]
    columns = jnp.transpose(rows)
    return rows, columns


def link_matrix(rows, columns):
    row, column = iotas(GROUP, SPAN)
    linked = (columns[:GROUP, 2:3] == rows[2:3, :]) & (row >= column % GROUP)
    return jnp.exp(jnp.where(linked, columns[:GROUP, 0:1] - rows[0:1, :], -1e30))


def twice(values):
    return jnp.concatenate([values, values], axis=0)


def forward_kernel(
    q_in, k0_in, k1_in, v0_in, v1_in,
    bq, bk0, bk1, bv0, bv1,
    tq, tk0, tk1, tv0, tv1,
    mask_ref, vec_ref, start_ref,
    x_out, w_out, u_out, t_out, i_out, ok_out, o_out, state_out,
    ext_ref, q_ref, k_ref, v_ref,
):
    length = q_in.shape[0]
    chunks = length // GROUP
    conv = []
    for channel, border, tap in (
        (q_in, bq, tq), (k0_in, bk0, tk0), (k1_in, bk1, tk1), (v0_in, bv0, tv0), (v1_in, bv1, tv1),
    ):
        conv.append(silu_pair(conv_block(channel[...], border[...], tap[...], mask_ref, ext_ref))[0])
    q_ref[...] = unit_rows(conv[0])[0] * DK ** (-0.5)
    for step in range(NH):
        k_ref[step] = unit_rows(conv[1 + step])[0]
        v_ref[step] = conv[1 + NH + step]
    strict, pair, levels, eye = order_masks()
    items = []
    lowers = []
    for chunk in range(chunks):
        here = slice(chunk * GROUP, (chunk + 1) * GROUP)
        rows, columns = chunk_vectors(vec_ref, chunk)
        keys = k_ref[:, here, :].reshape(SPAN, DK)
        values = v_ref[:, here, :].reshape(SPAN, DV)
        queries = q_ref[here, :]
        link = link_matrix(rows, columns)
        lower = jnp.where(strict, columns[:, 1:2] * twice(link) * mm3(keys, keys, 1, 1), 0.0)
        reading = link * mm3(queries, keys, 1, 1)
        lowers.append(lower)
        items.append((rows, columns, keys, values, queries, reading))
    inverses = unit_inverses(lowers, pair, levels, eye)
    state = start_ref[0]
    for chunk in range(chunks):
        rows, columns, keys, values, queries, reading = items[chunk]
        inverse = inverses[chunk]
        here = slice(chunk * GROUP, (chunk + 1) * GROUP)
        beta, scale, tail = columns[:, 1:2], columns[:, 3:4], columns[:, 4:5]
        key_part = mm3(inverse, beta * scale * keys)
        value_part = mm3(inverse, beta * values)
        tail_keys = tail * keys
        transfer = mm3(key_part, tail_keys, 0, 0)
        inject = mm3(value_part, tail_keys, 0, 0)
        x_out[0, chunk] = inverse.astype(x_out.dtype)
        w_out[0, chunk] = key_part.astype(w_out.dtype)
        u_out[0, chunk] = value_part.astype(u_out.dtype)
        t_out[0, chunk] = transfer.astype(t_out.dtype)
        i_out[0, chunk] = inject
        ok_out[0, chunk] = (columns[:GROUP, 3:4] * queries - mm3(reading, key_part)).astype(ok_out.dtype)
        o_out[0, chunk] = mm3(reading, value_part)
        state = rows[3:4, GROUP - 1 : GROUP] * state - mm3(state, transfer) + inject
    state_out[0] = state


def chain_kernel(vec_ref, t_in, start_ref, state_out):
    chunks = t_in.shape[1]
    state = start_ref[0]
    for chunk in range(chunks):
        state = vec_ref[0, chunk, 3:4, GROUP - 1 : GROUP] * state - mm3(state, t_in[0, chunk])
    state_out[0] = state


def readout_kernel(vec_ref, w_in, u_in, t_in, i_in, ok_in, o_in, entry_ref, gate_ref, gain_ref, gated_out, mixed_out, u_out, s_out):
    chunks = w_in.shape[1]
    state = entry_ref[0]
    states = []
    for chunk in range(chunks):
        states.append(state)
        state = vec_ref[0, chunk, 3:4, GROUP - 1 : GROUP] * state - mm3(state, t_in[0, chunk]) + i_in[0, chunk]
    for chunk in range(chunks):
        here = slice(chunk * GROUP, (chunk + 1) * GROUP)
        state = states[chunk]
        s_out[0, chunk] = state
        u_out[0, chunk] = (u_in[0, chunk].astype(jnp.float32) - mm3(w_in[0, chunk], state, 1, 1)).astype(u_out.dtype)
        mixed = o_in[0, chunk] + mm3(ok_in[0, chunk], state, 1, 1)
        mixed_out[here, :] = mixed
        inv = lax.rsqrt(jnp.mean(mixed * mixed, axis=1, keepdims=True) + EPSILON)
        gate = silu_pair(gate_ref[here, :])[0]
        gated_out[here, :] = (mixed * inv * gain_ref[0:1, :] * gate).astype(gated_out.dtype)


def readout_back_kernel(vec_ref, t_in, ok_in, mixed_in, gate_ref, gain_ref, d_ref, start_ref, d_mixed_out, d_gate_out, local_out, state_out, gain_out):
    chunks = t_in.shape[1]
    gain = gain_ref[0:1, :]
    gain_grad = jnp.zeros((1, DV), jnp.float32)
    locals_ = []
    for chunk in range(chunks):
        here = slice(chunk * GROUP, (chunk + 1) * GROUP)
        mixed = mixed_in[here, :]
        inv = lax.rsqrt(jnp.mean(mixed * mixed, axis=1, keepdims=True) + EPSILON)
        unit = mixed * inv
        gate = gate_ref[here, :]
        open_, sig = silu_pair(gate)
        d_gated = d_ref[here, :]
        d_scaled = d_gated * open_
        d_gate_out[here, :] = (d_gated * unit * gain * sig * (1.0 + gate * (1.0 - sig))).astype(d_gate_out.dtype)
        gain_grad = gain_grad + jnp.sum(d_scaled * unit, axis=0, keepdims=True)
        d_unit = d_scaled * gain
        d_mixed = inv * (d_unit - unit * jnp.mean(d_unit * unit, axis=1, keepdims=True))
        d_mixed_low = d_mixed
        d_mixed_out[here, :] = d_mixed_low
        local = mm3(d_mixed_low, ok_in[0, chunk], 0, 0)
        local_out[0, chunk] = local
        locals_.append(local)
    gain_out[0] = jnp.broadcast_to(gain_grad, (8, DV))
    state = start_ref[0]
    for chunk in reversed(range(chunks)):
        state = vec_ref[0, chunk, 3:4, GROUP - 1 : GROUP] * state - mm3(state, t_in[0, chunk], 1, 1) + locals_[chunk]
    state_out[0] = state


def backward_kernel(
    q_in, k0_in, k1_in, v0_in, v1_in,
    bq, bk0, bk1, bv0, bv1,
    tq, tk0, tk1, tv0, tv1,
    mask_ref, vec_ref, t_in, x_in, u_in, s_in, d_mixed_in, local_in, exit_ref,
    dq_out, dk0_out, dk1_out, dv0_out, dv1_out,
    eq_out, ek0_out, ek1_out, ev0_out, ev1_out,
    gq_out, gk0_out, gk1_out, gv0_out, gv1_out,
    d_vec_out,
    ext_ref, pre_ref, q_ref, k_ref, v_ref, inv_ref, d_ref, z_ref,
):
    length = q_in.shape[0]
    chunks = length // GROUP
    channels = (q_in, k0_in, k1_in, v0_in, v1_in)
    taps = (tq, tk0, tk1, tv0, tv1)
    for part, (channel, border, tap) in enumerate(zip(channels, (bq, bk0, bk1, bv0, bv1), taps)):
        pre = conv_block(channel[...], border[...], tap[...], mask_ref, ext_ref.at[part])
        pre_ref[part] = pre
        value = silu_pair(pre)[0]
        if part == 0:
            unit, inv = unit_rows(value)
            q_ref[...] = unit * DK ** (-0.5)
            inv_ref[0] = jnp.broadcast_to(inv, (length, DK))
        elif part <= NH:
            unit, inv = unit_rows(value)
            k_ref[part - 1] = unit
            inv_ref[part] = jnp.broadcast_to(inv, (length, DK))
        else:
            v_ref[part - 1 - NH] = value
    strict, pair, levels, eye = order_masks()
    column_index = iotas(SPAN, 8)[1]
    exit_grads = [None] * chunks
    grad = exit_ref[0]
    for chunk in reversed(range(chunks)):
        exit_grads[chunk] = grad
        grad = vec_ref[0, chunk, 3:4, GROUP - 1 : GROUP] * grad - mm3(grad, t_in[0, chunk], 1, 1) + local_in[0, chunk]
    for chunk in reversed(range(chunks)):
        here = slice(chunk * GROUP, (chunk + 1) * GROUP)
        rows, columns = chunk_vectors(vec_ref, chunk)
        beta, scale, tail = columns[:, 1:2], columns[:, 3:4], columns[:, 4:5]
        keys = k_ref[:, here, :].reshape(SPAN, DK)
        values = v_ref[:, here, :].reshape(SPAN, DV)
        queries = q_ref[here, :]
        link = link_matrix(rows, columns)
        link_gram = jnp.where(strict, twice(link) * mm3(keys, keys, 1, 1), 0.0)
        reading = link * mm3(queries, keys, 1, 1)
        d_exit = exit_grads[chunk]
        solved = u_in[0, chunk]
        entry = s_in[0, chunk]
        d_mixed = d_mixed_in[here, :]
        tail_keys = tail * keys
        d_solved = mm3(reading, d_mixed, 0, 0) + mm3(tail_keys, d_exit, 1, 1)
        d_right = mm3(x_in[0, chunk], d_solved, 0, 0)
        d_lower = jnp.where(strict, -mm3(d_right, solved, 1, 1), 0.0)
        d_tail_keys = mm3(solved, d_exit)
        d_right_entry = mm3(d_right, entry)
        d_reading = mm3(d_mixed, solved, 1, 1)
        d_query_entry = mm3(d_mixed, entry)
        both_scale = -jnp.sum(d_right_entry * keys, axis=1, keepdims=True)
        lower_weight = d_lower * link_gram
        d_beta = (
            jnp.sum(d_right * values, axis=1, keepdims=True)
            + scale * both_scale
            + jnp.sum(lower_weight, axis=1, keepdims=True)
        )
        lower_moment = lower_weight * beta
        reading_moment = d_reading * reading
        d_gram = beta * twice(link) * d_lower
        d_gram = d_gram + jnp.transpose(d_gram)
        d_query_gram = link * d_reading
        d_keys = (
            tail * d_tail_keys
            - beta * scale * d_right_entry
            + mm3(d_gram, keys)
            + mm3(d_query_gram, queries, 0, 0)
        )
        d_queries = mm3(d_query_gram, keys) + scale[:GROUP] * d_query_entry
        d_values = beta * d_right
        none = jnp.zeros((GROUP, 1), jnp.float32)
        d_gap = jnp.sum(lower_moment, axis=1, keepdims=True) + jnp.concatenate(
            [jnp.sum(reading_moment, axis=1, keepdims=True), none], axis=0
        )
        last = jnp.sum(jnp.sum(d_exit * entry.astype(jnp.float32), axis=1, keepdims=True), axis=0, keepdims=True)
        own_scale = jnp.sum(d_query_entry * queries, axis=1, keepdims=True)
        own_scale = own_scale + jnp.where(iotas(GROUP, 1)[0] == GROUP - 1, last, 0.0)
        d_scale = beta * both_scale + jnp.concatenate([own_scale, none], axis=0)
        d_tail = jnp.sum(d_tail_keys * keys, axis=1, keepdims=True)
        grads = jnp.where(
            column_index == 0,
            d_gap,
            jnp.where(
                column_index == 1,
                d_beta,
                jnp.where(column_index == 3, d_scale, jnp.where(column_index == 4, d_tail, 0.0)),
            ),
        )
        grads = jnp.transpose(grads)
        sums = jnp.sum(lower_moment, axis=0, keepdims=True) + jnp.sum(reading_moment, axis=0, keepdims=True)
        grads = grads - jnp.where(iotas(8, SPAN)[0] == 0, sums, 0.0)
        d_vec_out[0, chunk] = grads
        d_ref[0, here, :] = d_queries
        for step in range(NH):
            mine = slice(step * GROUP, (step + 1) * GROUP)
            d_ref[1 + step, here, :] = d_keys[mine]
            d_ref[1 + NH + step, here, :] = d_values[mine]
    outs = (dq_out, dk0_out, dk1_out, dv0_out, dv1_out)
    edges = (eq_out, ek0_out, ek1_out, ev0_out, ev1_out)
    tap_grads = (gq_out, gk0_out, gk1_out, gv0_out, gv1_out)
    z_ref[0:8, :] = jnp.zeros((8, DK), jnp.float32)
    z_ref[8 + length : 16 + length, :] = jnp.zeros((8, DK), jnp.float32)
    for part in range(1 + 2 * NH):
        grad = d_ref[part]
        if part <= NH:
            unit = q_ref[...] * DK ** 0.5 if part == 0 else k_ref[part - 1]
            if part == 0:
                grad = grad * DK ** (-0.5)
            grad = inv_ref[part] * (grad - unit * jnp.sum(grad * unit, axis=1, keepdims=True))
        pre = pre_ref[part]
        sig = jax.nn.sigmoid(pre)
        grad = grad * sig * (1.0 + pre * (1.0 - sig))
        tap = taps[part]
        total = grad * tap[0:1, :]
        edge = jnp.zeros((8, DK), jnp.float32)
        tap_rows = [jnp.sum(grad * channels[part][...], axis=0, keepdims=True)]
        for index in range(1, 4):
            shifted = grad * mask_ref[index - 1]
            tap_rows.append(
                jnp.sum(shifted * ext_ref[part, 8 - index : 8 - index + length, :], axis=0, keepdims=True)
            )
            z_ref[8 : 8 + length, :] = shifted * tap[index : index + 1, :]
            total = total + z_ref[8 + index : 8 + index + length, :]
            edge = edge + z_ref[index : index + 8, :]
        outs[part][...] = total.astype(outs[part].dtype)
        edges[part][0:8, :] = edge
        edges[part][8:16, :] = total[length - 8 :, :]
        tap_grads[part][...] = jnp.concatenate(tap_rows + [jnp.zeros((4, DK), jnp.float32)], axis=0)


MESH = pl.DeviceIdType.MESH
ZS = 4
STACK = (ZS, 2, 2, 2)
STAGES = 6


def place():
    dp, seq = lax.axis_index("dp"), lax.axis_index("seq")
    return dp // 4, (dp // 2) % 2, dp % 2, seq


def device_at(z, x, core, y):
    return (z * 4 + x * 2 + core, y)


def peers():
    z, x, core, y = place()
    ring = [device_at((z + step) % ZS, x, core, y) for step in range(1, ZS)]
    return ring + [device_at(z, 1 - x, core, y), device_at(z, x, core, 1 - y), device_at(z, x, 1 - core, y)]


def meet(devices):
    barrier = pltpu.get_barrier_semaphore()
    for device in devices:
        pl.semaphore_signal(barrier, inc=1, device_id=device, device_id_type=MESH)
    pl.semaphore_wait(barrier, len(devices))


class Gather:
    def __init__(self, source, target, x_first, sems, index):
        self.source, self.target, self.x_first = source, target, x_first
        self.send, self.recv, self.local = sems
        self.index = index
        self.copies = []

    def remote(self, source, target, slot):
        copy = pltpu.make_async_remote_copy(
            src_ref=source, dst_ref=target,
            send_sem=self.send.at[self.index, slot], recv_sem=self.recv.at[self.index, slot],
            device_id=peers()[slot], device_id_type=MESH,
        )
        copy.start()
        self.copies.append(copy)
        return copy

    def begin(self):
        z, x, core, y = place()
        mine = self.target(z, x, core, y)
        self.own = pltpu.make_async_copy(self.source, mine, self.local.at[self.index])
        self.own.start()
        self.waiting = [self.remote(self.source, mine, slot) for slot in range(ZS - 1)]

    def second(self):
        z, x, core, y = place()
        self.own.wait()
        for copy in self.waiting:
            copy.wait_recv()
        block = self.target(slice(None), x, core, y)
        self.waiting = [self.remote(block, block, ZS - 1 if self.x_first else ZS)]

    def third(self):
        z, x, core, y = place()
        self.waiting[0].wait_recv()
        every = slice(None)
        block = self.target(every, every, core, y) if self.x_first else self.target(every, x, core, every)
        self.waiting = [self.remote(block, block, ZS if self.x_first else ZS - 1)]

    def fourth(self):
        z, x, core, y = place()
        self.waiting[0].wait_recv()
        every = slice(None)
        block = self.target(every, every, core, every)
        self.waiting = [self.remote(block, block, ZS + 1)]

    def finish(self):
        self.waiting[0].wait_recv()
        for copy in self.copies:
            copy.wait_send()


def columns_of(ref, first, width):
    return lambda z, x, core, y: ref.at[z, x, core, y, :, pl.ds(first, width)]


class Spread:
    def __init__(self, source, target, lane, width, sems, first=0):
        self.first = first
        self.source, self.target, self.lane, self.width = source, target, lane, width
        self.send_sem, self.recv_sem, self.local_sem = sems
        self.place, self.peers = place(), peers()

    def here(self, index):
        return pl.ds(pl.multiple_of((2 * (index - self.first) + self.lane) * self.width, self.width), self.width)

    def block(self, index, stage):
        z, x, core, y = self.place
        every = slice(None)
        here = self.here(index)
        if stage == 0:
            return self.target.at[z, x, core, y, :, here]
        if stage == 1:
            return self.target.at[:, x, core, y, :, here]
        if stage == 2:
            if self.lane == 0:
                return self.target.at[:, :, core, y, :, here]
            return self.target.at[:, x, core, :, :, here]
        return self.target.at[:, :, core, :, :, here]

    def copies(self, index, stage):
        near, far = (ZS - 1, ZS) if self.lane == 0 else (ZS, ZS - 1)
        slots = (0, 1, 2) if stage == 0 else ((near,), (far,), (ZS + 1,))[stage - 1]
        target = self.block(index, stage)
        source = self.source.at[:, self.here(index)] if stage == 0 else target
        ring = lax.rem(index, RING)
        return [
            pltpu.make_async_remote_copy(
                src_ref=source, dst_ref=target,
                send_sem=self.send_sem.at[self.lane, slot, ring], recv_sem=self.recv_sem.at[self.lane, slot, ring],
                device_id=self.peers[slot], device_id_type=MESH,
            )
            for slot in slots
        ]

    def own(self, index):
        return pltpu.make_async_copy(
            self.source.at[:, self.here(index)], self.block(index, 0), self.local_sem.at[self.lane, lax.rem(index, RING)]
        )

    def step(self, index, stage):
        if stage > 0:
            for copy in self.copies(index, stage - 1):
                copy.wait_recv()
                copy.wait_send()
        if stage == 1:
            self.own(index).wait()
        if stage == 0:
            self.own(index).start()
        if stage < SPREAD_STAGES - 1:
            for copy in self.copies(index, stage):
                copy.start()


SPREAD_STAGES = 5
SPREAD_TICKS = 2
SPREAD_FILL = (SPREAD_STAGES - 1) * SPREAD_TICKS
FINE = 256


def gather_project_kernel(
    x_ref, small_in, mix_in, out_in, down_in,
    mix_out, out_out, down_out, small_out, normed_ref, normed_t_ref, channels_out, gate_out, gates_ref, border_ref, gains_ref,
    mix_ref, small_ref, slab_ref,
    small_send, small_recv, small_local, send, recv, local, store_mix, store_slab, store_small, store_down, edge_send, edge_recv,
):
    parts, heads = channels_out.shape[0], channels_out.shape[1]
    length = x_ref.shape[0]
    block = 2 * FINE
    count = mix_in.shape[1] // block
    more = out_in.shape[1] // block
    per_part, across = heads * DK // block, block // DK
    z, x, core, y = place()
    sems = (send, recv, local)
    small = Gather(small_in, lambda z, x, core, y: small_ref.at[z, x, core, y], True, (small_send, small_recv, small_local), 0)
    mix_lanes = [Spread(mix_in, mix_ref, lane, FINE, sems) for lane in range(2)]
    out_lanes = [Spread(out_in, out_out, lane, FINE, sems, count) for lane in range(2)]

    def here(index):
        return pl.ds(pl.multiple_of(index * block, block), block)

    def slab_copies(index):
        slot, first = lax.rem(index, 2), lax.rem(index, per_part) * across
        return [
            [
                pltpu.make_async_copy(
                    slab_ref.at[slot, :, half * DK : (half + 1) * DK], target.at[first + half], store_slab.at[slot, half]
                )
                for half in range(across)
            ]
            for target in (channels_out.at[jnp.minimum(index // per_part, parts - 1)], gate_out)
        ]

    def edge(index):
        return pltpu.make_async_remote_copy(
            src_ref=slab_ref.at[lax.rem(index, 2), length - 8 :, :], dst_ref=border_ref.at[:, here(index)],
            send_sem=edge_send.at[lax.rem(index, 2)], recv_sem=edge_recv.at[index],
            device_id=device_at(z, x, core, 1 - y), device_id_type=MESH,
        )

    def kept(index):
        return pltpu.make_async_copy(
            mix_ref.at[:, :, :, :, :, here(index)], mix_out.at[:, :, :, :, :, here(index)], store_mix.at[lax.rem(index, 2)]
        )

    def release(index):
        for copy in slab_copies(index)[0]:
            copy.wait()
        kept(index).wait()

        @pl.when(index < parts * per_part)
        def _():
            edge(index).wait_send()

    def project(index):
        @pl.when(index >= 2)
        def _():
            release(index - 2)

        kept(index).start()
        weights = mix_ref[:, :, :, :, :, here(index)].reshape(-1, block)
        slab_ref[lax.rem(index, 2)] = mm(normed_ref[...], weights)
        channels, gates = slab_copies(index)

        @pl.when(index < parts * per_part)
        def _():
            for copy in channels:
                copy.start()
            edge(index).start()

        @pl.when(index >= parts * per_part)
        def _():
            for copy in gates:
                copy.start()

    def tick(number):
        for stage in reversed(range(SPREAD_STAGES)):
            index = number - stage * SPREAD_TICKS

            @pl.when((index >= 0) & (index < count))
            def _():
                for lane in mix_lanes:
                    lane.step(index, stage)

            @pl.when((index >= count) & (index < count + more))
            def _():
                for lane in out_lanes:
                    lane.step(index, stage)

        @pl.when((number >= SPREAD_FILL) & (number < count + SPREAD_FILL))
        def _():
            project(number - SPREAD_FILL)

    meet(peers())
    small.begin()
    for number in range(SPREAD_FILL):
        tick(number)
        if number == 0:
            values = x_ref[...].astype(jnp.float32)
            scaled = values * lax.rsqrt(jnp.mean(values * values, axis=1, keepdims=True) + EPSILON)
        if number % SPREAD_TICKS == SPREAD_TICKS - 1:
            (small.second, small.third, small.fourth, small.finish)[number // SPREAD_TICKS]()
    smalls = small_ref[...].reshape(-1, small_in.shape[1])
    gains_ref[...] = jnp.transpose(smalls.astype(jnp.float32))[24:32, :]
    normed = (scaled * gains_ref[0:1, :]).astype(jnp.bfloat16)
    normed_ref[...] = normed
    keep_small = pltpu.make_async_copy(small_ref, small_out, store_small)
    keep_small.start()
    keep_down = pltpu.make_async_copy(down_in, down_out, store_down)
    keep_down.start()

    def loop(number, carry):
        tick(number)
        return carry

    lax.fori_loop(SPREAD_FILL, 2 * SPREAD_FILL, loop, 0)
    gates_ref[...] = mm(normed_ref[...], smalls)
    flipped = jnp.transpose(normed_ref[...].astype(jnp.float32)).astype(jnp.bfloat16)
    normed_t_ref[...] = flipped.reshape(normed_t_ref.shape)
    lax.fori_loop(2 * SPREAD_FILL, count + more + SPREAD_FILL, loop, 0)
    release(count - 2)
    release(count - 1)
    keep_small.wait()
    keep_down.wait()

    def last(index, carry):
        edge(index).wait_recv()
        return carry

    lax.fori_loop(0, parts * per_part, last, 0)


def gather_project_call(x, small, mix, out, down):
    length = x.shape[0]
    rows, width = mix.shape
    everywhere = pl.BlockSpec(memory_space=pl.ANY)
    held = pl.BlockSpec(memory_space=pltpu.VMEM)
    full = STACK + (rows,)
    block = 2 * FINE
    parts = width // (H * DK) - 1
    outs = pl.pallas_call(
        gather_project_kernel,
        out_shape=[
            jax.ShapeDtypeStruct(full + (width,), jnp.bfloat16),
            jax.ShapeDtypeStruct(full + (out.shape[1],), jnp.bfloat16),
            jax.ShapeDtypeStruct(down.shape, jnp.bfloat16),
            jax.ShapeDtypeStruct(full + (small.shape[1],), jnp.bfloat16),
            jax.ShapeDtypeStruct(x.shape, jnp.bfloat16),
            jax.ShapeDtypeStruct(full + (length,), jnp.bfloat16),
            jax.ShapeDtypeStruct((parts, H, length, DK), jnp.float32),
            jax.ShapeDtypeStruct((H, length, DK), jnp.float32),
            jax.ShapeDtypeStruct((length, small.shape[1]), jnp.float32),
            jax.ShapeDtypeStruct((8, parts * H * DK), jnp.float32),
            jax.ShapeDtypeStruct((8, x.shape[1]), jnp.float32),
        ],
        in_specs=[held, everywhere, everywhere, everywhere, everywhere],
        out_specs=[everywhere, everywhere, everywhere, everywhere, held, held, everywhere, everywhere, held, held, held],
        scratch_shapes=[
            pltpu.VMEM(full + (width,), jnp.bfloat16),
            pltpu.VMEM(full + (small.shape[1],), jnp.bfloat16),
            pltpu.VMEM((2, length, block), jnp.float32),
            pltpu.SemaphoreType.DMA((1, STAGES)),
            pltpu.SemaphoreType.DMA((1, STAGES)),
            pltpu.SemaphoreType.DMA((1,)),
            pltpu.SemaphoreType.DMA((2, STAGES, RING)),
            pltpu.SemaphoreType.DMA((2, STAGES, RING)),
            pltpu.SemaphoreType.DMA((2, RING)),
            pltpu.SemaphoreType.DMA((2,)),
            pltpu.SemaphoreType.DMA((2, block // DK)),
            pltpu.SemaphoreType.DMA,
            pltpu.SemaphoreType.DMA,
            pltpu.SemaphoreType.DMA((2,)),
            pltpu.SemaphoreType.DMA((parts * H * DK // block,)),
        ],
        compiler_params=pltpu.CompilerParams(collective_id=1, has_side_effects=True, vmem_limit_bytes=LIMIT),
        cost_estimate=pl.CostEstimate(flops=2 * length * width * 1024, bytes_accessed=60_000_000, transcendentals=0),
    )(x, small, mix, out, down)
    return [part.reshape((-1,) + part.shape[5:]) if index in (0, 1, 3) else part for index, part in enumerate(outs)]


PAIR = 2


def mixer_kernel(
    channel_ref, gate_ref, vec_ref, mask_ref, tap_ref, border_ref, gain_ref, shard_in,
    xt_out, ok_out, us_out, gated_out, mixed_out, gathered_out,
    w_ref, u_ref, t_ref, i_ref, k_read_ref, v_read_ref, relay_send, relay_recv,
    ext_ref, q_ref, k_ref, v_ref,
    relay_sems, send_sem, recv_sem, local_sem,
):
    step = pl.program_id(0)
    steps = H // PAIR
    parts = channel_ref.shape[0]
    length = channel_ref.shape[2]
    chunks = length // GROUP
    z, x, core, y = place()
    count = shard_in.shape[1] // (2 * WIDE)
    lanes = [Spread(shard_in, gathered_out, lane, WIDE, (send_sem, recv_sem, local_sem)) for lane in range(2)]

    def tick(number):
        for stage in reversed(range(SPREAD_STAGES)):
            index = number - stage * SPREAD_TICKS

            @pl.when((index >= 0) & (index < count))
            def _():
                for lane in lanes:
                    lane.step(index, stage)

    def convolve(pair):
        head = step * PAIR + pair
        column = lambda part: pl.ds(pl.multiple_of((part * H + head) * DK, DK), DK)
        for part in range(parts):
            value = silu_pair(
                conv_block(
                    channel_ref[part, pair], border_ref[:, column(part)], tap_ref[:, column(part)], mask_ref,
                    ext_ref.at[pair],
                )
            )[0]
            if part == 0:
                q_ref[pair] = unit_rows(value)[0] * DK ** (-0.5)
            elif part <= NH:
                k_ref[pair, part - 1] = unit_rows(value)[0]
            else:
                v_ref[pair, part - 1 - NH] = value
            yield

    def chunk_terms(pair, chunk, masks):
        strict, same, levels, eye = masks
        head = step * PAIR + pair
        here = slice(chunk * GROUP, (chunk + 1) * GROUP)
        rows = vec_ref[head, chunk]
        columns = jnp.transpose(rows)
        keys = k_ref[pair, :, here, :].reshape(SPAN, DK)
        beta, scale, tail = columns[:, 1:2], columns[:, 3:4], columns[:, 4:5]
        link = link_matrix(rows, columns)
        lower = jnp.where(strict, beta * twice(link) * mm3(keys, keys, 1, 1), 0.0)
        yield
        inverse = eye - jnp.where(same, lower, 0.0)
        for level in levels:
            part = mm3(jnp.where(level, lower, 0.0), inverse)
            yield
            inverse = inverse - mm3(inverse, part)
            yield
        xt_out[pair, 0, chunk] = inverse

    def chunk_rest(pair, chunk):
        head = step * PAIR + pair
        here = slice(chunk * GROUP, (chunk + 1) * GROUP)
        rows = vec_ref[head, chunk]
        columns = jnp.transpose(rows)
        keys = k_ref[pair, :, here, :].reshape(SPAN, DK)
        values = v_ref[pair, :, here, :].reshape(SPAN, DV)
        queries = q_ref[pair, here, :]
        beta, scale, tail = columns[:, 1:2], columns[:, 3:4], columns[:, 4:5]
        inverse = xt_out[pair, 0, chunk]
        reading = link_matrix(rows, columns) * mm3(queries, keys, 1, 1)
        key_part = mm3(inverse, beta * scale * keys)
        value_part = mm3(inverse, beta * values)
        w_ref[head, chunk] = key_part
        u_ref[head, chunk] = value_part
        yield
        tail_keys = tail * keys
        transfer = mm3(key_part, tail_keys, 0, 0)
        inject = mm3(value_part, tail_keys, 0, 0)
        t_ref[head, chunk] = transfer
        xt_out[pair, 1, chunk] = transfer
        i_ref[head, chunk] = inject
        yield
        read_keys = scale[:GROUP] * queries - mm3(reading, key_part)
        k_read_ref[head, chunk] = read_keys
        ok_out[pair, chunk] = read_keys
        v_read_ref[head, chunk] = mm3(reading, value_part)

    def final_state(pair):
        head = step * PAIR + pair
        state = jnp.zeros((DV, DK), jnp.float32)
        for chunk in range(chunks):
            state = (
                vec_ref[head, chunk, 3:4, GROUP - 1 : GROUP] * state - mm3(state, t_ref[head, chunk]) + i_ref[head, chunk]
            )
            yield
        relay_send[head] = state.astype(jnp.bfloat16)

    def readout(pair):
        head = (step - steps) * PAIR + pair
        state = jnp.where(y == 0, 0.0, 1.0) * relay_recv[head].astype(jnp.float32)
        for chunk in range(chunks):
            here = slice(chunk * GROUP, (chunk + 1) * GROUP)
            us_out[pair, 1, chunk] = state
            later = (
                vec_ref[head, chunk, 3:4, GROUP - 1 : GROUP] * state - mm3(state, t_ref[head, chunk]) + i_ref[head, chunk]
            )
            us_out[pair, 0, chunk] = u_ref[head, chunk] - mm3(w_ref[head, chunk], state, 1, 1)
            mixed = v_read_ref[head, chunk] + mm3(k_read_ref[head, chunk], state, 1, 1)
            yield
            mixed_out[pair, here, :] = mixed
            inv = lax.rsqrt(jnp.mean(mixed * mixed, axis=1, keepdims=True) + EPSILON)
            gate = silu_pair(gate_ref[pair, here, :])[0]
            gated = mixed * inv * gain_ref[0:1, :] * gate
            gated_out[here, pair * DV : (pair + 1) * DV] = gated.astype(gated_out.dtype)
            state = later

    relay = pltpu.make_async_remote_copy(
        src_ref=relay_send, dst_ref=relay_recv, send_sem=relay_sems.at[0], recv_sem=relay_sems.at[1],
        device_id=device_at(z, x, core, 1 - y), device_id_type=MESH,
    )

    @pl.when(step == 0)
    def _():
        meet(peers())

    @pl.when(step < steps)
    def _():
        def early_tick(number, carry):
            tick(number)
            return carry

        lax.fori_loop(jnp.where(step == 0, 0, step * 3 + 1), step * 3 + 2, early_tick, 0)
        together([convolve(pair) for pair in range(PAIR)])
        masks = order_masks()
        together([chunk_terms(pair, chunk, masks) for pair in range(PAIR) for chunk in range(chunks)])
        tick(step * 3 + 2)
        together([chunk_rest(pair, chunk) for pair in range(PAIR) for chunk in range(chunks)])
        together([final_state(pair) for pair in range(PAIR)])
        tick(step * 3 + 3)

    @pl.when(step == steps - 1)
    def _():
        relay.start()

    @pl.when(step == steps)
    def _():
        relay.wait()

    @pl.when(step >= steps)
    def _():
        tick(steps * 3 + 1 + step - steps)
        together([readout(pair) for pair in range(PAIR)])

    @pl.when(step == 2 * steps - 1)
    def _():
        def drain(number, carry):
            tick(number)
            return carry

        lax.fori_loop(steps * 4 + 1, max(count + SPREAD_FILL, steps * 4 + 1), drain, 0)


def held_specs(count):
    return [pl.BlockSpec(memory_space=pltpu.VMEM)] * count


def mixer_call(channels, gate, vec, masks, taps, border, gain, shard):
    parts, heads, length, width = channels.shape
    chunks = length // GROUP
    steps = H // PAIR

    def early(step):
        return jnp.minimum(step, steps - 1)

    def late(step):
        return jnp.maximum(step - steps, 0)

    def heads_spec(shape, which):
        rank = len(shape)
        return pl.BlockSpec((PAIR,) + shape, lambda step: (which(step),) + (0,) * rank)

    square = (chunks, SPAN, DK)
    anywhere = pl.BlockSpec(memory_space=pl.ANY)
    return pl.pallas_call(
        mixer_kernel,
        grid=(2 * steps,),
        out_shape=[
            per_head((2,) + square),
            per_head((chunks, GROUP, DK)),
            per_head((2,) + square),
            jax.ShapeDtypeStruct((length, H * DV), jnp.bfloat16),
            per_head((length, DV)),
            jax.ShapeDtypeStruct(STACK + shard.shape, jnp.bfloat16),
        ],
        in_specs=[
            pl.BlockSpec((parts, PAIR, length, DK), lambda step: (0, early(step), 0, 0)),
            heads_spec((length, DV), late),
        ]
        + held_specs(5)
        + [anywhere],
        out_specs=[
            heads_spec((2,) + square, early),
            heads_spec((chunks, GROUP, DK), early),
            heads_spec((2,) + square, late),
            pl.BlockSpec((length, PAIR * DV), lambda step: (0, late(step))),
            heads_spec((length, DV), late),
            anywhere,
        ],
        scratch_shapes=[pltpu.VMEM((H,) + square, jnp.float32)] * 4
        + [pltpu.VMEM((H, chunks, GROUP, DK), jnp.float32)] * 2
        + [pltpu.VMEM((H, DV, DK), jnp.bfloat16)] * 2
        + [
            pltpu.VMEM((PAIR, length + 8, DK), jnp.float32),
            pltpu.VMEM((PAIR, length, DK), jnp.float32),
            pltpu.VMEM((PAIR, NH, length, DK), jnp.float32),
            pltpu.VMEM((PAIR, NH, length, DK), jnp.float32),
            pltpu.SemaphoreType.DMA((2,)),
            pltpu.SemaphoreType.DMA((2, STAGES, RING)),
            pltpu.SemaphoreType.DMA((2, STAGES, RING)),
            pltpu.SemaphoreType.DMA((2, RING)),
        ],
        compiler_params=pltpu.CompilerParams(
            dimension_semantics=("arbitrary",), collective_id=4, has_side_effects=True, vmem_limit_bytes=58 * 1024 * 1024
        ),
        cost_estimate=pl.CostEstimate(
            flops=H * chunks * 24 * 2 * SPAN**3 * 4, bytes_accessed=80_000_000, transcendentals=0
        ),
    )(channels, gate, vec, masks, taps, border, gain, shard)


WIDE = 256
RING = 4
SPAN_TICKS = 2
REDUCE_STAGES = 5
CORE, NEAR, FAR, RINGS = 0, 1, 2, 3


class Reduce:
    def __init__(self, refs, lane, count):
        (
            self.both, self.first, self.near_kept, self.near_send, self.near,
            self.far_kept, self.far_send, self.far, self.last_kept, self.last_send, self.last,
            self.send_sem, self.recv_sem,
        ) = refs
        self.lane, self.count = lane, count
        self.z, self.x, self.core, self.y = place()
        self.peers = peers()
        self.x_first = lane == 0
        self.columns = slice(lane * WIDE, (lane + 1) * WIDE)

    def copy(self, source, target, slot_of, stage, index, device):
        lane = self.lane
        return pltpu.make_async_remote_copy(
            src_ref=source, dst_ref=target,
            send_sem=self.send_sem.at[lane, stage, lax.rem(index, 2)],
            recv_sem=self.recv_sem.at[lane, stage, lax.rem(index, RING)],
            device_id=device, device_id_type=MESH,
        )

    def core_copy(self, index):
        source = self.both.at[lax.rem(index, 2), :, :, 1 - self.core, :, :, self.columns]
        return self.copy(source, self.first.at[self.lane, lax.rem(index, RING)], None, CORE, index, self.peers[ZS + 1])

    def near_copy(self, index):
        lane = self.lane
        return self.copy(
            self.near_send.at[lane, lax.rem(index, 2)], self.near.at[lane, lax.rem(index, RING)], None, NEAR, index,
            self.peers[ZS - 1 if self.x_first else ZS],
        )

    def far_copy(self, index):
        lane = self.lane
        return self.copy(
            self.far_send.at[lane, lax.rem(index, 2)], self.far.at[lane, lax.rem(index, RING)], None, FAR, index,
            self.peers[ZS if self.x_first else ZS - 1],
        )

    def ring_copies(self, index):
        lane = self.lane
        return [
            self.copy(
                self.last_send.at[lane, lax.rem(index, 2), step], self.last.at[lane, lax.rem(index, RING), step],
                None, RINGS + step, index, self.peers[step],
            )
            for step in range(ZS - 1)
        ]

    def from_core(self, index):
        lane, slot, ring = self.lane, lax.rem(index, 2), lax.rem(index, RING)
        arrived = self.core_copy(index)
        arrived.wait_recv()
        arrived.wait_send()

        def one(z, carry):
            if self.x_first:
                pick = lambda half: self.both[slot, z, half, self.core, :, :, self.columns]
                pick_got = lambda half: self.first[lane, ring, z, half]
                mine = self.x
            else:
                pick = lambda half: self.both[slot, z, :, self.core, half, :, self.columns]
                pick_got = lambda half: self.first[lane, ring, z, :, half]
                mine = self.y
            kept = pick(mine).astype(jnp.float32) + pick_got(mine).astype(jnp.float32)
            sent = pick(1 - mine).astype(jnp.float32) + pick_got(1 - mine).astype(jnp.float32)
            self.near_kept[lane, slot, z] = kept
            self.near_send[lane, slot, z] = sent.astype(jnp.bfloat16)
            return carry

        lax.fori_loop(0, ZS, one, 0)
        self.near_copy(index).start()

    def from_near(self, index):
        lane, slot, ring = self.lane, lax.rem(index, 2), lax.rem(index, RING)
        arrived = self.near_copy(index)
        arrived.wait_recv()
        arrived.wait_send()
        mine = self.y if self.x_first else self.x

        def one(z, carry):
            kept = self.near_kept[lane, slot, z, mine] + self.near[lane, ring, z, mine].astype(jnp.float32)
            sent = self.near_kept[lane, slot, z, 1 - mine] + self.near[lane, ring, z, 1 - mine].astype(jnp.float32)
            self.far_kept[lane, slot, z] = kept
            self.far_send[lane, slot, z] = sent.astype(jnp.bfloat16)
            return carry

        lax.fori_loop(0, ZS, one, 0)
        self.far_copy(index).start()

    def from_far(self, index):
        lane, slot, ring = self.lane, lax.rem(index, 2), lax.rem(index, RING)
        arrived = self.far_copy(index)
        arrived.wait_recv()
        arrived.wait_send()

        def total(z):
            return self.far_kept[lane, slot, z] + self.far[lane, ring, z].astype(jnp.float32)

        self.last_kept[lane, slot] = total(self.z)
        for step, copy in enumerate(self.ring_copies(index)):
            self.last_send[lane, slot, step] = total(lax.rem(self.z + 1 + step, ZS)).astype(jnp.bfloat16)
            copy.start()

    def from_ring(self, index):
        lane, slot, ring = self.lane, lax.rem(index, 2), lax.rem(index, RING)
        total = self.last_kept[lane, slot]
        for step, copy in enumerate(self.ring_copies(index)):
            copy.wait_recv()
            copy.wait_send()
            total = total + self.last[lane, ring, step].astype(jnp.float32)
        return total


def reduce_scratch(rows):
    half = (2, 2, rows, WIDE)
    lanes = 2
    return [
        pltpu.VMEM((2,) + STACK + (rows, lanes * WIDE), jnp.bfloat16),
        pltpu.VMEM((lanes, RING, ZS) + half, jnp.bfloat16),
        pltpu.VMEM((lanes, 2, ZS, 2, rows, WIDE), jnp.float32),
        pltpu.VMEM((lanes, 2, ZS, 2, rows, WIDE), jnp.bfloat16),
        pltpu.VMEM((lanes, RING, ZS, 2, rows, WIDE), jnp.bfloat16),
        pltpu.VMEM((lanes, 2, ZS, rows, WIDE), jnp.float32),
        pltpu.VMEM((lanes, 2, ZS, rows, WIDE), jnp.bfloat16),
        pltpu.VMEM((lanes, RING, ZS, rows, WIDE), jnp.bfloat16),
        pltpu.VMEM((lanes, 2, rows, WIDE), jnp.float32),
        pltpu.VMEM((lanes, 2, ZS - 1, rows, WIDE), jnp.bfloat16),
        pltpu.VMEM((lanes, RING, ZS - 1, rows, WIDE), jnp.bfloat16),
        pltpu.SemaphoreType.DMA((lanes, RINGS + ZS - 1, 2)),
        pltpu.SemaphoreType.DMA((lanes, RINGS + ZS - 1, RING)),
    ]


def make_back_kernel(length, width, hidden):
    chunks = length // GROUP
    parts = 1 + 2 * NH
    blocks = hidden // WIDE
    halves = width // WIDE // 2
    down_first = blocks
    out_first = down_first + 3 * halves
    gate_first = out_first + halves
    head_first = gate_first + halves
    count = head_first + parts * (H // 2) // 2
    ticks = count + (REDUCE_STAGES - 1) * SPAN_TICKS
    rows = 32
    shard = hidden // 32
    early = blocks + 2
    late = early + H
    last = late + H
    early_tick = blocks
    late_tick = early_tick + H // 2

    def kernel(
        xt_in, ok_in, mixed_in, gate_ref, channel_ref, us_in, wg_ref, wu_ref, wd_ref,
        vec_ref, mask_ref, tap_ref, border_ref, gain_ref, out_ref, mlp_gain_ref,
        x_in, gated_in, cot_in, mix_in, normed_in,
        d_projected_out, y_out, d_hidden_out, d_normed_out,
        gain_out, d_vec_out, tap_out, mlp_gain_out, gu_out, down_out, out_out, mix_out,
        d_mixed_ref, local_ref, all_ref, relay_send, relay_recv, edge_send, edge_recv, tail_ref,
        ext_ref, pre_ref, q_ref, k_ref, inv_ref, d_ref, z_ref,
        cot_ref, left_ref, act_t_ref, right_ref, d_mixer_ref,
        relay_sems, edge_send_sem, edge_recv_sem, store_sem, load_sem, out_sem, mix_sem, *engine_refs,
    ):
        step = pl.program_id(0)
        z, x, core, y = place()
        y_peer = device_at(z, x, core, 1 - y)
        lanes = [Reduce(engine_refs, lane, count) for lane in range(2)]
        first_device = jnp.where(y == 0, 1.0, 0.0)
        halves_of_width = width // 2 // WIDE

        def wide(first):
            return pl.ds(pl.multiple_of(first, WIDE), WIDE)

        def down_item(lane, index):
            within = index - down_first
            return lane * halves_of_width + within // 3, lax.rem(within, 3)

        def mix_item(lane, index):
            within = 2 * (index - head_first) + lane
            is_gate = index < head_first
            part = jnp.where(is_gate, parts, lax.rem(within, parts))
            column = jnp.where(is_gate, 2 * (index - gate_first) + lane, within // parts) * WIDE
            return part, column

        def begin(index):
            slot = lax.rem(index, 2)
            is_down = (index >= down_first) & (index < out_first)

            def product(left):
                made = mm(left.reshape(-1, length), right_ref[...]).astype(jnp.bfloat16)
                lanes[0].both[slot] = made.reshape(STACK + (rows, 2 * WIDE))

            def pair(column):
                return pl.ds(pl.multiple_of(column * 2 * WIDE, 2 * WIDE), 2 * WIDE)

            @pl.when(is_down)
            def _():
                for lane in range(2):
                    right_ref[:, lane * WIDE : (lane + 1) * WIDE] = cot_ref[:, wide(down_item(lane, index)[0] * WIDE)]
                here = pl.ds(pl.multiple_of(down_item(0, index)[1] * rows, rows), rows)
                product(act_t_ref[:, :, :, :, here, :])

            @pl.when((index >= out_first) & (index < gate_first))
            def _():
                right_ref[...] = d_mixer_ref[:, pair(index - out_first)]

            @pl.when((index >= gate_first) & (index < head_first))
            def _():
                right_ref[...] = all_ref[parts, :, pair(index - gate_first)]

            @pl.when(index >= head_first)
            def _():
                for lane in range(2):
                    part, column = mix_item(lane, index)
                    right_ref[:, lane * WIDE : (lane + 1) * WIDE] = all_ref[part, :, wide(column)]

            @pl.when(jnp.logical_not(is_down))
            def _():
                product(left_ref[jnp.where(index < down_first, 0, jnp.where(index < gate_first, 1, 2))])

            for engine in lanes:
                engine.core_copy(index).start()

        def end(lane, index):
            total = lanes[lane].from_ring(index)

            @pl.when(index < down_first)
            def _():
                gu_out[:, wide(lane * hidden + index * WIDE)] = total

            @pl.when((index >= down_first) & (index < out_first))
            def _():
                column, block = down_item(lane, index)
                down_out[block, :, wide(column * WIDE)] = total

            @pl.when((index >= out_first) & (index < gate_first))
            def _():
                out_out[:, wide((2 * (index - out_first) + lane) * WIDE)] = total

            @pl.when(index >= gate_first)
            def _():
                part, column = mix_item(lane, index)
                mix_out[:, wide(part * (H * DK) + column)] = total

        def tick(number):
            for stage in reversed(range(REDUCE_STAGES)):
                index = number - stage * SPAN_TICKS

                @pl.when((index >= 0) & (index < count))
                def _():
                    if stage == 0:
                        begin(index)
                    for lane, engine in enumerate(lanes):
                        if stage == 1:
                            engine.from_core(index)
                        elif stage == 2:
                            engine.from_near(index)
                        elif stage == 3:
                            engine.from_far(index)
                        elif stage == 4:
                            end(lane, index)

        def transposed(values):
            flipped = jnp.transpose(values.astype(jnp.float32)).astype(jnp.bfloat16)
            return flipped.reshape(STACK + (rows, length))

        def head_slices():
            return [slice(head * DV, (head + 1) * DV) for head in range(H)]

        def joined(ref, first):
            quarter = length // SPAN
            return jnp.concatenate(
                [ref[head, first * quarter : (first + 1) * quarter].reshape(length, DV) for head in range(H)], axis=1
            )

        def split(ref, first, values):
            quarter = length // SPAN
            for head, here in enumerate(head_slices()):
                ref[head, first * quarter : (first + 1) * quarter] = values[:, here].reshape(quarter, SPAN, DV)

        def enter_mlp():
            loads = [
                pltpu.make_async_copy(source, target, load_sem.at[index])
                for index, (source, target) in enumerate(
                    ((gated_in, all_ref.at[1]), (x_in, all_ref.at[0]), (cot_in, cot_ref), (normed_in, left_ref.at[2]))
                )
            ]
            for load in loads:
                load.start()
            for load in loads:
                load.wait()
            split(local_ref, 1, mm(all_ref[1], out_ref[...]))
            quarter = length // SPAN

            def one(index, carry):
                here = pl.ds(pl.multiple_of(index * SPAN, SPAN), SPAN)
                mixed_rows = jnp.concatenate([local_ref[head, quarter + index] for head in range(H)], axis=1)
                hidden_rows = all_ref[0, here].astype(jnp.float32) + mixed_rows
                inv = lax.rsqrt(jnp.mean(hidden_rows * hidden_rows, axis=1, keepdims=True) + EPSILON)
                all_ref[3, here] = (hidden_rows * inv * mlp_gain_ref[0:1, :]).astype(jnp.bfloat16)
                for head, columns in enumerate(head_slices()):
                    local_ref[head, index] = hidden_rows[:, columns]
                    local_ref[head, quarter + index] = hidden_rows[:, columns]
                return carry

            lax.fori_loop(0, quarter, one, 0)
            d_mixed_ref[...] = jnp.zeros_like(d_mixed_ref)
            left_ref[0] = transposed(all_ref[3])

        def mlp_block(block):
            mlp_in = all_ref[3]
            gate = mm(mlp_in, wg_ref[...])
            up = mm(mlp_in, wu_ref[...])
            open_, sig = silu_pair(gate)
            act = (open_ * up).astype(jnp.bfloat16)
            d_act = mm(cot_ref[...], wd_ref[...], 1, 1)
            d_gate = (d_act * up * sig * (1.0 + gate * (1.0 - sig))).astype(jnp.bfloat16)
            d_up = (d_act * open_).astype(jnp.bfloat16)
            right_ref[:, :WIDE] = d_gate
            right_ref[:, WIDE:] = d_up
            split(local_ref, 0, joined(local_ref, 0) + mm(act, wd_ref[...]))
            d_in = mm(d_gate, wg_ref[...], 1, 1) + mm(d_up, wu_ref[...], 1, 1)
            for head, here in enumerate(head_slices()):
                d_mixed_ref[head] = d_mixed_ref[head] + d_in[:, here]
            act_t = jnp.transpose(act.astype(jnp.float32))
            for group in range(WIDE // 8):
                place_ = block * (WIDE // 8) + group
                owner, row = place_ // (shard // 8), lax.rem(place_, shard // 8) * 8
                act_t_ref[
                    owner // 8, lax.rem(owner // 4, 2), lax.rem(owner // 2, 2), lax.rem(owner, 2),
                    pl.ds(pl.multiple_of(row, 8), 8), :,
                ] = act_t[group * 8 : (group + 1) * 8]

        y_store = pltpu.make_async_copy(all_ref.at[0], y_out, out_sem.at[0])

        def leave_mlp():
            quarter = length // SPAN

            def tile(ref, first, index):
                return jnp.concatenate([ref[head, first * quarter + index] for head in range(H)], axis=1)

            def one(index, gain_grad):
                here = pl.ds(pl.multiple_of(index * SPAN, SPAN), SPAN)
                all_ref[0, here] = tile(local_ref, 0, index).astype(jnp.bfloat16)
                hidden_rows = tile(local_ref, 1, index)
                d_in = jnp.concatenate([d_mixed_ref[head, here] for head in range(H)], axis=1)
                inv = lax.rsqrt(jnp.mean(hidden_rows * hidden_rows, axis=1, keepdims=True) + EPSILON)
                unit = hidden_rows * inv
                d_unit = d_in * mlp_gain_ref[0:1, :]
                d_norm = inv * (d_unit - unit * jnp.mean(d_unit * unit, axis=1, keepdims=True))
                d_hidden = cot_ref[here].astype(jnp.float32) + d_norm
                for head, columns in enumerate(head_slices()):
                    local_ref[head, quarter + index] = d_hidden[:, columns]
                d_mixer_ref[here] = d_hidden.astype(jnp.bfloat16)
                return gain_grad + jnp.sum(d_in * unit, axis=0, keepdims=True)

            gain_grad = lax.fori_loop(0, quarter, one, jnp.zeros((1, width), jnp.float32))
            mlp_gain_out[...] = jnp.broadcast_to(gain_grad, (8, width))
            y_store.start()
            stores = [
                pltpu.make_async_copy(
                    local_ref.at[head, quarter : 2 * quarter], d_hidden_out.at[:, :, here], out_sem.at[1 + head]
                )
                for head, here in enumerate(head_slices())
            ]
            for store in stores:
                store.start()
            d_normed_rows = mm(d_mixer_ref[...], out_ref[...], 1, 1)
            for head, here in enumerate(head_slices()):
                d_mixed_ref[head] = d_normed_rows[:, here]
            for store in stores:
                store.wait()

        def readout_back(head):
            gain = gain_ref[0:1, :]
            gain_grad = jnp.zeros((1, DV), jnp.float32)
            column = pl.ds(pl.multiple_of(head * DV, DV), DV)
            state = jnp.zeros((DV, DK), jnp.float32)
            for chunk in reversed(range(chunks)):
                here = slice(chunk * GROUP, (chunk + 1) * GROUP)
                mixed = mixed_in[0, here, :]
                inv = lax.rsqrt(jnp.mean(mixed * mixed, axis=1, keepdims=True) + EPSILON)
                unit = mixed * inv
                gate = gate_ref[0, here, :]
                open_, sig = silu_pair(gate)
                d_gated = d_mixed_ref[head, here]
                d_scaled = d_gated * open_
                d_gate = d_gated * unit * gain * sig * (1.0 + gate * (1.0 - sig))
                all_ref[parts, here, column] = d_gate.astype(jnp.bfloat16)
                gain_grad = gain_grad + jnp.sum(d_scaled * unit, axis=0, keepdims=True)
                d_unit = d_scaled * gain
                d_mixed = inv * (d_unit - unit * jnp.mean(d_unit * unit, axis=1, keepdims=True))
                d_mixed_ref[head, here] = d_mixed
                local = mm3(d_mixed, ok_in[0, chunk], 0, 0)
                local_ref[head, chunk] = local
                state = (
                    vec_ref[head, chunk, 3:4, GROUP - 1 : GROUP] * state
                    - mm3(state, xt_in[0, 1, chunk], 1, 1)
                    + local
                )
            gain_out[head] = jnp.broadcast_to(gain_grad, (8, DV))
            relay_send[head] = state.astype(jnp.bfloat16)

        def head_columns(part, head):
            return pl.ds(pl.multiple_of((part * H + head) * DK, DK), DK)

        def prepare(head):
            for part in range(parts):
                here = head_columns(part, head)
                pre = conv_block(channel_ref[part], border_ref[:, here], tap_ref[:, here], mask_ref, ext_ref.at[part])
                yield
                pre_ref[part] = pre
                if part > NH:
                    continue
                value = silu_pair(pre)[0]
                if part == 0:
                    unit, inv = unit_rows(value)
                    q_ref[...] = unit * DK ** (-0.5)
                    inv_ref[:, 0:1] = inv
                else:
                    unit, inv = unit_rows(value)
                    k_ref[part - 1] = unit
                    inv_ref[:, part : part + 1] = inv

        def chain(head, exit_grads):
            grad = first_device * relay_recv[head].astype(jnp.float32)
            for chunk in reversed(range(chunks)):
                exit_grads[chunk] = grad
                grad = (
                    vec_ref[head, chunk, 3:4, GROUP - 1 : GROUP] * grad
                    - mm3(grad, xt_in[0, 1, chunk], 1, 1)
                    + local_ref[head, chunk]
                )
                yield

        def one_chunk(chunk, head, d_exit):
            strict = order_masks()[0]
            column_index = iotas(SPAN, 8)[1]
            here = slice(chunk * GROUP, (chunk + 1) * GROUP)
            rows_ = vec_ref[head, chunk]
            columns = jnp.transpose(rows_)
            beta, scale, tail = columns[:, 1:2], columns[:, 3:4], columns[:, 4:5]
            keys = k_ref[:, here, :].reshape(SPAN, DK)
            values = silu_pair(pre_ref[1 + NH :, here, :].reshape(SPAN, DV))[0]
            queries = q_ref[here, :]
            link = link_matrix(rows_, columns)
            link_gram = jnp.where(strict, twice(link) * mm3(keys, keys, 1, 1), 0.0)
            reading = link * mm3(queries, keys, 1, 1)
            yield
            solved = us_in[0, 0, chunk]
            entry = us_in[0, 1, chunk]
            d_mixed = d_mixed_ref[head, here]
            tail_keys = tail * keys
            d_solved = mm3(reading, d_mixed, 0, 0) + mm3(tail_keys, d_exit, 1, 1)
            yield
            d_right = mm3(xt_in[0, 0, chunk], d_solved, 0, 0)
            yield
            d_lower = jnp.where(strict, -mm3(d_right, solved, 1, 1), 0.0)
            yield
            d_tail_keys = mm3(solved, d_exit)
            d_right_entry = mm3(d_right, entry)
            d_reading = mm3(d_mixed, solved, 1, 1)
            d_query_entry = mm3(d_mixed, entry)
            yield
            both_scale = -jnp.sum(d_right_entry * keys, axis=1, keepdims=True)
            lower_weight = d_lower * link_gram
            d_beta = (
                jnp.sum(d_right * values, axis=1, keepdims=True)
                + scale * both_scale
                + jnp.sum(lower_weight, axis=1, keepdims=True)
            )
            lower_moment = lower_weight * beta
            reading_moment = d_reading * reading
            d_gram = beta * twice(link) * d_lower
            d_gram = d_gram + jnp.transpose(d_gram)
            yield
            d_query_gram = link * d_reading
            d_keys = (
                tail * d_tail_keys
                - beta * scale * d_right_entry
                + mm(d_gram, keys)
                + mm(d_query_gram, queries, 0, 0)
            )
            d_queries = mm(d_query_gram, keys) + scale[:GROUP] * d_query_entry
            d_values = beta * d_right
            yield
            none = jnp.zeros((GROUP, 1), jnp.float32)
            d_gap = jnp.sum(lower_moment, axis=1, keepdims=True) + jnp.concatenate(
                [jnp.sum(reading_moment, axis=1, keepdims=True), none], axis=0
            )
            last = jnp.sum(jnp.sum(d_exit * entry, axis=1, keepdims=True), axis=0, keepdims=True)
            own_scale = jnp.sum(d_query_entry * queries, axis=1, keepdims=True)
            own_scale = own_scale + jnp.where(iotas(GROUP, 1)[0] == GROUP - 1, last, 0.0)
            d_scale = beta * both_scale + jnp.concatenate([own_scale, none], axis=0)
            d_tail = jnp.sum(d_tail_keys * keys, axis=1, keepdims=True)
            grads = jnp.where(
                column_index == 0,
                d_gap,
                jnp.where(
                    column_index == 1,
                    d_beta,
                    jnp.where(column_index == 3, d_scale, jnp.where(column_index == 4, d_tail, 0.0)),
                ),
            )
            grads = jnp.transpose(grads)
            sums = jnp.sum(lower_moment, axis=0, keepdims=True) + jnp.sum(reading_moment, axis=0, keepdims=True)
            d_vec_out[head, chunk] = grads - jnp.where(iotas(8, SPAN)[0] == 0, sums, 0.0)
            d_ref[0, here, :] = d_queries
            for house in range(NH):
                mine = slice(house * GROUP, (house + 1) * GROUP)
                d_ref[1 + house, here, :] = d_keys[mine]
                d_ref[1 + NH + house, here, :] = d_values[mine]

        def finish_head(head):
            column = pl.ds(pl.multiple_of(head * DK, DK), DK)
            z_ref[0:8, :] = jnp.zeros((8, DK), jnp.float32)
            z_ref[8 + length : 16 + length, :] = jnp.zeros((8, DK), jnp.float32)
            for part in range(parts):
                grad = d_ref[part]
                if part <= NH:
                    unit = q_ref[...] * DK ** 0.5 if part == 0 else k_ref[part - 1]
                    if part == 0:
                        grad = grad * DK ** (-0.5)
                    grad = inv_ref[:, part : part + 1] * (grad - unit * jnp.sum(grad * unit, axis=1, keepdims=True))
                pre = pre_ref[part]
                sig = jax.nn.sigmoid(pre)
                grad = grad * sig * (1.0 + pre * (1.0 - sig))
                here = head_columns(part, head)
                tap = tap_ref[:, here]
                total = grad * tap[0:1, :]
                edge = jnp.zeros((8, DK), jnp.float32)
                tap_rows = [jnp.sum(grad * channel_ref[part], axis=0, keepdims=True)]
                for index in range(1, 4):
                    shifted = grad * mask_ref[index - 1].astype(jnp.float32)
                    tap_rows.append(
                        jnp.sum(shifted * ext_ref[part, 8 - index : 8 - index + length, :], axis=0, keepdims=True)
                    )
                    z_ref[8 : 8 + length, :] = shifted * tap[index : index + 1, :]
                    total = total + z_ref[8 + index : 8 + index + length, :]
                    edge = edge + z_ref[index : index + 8, :]
                all_ref[part, :, column] = total.astype(jnp.bfloat16)
                edge_send[lax.rem(head, 2), part] = edge
                tail_ref[part] = total[length - 16 :, :]
                tap_out[:, here] = jnp.concatenate(tap_rows + [jnp.zeros((4, DK), jnp.float32)], axis=0)

        @pl.when(step == 0)
        def _():
            meet(peers())
            enter_mlp()

        @pl.when((step >= 1) & (step <= blocks))
        def _():
            mlp_block(step - 1)

            @pl.when(step == 2)
            def _():
                left_ref[1] = transposed(all_ref[1])
                act_t_ref[:, :, :, :, shard:, :] = jnp.zeros(STACK + (act_t_ref.shape[4] - shard, length), jnp.float32)

        @pl.when(step == blocks + 1)
        def _():
            leave_mlp()

        early_head = step - early

        @pl.when((step >= early) & (step < late))
        def _():
            readout_back(early_head)

        relay = pltpu.make_async_remote_copy(
            src_ref=relay_send, dst_ref=relay_recv, send_sem=relay_sems.at[0], recv_sem=relay_sems.at[1],
            device_id=y_peer, device_id_type=MESH,
        )

        @pl.when(step == late - 1)
        def _():
            relay.start()

        @pl.when(step == late)
        def _():
            relay.wait()
            y_store.wait()

        def edge_copy(head):
            slot = lax.rem(head, 2)
            return pltpu.make_async_remote_copy(
                src_ref=edge_send.at[slot], dst_ref=edge_recv.at[slot], send_sem=edge_send_sem.at[slot],
                recv_sem=edge_recv_sem.at[slot], device_id=y_peer, device_id_type=MESH,
            )

        def fix_edges(head):
            edge_copy(head).wait()
            here = pl.ds(pl.multiple_of(head * DK, DK), DK)
            for part in range(parts):
                fixed = tail_ref[part, 8:16] + first_device * edge_recv[lax.rem(head, 2), part]
                both = jnp.concatenate([tail_ref[part, 0:8], fixed], axis=0)
                all_ref[part, length - 16 : length, here] = both.astype(jnp.bfloat16)

        @pl.when((step >= late) & (step < last))
        def _():
            head = step - late
            exit_grads = [None] * chunks
            together([chain(head, exit_grads), prepare(head)])

            @pl.when(head > 0)
            def _():
                fix_edges(head - 1)

            tick(late_tick + jnp.minimum(2 * head, head + 5))
            together([one_chunk(chunk, head, exit_grads[chunk]) for chunk in reversed(range(chunks))])

            finish_head(head)
            edge_copy(head).start()

        late_head = step - late
        in_mlp = (step >= 1) & (step <= blocks)
        in_early = (step >= early) & (step < late) & (lax.rem(early_head, 2) == 0)
        in_late = (late_head >= 0) & (late_head < 5)
        number = jnp.where(
            in_mlp, step - 1, jnp.where(in_early, early_tick + early_head // 2, late_tick + 2 * late_head + 1)
        )

        @pl.when(in_mlp | in_early | in_late)
        def _():
            tick(number)

        @pl.when(step == last)
        def _():
            fix_edges(H - 1)
            stores = [
                pltpu.make_async_copy(
                    all_ref.at[part], d_projected_out.at[:, pl.ds(part * H * DK, H * DK)], store_sem.at[part]
                )
                for part in range(parts + 1)
            ]
            for store in stores:
                store.start()
            loads = mix_in.shape[5] // length

            def load(index):
                here = pl.ds(pl.multiple_of(index * length, length), length)
                slot = lax.rem(index, 2)
                return pltpu.make_async_copy(mix_in.at[:, :, :, :, :, here], left_ref.at[slot], mix_sem.at[slot])

            load(0).start()
            load(1).start()
            d_mixed_ref[...] = jnp.zeros_like(d_mixed_ref)
            per_part = H * DK // length

            d_normed_stores = [
                pltpu.make_async_copy(d_mixed_ref.at[head], d_normed_out.at[:, here], out_sem.at[head])
                for head, here in enumerate(head_slices())
            ]

            def drain(turn, carry):
                tick(late_tick + H + 5 + turn)

                @pl.when(turn < loads // 2)
                def _():
                    for slot in range(2):
                        index = 2 * turn + slot
                        load(index).wait()
                        here = pl.ds(pl.multiple_of(lax.rem(index, per_part) * length, length), length)
                        left = all_ref[index // per_part, :, here]
                        added = mm(left, left_ref[slot].reshape(-1, length), 1, 1)
                        for head, place_ in enumerate(head_slices()):
                            d_mixed_ref[head] = d_mixed_ref[head] + added[:, place_]

                        @pl.when(index + 2 < loads)
                        def _():
                            load(index + 2).start()

                @pl.when(turn == loads // 2)
                def _():
                    for store in d_normed_stores:
                        store.start()

                return carry

            turns = ticks - (late_tick + H + 5)
            assert turns > loads // 2
            lax.fori_loop(0, turns, drain, 0)
            stores.extend(d_normed_stores)
            for store in stores:
                store.wait()

    return kernel, ticks


def back_call(
    xt, out_keys, mixed, gate, channels, us, gu, down, vec, masks, taps, border, gain, out, mlp_gain,
    x, gated, cot, mix, normed_t,
):
    parts, heads, length, width = channels.shape
    chunks = length // GROUP
    model, hidden = gu.shape[0], down.shape[0]
    rows, blocks = 32, hidden // WIDE
    padded = -(-(hidden // 32) // rows) * rows
    kernel, ticks = make_back_kernel(length, model, hidden)
    first = blocks + 2

    def either(step):
        return lax.rem(jnp.maximum(step - first, 0), H)

    def early(step):
        return jnp.clip(step - first, 0, H - 1)

    def late(step):
        return jnp.clip(step - first - H, 0, H - 1)

    def block(step):
        return jnp.clip(step - 1, 0, blocks - 1)

    def heads_spec(shape, which):
        rank = len(shape)
        return pl.BlockSpec((1,) + shape, lambda step: (which(step),) + (0,) * rank)

    square = (chunks, SPAN, DK)
    anywhere = pl.BlockSpec(memory_space=pl.ANY)
    in_specs = (
        [
            heads_spec((2,) + square, either), heads_spec((chunks, GROUP, DK), early), heads_spec((length, DV), early),
            heads_spec((length, DV), early),
            pl.BlockSpec((parts, None, length, DK), lambda step: (0, late(step), 0, 0)), heads_spec((2,) + square, late),
            pl.BlockSpec((model, WIDE), lambda step: (0, block(step))),
            pl.BlockSpec((model, WIDE), lambda step: (0, blocks + block(step))),
            pl.BlockSpec((WIDE, model), lambda step: (block(step), 0)),
        ]
        + held_specs(7)
        + [anywhere] * 5
    )
    out_shape = [
        jax.ShapeDtypeStruct((length, (parts + 1) * H * DK), jnp.bfloat16),
        jax.ShapeDtypeStruct((length, model), jnp.bfloat16),
        jax.ShapeDtypeStruct((length // SPAN, SPAN, model), jnp.float32),
        jax.ShapeDtypeStruct((length, model), jnp.float32),
        per_head((8, DV)),
        per_head((chunks, 8, SPAN)),
        jax.ShapeDtypeStruct((8, parts * H * DK), jnp.float32),
        jax.ShapeDtypeStruct((8, model), jnp.float32),
        jax.ShapeDtypeStruct((rows, gu.shape[1]), jnp.float32),
        jax.ShapeDtypeStruct((padded // rows, rows, model), jnp.float32),
        jax.ShapeDtypeStruct((rows, model), jnp.float32),
        jax.ShapeDtypeStruct((rows, (parts + 1) * H * DK), jnp.float32),
    ]
    tall = pltpu.VMEM((parts, length, DK), jnp.float32)
    scratch = [
        pltpu.VMEM((H, length, DV), jnp.float32),
        pltpu.VMEM((H,) + square, jnp.float32),
        pltpu.VMEM((parts + 1, length, H * DK), jnp.bfloat16),
        pltpu.VMEM((H, DV, DK), jnp.bfloat16),
        pltpu.VMEM((H, DV, DK), jnp.bfloat16),
        pltpu.VMEM((2, parts, 8, DK), jnp.float32),
        pltpu.VMEM((2, parts, 8, DK), jnp.float32),
        pltpu.VMEM((parts, 16, DK), jnp.float32),
        pltpu.VMEM((parts, length + 8, DK), jnp.float32),
        tall,
        pltpu.VMEM((length, DK), jnp.float32),
        pltpu.VMEM((NH, length, DK), jnp.float32),
        pltpu.VMEM((length, DK), jnp.float32),
        tall,
        pltpu.VMEM((length + 16, DK), jnp.float32),
        pltpu.VMEM((length, model), jnp.bfloat16),
        pltpu.VMEM((3,) + STACK + (rows, length), jnp.bfloat16),
        pltpu.VMEM(STACK + (padded, length), jnp.float32),
        pltpu.VMEM((length, 2 * WIDE), jnp.bfloat16),
        pltpu.VMEM((length, model), jnp.bfloat16),
        pltpu.SemaphoreType.DMA((2,)),
        pltpu.SemaphoreType.DMA((2,)),
        pltpu.SemaphoreType.DMA((2,)),
        pltpu.SemaphoreType.DMA((parts + 1,)),
        pltpu.SemaphoreType.DMA((4,)),
        pltpu.SemaphoreType.DMA((1 + H,)),
        pltpu.SemaphoreType.DMA((2,)),
    ] + reduce_scratch(rows)
    return pl.pallas_call(
        kernel,
        grid=(first + 2 * H + 1,),
        out_shape=out_shape,
        in_specs=in_specs,
        out_specs=[anywhere] * 4 + held_specs(len(out_shape) - 4),
        scratch_shapes=scratch,
        compiler_params=pltpu.CompilerParams(
            dimension_semantics=("arbitrary",), collective_id=2, has_side_effects=True, vmem_limit_bytes=255 * 256 * 1024
        ),
        cost_estimate=pl.CostEstimate(
            flops=H * chunks * 14 * 2 * SPAN**3 * 4, bytes_accessed=100_000_000, transcendentals=0
        ),
    )(
        xt, out_keys, mixed, gate, channels, us, gu, gu, down, vec, masks, taps, border, gain, out, mlp_gain,
        x, gated, cot, mix, normed_t,
    )


def total_kernel(
    packed_ref, sums_ref, packed_out, sums_out, first, near, far, last, kept, low, pair, ring, send, recv
):
    z, x, core, y = place()
    targets = peers()
    meet(targets)

    def copy(source, target, slot, device):
        made = pltpu.make_async_remote_copy(
            src_ref=source, dst_ref=target, send_sem=send.at[slot], recv_sem=recv.at[slot],
            device_id=device, device_id_type=MESH,
        )
        made.start()
        return made

    def swap(source, target, index, device):
        pair[2 * index] = sums_out[...]
        copies = [
            copy(source, target, 2 * index, device),
            copy(pair.at[2 * index], pair.at[2 * index + 1], 2 * index + 1, device),
        ]
        for made in copies:
            made.wait()
        sums_out[...] = sums_out[...] + pair[2 * index + 1]

    sums_out[...] = sums_ref[...]
    low[...] = packed_ref[:, :, 1 - core].astype(jnp.bfloat16)
    swap(low, first, 0, targets[ZS + 1])
    kept[...] = packed_ref[:, :, core] + first[...].astype(jnp.float32)
    low[:, 0] = kept[:, 1 - x].astype(jnp.bfloat16)
    swap(low.at[:, 0], near, 1, targets[ZS - 1])
    kept[:, 0] = kept[:, x] + near[...].astype(jnp.float32)
    low[:, 0, 0] = kept[:, 0, 1 - y].astype(jnp.bfloat16)
    swap(low.at[:, 0, 0], far, 2, targets[ZS])
    kept[:, 0, 0] = kept[:, 0, y] + far[...].astype(jnp.float32)
    low[:, 0, 0] = kept[:, 0, 0].astype(jnp.bfloat16)
    ring[z] = sums_out[...]
    copies = []
    for step in range(ZS - 1):
        other = lax.rem(z + 1 + step, ZS)
        copies.append(copy(low.at[other, 0, 0], last.at[step], 6 + 2 * step, targets[step]))
        copies.append(copy(ring.at[z], ring.at[z], 7 + 2 * step, targets[step]))
    for made in copies:
        made.wait()
    packed_out[...] = kept[z, 0, 0] + sum(last[step].astype(jnp.float32) for step in range(ZS - 1))
    sums_out[...] = ring[0] + ring[1] + ring[2] + ring[3]


def total_call(packed, sums):
    rows, wide = packed.shape[4], packed.shape[5]
    held = pl.BlockSpec(memory_space=pltpu.VMEM)
    return pl.pallas_call(
        total_kernel,
        out_shape=[jax.ShapeDtypeStruct((rows, wide), jnp.float32), jax.ShapeDtypeStruct(sums.shape, jnp.float32)],
        in_specs=[held, held],
        out_specs=[held, held],
        scratch_shapes=[
            pltpu.VMEM((ZS, 2, 2, rows, wide), jnp.bfloat16),
            pltpu.VMEM((ZS, 2, rows, wide), jnp.bfloat16),
            pltpu.VMEM((ZS, rows, wide), jnp.bfloat16),
            pltpu.VMEM((ZS - 1, rows, wide), jnp.bfloat16),
            pltpu.VMEM((ZS, 2, 2, rows, wide), jnp.float32),
            pltpu.VMEM((ZS, 2, 2, rows, wide), jnp.bfloat16),
            pltpu.VMEM((6,) + sums.shape, jnp.float32),
            pltpu.VMEM((ZS,) + sums.shape, jnp.float32),
            pltpu.SemaphoreType.DMA((12,)),
            pltpu.SemaphoreType.DMA((12,)),
        ],
        compiler_params=pltpu.CompilerParams(collective_id=3, has_side_effects=True, vmem_limit_bytes=LIMIT),
        cost_estimate=pl.CostEstimate(flops=1000000, bytes_accessed=2_000_000, transcendentals=0),
    )(packed, sums)


def from_behind(block, axis, distance):
    devices = range(lax.axis_size(axis))
    route = [(i - distance, i) for i in devices if i - distance in devices]
    return lax.ppermute(block, axis, route)


def rms_scale(values, scale_gain):
    return (
        values * lax.rsqrt(jnp.mean(values * values, axis=-1, keepdims=True) + EPSILON) * scale_gain
    )


def swiglu(gate_up):
    half_width = gate_up.shape[-1] // 2
    return jax.nn.silu(gate_up[:, :half_width]) * gate_up[:, half_width:]


def exchange(block, axis, bit):
    route = [(i, i ^ (1 << bit)) for i in range(lax.axis_size(axis))]
    return lax.ppermute(block, axis, route)


def axis_bits(axis):
    return lax.axis_size(axis).bit_length() - 1


def bit_orders():
    dp_bits = [("dp", bit) for bit in range(axis_bits("dp"))]
    seq_bits = [("seq", bit) for bit in range(axis_bits("seq"))]
    first, rest = dp_bits[:1], dp_bits[1:]
    inner = rest[:1] + seq_bits[:1]
    outer = rest[1:] + seq_bits[1:]
    return first + inner + outer, first + inner[::-1] + outer


def scatter_sum(part, order):
    dp_bits, seq_bits = axis_bits("dp"), axis_bits("seq")
    dims = [("dp", bit) for bit in reversed(range(dp_bits))] + [("seq", bit) for bit in reversed(range(seq_bits))]
    rows = part.shape[0] >> len(dims)
    part = part.reshape((2,) * len(dims) + (rows, part.shape[1]))
    for axis, bit in order:
        place = dims.index((axis, bit))
        dims.pop(place)
        mine = (lax.axis_index(axis) >> bit) & 1
        sent = lax.dynamic_index_in_dim(part, 1 - mine, place, keepdims=False)
        kept = lax.dynamic_index_in_dim(part, mine, place, keepdims=False)
        got = exchange(sent.astype(jnp.bfloat16), axis, bit)
        part = kept.astype(jnp.float32) + got.astype(jnp.float32)
    return part


def scatter_halves(part):
    half = part.shape[1] // 2
    orders = bit_orders()
    return jnp.concatenate(
        [scatter_sum(part[:, :half], orders[0]), scatter_sum(part[:, half:], orders[1])], axis=1
    )


def total_sum(block):
    for axis in ("dp", "seq"):
        for bit in range(axis_bits(axis)):
            block = block + exchange(block, axis, bit)
    return block


def gate_vectors(seg_now, seg_prev, gates_raw, decay_log):
    length = gates_raw.shape[0]
    chunks = length // GROUP
    beta = jax.nn.sigmoid(gates_raw[:, : NH * H]).reshape(chunks, GROUP, NH, H)
    rate = -jnp.exp(decay_log) * jax.nn.softplus(gates_raw[:, NH * H :])
    lower = jnp.tril(jnp.ones((GROUP, GROUP), jnp.float32))
    total = jnp.einsum("ts,csh->cth", lower, rate.reshape(chunks, GROUP, H), precision=HIGHEST)
    seg = seg_now.reshape(chunks, GROUP)
    before = jnp.concatenate([seg_prev.reshape(1), seg[:-1, -1]])
    scale = jnp.exp(total) * (seg == before[:, None]).astype(jnp.float32)[:, :, None]
    tail = jnp.exp(total[:, -1:, :] - total) * (seg == seg[:, -1:]).astype(jnp.float32)[:, :, None]

    def both(values):
        moved = jnp.moveaxis(values, 2, 0)
        return jnp.concatenate([moved, moved], axis=-1)

    beta_rows = beta.transpose(3, 0, 2, 1).reshape(H, chunks, SPAN)
    seg_rows = jnp.broadcast_to(jnp.concatenate([seg, seg], axis=1).astype(jnp.float32), (H, chunks, SPAN))
    none = jnp.zeros((H, chunks, SPAN), jnp.float32)
    return jnp.stack([both(total), beta_rows, seg_rows, both(scale), both(tail), none, none, none], axis=2)


def head_spec(shape):
    rank = len(shape)
    return pl.BlockSpec((1,) + shape, lambda head: (head,) + (0,) * rank)


def column_spec(rows, first):
    return pl.BlockSpec((rows, DK), lambda head: (0, first + head))


def whole_spec(shape):
    rank = len(shape)
    return pl.BlockSpec(shape, lambda head: (0,) * rank)


def per_head(shape, dtype=jnp.float32):
    return jax.ShapeDtypeStruct((H,) + shape, dtype)


def call(kernel, out_shape, in_specs, out_specs, scratch, flops, bytes_accessed):
    return pl.pallas_call(
        kernel,
        grid=(H,),
        out_shape=out_shape,
        in_specs=in_specs,
        out_specs=out_specs,
        scratch_shapes=scratch,
        compiler_params=pltpu.CompilerParams(
            dimension_semantics=("arbitrary",), vmem_limit_bytes=LIMIT
        ),
        cost_estimate=pl.CostEstimate(flops=flops, bytes_accessed=bytes_accessed, transcendentals=0),
    )


def conv_specs(length):
    return (
        [column_spec(length, H * part) for part in range(1 + 2 * NH)]
        + [column_spec(8, H * part) for part in range(1 + 2 * NH)] * 2
        + [whole_spec((3, length, DK))]
    )


def forward_call(projected, border, taps, masks, vec, start):
    length = projected.shape[0]
    chunks = length // GROUP
    square = (chunks, SPAN, DK)
    outs = [
        (square, jnp.float32),
        (square, jnp.float32),
        (square, jnp.float32),
        (square, jnp.float32),
        (square, jnp.float32),
        ((chunks, GROUP, DK), jnp.float32),
        ((chunks, GROUP, DV), jnp.float32),
        ((DV, DK), jnp.float32),
    ]
    parts = 1 + 2 * NH
    return call(
        forward_kernel,
        [per_head(*out) for out in outs],
        conv_specs(length) + [head_spec((chunks, 8, SPAN)), head_spec((DV, DK))],
        [head_spec(out[0]) for out in outs],
        [
            pltpu.VMEM((length + 8, DK), jnp.float32),
            pltpu.VMEM((length, DK), jnp.float32),
            pltpu.VMEM((NH, length, DK), jnp.float32),
            pltpu.VMEM((NH, length, DK), jnp.float32),
        ],
        H * chunks * 20 * 2 * SPAN**3 * 4,
        H * chunks * 8 * SPAN * DK * 4,
    )(*[projected] * parts, *[border] * parts, *[taps] * parts, masks, vec, start)


def chain_call(vec, transfer, start):
    chunks = transfer.shape[1]
    return call(
        chain_kernel,
        per_head((DV, DK)),
        [head_spec((chunks, 8, SPAN)), head_spec((chunks, SPAN, DK)), head_spec((DV, DK))],
        head_spec((DV, DK)),
        [],
        H * chunks * 2 * SPAN**3,
        H * chunks * SPAN * DK * 4,
    )(vec, transfer, start)


def readout_call(vec, key_part, value_part, transfer, inject, out_keys, out_values, entry, projected, gain):
    length = projected.shape[0]
    chunks = length // GROUP
    square = head_spec((chunks, SPAN, DK))
    half = head_spec((chunks, GROUP, DK))
    return call(
        readout_kernel,
        [
            jax.ShapeDtypeStruct((length, H * DV), jnp.bfloat16),
            jax.ShapeDtypeStruct((length, H * DV), jnp.float32),
            per_head((chunks, SPAN, DK)),
            per_head((chunks, SPAN, DK)),
        ],
        [
            head_spec((chunks, 8, SPAN)), square, square, square, square, half, half,
            head_spec((DV, DK)), column_spec(length, (1 + 2 * NH) * H), whole_spec((8, DV)),
        ],
        [column_spec(length, 0), column_spec(length, 0), square, square],
        [],
        H * chunks * 4 * 2 * SPAN**3 * 4,
        H * chunks * 8 * SPAN * DK * 4,
    )(vec, key_part, value_part, transfer, inject, out_keys, out_values, entry, projected, gain)


def readout_back_call(vec, transfer, out_keys, mixed, projected, gain, d_gated, start):
    length = projected.shape[0]
    chunks = length // GROUP
    square = head_spec((chunks, SPAN, DK))
    return call(
        readout_back_kernel,
        [
            jax.ShapeDtypeStruct((length, H * DV), jnp.float32),
            jax.ShapeDtypeStruct((length, H * DV), jnp.bfloat16),
            per_head((chunks, SPAN, DK)),
            per_head((DV, DK)),
            per_head((8, DV)),
        ],
        [
            head_spec((chunks, 8, SPAN)), square, head_spec((chunks, GROUP, DK)),
            column_spec(length, 0), column_spec(length, (1 + 2 * NH) * H), whole_spec((8, DV)),
            column_spec(length, 0), head_spec((DV, DK)),
        ],
        [column_spec(length, 0), column_spec(length, 0), square, head_spec((DV, DK)), head_spec((8, DV))],
        [],
        H * chunks * 4 * 2 * SPAN**3 * 4,
        H * chunks * 8 * SPAN * DK * 4,
    )(vec, transfer, out_keys, mixed, projected, gain, d_gated, start)


def backward_call(projected, border, taps, masks, vec, transfer, inverse, solved, entries, d_mixed, local, exit_grad):
    length = projected.shape[0]
    chunks = length // GROUP
    parts = 1 + 2 * NH
    square = head_spec((chunks, SPAN, DK))
    outs = (
        [jax.ShapeDtypeStruct((length, H * DK), jnp.bfloat16)] * parts
        + [jax.ShapeDtypeStruct((16, H * DK), jnp.float32)] * parts
        + [jax.ShapeDtypeStruct((8, H * DK), jnp.float32)] * parts
        + [per_head((chunks, 8, SPAN))]
    )
    out_specs = (
        [column_spec(length, 0)] * parts
        + [column_spec(16, 0)] * parts
        + [column_spec(8, 0)] * parts
        + [head_spec((chunks, 8, SPAN))]
    )
    tall = pltpu.VMEM((parts, length, DK), jnp.float32)
    return call(
        backward_kernel,
        outs,
        conv_specs(length)
        + [head_spec((chunks, 8, SPAN)), square, square, square, square, column_spec(length, 0), square, head_spec((DV, DK))],
        out_specs,
        [
            pltpu.VMEM((parts, length + 8, DK), jnp.float32),
            tall,
            pltpu.VMEM((length, DK), jnp.float32),
            pltpu.VMEM((NH, length, DK), jnp.float32),
            pltpu.VMEM((NH, length, DK), jnp.float32),
            pltpu.VMEM((1 + NH, length, DK), jnp.float32),
            tall,
            pltpu.VMEM((length + 16, DK), jnp.float32),
        ],
        H * chunks * 14 * 2 * SPAN**3 * 4,
        H * chunks * 16 * SPAN * DK * 4,
    )(*[projected] * parts, *[border] * parts, *[taps] * parts, masks, vec, transfer, inverse, solved, entries, d_mixed, local, exit_grad)


def gather(block, dim=0):
    return lax.all_gather(block, ("dp", "seq"), axis=dim, tiled=True)


def on_device(
    block_input, doc_starts, norm_in, w_mix, w_small, conv_w, decay_log, norm_out,
    w_out, norm_mlp, w_gu, w_down, cotangent,
):
    row_count, seg_len, width = block_input.shape
    tap_count = conv_w.shape[0]
    key_width = H * DK
    parts = 1 + 2 * NH
    seqs = lax.axis_size("seq")
    residual_in = block_input.astype(jnp.float32).reshape(seg_len, width)
    smalls, rows = w_small.shape[1], w_mix.shape[0]
    fast = lax.axis_size("dp") == 4 * ZS and seqs == 2 and rows % 16 == 0
    if fast:
        small = jnp.concatenate(
            [w_small, norm_in[:, None], norm_mlp[:, None], conv_w.reshape(tap_count, rows, -1).transpose(1, 2, 0).reshape(rows, -1)], axis=1
        )
        small = jnp.concatenate([small, jnp.zeros((rows, DK - small.shape[1]), small.dtype)], axis=1)
        mix_all, out_all, down_own, small_pack, normed_low, normed_t, channels, gate, gates_raw, border, gains = gather_project_call(
            block_input.reshape(seg_len, width), small, w_mix, w_out, w_down
        )
        small_all = small_pack[:, :smalls]
        gates_raw = gates_raw[:, :smalls]
        norm_in_all, norm_mlp_all = gains[0], gains[1]
        per_row = conv_w.shape[1] // rows
        conv_all = small_pack[:, smalls + 2 : smalls + 2 + per_row * tap_count]
        conv_all = conv_all.reshape(-1, tap_count).transpose(1, 0)
        normed, norm_in_back = jax.vjp(rms_scale, residual_in, norm_in_all)
    else:
        mix_all, small_all, conv_all, out_all = gather(w_mix), gather(w_small), gather(conv_w, 1), gather(w_out)
        norm_in_all = gather(norm_in).astype(jnp.float32)
        norm_mlp_all = gather(norm_mlp).astype(jnp.float32)
        normed, norm_in_back = jax.vjp(rms_scale, residual_in, norm_in_all)
        normed_low = normed.astype(jnp.bfloat16)
        projected = jnp.dot(normed_low, mix_all, preferred_element_type=jnp.float32)
        gates_raw = jnp.dot(normed_low, small_all, preferred_element_type=jnp.float32)
    if fast:
        down_all = gather(down_own)
    else:
        gu_all, down_all = gather(w_gu), gather(w_down)
        border = from_behind(projected[seg_len - tap_count + 1 :, : parts * key_width], "seq", 1)
        border = jnp.concatenate([jnp.zeros((9 - tap_count, parts * key_width), jnp.float32), border], axis=0)
    positions = lax.axis_index("seq") * seg_len + jnp.arange(1 - tap_count, seg_len, dtype=jnp.int32)
    seg_ext = jnp.sum((positions[:, None] >= doc_starts[0][None, :]).astype(jnp.int32), axis=1)
    seg_ext = jnp.where(positions < 0, -1, seg_ext)
    seg_now = seg_ext[tap_count - 1 :]
    masks = jnp.stack(
        [seg_ext[tap_count - 1 - tap : tap_count - 1 - tap + seg_len] == seg_now for tap in range(1, tap_count)]
    ).astype(jnp.float32)
    masks = jnp.broadcast_to(masks[:, :, None], (tap_count - 1, seg_len, DK))
    if fast:
        masks = masks.astype(jnp.bfloat16)
    taps = jnp.concatenate([conv_all.astype(jnp.float32), jnp.zeros((8 - tap_count, parts * key_width), jnp.float32)], axis=0)
    vec, vec_back = jax.vjp(
        partial(gate_vectors, seg_now, seg_ext[tap_count - 2]), gates_raw, decay_log.astype(jnp.float32)
    )
    gain = jnp.broadcast_to(norm_out.astype(jnp.float32)[None, :], (8, DV))
    if fast:
        xt, out_keys, us, normed_out_low, mixed, gu_all = mixer_call(channels, gate, vec, masks, taps, border, gain, w_gu)
        gu_all = gu_all.reshape(width, -1)
    else:
        zero_state = jnp.zeros((H, DV, DK), jnp.float32)
        inverse, key_part, value_part, transfer, inject, out_keys, out_values, final_state = forward_call(
            projected, border, taps, masks, vec, zero_state
        )
        entry = zero_state
        device_transfer = None
        if seqs > 2:
            eye = jnp.broadcast_to(jnp.eye(DK, dtype=jnp.float32), (H, DK, DK))
            device_transfer = chain_call(vec, transfer, eye)
        for turn in range(seqs - 1):
            leaving = final_state
            if turn > 0:
                leaving = leaving + jnp.einsum("hvk,hkl->hvl", entry, device_transfer, precision=HIGHEST)
            entry = from_behind(leaving.astype(jnp.bfloat16), "seq", 1).astype(jnp.float32)
        normed_out_low, mixed, solved, entries = readout_call(
            vec, key_part, value_part, transfer, inject, out_keys, out_values, entry, projected, gain
        )
    if fast:
        mlp_gain = jnp.broadcast_to(norm_mlp_all[None, :], (8, width))
        backs = back_call(
            xt, out_keys, mixed, gate, channels, us, gu_all, down_all, vec, masks, taps, border, gain,
            out_all, mlp_gain,
            block_input.reshape(seg_len, width), normed_out_low, cotangent.reshape(seg_len, width), mix_all.reshape(STACK + (rows, -1)), normed_t,
        )
        d_projected, block_output, d_hidden, d_normed, gain_parts, d_vec, grad_conv, mlp_gain_parts = backs[:8]
        grad_gu, grad_down, grad_out, grad_mix = backs[8:]
        block_output = block_output.reshape(block_input.shape)
        d_hidden = d_hidden.reshape(seg_len, width)
        grad_norm_mlp = mlp_gain_parts[0]
        grad_down = grad_down.reshape(-1, width)[: w_down.shape[0]]
    else:
        hidden = residual_in + jnp.dot(normed_out_low, out_all, preferred_element_type=jnp.float32)
        mlp_in, norm_mlp_back = jax.vjp(rms_scale, hidden, norm_mlp_all)
        mlp_in_low = mlp_in.astype(jnp.bfloat16)
        gate_up = jnp.dot(mlp_in_low, gu_all, preferred_element_type=jnp.float32)
        activated, act_back = jax.vjp(swiglu, gate_up)
        activated_low = activated.astype(jnp.bfloat16)
        result = hidden + jnp.dot(activated_low, down_all, preferred_element_type=jnp.float32)
        block_output = result.astype(jnp.bfloat16).reshape(block_input.shape)

        d_result_low = cotangent.reshape(seg_len, width)
        d_result = d_result_low.astype(jnp.float32)
        grad_down = jnp.einsum("nf,nd->fd", activated_low, d_result_low, preferred_element_type=jnp.float32)
        d_activated = jnp.einsum("nd,fd->nf", d_result_low, down_all, preferred_element_type=jnp.float32)
        (d_gate_up,) = act_back(d_activated)
        d_gate_low = d_gate_up.astype(jnp.bfloat16)
        grad_gu = jnp.einsum("nd,nf->df", mlp_in_low, d_gate_low, preferred_element_type=jnp.float32)
        d_mlp_in = jnp.einsum("nf,df->nd", d_gate_low, gu_all, preferred_element_type=jnp.float32)
        d_hidden_norm, grad_norm_mlp = norm_mlp_back(d_mlp_in)
        d_hidden = d_result + d_hidden_norm
        d_mixer_low = d_hidden.astype(jnp.bfloat16)
        grad_out = jnp.einsum("nh,nd->hd", normed_out_low, d_mixer_low, preferred_element_type=jnp.float32)
        d_normed_out = jnp.einsum("nd,hd->nh", d_mixer_low, out_all, preferred_element_type=jnp.float32)
        grad_gu = scatter_halves(grad_gu.astype(jnp.bfloat16))
        grad_down = scatter_halves(grad_down.astype(jnp.bfloat16))
        grad_out = scatter_halves(grad_out.astype(jnp.bfloat16))
        d_mixed, d_out_gate, local, own_entry, gain_parts = readout_back_call(
            vec, transfer, out_keys, mixed, projected, gain, d_normed_out, zero_state
        )
        exit_grad = zero_state
        for turn in range(seqs - 1):
            leaving = own_entry
            if turn > 0:
                leaving = leaving + jnp.einsum("hvl,hkl->hvk", exit_grad, device_transfer, precision=HIGHEST)
            exit_grad = from_behind(leaving.astype(jnp.bfloat16), "seq", -1).astype(jnp.float32)
        backs = backward_call(
            projected, border, taps, masks, vec, transfer, inverse, solved, entries, d_mixed, local, exit_grad
        )
        d_columns, edges, tap_grads, d_vec = backs[:parts], backs[parts : 2 * parts], backs[2 * parts : 3 * parts], backs[-1]
        edge = jnp.concatenate(edges, axis=1)
        returned = from_behind(edge[9 - tap_count : 8].astype(jnp.bfloat16), "seq", -1).astype(jnp.float32)
        fixed = (edge[17 - tap_count :] + returned).astype(jnp.bfloat16)
        d_projected = jnp.concatenate(list(d_columns) + [d_out_gate], axis=1)
        d_projected = lax.dynamic_update_slice(d_projected, fixed, (seg_len - tap_count + 1, 0))
        grad_mix = jnp.einsum("nd,nc->dc", normed_low, d_projected, preferred_element_type=jnp.float32)
        grad_mix = scatter_halves(grad_mix.astype(jnp.bfloat16))
        grad_conv = jnp.concatenate(tap_grads, axis=1)
    grad_norm_out = jnp.sum(gain_parts[:, 0, :], axis=0)
    d_gates_raw, grad_decay = vec_back(d_vec)
    d_gates_low = d_gates_raw.astype(jnp.bfloat16)
    grad_small = jnp.einsum("nd,nc->dc", normed_low, d_gates_low, preferred_element_type=jnp.float32)
    if not fast:
        d_normed = jnp.einsum("nc,dc->nd", d_projected, mix_all, preferred_element_type=jnp.float32)
    d_normed = d_normed + jnp.einsum("nc,dc->nd", d_gates_low, small_all, preferred_element_type=jnp.float32)
    d_input_norm, grad_norm_in = norm_in_back(d_normed)
    input_grad = (d_hidden + d_input_norm).astype(jnp.bfloat16).reshape(block_input.shape)

    grad_conv = grad_conv[:tap_count]
    devices = lax.axis_size("dp") * seqs
    conv_rows = grad_conv.reshape(tap_count, devices, -1).transpose(1, 0, 2).reshape(width, -1)
    packed = jnp.concatenate([grad_small, grad_norm_in[:, None], grad_norm_mlp[:, None], conv_rows], axis=1)
    packed = jnp.concatenate([packed, jnp.zeros((width, 128 - packed.shape[1]), jnp.float32)], axis=1)
    if fast:
        sums = jnp.stack([grad_norm_out, jnp.pad(grad_decay, (0, DV - H))] + [jnp.zeros((DV,), jnp.float32)] * 6)
        packed, sums = total_call(packed.reshape(STACK + (rows, -1)), sums)
        grad_norm_out, grad_decay = sums[0], sums[1, :H]
    else:
        packed = scatter_sum(packed, bit_orders()[0])
        sums = total_sum(jnp.concatenate([grad_norm_out, grad_decay]))
        grad_norm_out, grad_decay = sums[:DV], sums[DV:]
    smalls = grad_small.shape[1]
    grad_small = packed[:, :smalls]
    grad_norm_in, grad_norm_mlp = packed[:, smalls], packed[:, smalls + 1]
    grad_conv = packed[:, smalls + 2 : smalls + 2 + conv_rows.shape[1]].reshape(tap_count, -1)
    return (
        block_output, input_grad, grad_norm_in, grad_mix, grad_small, grad_conv, grad_decay,
        grad_norm_out, grad_out, grad_norm_mlp, grad_gu, grad_down,
    )


def solution(mesh):
    sharded = ("dp", "seq")
    in_specs = (
        P("dp", "seq", None), P("dp", None), P(sharded), P(sharded, None), P(sharded, None),
        P(None, sharded), P(), P(), P(sharded, None), P(sharded), P(sharded, None),
        P(sharded, None), P("dp", "seq", None),
    )
    out_specs = (
        P("dp", "seq", None), P("dp", "seq", None), P(sharded), P(sharded, None), P(sharded, None),
        P(None, sharded), P(), P(), P(sharded, None), P(sharded), P(sharded, None), P(sharded, None),
    )
    return jax.shard_map(
        on_device, mesh=mesh, in_specs=in_specs, out_specs=out_specs, check_vma=False
    )
```

```python
from functools import partial

import jax
import jax.numpy as jnp
from jax import lax
from jax.experimental import pallas as pl
from jax.experimental.pallas import tpu as pltpu
from jax.sharding import PartitionSpec as P

H = 8
DK = 128
DV = 128
NH = 2
GROUP = 64
SPAN = NH * GROUP
LEVELS = 6
EPSILON = 1e-06
HIGHEST = lax.Precision.HIGHEST
LIMIT = 50 * 1024 * 1024
MOST = 255 * 256 * 1024


def mm(left, right, left_dim=1, right_dim=0):
    return lax.dot_general(
        left.astype(jnp.bfloat16),
        right.astype(jnp.bfloat16),
        (((left_dim,), (right_dim,)), ((), ())),
        preferred_element_type=jnp.float32,
    )


def halves_of(values):
    high = values.astype(jnp.bfloat16)
    return high, (values - high.astype(jnp.float32)).astype(jnp.bfloat16)


def mm3(left, right, left_dim=1, right_dim=0):
    left_high, left_low = halves_of(left)
    right_high, right_low = halves_of(right)
    wide = right.shape[1 - right_dim]
    lefts = jnp.concatenate([left_high, left_low], axis=left_dim)
    rights = jnp.concatenate(
        [
            jnp.concatenate([right_high, right_high], axis=right_dim),
            jnp.concatenate([right_low, jnp.zeros_like(right_low)], axis=right_dim),
        ],
        axis=1 - right_dim,
    )
    both = mm(lefts, rights, left_dim, right_dim)
    return both[:, :wide] + both[:, wide:]


def iotas(rows, columns):
    return (
        lax.broadcasted_iota(jnp.int32, (rows, columns), 0),
        lax.broadcasted_iota(jnp.int32, (rows, columns), 1),
    )


def order_masks():
    row, column = iotas(SPAN, SPAN)
    row_tok, column_tok = row % GROUP, column % GROUP
    row_step, column_step = row // GROUP, column // GROUP
    pair = (row_tok == column_tok) & (row_step > column_step)
    strict = (row_tok > column_tok) | pair
    levels = []
    for level in range(LEVELS):
        row_half, column_half = row_tok >> level, column_tok >> level
        levels.append((row_half == column_half + 1) & (row_half % 2 == 1))
    eye = jnp.where(row == column, 1.0, 0.0)
    return strict, pair, levels, eye


TOGETHER = 16


def together(runs):
    for first in range(0, len(runs), TOGETHER):
        group = runs[first : first + TOGETHER]
        while group:
            group = [run for run in group if next(run, "done") != "done"]


def unit_inverses(lowers, pair, levels, eye):
    inverses = [eye - jnp.where(pair, lower, 0.0) for lower in lowers]
    for level in levels:
        parts = [mm3(jnp.where(level, lower, 0.0), inv) for lower, inv in zip(lowers, inverses)]
        inverses = [inv - mm3(inv, part) for part, inv in zip(parts, inverses)]
    return inverses


def silu_pair(values):
    sig = jax.nn.sigmoid(values)
    return values * sig, sig


def conv_block(channels, border, taps, mask_ref, ext_ref):
    length = channels.shape[0]
    ext_ref[0:8, :] = border
    ext_ref[8 : 8 + length, :] = channels
    summed = channels * taps[0:1, :]
    for tap in range(1, 4):
        summed = summed + ext_ref[8 - tap : 8 - tap + length, :] * taps[tap : tap + 1, :] * mask_ref[tap - 1].astype(jnp.float32)
    return summed


def unit_rows(values):
    inv = lax.rsqrt(jnp.sum(values * values, axis=1, keepdims=True) + EPSILON)
    return values * inv, inv


def chunk_vectors(vec_ref, chunk):
    rows = vec_ref[0, chunk]
    columns = jnp.transpose(rows)
    return rows, columns


def link_matrix(rows, columns):
    row, column = iotas(GROUP, SPAN)
    linked = (columns[:GROUP, 2:3] == rows[2:3, :]) & (row >= column % GROUP)
    return jnp.exp(jnp.where(linked, columns[:GROUP, 0:1] - rows[0:1, :], -1e30))


def twice(values):
    return jnp.concatenate([values, values], axis=0)


def forward_kernel(
    q_in, k0_in, k1_in, v0_in, v1_in,
    bq, bk0, bk1, bv0, bv1,
    tq, tk0, tk1, tv0, tv1,
    mask_ref, vec_ref, start_ref,
    x_out, w_out, u_out, t_out, i_out, ok_out, o_out, state_out,
    ext_ref, q_ref, k_ref, v_ref,
):
    length = q_in.shape[0]
    chunks = length // GROUP
    conv = []
    for channel, border, tap in (
        (q_in, bq, tq), (k0_in, bk0, tk0), (k1_in, bk1, tk1), (v0_in, bv0, tv0), (v1_in, bv1, tv1),
    ):
        conv.append(silu_pair(conv_block(channel[...], border[...], tap[...], mask_ref, ext_ref))[0])
    q_ref[...] = unit_rows(conv[0])[0] * DK ** (-0.5)
    for step in range(NH):
        k_ref[step] = unit_rows(conv[1 + step])[0]
        v_ref[step] = conv[1 + NH + step]
    strict, pair, levels, eye = order_masks()
    items = []
    lowers = []
    for chunk in range(chunks):
        here = slice(chunk * GROUP, (chunk + 1) * GROUP)
        rows, columns = chunk_vectors(vec_ref, chunk)
        keys = k_ref[:, here, :].reshape(SPAN, DK)
        values = v_ref[:, here, :].reshape(SPAN, DV)
        queries = q_ref[here, :]
        link = link_matrix(rows, columns)
        lower = jnp.where(strict, columns[:, 1:2] * twice(link) * mm3(keys, keys, 1, 1), 0.0)
        reading = link * mm3(queries, keys, 1, 1)
        lowers.append(lower)
        items.append((rows, columns, keys, values, queries, reading))
    inverses = unit_inverses(lowers, pair, levels, eye)
    state = start_ref[0]
    for chunk in range(chunks):
        rows, columns, keys, values, queries, reading = items[chunk]
        inverse = inverses[chunk]
        here = slice(chunk * GROUP, (chunk + 1) * GROUP)
        beta, scale, tail = columns[:, 1:2], columns[:, 3:4], columns[:, 4:5]
        key_part = mm3(inverse, beta * scale * keys)
        value_part = mm3(inverse, beta * values)
        tail_keys = tail * keys
        transfer = mm3(key_part, tail_keys, 0, 0)
        inject = mm3(value_part, tail_keys, 0, 0)
        x_out[0, chunk] = inverse.astype(x_out.dtype)
        w_out[0, chunk] = key_part.astype(w_out.dtype)
        u_out[0, chunk] = value_part.astype(u_out.dtype)
        t_out[0, chunk] = transfer.astype(t_out.dtype)
        i_out[0, chunk] = inject
        ok_out[0, chunk] = (columns[:GROUP, 3:4] * queries - mm3(reading, key_part)).astype(ok_out.dtype)
        o_out[0, chunk] = mm3(reading, value_part)
        state = rows[3:4, GROUP - 1 : GROUP] * state - mm3(state, transfer) + inject
    state_out[0] = state


def chain_kernel(vec_ref, t_in, start_ref, state_out):
    chunks = t_in.shape[1]
    state = start_ref[0]
    for chunk in range(chunks):
        state = vec_ref[0, chunk, 3:4, GROUP - 1 : GROUP] * state - mm3(state, t_in[0, chunk])
    state_out[0] = state


def readout_kernel(vec_ref, w_in, u_in, t_in, i_in, ok_in, o_in, entry_ref, gate_ref, gain_ref, gated_out, mixed_out, u_out, s_out):
    chunks = w_in.shape[1]
    state = entry_ref[0]
    states = []
    for chunk in range(chunks):
        states.append(state)
        state = vec_ref[0, chunk, 3:4, GROUP - 1 : GROUP] * state - mm3(state, t_in[0, chunk]) + i_in[0, chunk]
    for chunk in range(chunks):
        here = slice(chunk * GROUP, (chunk + 1) * GROUP)
        state = states[chunk]
        s_out[0, chunk] = state
        u_out[0, chunk] = (u_in[0, chunk].astype(jnp.float32) - mm3(w_in[0, chunk], state, 1, 1)).astype(u_out.dtype)
        mixed = o_in[0, chunk] + mm3(ok_in[0, chunk], state, 1, 1)
        mixed_out[here, :] = mixed
        inv = lax.rsqrt(jnp.mean(mixed * mixed, axis=1, keepdims=True) + EPSILON)
        gate = silu_pair(gate_ref[here, :])[0]
        gated_out[here, :] = (mixed * inv * gain_ref[0:1, :] * gate).astype(gated_out.dtype)


def readout_back_kernel(vec_ref, t_in, ok_in, mixed_in, gate_ref, gain_ref, d_ref, start_ref, d_mixed_out, d_gate_out, local_out, state_out, gain_out):
    chunks = t_in.shape[1]
    gain = gain_ref[0:1, :]
    gain_grad = jnp.zeros((1, DV), jnp.float32)
    locals_ = []
    for chunk in range(chunks):
        here = slice(chunk * GROUP, (chunk + 1) * GROUP)
        mixed = mixed_in[here, :]
        inv = lax.rsqrt(jnp.mean(mixed * mixed, axis=1, keepdims=True) + EPSILON)
        unit = mixed * inv
        gate = gate_ref[here, :]
        open_, sig = silu_pair(gate)
        d_gated = d_ref[here, :]
        d_scaled = d_gated * open_
        d_gate_out[here, :] = (d_gated * unit * gain * sig * (1.0 + gate * (1.0 - sig))).astype(d_gate_out.dtype)
        gain_grad = gain_grad + jnp.sum(d_scaled * unit, axis=0, keepdims=True)
        d_unit = d_scaled * gain
        d_mixed = inv * (d_unit - unit * jnp.mean(d_unit * unit, axis=1, keepdims=True))
        d_mixed_low = d_mixed
        d_mixed_out[here, :] = d_mixed_low
        local = mm3(d_mixed_low, ok_in[0, chunk], 0, 0)
        local_out[0, chunk] = local
        locals_.append(local)
    gain_out[0] = jnp.broadcast_to(gain_grad, (8, DV))
    state = start_ref[0]
    for chunk in reversed(range(chunks)):
        state = vec_ref[0, chunk, 3:4, GROUP - 1 : GROUP] * state - mm3(state, t_in[0, chunk], 1, 1) + locals_[chunk]
    state_out[0] = state


def backward_kernel(
    q_in, k0_in, k1_in, v0_in, v1_in,
    bq, bk0, bk1, bv0, bv1,
    tq, tk0, tk1, tv0, tv1,
    mask_ref, vec_ref, t_in, x_in, u_in, s_in, d_mixed_in, local_in, exit_ref,
    dq_out, dk0_out, dk1_out, dv0_out, dv1_out,
    eq_out, ek0_out, ek1_out, ev0_out, ev1_out,
    gq_out, gk0_out, gk1_out, gv0_out, gv1_out,
    d_vec_out,
    ext_ref, pre_ref, q_ref, k_ref, v_ref, inv_ref, d_ref, z_ref,
):
    length = q_in.shape[0]
    chunks = length // GROUP
    channels = (q_in, k0_in, k1_in, v0_in, v1_in)
    taps = (tq, tk0, tk1, tv0, tv1)
    for part, (channel, border, tap) in enumerate(zip(channels, (bq, bk0, bk1, bv0, bv1), taps)):
        pre = conv_block(channel[...], border[...], tap[...], mask_ref, ext_ref.at[part])
        pre_ref[part] = pre
        value = silu_pair(pre)[0]
        if part == 0:
            unit, inv = unit_rows(value)
            q_ref[...] = unit * DK ** (-0.5)
            inv_ref[0] = jnp.broadcast_to(inv, (length, DK))
        elif part <= NH:
            unit, inv = unit_rows(value)
            k_ref[part - 1] = unit
            inv_ref[part] = jnp.broadcast_to(inv, (length, DK))
        else:
            v_ref[part - 1 - NH] = value
    strict, pair, levels, eye = order_masks()
    column_index = iotas(SPAN, 8)[1]
    exit_grads = [None] * chunks
    grad = exit_ref[0]
    for chunk in reversed(range(chunks)):
        exit_grads[chunk] = grad
        grad = vec_ref[0, chunk, 3:4, GROUP - 1 : GROUP] * grad - mm3(grad, t_in[0, chunk], 1, 1) + local_in[0, chunk]
    for chunk in reversed(range(chunks)):
        here = slice(chunk * GROUP, (chunk + 1) * GROUP)
        rows, columns = chunk_vectors(vec_ref, chunk)
        beta, scale, tail = columns[:, 1:2], columns[:, 3:4], columns[:, 4:5]
        keys = k_ref[:, here, :].reshape(SPAN, DK)
        values = v_ref[:, here, :].reshape(SPAN, DV)
        queries = q_ref[here, :]
        link = link_matrix(rows, columns)
        link_gram = jnp.where(strict, twice(link) * mm3(keys, keys, 1, 1), 0.0)
        reading = link * mm3(queries, keys, 1, 1)
        d_exit = exit_grads[chunk]
        solved = u_in[0, chunk]
        entry = s_in[0, chunk]
        d_mixed = d_mixed_in[here, :]
        tail_keys = tail * keys
        d_solved = mm3(reading, d_mixed, 0, 0) + mm3(tail_keys, d_exit, 1, 1)
        d_right = mm3(x_in[0, chunk], d_solved, 0, 0)
        d_lower = jnp.where(strict, -mm3(d_right, solved, 1, 1), 0.0)
        d_tail_keys = mm3(solved, d_exit)
        d_right_entry = mm3(d_right, entry)
        d_reading = mm3(d_mixed, solved, 1, 1)
        d_query_entry = mm3(d_mixed, entry)
        both_scale = -jnp.sum(d_right_entry * keys, axis=1, keepdims=True)
        lower_weight = d_lower * link_gram
        d_beta = (
            jnp.sum(d_right * values, axis=1, keepdims=True)
            + scale * both_scale
            + jnp.sum(lower_weight, axis=1, keepdims=True)
        )
        lower_moment = lower_weight * beta
        reading_moment = d_reading * reading
        d_gram = beta * twice(link) * d_lower
        d_gram = d_gram + jnp.transpose(d_gram)
        d_query_gram = link * d_reading
        d_keys = (
            tail * d_tail_keys
            - beta * scale * d_right_entry
            + mm3(d_gram, keys)
            + mm3(d_query_gram, queries, 0, 0)
        )
        d_queries = mm3(d_query_gram, keys) + scale[:GROUP] * d_query_entry
        d_values = beta * d_right
        none = jnp.zeros((GROUP, 1), jnp.float32)
        d_gap = jnp.sum(lower_moment, axis=1, keepdims=True) + jnp.concatenate(
            [jnp.sum(reading_moment, axis=1, keepdims=True), none], axis=0
        )
        last = jnp.sum(jnp.sum(d_exit * entry.astype(jnp.float32), axis=1, keepdims=True), axis=0, keepdims=True)
        own_scale = jnp.sum(d_query_entry * queries, axis=1, keepdims=True)
        own_scale = own_scale + jnp.where(iotas(GROUP, 1)[0] == GROUP - 1, last, 0.0)
        d_scale = beta * both_scale + jnp.concatenate([own_scale, none], axis=0)
        d_tail = jnp.sum(d_tail_keys * keys, axis=1, keepdims=True)
        grads = jnp.where(
            column_index == 0,
            d_gap,
            jnp.where(
                column_index == 1,
                d_beta,
                jnp.where(column_index == 3, d_scale, jnp.where(column_index == 4, d_tail, 0.0)),
            ),
        )
        grads = jnp.transpose(grads)
        sums = jnp.sum(lower_moment, axis=0, keepdims=True) + jnp.sum(reading_moment, axis=0, keepdims=True)
        grads = grads - jnp.where(iotas(8, SPAN)[0] == 0, sums, 0.0)
        d_vec_out[0, chunk] = grads
        d_ref[0, here, :] = d_queries
        for step in range(NH):
            mine = slice(step * GROUP, (step + 1) * GROUP)
            d_ref[1 + step, here, :] = d_keys[mine]
            d_ref[1 + NH + step, here, :] = d_values[mine]
    outs = (dq_out, dk0_out, dk1_out, dv0_out, dv1_out)
    edges = (eq_out, ek0_out, ek1_out, ev0_out, ev1_out)
    tap_grads = (gq_out, gk0_out, gk1_out, gv0_out, gv1_out)
    z_ref[0:8, :] = jnp.zeros((8, DK), jnp.float32)
    z_ref[8 + length : 16 + length, :] = jnp.zeros((8, DK), jnp.float32)
    for part in range(1 + 2 * NH):
        grad = d_ref[part]
        if part <= NH:
            unit = q_ref[...] * DK ** 0.5 if part == 0 else k_ref[part - 1]
            if part == 0:
                grad = grad * DK ** (-0.5)
            grad = inv_ref[part] * (grad - unit * jnp.sum(grad * unit, axis=1, keepdims=True))
        pre = pre_ref[part]
        sig = jax.nn.sigmoid(pre)
        grad = grad * sig * (1.0 + pre * (1.0 - sig))
        tap = taps[part]
        total = grad * tap[0:1, :]
        edge = jnp.zeros((8, DK), jnp.float32)
        tap_rows = [jnp.sum(grad * channels[part][...], axis=0, keepdims=True)]
        for index in range(1, 4):
            shifted = grad * mask_ref[index - 1]
            tap_rows.append(
                jnp.sum(shifted * ext_ref[part, 8 - index : 8 - index + length, :], axis=0, keepdims=True)
            )
            z_ref[8 : 8 + length, :] = shifted * tap[index : index + 1, :]
            total = total + z_ref[8 + index : 8 + index + length, :]
            edge = edge + z_ref[index : index + 8, :]
        outs[part][...] = total.astype(outs[part].dtype)
        edges[part][0:8, :] = edge
        edges[part][8:16, :] = total[length - 8 :, :]
        tap_grads[part][...] = jnp.concatenate(tap_rows + [jnp.zeros((4, DK), jnp.float32)], axis=0)


MESH = pl.DeviceIdType.MESH
ZS = 4
STACK = (ZS, 2, 2, 2)
STAGES = 6


def place():
    dp, seq = lax.axis_index("dp"), lax.axis_index("seq")
    return dp // 4, (dp // 2) % 2, dp % 2, seq


def device_at(z, x, core, y):
    return (z * 4 + x * 2 + core, y)


def peers():
    z, x, core, y = place()
    ring = [device_at((z + step) % ZS, x, core, y) for step in range(1, ZS)]
    return ring + [device_at(z, 1 - x, core, y), device_at(z, x, core, 1 - y), device_at(z, x, 1 - core, y)]


def meet(devices):
    barrier = pltpu.get_barrier_semaphore()
    for device in devices:
        pl.semaphore_signal(barrier, inc=1, device_id=device, device_id_type=MESH)
    pl.semaphore_wait(barrier, len(devices))


class Gather:
    def __init__(self, source, target, x_first, sems, index):
        self.source, self.target, self.x_first = source, target, x_first
        self.send, self.recv, self.local = sems
        self.index = index
        self.copies = []

    def remote(self, source, target, slot):
        copy = pltpu.make_async_remote_copy(
            src_ref=source, dst_ref=target,
            send_sem=self.send.at[self.index, slot], recv_sem=self.recv.at[self.index, slot],
            device_id=peers()[slot], device_id_type=MESH,
        )
        copy.start()
        self.copies.append(copy)
        return copy

    def begin(self):
        z, x, core, y = place()
        mine = self.target(z, x, core, y)
        self.own = pltpu.make_async_copy(self.source, mine, self.local.at[self.index])
        self.own.start()
        self.waiting = [self.remote(self.source, mine, slot) for slot in range(ZS - 1)]

    def second(self):
        z, x, core, y = place()
        self.own.wait()
        for copy in self.waiting:
            copy.wait_recv()
        block = self.target(slice(None), x, core, y)
        self.waiting = [self.remote(block, block, ZS - 1 if self.x_first else ZS)]

    def third(self):
        z, x, core, y = place()
        self.waiting[0].wait_recv()
        every = slice(None)
        block = self.target(every, every, core, y) if self.x_first else self.target(every, x, core, every)
        self.waiting = [self.remote(block, block, ZS if self.x_first else ZS - 1)]

    def fourth(self):
        z, x, core, y = place()
        self.waiting[0].wait_recv()
        every = slice(None)
        block = self.target(every, every, core, every)
        self.waiting = [self.remote(block, block, ZS + 1)]

    def finish(self):
        self.waiting[0].wait_recv()
        for copy in self.copies:
            copy.wait_send()


def columns_of(ref, first, width):
    return lambda z, x, core, y: ref.at[z, x, core, y, :, pl.ds(first, width)]


class Spread:
    def __init__(self, source, target, lane, width, sems, first=0):
        self.first = first
        self.source, self.target, self.lane, self.width = source, target, lane, width
        self.send_sem, self.recv_sem, self.local_sem = sems
        self.place, self.peers = place(), peers()

    def here(self, index):
        return pl.ds(pl.multiple_of((2 * (index - self.first) + self.lane) * self.width, self.width), self.width)

    def block(self, index, stage):
        z, x, core, y = self.place
        every = slice(None)
        here = self.here(index)
        if stage == 0:
            return self.target.at[z, x, core, y, :, here]
        if stage == 1:
            return self.target.at[:, x, core, y, :, here]
        if stage == 2:
            if self.lane == 0:
                return self.target.at[:, :, core, y, :, here]
            return self.target.at[:, x, core, :, :, here]
        return self.target.at[:, :, core, :, :, here]

    def copies(self, index, stage):
        near, far = (ZS - 1, ZS) if self.lane == 0 else (ZS, ZS - 1)
        slots = (0, 1, 2) if stage == 0 else ((near,), (far,), (ZS + 1,))[stage - 1]
        target = self.block(index, stage)
        source = self.source.at[:, self.here(index)] if stage == 0 else target
        ring = lax.rem(index, RING)
        return [
            pltpu.make_async_remote_copy(
                src_ref=source, dst_ref=target,
                send_sem=self.send_sem.at[self.lane, slot, ring], recv_sem=self.recv_sem.at[self.lane, slot, ring],
                device_id=self.peers[slot], device_id_type=MESH,
            )
            for slot in slots
        ]

    def own(self, index):
        return pltpu.make_async_copy(
            self.source.at[:, self.here(index)], self.block(index, 0), self.local_sem.at[self.lane, lax.rem(index, RING)]
        )

    def step(self, index, stage):
        if stage > 0:
            for copy in self.copies(index, stage - 1):
                copy.wait_recv()
                copy.wait_send()
        if stage == 1:
            self.own(index).wait()
        if stage == 0:
            self.own(index).start()
        if stage < SPREAD_STAGES - 1:
            for copy in self.copies(index, stage):
                copy.start()


SPREAD_STAGES = 5
SPREAD_TICKS = 2
SPREAD_FILL = (SPREAD_STAGES - 1) * SPREAD_TICKS
FINE = 256


def gather_project_kernel(
    x_ref, small_in, mix_in, out_in, down_in,
    mix_out, out_out, down_out, small_out, normed_ref, normed_t_ref, channels_out, gate_out, gates_ref, border_ref, gains_ref,
    mix_ref, small_ref, slab_ref,
    small_send, small_recv, small_local, send, recv, local, store_mix, store_slab, store_small, store_down, edge_send, edge_recv,
):
    parts, heads = channels_out.shape[0], channels_out.shape[1]
    length = x_ref.shape[0]
    block = 2 * FINE
    count = mix_in.shape[1] // block
    more = out_in.shape[1] // block
    per_part, across = heads * DK // block, block // DK
    z, x, core, y = place()
    sems = (send, recv, local)
    small = Gather(small_in, lambda z, x, core, y: small_ref.at[z, x, core, y], True, (small_send, small_recv, small_local), 0)
    mix_lanes = [Spread(mix_in, mix_ref, lane, FINE, sems) for lane in range(2)]
    out_lanes = [Spread(out_in, out_out, lane, FINE, sems, count) for lane in range(2)]

    def here(index):
        return pl.ds(pl.multiple_of(index * block, block), block)

    def slab_copies(index):
        slot, first = lax.rem(index, 2), lax.rem(index, per_part) * across
        return [
            [
                pltpu.make_async_copy(
                    slab_ref.at[slot, :, half * DK : (half + 1) * DK], target.at[first + half], store_slab.at[slot, half]
                )
                for half in range(across)
            ]
            for target in (channels_out.at[jnp.minimum(index // per_part, parts - 1)], gate_out)
        ]

    def edge(index):
        return pltpu.make_async_remote_copy(
            src_ref=slab_ref.at[lax.rem(index, 2), length - 8 :, :], dst_ref=border_ref.at[:, here(index)],
            send_sem=edge_send.at[lax.rem(index, 2)], recv_sem=edge_recv.at[index],
            device_id=device_at(z, x, core, 1 - y), device_id_type=MESH,
        )

    def kept(index):
        return pltpu.make_async_copy(
            mix_ref.at[:, :, :, :, :, here(index)], mix_out.at[:, :, :, :, :, here(index)], store_mix.at[lax.rem(index, 2)]
        )

    def release(index):
        for copy in slab_copies(index)[0]:
            copy.wait()
        kept(index).wait()

        @pl.when(index < parts * per_part)
        def _():
            edge(index).wait_send()

    def project(index):
        @pl.when(index >= 2)
        def _():
            release(index - 2)

        kept(index).start()
        weights = mix_ref[:, :, :, :, :, here(index)].reshape(-1, block)
        slab_ref[lax.rem(index, 2)] = mm(normed_ref[...], weights)
        channels, gates = slab_copies(index)

        @pl.when(index < parts * per_part)
        def _():
            for copy in channels:
                copy.start()
            edge(index).start()

        @pl.when(index >= parts * per_part)
        def _():
            for copy in gates:
                copy.start()

    def tick(number):
        for stage in reversed(range(SPREAD_STAGES)):
            index = number - stage * SPREAD_TICKS

            @pl.when((index >= 0) & (index < count))
            def _():
                for lane in mix_lanes:
                    lane.step(index, stage)

            @pl.when((index >= count) & (index < count + more))
            def _():
                for lane in out_lanes:
                    lane.step(index, stage)

        @pl.when((number >= SPREAD_FILL) & (number < count + SPREAD_FILL))
        def _():
            project(number - SPREAD_FILL)

    meet(peers())
    small.begin()
    for number in range(SPREAD_FILL):
        tick(number)
        if number == 0:
            values = x_ref[...].astype(jnp.float32)
            scaled = values * lax.rsqrt(jnp.mean(values * values, axis=1, keepdims=True) + EPSILON)
        if number % SPREAD_TICKS == SPREAD_TICKS - 1:
            (small.second, small.third, small.fourth, small.finish)[number // SPREAD_TICKS]()
    smalls = small_ref[...].reshape(-1, small_in.shape[1])
    gains_ref[...] = jnp.transpose(smalls.astype(jnp.float32))[24:32, :]
    normed = (scaled * gains_ref[0:1, :]).astype(jnp.bfloat16)
    normed_ref[...] = normed
    keep_small = pltpu.make_async_copy(small_ref, small_out, store_small)
    keep_small.start()
    keep_down = pltpu.make_async_copy(down_in, down_out, store_down)
    keep_down.start()

    def loop(number, carry):
        tick(number)
        return carry

    lax.fori_loop(SPREAD_FILL, 2 * SPREAD_FILL, loop, 0)
    gates_ref[...] = mm(normed_ref[...], smalls)
    flipped = jnp.transpose(normed_ref[...].astype(jnp.float32)).astype(jnp.bfloat16)
    normed_t_ref[...] = flipped.reshape(normed_t_ref.shape)
    lax.fori_loop(2 * SPREAD_FILL, count + more + SPREAD_FILL, loop, 0)
    release(count - 2)
    release(count - 1)
    keep_small.wait()
    keep_down.wait()

    def last(index, carry):
        edge(index).wait_recv()
        return carry

    lax.fori_loop(0, parts * per_part, last, 0)


def gather_project_call(x, small, mix, out, down):
    length = x.shape[0]
    rows, width = mix.shape
    everywhere = pl.BlockSpec(memory_space=pl.ANY)
    held = pl.BlockSpec(memory_space=pltpu.VMEM)
    full = STACK + (rows,)
    block = 2 * FINE
    parts = width // (H * DK) - 1
    outs = pl.pallas_call(
        gather_project_kernel,
        out_shape=[
            jax.ShapeDtypeStruct(full + (width,), jnp.bfloat16),
            jax.ShapeDtypeStruct(full + (out.shape[1],), jnp.bfloat16),
            jax.ShapeDtypeStruct(down.shape, jnp.bfloat16),
            jax.ShapeDtypeStruct(full + (small.shape[1],), jnp.bfloat16),
            jax.ShapeDtypeStruct(x.shape, jnp.bfloat16),
            jax.ShapeDtypeStruct(full + (length,), jnp.bfloat16),
            jax.ShapeDtypeStruct((parts, H, length, DK), jnp.float32),
            jax.ShapeDtypeStruct((H, length, DK), jnp.float32),
            jax.ShapeDtypeStruct((length, small.shape[1]), jnp.float32),
            jax.ShapeDtypeStruct((8, parts * H * DK), jnp.float32),
            jax.ShapeDtypeStruct((8, x.shape[1]), jnp.float32),
        ],
        in_specs=[held, everywhere, everywhere, everywhere, everywhere],
        out_specs=[everywhere, everywhere, everywhere, everywhere, held, held, everywhere, everywhere, held, held, held],
        scratch_shapes=[
            pltpu.VMEM(full + (width,), jnp.bfloat16),
            pltpu.VMEM(full + (small.shape[1],), jnp.bfloat16),
            pltpu.VMEM((2, length, block), jnp.float32),
            pltpu.SemaphoreType.DMA((1, STAGES)),
            pltpu.SemaphoreType.DMA((1, STAGES)),
            pltpu.SemaphoreType.DMA((1,)),
            pltpu.SemaphoreType.DMA((2, STAGES, RING)),
            pltpu.SemaphoreType.DMA((2, STAGES, RING)),
            pltpu.SemaphoreType.DMA((2, RING)),
            pltpu.SemaphoreType.DMA((2,)),
            pltpu.SemaphoreType.DMA((2, block // DK)),
            pltpu.SemaphoreType.DMA,
            pltpu.SemaphoreType.DMA,
            pltpu.SemaphoreType.DMA((2,)),
            pltpu.SemaphoreType.DMA((parts * H * DK // block,)),
        ],
        compiler_params=pltpu.CompilerParams(collective_id=1, has_side_effects=True, vmem_limit_bytes=LIMIT),
        cost_estimate=pl.CostEstimate(flops=2 * length * width * 1024, bytes_accessed=60_000_000, transcendentals=0),
    )(x, small, mix, out, down)
    return [part.reshape((-1,) + part.shape[5:]) if index in (0, 1, 3) else part for index, part in enumerate(outs)]


PAIR = 2


def mixer_kernel(
    channel_ref, gate_ref, vec_ref, mask_ref, tap_ref, border_ref, gain_ref, shard_in,
    xt_out, ok_out, us_out, gated_out, mixed_out, gathered_out,
    w_ref, u_ref, t_ref, i_ref, k_read_ref, v_read_ref, relay_send, relay_recv,
    ext_ref, q_ref, k_ref, v_ref,
    relay_sems, send_sem, recv_sem, local_sem,
):
    step = pl.program_id(0)
    steps = H // PAIR
    parts = channel_ref.shape[0]
    length = channel_ref.shape[2]
    chunks = length // GROUP
    z, x, core, y = place()
    count = shard_in.shape[1] // (2 * WIDE)
    lanes = [Spread(shard_in, gathered_out, lane, WIDE, (send_sem, recv_sem, local_sem)) for lane in range(2)]

    def tick(number):
        for stage in reversed(range(SPREAD_STAGES)):
            index = number - stage * SPREAD_TICKS

            @pl.when((index >= 0) & (index < count))
            def _():
                for lane in lanes:
                    lane.step(index, stage)

    def convolve(pair):
        head = step * PAIR + pair
        column = lambda part: pl.ds(pl.multiple_of((part * H + head) * DK, DK), DK)
        for part in range(parts):
            value = silu_pair(
                conv_block(
                    channel_ref[part, pair], border_ref[:, column(part)], tap_ref[:, column(part)], mask_ref,
                    ext_ref.at[pair],
                )
            )[0]
            if part == 0:
                q_ref[pair] = unit_rows(value)[0] * DK ** (-0.5)
            elif part <= NH:
                k_ref[pair, part - 1] = unit_rows(value)[0]
            else:
                v_ref[pair, part - 1 - NH] = value
            yield

    def chunk_terms(pair, chunk, masks):
        strict, same, levels, eye = masks
        head = step * PAIR + pair
        here = slice(chunk * GROUP, (chunk + 1) * GROUP)
        rows = vec_ref[head, chunk]
        columns = jnp.transpose(rows)
        keys = k_ref[pair, :, here, :].reshape(SPAN, DK)
        beta, scale, tail = columns[:, 1:2], columns[:, 3:4], columns[:, 4:5]
        link = link_matrix(rows, columns)
        lower = jnp.where(strict, beta * twice(link) * mm3(keys, keys, 1, 1), 0.0)
        yield
        inverse = eye - jnp.where(same, lower, 0.0)
        for level in levels:
            part = mm3(jnp.where(level, lower, 0.0), inverse)
            yield
            inverse = inverse - mm3(inverse, part)
            yield
        xt_out[pair, 0, chunk] = inverse

    def chunk_rest(pair, chunk):
        head = step * PAIR + pair
        here = slice(chunk * GROUP, (chunk + 1) * GROUP)
        rows = vec_ref[head, chunk]
        columns = jnp.transpose(rows)
        keys = k_ref[pair, :, here, :].reshape(SPAN, DK)
        values = v_ref[pair, :, here, :].reshape(SPAN, DV)
        queries = q_ref[pair, here, :]
        beta, scale, tail = columns[:, 1:2], columns[:, 3:4], columns[:, 4:5]
        inverse = xt_out[pair, 0, chunk]
        reading = link_matrix(rows, columns) * mm3(queries, keys, 1, 1)
        key_part = mm3(inverse, beta * scale * keys)
        value_part = mm3(inverse, beta * values)
        w_ref[head, chunk] = key_part
        u_ref[head, chunk] = value_part
        yield
        tail_keys = tail * keys
        transfer = mm3(key_part, tail_keys, 0, 0)
        inject = mm3(value_part, tail_keys, 0, 0)
        t_ref[head, chunk] = transfer
        xt_out[pair, 1, chunk] = transfer
        i_ref[head, chunk] = inject
        yield
        read_keys = scale[:GROUP] * queries - mm3(reading, key_part)
        k_read_ref[head, chunk] = read_keys
        ok_out[pair, chunk] = read_keys
        v_read_ref[head, chunk] = mm3(reading, value_part)

    def final_state(pair):
        head = step * PAIR + pair
        state = jnp.zeros((DV, DK), jnp.float32)
        for chunk in range(chunks):
            state = (
                vec_ref[head, chunk, 3:4, GROUP - 1 : GROUP] * state - mm3(state, t_ref[head, chunk]) + i_ref[head, chunk]
            )
            yield
        relay_send[head] = state.astype(jnp.bfloat16)

    def readout(pair):
        head = (step - steps) * PAIR + pair
        state = jnp.where(y == 0, 0.0, 1.0) * relay_recv[head].astype(jnp.float32)
        for chunk in range(chunks):
            here = slice(chunk * GROUP, (chunk + 1) * GROUP)
            us_out[pair, 1, chunk] = state
            later = (
                vec_ref[head, chunk, 3:4, GROUP - 1 : GROUP] * state - mm3(state, t_ref[head, chunk]) + i_ref[head, chunk]
            )
            us_out[pair, 0, chunk] = u_ref[head, chunk] - mm3(w_ref[head, chunk], state, 1, 1)
            mixed = v_read_ref[head, chunk] + mm3(k_read_ref[head, chunk], state, 1, 1)
            yield
            mixed_out[pair, here, :] = mixed
            inv = lax.rsqrt(jnp.mean(mixed * mixed, axis=1, keepdims=True) + EPSILON)
            gate = silu_pair(gate_ref[pair, here, :])[0]
            gated = mixed * inv * gain_ref[0:1, :] * gate
            gated_out[here, pair * DV : (pair + 1) * DV] = gated.astype(gated_out.dtype)
            state = later

    relay = pltpu.make_async_remote_copy(
        src_ref=relay_send, dst_ref=relay_recv, send_sem=relay_sems.at[0], recv_sem=relay_sems.at[1],
        device_id=device_at(z, x, core, 1 - y), device_id_type=MESH,
    )

    @pl.when(step == 0)
    def _():
        meet(peers())

    @pl.when(step < steps)
    def _():
        def early_tick(number, carry):
            tick(number)
            return carry

        lax.fori_loop(jnp.where(step == 0, 0, step * 3 + 1), step * 3 + 2, early_tick, 0)
        together([convolve(pair) for pair in range(PAIR)])
        masks = order_masks()
        together([chunk_terms(pair, chunk, masks) for pair in range(PAIR) for chunk in range(chunks)])
        tick(step * 3 + 2)
        together([chunk_rest(pair, chunk) for pair in range(PAIR) for chunk in range(chunks)])
        together([final_state(pair) for pair in range(PAIR)])
        tick(step * 3 + 3)

    @pl.when(step == steps - 1)
    def _():
        relay.start()

    @pl.when(step == steps)
    def _():
        relay.wait()

    @pl.when(step >= steps)
    def _():
        tick(steps * 3 + 1 + step - steps)
        together([readout(pair) for pair in range(PAIR)])

    @pl.when(step == 2 * steps - 1)
    def _():
        def drain(number, carry):
            tick(number)
            return carry

        lax.fori_loop(steps * 4 + 1, max(count + SPREAD_FILL, steps * 4 + 1), drain, 0)


def held_specs(count):
    return [pl.BlockSpec(memory_space=pltpu.VMEM)] * count


def mixer_call(channels, gate, vec, masks, taps, border, gain, shard):
    parts, heads, length, width = channels.shape
    chunks = length // GROUP
    steps = H // PAIR

    def early(step):
        return jnp.minimum(step, steps - 1)

    def late(step):
        return jnp.maximum(step - steps, 0)

    def heads_spec(shape, which):
        rank = len(shape)
        return pl.BlockSpec((PAIR,) + shape, lambda step: (which(step),) + (0,) * rank)

    square = (chunks, SPAN, DK)
    anywhere = pl.BlockSpec(memory_space=pl.ANY)
    return pl.pallas_call(
        mixer_kernel,
        grid=(2 * steps,),
        out_shape=[
            per_head((2,) + square),
            per_head((chunks, GROUP, DK)),
            per_head((2,) + square),
            jax.ShapeDtypeStruct((length, H * DV), jnp.bfloat16),
            per_head((length, DV)),
            jax.ShapeDtypeStruct(STACK + shard.shape, jnp.bfloat16),
        ],
        in_specs=[
            pl.BlockSpec((parts, PAIR, length, DK), lambda step: (0, early(step), 0, 0)),
            heads_spec((length, DV), late),
        ]
        + held_specs(5)
        + [anywhere],
        out_specs=[
            heads_spec((2,) + square, early),
            heads_spec((chunks, GROUP, DK), early),
            heads_spec((2,) + square, late),
            pl.BlockSpec((length, PAIR * DV), lambda step: (0, late(step))),
            heads_spec((length, DV), late),
            anywhere,
        ],
        scratch_shapes=[pltpu.VMEM((H,) + square, jnp.float32)] * 4
        + [pltpu.VMEM((H, chunks, GROUP, DK), jnp.float32)] * 2
        + [pltpu.VMEM((H, DV, DK), jnp.bfloat16)] * 2
        + [
            pltpu.VMEM((PAIR, length + 8, DK), jnp.float32),
            pltpu.VMEM((PAIR, length, DK), jnp.float32),
            pltpu.VMEM((PAIR, NH, length, DK), jnp.float32),
            pltpu.VMEM((PAIR, NH, length, DK), jnp.float32),
            pltpu.SemaphoreType.DMA((2,)),
            pltpu.SemaphoreType.DMA((2, STAGES, RING)),
            pltpu.SemaphoreType.DMA((2, STAGES, RING)),
            pltpu.SemaphoreType.DMA((2, RING)),
        ],
        compiler_params=pltpu.CompilerParams(
            dimension_semantics=("arbitrary",), collective_id=4, has_side_effects=True, vmem_limit_bytes=58 * 1024 * 1024
        ),
        cost_estimate=pl.CostEstimate(
            flops=H * chunks * 24 * 2 * SPAN**3 * 4, bytes_accessed=80_000_000, transcendentals=0
        ),
    )(channels, gate, vec, masks, taps, border, gain, shard)


WIDE = 256
RING = 4
SPAN_TICKS = 2
REDUCE_STAGES = 5
CORE, NEAR, FAR, RINGS = 0, 1, 2, 3


class Reduce:
    def __init__(self, refs, lane, count):
        (
            self.both, self.first, self.near_kept, self.near_send, self.near,
            self.far_kept, self.far_send, self.far, self.last_kept, self.last_send, self.last,
            self.send_sem, self.recv_sem,
        ) = refs
        self.lane, self.count = lane, count
        self.z, self.x, self.core, self.y = place()
        self.peers = peers()
        self.x_first = lane == 0
        self.columns = slice(lane * WIDE, (lane + 1) * WIDE)

    def copy(self, source, target, slot_of, stage, index, device):
        lane = self.lane
        return pltpu.make_async_remote_copy(
            src_ref=source, dst_ref=target,
            send_sem=self.send_sem.at[lane, stage, lax.rem(index, 2)],
            recv_sem=self.recv_sem.at[lane, stage, lax.rem(index, RING)],
            device_id=device, device_id_type=MESH,
        )

    def core_copy(self, index):
        source = self.both.at[lax.rem(index, 2), :, :, 1 - self.core, :, :, self.columns]
        return self.copy(source, self.first.at[self.lane, lax.rem(index, RING)], None, CORE, index, self.peers[ZS + 1])

    def near_copy(self, index):
        lane = self.lane
        return self.copy(
            self.near_send.at[lane, lax.rem(index, 2)], self.near.at[lane, lax.rem(index, RING)], None, NEAR, index,
            self.peers[ZS - 1 if self.x_first else ZS],
        )

    def far_copy(self, index):
        lane = self.lane
        return self.copy(
            self.far_send.at[lane, lax.rem(index, 2)], self.far.at[lane, lax.rem(index, RING)], None, FAR, index,
            self.peers[ZS if self.x_first else ZS - 1],
        )

    def ring_copies(self, index):
        lane = self.lane
        return [
            self.copy(
                self.last_send.at[lane, lax.rem(index, 2), step], self.last.at[lane, lax.rem(index, RING), step],
                None, RINGS + step, index, self.peers[step],
            )
            for step in range(ZS - 1)
        ]

    def from_core(self, index):
        lane, slot, ring = self.lane, lax.rem(index, 2), lax.rem(index, RING)
        arrived = self.core_copy(index)
        arrived.wait_recv()
        arrived.wait_send()

        def one(z, carry):
            if self.x_first:
                pick = lambda half: self.both[slot, z, half, self.core, :, :, self.columns]
                pick_got = lambda half: self.first[lane, ring, z, half]
                mine = self.x
            else:
                pick = lambda half: self.both[slot, z, :, self.core, half, :, self.columns]
                pick_got = lambda half: self.first[lane, ring, z, :, half]
                mine = self.y
            kept = pick(mine).astype(jnp.float32) + pick_got(mine).astype(jnp.float32)
            sent = pick(1 - mine).astype(jnp.float32) + pick_got(1 - mine).astype(jnp.float32)
            self.near_kept[lane, slot, z] = kept
            self.near_send[lane, slot, z] = sent.astype(jnp.bfloat16)
            return carry

        lax.fori_loop(0, ZS, one, 0)
        self.near_copy(index).start()

    def from_near(self, index):
        lane, slot, ring = self.lane, lax.rem(index, 2), lax.rem(index, RING)
        arrived = self.near_copy(index)
        arrived.wait_recv()
        arrived.wait_send()
        mine = self.y if self.x_first else self.x

        def one(z, carry):
            kept = self.near_kept[lane, slot, z, mine] + self.near[lane, ring, z, mine].astype(jnp.float32)
            sent = self.near_kept[lane, slot, z, 1 - mine] + self.near[lane, ring, z, 1 - mine].astype(jnp.float32)
            self.far_kept[lane, slot, z] = kept
            self.far_send[lane, slot, z] = sent.astype(jnp.bfloat16)
            return carry

        lax.fori_loop(0, ZS, one, 0)
        self.far_copy(index).start()

    def from_far(self, index):
        lane, slot, ring = self.lane, lax.rem(index, 2), lax.rem(index, RING)
        arrived = self.far_copy(index)
        arrived.wait_recv()
        arrived.wait_send()

        def total(z):
            return self.far_kept[lane, slot, z] + self.far[lane, ring, z].astype(jnp.float32)

        self.last_kept[lane, slot] = total(self.z)
        for step, copy in enumerate(self.ring_copies(index)):
            self.last_send[lane, slot, step] = total(lax.rem(self.z + 1 + step, ZS)).astype(jnp.bfloat16)
            copy.start()

    def from_ring(self, index):
        lane, slot, ring = self.lane, lax.rem(index, 2), lax.rem(index, RING)
        total = self.last_kept[lane, slot]
        for step, copy in enumerate(self.ring_copies(index)):
            copy.wait_recv()
            copy.wait_send()
            total = total + self.last[lane, ring, step].astype(jnp.float32)
        return total


def reduce_scratch(rows):
    half = (2, 2, rows, WIDE)
    lanes = 2
    return [
        pltpu.VMEM((2,) + STACK + (rows, lanes * WIDE), jnp.bfloat16),
        pltpu.VMEM((lanes, RING, ZS) + half, jnp.bfloat16),
        pltpu.VMEM((lanes, 2, ZS, 2, rows, WIDE), jnp.float32),
        pltpu.VMEM((lanes, 2, ZS, 2, rows, WIDE), jnp.bfloat16),
        pltpu.VMEM((lanes, RING, ZS, 2, rows, WIDE), jnp.bfloat16),
        pltpu.VMEM((lanes, 2, ZS, rows, WIDE), jnp.float32),
        pltpu.VMEM((lanes, 2, ZS, rows, WIDE), jnp.bfloat16),
        pltpu.VMEM((lanes, RING, ZS, rows, WIDE), jnp.bfloat16),
        pltpu.VMEM((lanes, 2, rows, WIDE), jnp.float32),
        pltpu.VMEM((lanes, 2, ZS - 1, rows, WIDE), jnp.bfloat16),
        pltpu.VMEM((lanes, RING, ZS - 1, rows, WIDE), jnp.bfloat16),
        pltpu.SemaphoreType.DMA((lanes, RINGS + ZS - 1, 2)),
        pltpu.SemaphoreType.DMA((lanes, RINGS + ZS - 1, RING)),
    ]


def make_back_kernel(length, width, hidden):
    chunks = length // GROUP
    parts = 1 + 2 * NH
    blocks = hidden // WIDE
    halves = width // WIDE // 2
    down_first = blocks
    out_first = down_first + 3 * halves
    gate_first = out_first + halves
    head_first = gate_first + halves
    count = head_first + parts * (H // 2) // 2
    ticks = count + (REDUCE_STAGES - 1) * SPAN_TICKS
    rows = 32
    shard = hidden // 32
    early = blocks + 2
    late = early + H
    last = late + H
    early_tick = blocks
    late_tick = early_tick + H // 2

    def kernel(
        xt_in, ok_in, mixed_in, gate_ref, channel_ref, us_in, wg_ref, wu_ref, wd_ref,
        vec_ref, mask_ref, tap_ref, border_ref, gain_ref, out_ref, mlp_gain_ref,
        x_in, gated_in, cot_in, mix_in, normed_in,
        d_projected_out, y_out, d_hidden_out, d_normed_out,
        gain_out, d_vec_out, tap_out, mlp_gain_out, gu_out, down_out, out_out, mix_out,
        d_mixed_ref, local_ref, all_ref, relay_send, relay_recv, edge_send, edge_recv, tail_ref,
        ext_ref, pre_ref, q_ref, k_ref, inv_ref, d_ref, z_ref,
        cot_ref, left_ref, act_t_ref, right_ref, d_mixer_ref,
        relay_sems, edge_send_sem, edge_recv_sem, store_sem, load_sem, out_sem, mix_sem, *engine_refs,
    ):
        step = pl.program_id(0)
        z, x, core, y = place()
        y_peer = device_at(z, x, core, 1 - y)
        lanes = [Reduce(engine_refs, lane, count) for lane in range(2)]
        first_device = jnp.where(y == 0, 1.0, 0.0)
        halves_of_width = width // 2 // WIDE

        def wide(first):
            return pl.ds(pl.multiple_of(first, WIDE), WIDE)

        def down_item(lane, index):
            within = index - down_first
            return lane * halves_of_width + within // 3, lax.rem(within, 3)

        def mix_item(lane, index):
            within = 2 * (index - head_first) + lane
            is_gate = index < head_first
            part = jnp.where(is_gate, parts, lax.rem(within, parts))
            column = jnp.where(is_gate, 2 * (index - gate_first) + lane, within // parts) * WIDE
            return part, column

        def begin(index):
            slot = lax.rem(index, 2)
            is_down = (index >= down_first) & (index < out_first)

            def product(left):
                made = mm(left.reshape(-1, length), right_ref[...]).astype(jnp.bfloat16)
                lanes[0].both[slot] = made.reshape(STACK + (rows, 2 * WIDE))

            def pair(column):
                return pl.ds(pl.multiple_of(column * 2 * WIDE, 2 * WIDE), 2 * WIDE)

            @pl.when(is_down)
            def _():
                for lane in range(2):
                    right_ref[:, lane * WIDE : (lane + 1) * WIDE] = cot_ref[:, wide(down_item(lane, index)[0] * WIDE)]
                here = pl.ds(pl.multiple_of(down_item(0, index)[1] * rows, rows), rows)
                product(act_t_ref[:, :, :, :, here, :])

            @pl.when((index >= out_first) & (index < gate_first))
            def _():
                right_ref[...] = d_mixer_ref[:, pair(index - out_first)]

            @pl.when((index >= gate_first) & (index < head_first))
            def _():
                right_ref[...] = all_ref[parts, :, pair(index - gate_first)]

            @pl.when(index >= head_first)
            def _():
                for lane in range(2):
                    part, column = mix_item(lane, index)
                    right_ref[:, lane * WIDE : (lane + 1) * WIDE] = all_ref[part, :, wide(column)]

            @pl.when(jnp.logical_not(is_down))
            def _():
                product(left_ref[jnp.where(index < down_first, 0, jnp.where(index < gate_first, 1, 2))])

            for engine in lanes:
                engine.core_copy(index).start()

        def end(lane, index):
            total = lanes[lane].from_ring(index)

            @pl.when(index < down_first)
            def _():
                gu_out[:, wide(lane * hidden + index * WIDE)] = total

            @pl.when((index >= down_first) & (index < out_first))
            def _():
                column, block = down_item(lane, index)
                down_out[block, :, wide(column * WIDE)] = total

            @pl.when((index >= out_first) & (index < gate_first))
            def _():
                out_out[:, wide((2 * (index - out_first) + lane) * WIDE)] = total

            @pl.when(index >= gate_first)
            def _():
                part, column = mix_item(lane, index)
                mix_out[:, wide(part * (H * DK) + column)] = total

        def tick(number):
            for stage in reversed(range(REDUCE_STAGES)):
                index = number - stage * SPAN_TICKS

                @pl.when((index >= 0) & (index < count))
                def _():
                    if stage == 0:
                        begin(index)
                    for lane, engine in enumerate(lanes):
                        if stage == 1:
                            engine.from_core(index)
                        elif stage == 2:
                            engine.from_near(index)
                        elif stage == 3:
                            engine.from_far(index)
                        elif stage == 4:
                            end(lane, index)

        def transposed(values):
            flipped = jnp.transpose(values.astype(jnp.float32)).astype(jnp.bfloat16)
            return flipped.reshape(STACK + (rows, length))

        def head_slices():
            return [slice(head * DV, (head + 1) * DV) for head in range(H)]

        def joined(ref, first):
            quarter = length // SPAN
            return jnp.concatenate(
                [ref[head, first * quarter : (first + 1) * quarter].reshape(length, DV) for head in range(H)], axis=1
            )

        def split(ref, first, values):
            quarter = length // SPAN
            for head, here in enumerate(head_slices()):
                ref[head, first * quarter : (first + 1) * quarter] = values[:, here].reshape(quarter, SPAN, DV)

        def enter_mlp():
            loads = [
                pltpu.make_async_copy(source, target, load_sem.at[index])
                for index, (source, target) in enumerate(
                    ((gated_in, all_ref.at[1]), (x_in, all_ref.at[0]), (cot_in, cot_ref), (normed_in, left_ref.at[2]))
                )
            ]
            for load in loads:
                load.start()
            for load in loads:
                load.wait()
            split(local_ref, 1, mm(all_ref[1], out_ref[...]))
            quarter = length // SPAN

            def one(index, carry):
                here = pl.ds(pl.multiple_of(index * SPAN, SPAN), SPAN)
                mixed_rows = jnp.concatenate([local_ref[head, quarter + index] for head in range(H)], axis=1)
                hidden_rows = all_ref[0, here].astype(jnp.float32) + mixed_rows
                inv = lax.rsqrt(jnp.mean(hidden_rows * hidden_rows, axis=1, keepdims=True) + EPSILON)
                all_ref[3, here] = (hidden_rows * inv * mlp_gain_ref[0:1, :]).astype(jnp.bfloat16)
                for head, columns in enumerate(head_slices()):
                    local_ref[head, index] = hidden_rows[:, columns]
                    local_ref[head, quarter + index] = hidden_rows[:, columns]
                return carry

            lax.fori_loop(0, quarter, one, 0)
            d_mixed_ref[...] = jnp.zeros_like(d_mixed_ref)
            left_ref[0] = transposed(all_ref[3])

        def mlp_block(block):
            mlp_in = all_ref[3]
            gate = mm(mlp_in, wg_ref[...])
            up = mm(mlp_in, wu_ref[...])
            open_, sig = silu_pair(gate)
            act = (open_ * up).astype(jnp.bfloat16)
            d_act = mm(cot_ref[...], wd_ref[...], 1, 1)
            d_gate = (d_act * up * sig * (1.0 + gate * (1.0 - sig))).astype(jnp.bfloat16)
            d_up = (d_act * open_).astype(jnp.bfloat16)
            right_ref[:, :WIDE] = d_gate
            right_ref[:, WIDE:] = d_up
            split(local_ref, 0, joined(local_ref, 0) + mm(act, wd_ref[...]))
            d_in = mm(d_gate, wg_ref[...], 1, 1) + mm(d_up, wu_ref[...], 1, 1)
            for head, here in enumerate(head_slices()):
                d_mixed_ref[head] = d_mixed_ref[head] + d_in[:, here]
            act_t = jnp.transpose(act.astype(jnp.float32))
            for group in range(WIDE // 8):
                place_ = block * (WIDE // 8) + group
                owner, row = place_ // (shard // 8), lax.rem(place_, shard // 8) * 8
                act_t_ref[
                    owner // 8, lax.rem(owner // 4, 2), lax.rem(owner // 2, 2), lax.rem(owner, 2),
                    pl.ds(pl.multiple_of(row, 8), 8), :,
                ] = act_t[group * 8 : (group + 1) * 8]

        y_store = pltpu.make_async_copy(all_ref.at[0], y_out, out_sem.at[0])

        def leave_mlp():
            quarter = length // SPAN

            def tile(ref, first, index):
                return jnp.concatenate([ref[head, first * quarter + index] for head in range(H)], axis=1)

            def one(index, gain_grad):
                here = pl.ds(pl.multiple_of(index * SPAN, SPAN), SPAN)
                all_ref[0, here] = tile(local_ref, 0, index).astype(jnp.bfloat16)
                hidden_rows = tile(local_ref, 1, index)
                d_in = jnp.concatenate([d_mixed_ref[head, here] for head in range(H)], axis=1)
                inv = lax.rsqrt(jnp.mean(hidden_rows * hidden_rows, axis=1, keepdims=True) + EPSILON)
                unit = hidden_rows * inv
                d_unit = d_in * mlp_gain_ref[0:1, :]
                d_norm = inv * (d_unit - unit * jnp.mean(d_unit * unit, axis=1, keepdims=True))
                d_hidden = cot_ref[here].astype(jnp.float32) + d_norm
                for head, columns in enumerate(head_slices()):
                    local_ref[head, quarter + index] = d_hidden[:, columns]
                d_mixer_ref[here] = d_hidden.astype(jnp.bfloat16)
                return gain_grad + jnp.sum(d_in * unit, axis=0, keepdims=True)

            gain_grad = lax.fori_loop(0, quarter, one, jnp.zeros((1, width), jnp.float32))
            mlp_gain_out[...] = jnp.broadcast_to(gain_grad, (8, width))
            y_store.start()
            stores = [
                pltpu.make_async_copy(
                    local_ref.at[head, quarter : 2 * quarter], d_hidden_out.at[:, :, here], out_sem.at[1 + head]
                )
                for head, here in enumerate(head_slices())
            ]
            for store in stores:
                store.start()
            d_normed_rows = mm(d_mixer_ref[...], out_ref[...], 1, 1)
            for head, here in enumerate(head_slices()):
                d_mixed_ref[head] = d_normed_rows[:, here]
            for store in stores:
                store.wait()

        def readout_back(head):
            gain = gain_ref[0:1, :]
            gain_grad = jnp.zeros((1, DV), jnp.float32)
            column = pl.ds(pl.multiple_of(head * DV, DV), DV)
            state = jnp.zeros((DV, DK), jnp.float32)
            for chunk in reversed(range(chunks)):
                here = slice(chunk * GROUP, (chunk + 1) * GROUP)
                mixed = mixed_in[0, here, :]
                inv = lax.rsqrt(jnp.mean(mixed * mixed, axis=1, keepdims=True) + EPSILON)
                unit = mixed * inv
                gate = gate_ref[0, here, :]
                open_, sig = silu_pair(gate)
                d_gated = d_mixed_ref[head, here]
                d_scaled = d_gated * open_
                d_gate = d_gated * unit * gain * sig * (1.0 + gate * (1.0 - sig))
                all_ref[parts, here, column] = d_gate.astype(jnp.bfloat16)
                gain_grad = gain_grad + jnp.sum(d_scaled * unit, axis=0, keepdims=True)
                d_unit = d_scaled * gain
                d_mixed = inv * (d_unit - unit * jnp.mean(d_unit * unit, axis=1, keepdims=True))
                d_mixed_ref[head, here] = d_mixed
                local = mm3(d_mixed, ok_in[0, chunk], 0, 0)
                local_ref[head, chunk] = local
                state = (
                    vec_ref[head, chunk, 3:4, GROUP - 1 : GROUP] * state
                    - mm3(state, xt_in[0, 1, chunk], 1, 1)
                    + local
                )
            gain_out[head] = jnp.broadcast_to(gain_grad, (8, DV))
            relay_send[head] = state.astype(jnp.bfloat16)

        def head_columns(part, head):
            return pl.ds(pl.multiple_of((part * H + head) * DK, DK), DK)

        def prepare(head):
            for part in range(parts):
                here = head_columns(part, head)
                pre = conv_block(channel_ref[part], border_ref[:, here], tap_ref[:, here], mask_ref, ext_ref.at[part])
                yield
                pre_ref[part] = pre
                if part > NH:
                    continue
                value = silu_pair(pre)[0]
                if part == 0:
                    unit, inv = unit_rows(value)
                    q_ref[...] = unit * DK ** (-0.5)
                    inv_ref[:, 0:1] = inv
                else:
                    unit, inv = unit_rows(value)
                    k_ref[part - 1] = unit
                    inv_ref[:, part : part + 1] = inv

        def chain(head, exit_grads):
            grad = first_device * relay_recv[head].astype(jnp.float32)
            for chunk in reversed(range(chunks)):
                exit_grads[chunk] = grad
                grad = (
                    vec_ref[head, chunk, 3:4, GROUP - 1 : GROUP] * grad
                    - mm3(grad, xt_in[0, 1, chunk], 1, 1)
                    + local_ref[head, chunk]
                )
                yield

        def one_chunk(chunk, head, d_exit):
            strict = order_masks()[0]
            column_index = iotas(SPAN, 8)[1]
            here = slice(chunk * GROUP, (chunk + 1) * GROUP)
            rows_ = vec_ref[head, chunk]
            columns = jnp.transpose(rows_)
            beta, scale, tail = columns[:, 1:2], columns[:, 3:4], columns[:, 4:5]
            keys = k_ref[:, here, :].reshape(SPAN, DK)
            values = silu_pair(pre_ref[1 + NH :, here, :].reshape(SPAN, DV))[0]
            queries = q_ref[here, :]
            link = link_matrix(rows_, columns)
            link_gram = jnp.where(strict, twice(link) * mm3(keys, keys, 1, 1), 0.0)
            yield
            reading = link * mm3(queries, keys, 1, 1)
            yield
            solved = us_in[0, 0, chunk]
            entry = us_in[0, 1, chunk]
            d_mixed = d_mixed_ref[head, here]
            tail_keys = tail * keys
            d_solved = mm3(reading, d_mixed, 0, 0)
            yield
            d_solved = d_solved + mm3(tail_keys, d_exit, 1, 1)
            yield
            d_right = mm3(xt_in[0, 0, chunk], d_solved, 0, 0)
            yield
            d_lower = jnp.where(strict, -mm3(d_right, solved, 1, 1), 0.0)
            yield
            d_tail_keys = mm3(solved, d_exit)
            yield
            d_right_entry = mm3(d_right, entry)
            yield
            d_reading = mm3(d_mixed, solved, 1, 1)
            yield
            d_query_entry = mm3(d_mixed, entry)
            yield
            both_scale = -jnp.sum(d_right_entry * keys, axis=1, keepdims=True)
            yield
            lower_weight = d_lower * link_gram
            d_beta = (
                jnp.sum(d_right * values, axis=1, keepdims=True)
                + scale * both_scale
                + jnp.sum(lower_weight, axis=1, keepdims=True)
            )
            lower_moment = lower_weight * beta
            yield
            reading_moment = d_reading * reading
            d_gram = beta * twice(link) * d_lower
            d_gram = d_gram + jnp.transpose(d_gram)
            yield
            d_query_gram = link * d_reading
            d_keys = (
                tail * d_tail_keys
                - beta * scale * d_right_entry
                + mm(d_gram, keys)
                + mm(d_query_gram, queries, 0, 0)
            )
            d_queries = mm(d_query_gram, keys) + scale[:GROUP] * d_query_entry
            d_values = beta * d_right
            yield
            none = jnp.zeros((GROUP, 1), jnp.float32)
            d_gap = jnp.sum(lower_moment, axis=1, keepdims=True) + jnp.concatenate(
                [jnp.sum(reading_moment, axis=1, keepdims=True), none], axis=0
            )
            last = jnp.sum(jnp.sum(d_exit * entry, axis=1, keepdims=True), axis=0, keepdims=True)
            own_scale = jnp.sum(d_query_entry * queries, axis=1, keepdims=True)
            own_scale = own_scale + jnp.where(iotas(GROUP, 1)[0] == GROUP - 1, last, 0.0)
            d_scale = beta * both_scale + jnp.concatenate([own_scale, none], axis=0)
            d_tail = jnp.sum(d_tail_keys * keys, axis=1, keepdims=True)
            grads = jnp.where(
                column_index == 0,
                d_gap,
                jnp.where(
                    column_index == 1,
                    d_beta,
                    jnp.where(column_index == 3, d_scale, jnp.where(column_index == 4, d_tail, 0.0)),
                ),
            )
            grads = jnp.transpose(grads)
            sums = jnp.sum(lower_moment, axis=0, keepdims=True) + jnp.sum(reading_moment, axis=0, keepdims=True)
            d_vec_out[head, chunk] = grads - jnp.where(iotas(8, SPAN)[0] == 0, sums, 0.0)
            d_ref[0, here, :] = d_queries
            for house in range(NH):
                mine = slice(house * GROUP, (house + 1) * GROUP)
                d_ref[1 + house, here, :] = d_keys[mine]
                d_ref[1 + NH + house, here, :] = d_values[mine]

        def finish_head(head):
            column = pl.ds(pl.multiple_of(head * DK, DK), DK)
            z_ref[0:8, :] = jnp.zeros((8, DK), jnp.float32)
            z_ref[8 + length : 16 + length, :] = jnp.zeros((8, DK), jnp.float32)
            for part in range(parts):
                grad = d_ref[part]
                if part <= NH:
                    unit = q_ref[...] * DK ** 0.5 if part == 0 else k_ref[part - 1]
                    if part == 0:
                        grad = grad * DK ** (-0.5)
                    grad = inv_ref[:, part : part + 1] * (grad - unit * jnp.sum(grad * unit, axis=1, keepdims=True))
                pre = pre_ref[part]
                sig = jax.nn.sigmoid(pre)
                grad = grad * sig * (1.0 + pre * (1.0 - sig))
                here = head_columns(part, head)
                tap = tap_ref[:, here]
                total = grad * tap[0:1, :]
                edge = jnp.zeros((8, DK), jnp.float32)
                tap_rows = [jnp.sum(grad * channel_ref[part], axis=0, keepdims=True)]
                for index in range(1, 4):
                    shifted = grad * mask_ref[index - 1].astype(jnp.float32)
                    tap_rows.append(
                        jnp.sum(shifted * ext_ref[part, 8 - index : 8 - index + length, :], axis=0, keepdims=True)
                    )
                    z_ref[8 : 8 + length, :] = shifted * tap[index : index + 1, :]
                    total = total + z_ref[8 + index : 8 + index + length, :]
                    edge = edge + z_ref[index : index + 8, :]
                all_ref[part, :, column] = total.astype(jnp.bfloat16)
                edge_send[lax.rem(head, 2), part] = edge
                tail_ref[part] = total[length - 16 :, :]
                tap_out[:, here] = jnp.concatenate(tap_rows + [jnp.zeros((4, DK), jnp.float32)], axis=0)

        @pl.when(step == 0)
        def _():
            meet(peers())
            enter_mlp()

        @pl.when((step >= 1) & (step <= blocks))
        def _():
            mlp_block(step - 1)

            @pl.when(step == 2)
            def _():
                left_ref[1] = transposed(all_ref[1])
                act_t_ref[:, :, :, :, shard:, :] = jnp.zeros(STACK + (act_t_ref.shape[4] - shard, length), jnp.float32)

        @pl.when(step == blocks + 1)
        def _():
            leave_mlp()

        early_head = step - early

        @pl.when((step >= early) & (step < late))
        def _():
            readout_back(early_head)

        relay = pltpu.make_async_remote_copy(
            src_ref=relay_send, dst_ref=relay_recv, send_sem=relay_sems.at[0], recv_sem=relay_sems.at[1],
            device_id=y_peer, device_id_type=MESH,
        )

        @pl.when(step == late - 1)
        def _():
            relay.start()

        @pl.when(step == late)
        def _():
            relay.wait()
            y_store.wait()

        def edge_copy(head):
            slot = lax.rem(head, 2)
            return pltpu.make_async_remote_copy(
                src_ref=edge_send.at[slot], dst_ref=edge_recv.at[slot], send_sem=edge_send_sem.at[slot],
                recv_sem=edge_recv_sem.at[slot], device_id=y_peer, device_id_type=MESH,
            )

        def fix_edges(head):
            edge_copy(head).wait()
            here = pl.ds(pl.multiple_of(head * DK, DK), DK)
            for part in range(parts):
                fixed = tail_ref[part, 8:16] + first_device * edge_recv[lax.rem(head, 2), part]
                both = jnp.concatenate([tail_ref[part, 0:8], fixed], axis=0)
                all_ref[part, length - 16 : length, here] = both.astype(jnp.bfloat16)

        @pl.when((step >= late) & (step < last))
        def _():
            head = step - late
            exit_grads = [None] * chunks
            together([chain(head, exit_grads), prepare(head)])

            @pl.when(head > 0)
            def _():
                fix_edges(head - 1)

            tick(late_tick + jnp.minimum(2 * head, head + 5))
            together([one_chunk(chunk, head, exit_grads[chunk]) for chunk in reversed(range(chunks))])

            finish_head(head)
            edge_copy(head).start()

        late_head = step - late
        in_mlp = (step >= 1) & (step <= blocks)
        in_early = (step >= early) & (step < late) & (lax.rem(early_head, 2) == 0)
        in_late = (late_head >= 0) & (late_head < 5)
        number = jnp.where(
            in_mlp, step - 1, jnp.where(in_early, early_tick + early_head // 2, late_tick + 2 * late_head + 1)
        )

        @pl.when(in_mlp | in_early | in_late)
        def _():
            tick(number)

        @pl.when(step == last)
        def _():
            fix_edges(H - 1)
            stores = [
                pltpu.make_async_copy(
                    all_ref.at[part], d_projected_out.at[:, pl.ds(part * H * DK, H * DK)], store_sem.at[part]
                )
                for part in range(parts + 1)
            ]
            for store in stores:
                store.start()
            loads = mix_in.shape[5] // length

            def load(index):
                here = pl.ds(pl.multiple_of(index * length, length), length)
                slot = lax.rem(index, 2)
                return pltpu.make_async_copy(mix_in.at[:, :, :, :, :, here], left_ref.at[slot], mix_sem.at[slot])

            load(0).start()
            load(1).start()
            d_mixed_ref[...] = jnp.zeros_like(d_mixed_ref)
            per_part = H * DK // length

            d_normed_stores = [
                pltpu.make_async_copy(d_mixed_ref.at[head], d_normed_out.at[:, here], out_sem.at[head])
                for head, here in enumerate(head_slices())
            ]

            def drain(turn, carry):
                tick(late_tick + H + 5 + turn)

                @pl.when(turn < loads // 2)
                def _():
                    for slot in range(2):
                        index = 2 * turn + slot
                        load(index).wait()
                        here = pl.ds(pl.multiple_of(lax.rem(index, per_part) * length, length), length)
                        left = all_ref[index // per_part, :, here]
                        added = mm(left, left_ref[slot].reshape(-1, length), 1, 1)
                        for head, place_ in enumerate(head_slices()):
                            d_mixed_ref[head] = d_mixed_ref[head] + added[:, place_]

                        @pl.when(index + 2 < loads)
                        def _():
                            load(index + 2).start()

                @pl.when(turn == loads // 2)
                def _():
                    for store in d_normed_stores:
                        store.start()

                return carry

            turns = ticks - (late_tick + H + 5)
            assert turns > loads // 2
            lax.fori_loop(0, turns, drain, 0)
            stores.extend(d_normed_stores)
            for store in stores:
                store.wait()

    return kernel, ticks


def back_call(
    xt, out_keys, mixed, gate, channels, us, gu, down, vec, masks, taps, border, gain, out, mlp_gain,
    x, gated, cot, mix, normed_t,
):
    parts, heads, length, width = channels.shape
    chunks = length // GROUP
    model, hidden = gu.shape[0], down.shape[0]
    rows, blocks = 32, hidden // WIDE
    padded = -(-(hidden // 32) // rows) * rows
    kernel, ticks = make_back_kernel(length, model, hidden)
    first = blocks + 2

    def either(step):
        return lax.rem(jnp.maximum(step - first, 0), H)

    def early(step):
        return jnp.clip(step - first, 0, H - 1)

    def late(step):
        return jnp.clip(step - first - H, 0, H - 1)

    def block(step):
        return jnp.clip(step - 1, 0, blocks - 1)

    def heads_spec(shape, which):
        rank = len(shape)
        return pl.BlockSpec((1,) + shape, lambda step: (which(step),) + (0,) * rank)

    square = (chunks, SPAN, DK)
    anywhere = pl.BlockSpec(memory_space=pl.ANY)
    in_specs = (
        [
            heads_spec((2,) + square, either), heads_spec((chunks, GROUP, DK), early), heads_spec((length, DV), early),
            heads_spec((length, DV), early),
            pl.BlockSpec((parts, None, length, DK), lambda step: (0, late(step), 0, 0)), heads_spec((2,) + square, late),
            pl.BlockSpec((model, WIDE), lambda step: (0, block(step))),
            pl.BlockSpec((model, WIDE), lambda step: (0, blocks + block(step))),
            pl.BlockSpec((WIDE, model), lambda step: (block(step), 0)),
        ]
        + held_specs(7)
        + [anywhere] * 5
    )
    out_shape = [
        jax.ShapeDtypeStruct((length, (parts + 1) * H * DK), jnp.bfloat16),
        jax.ShapeDtypeStruct((length, model), jnp.bfloat16),
        jax.ShapeDtypeStruct((length // SPAN, SPAN, model), jnp.float32),
        jax.ShapeDtypeStruct((length, model), jnp.float32),
        per_head((8, DV)),
        per_head((chunks, 8, SPAN)),
        jax.ShapeDtypeStruct((8, parts * H * DK), jnp.float32),
        jax.ShapeDtypeStruct((8, model), jnp.float32),
        jax.ShapeDtypeStruct((rows, gu.shape[1]), jnp.float32),
        jax.ShapeDtypeStruct((padded // rows, rows, model), jnp.float32),
        jax.ShapeDtypeStruct((rows, model), jnp.float32),
        jax.ShapeDtypeStruct((rows, (parts + 1) * H * DK), jnp.float32),
    ]
    tall = pltpu.VMEM((parts, length, DK), jnp.float32)
    scratch = [
        pltpu.VMEM((H, length, DV), jnp.float32),
        pltpu.VMEM((H,) + square, jnp.float32),
        pltpu.VMEM((parts + 1, length, H * DK), jnp.bfloat16),
        pltpu.VMEM((H, DV, DK), jnp.bfloat16),
        pltpu.VMEM((H, DV, DK), jnp.bfloat16),
        pltpu.VMEM((2, parts, 8, DK), jnp.float32),
        pltpu.VMEM((2, parts, 8, DK), jnp.float32),
        pltpu.VMEM((parts, 16, DK), jnp.float32),
        pltpu.VMEM((parts, length + 8, DK), jnp.float32),
        tall,
        pltpu.VMEM((length, DK), jnp.float32),
        pltpu.VMEM((NH, length, DK), jnp.float32),
        pltpu.VMEM((length, DK), jnp.float32),
        tall,
        pltpu.VMEM((length + 16, DK), jnp.float32),
        pltpu.VMEM((length, model), jnp.bfloat16),
        pltpu.VMEM((3,) + STACK + (rows, length), jnp.bfloat16),
        pltpu.VMEM(STACK + (padded, length), jnp.float32),
        pltpu.VMEM((length, 2 * WIDE), jnp.bfloat16),
        pltpu.VMEM((length, model), jnp.bfloat16),
        pltpu.SemaphoreType.DMA((2,)),
        pltpu.SemaphoreType.DMA((2,)),
        pltpu.SemaphoreType.DMA((2,)),
        pltpu.SemaphoreType.DMA((parts + 1,)),
        pltpu.SemaphoreType.DMA((4,)),
        pltpu.SemaphoreType.DMA((1 + H,)),
        pltpu.SemaphoreType.DMA((2,)),
    ] + reduce_scratch(rows)
    return pl.pallas_call(
        kernel,
        grid=(first + 2 * H + 1,),
        out_shape=out_shape,
        in_specs=in_specs,
        out_specs=[anywhere] * 4 + held_specs(len(out_shape) - 4),
        scratch_shapes=scratch,
        compiler_params=pltpu.CompilerParams(
            dimension_semantics=("arbitrary",), collective_id=2, has_side_effects=True, vmem_limit_bytes=MOST
        ),
        cost_estimate=pl.CostEstimate(
            flops=H * chunks * 14 * 2 * SPAN**3 * 4, bytes_accessed=100_000_000, transcendentals=0
        ),
    )(
        xt, out_keys, mixed, gate, channels, us, gu, gu, down, vec, masks, taps, border, gain, out, mlp_gain,
        x, gated, cot, mix, normed_t,
    )


def total_kernel(
    packed_ref, sums_ref, packed_out, sums_out, first, near, far, last, kept, low, pair, ring, send, recv
):
    z, x, core, y = place()
    targets = peers()
    meet(targets)

    def copy(source, target, slot, device):
        made = pltpu.make_async_remote_copy(
            src_ref=source, dst_ref=target, send_sem=send.at[slot], recv_sem=recv.at[slot],
            device_id=device, device_id_type=MESH,
        )
        made.start()
        return made

    def swap(source, target, index, device):
        pair[2 * index] = sums_out[...]
        copies = [
            copy(source, target, 2 * index, device),
            copy(pair.at[2 * index], pair.at[2 * index + 1], 2 * index + 1, device),
        ]
        for made in copies:
            made.wait()
        sums_out[...] = sums_out[...] + pair[2 * index + 1]

    sums_out[...] = sums_ref[...]
    low[...] = packed_ref[:, :, 1 - core].astype(jnp.bfloat16)
    swap(low, first, 0, targets[ZS + 1])
    kept[...] = packed_ref[:, :, core] + first[...].astype(jnp.float32)
    low[:, 0] = kept[:, 1 - x].astype(jnp.bfloat16)
    swap(low.at[:, 0], near, 1, targets[ZS - 1])
    kept[:, 0] = kept[:, x] + near[...].astype(jnp.float32)
    low[:, 0, 0] = kept[:, 0, 1 - y].astype(jnp.bfloat16)
    swap(low.at[:, 0, 0], far, 2, targets[ZS])
    kept[:, 0, 0] = kept[:, 0, y] + far[...].astype(jnp.float32)
    low[:, 0, 0] = kept[:, 0, 0].astype(jnp.bfloat16)
    ring[z] = sums_out[...]
    copies = []
    for step in range(ZS - 1):
        other = lax.rem(z + 1 + step, ZS)
        copies.append(copy(low.at[other, 0, 0], last.at[step], 6 + 2 * step, targets[step]))
        copies.append(copy(ring.at[z], ring.at[z], 7 + 2 * step, targets[step]))
    for made in copies:
        made.wait()
    packed_out[...] = kept[z, 0, 0] + sum(last[step].astype(jnp.float32) for step in range(ZS - 1))
    sums_out[...] = ring[0] + ring[1] + ring[2] + ring[3]


def total_call(packed, sums):
    rows, wide = packed.shape[4], packed.shape[5]
    held = pl.BlockSpec(memory_space=pltpu.VMEM)
    return pl.pallas_call(
        total_kernel,
        out_shape=[jax.ShapeDtypeStruct((rows, wide), jnp.float32), jax.ShapeDtypeStruct(sums.shape, jnp.float32)],
        in_specs=[held, held],
        out_specs=[held, held],
        scratch_shapes=[
            pltpu.VMEM((ZS, 2, 2, rows, wide), jnp.bfloat16),
            pltpu.VMEM((ZS, 2, rows, wide), jnp.bfloat16),
            pltpu.VMEM((ZS, rows, wide), jnp.bfloat16),
            pltpu.VMEM((ZS - 1, rows, wide), jnp.bfloat16),
            pltpu.VMEM((ZS, 2, 2, rows, wide), jnp.float32),
            pltpu.VMEM((ZS, 2, 2, rows, wide), jnp.bfloat16),
            pltpu.VMEM((6,) + sums.shape, jnp.float32),
            pltpu.VMEM((ZS,) + sums.shape, jnp.float32),
            pltpu.SemaphoreType.DMA((12,)),
            pltpu.SemaphoreType.DMA((12,)),
        ],
        compiler_params=pltpu.CompilerParams(collective_id=3, has_side_effects=True, vmem_limit_bytes=LIMIT),
        cost_estimate=pl.CostEstimate(flops=1000000, bytes_accessed=2_000_000, transcendentals=0),
    )(packed, sums)


def from_behind(block, axis, distance):
    devices = range(lax.axis_size(axis))
    route = [(i - distance, i) for i in devices if i - distance in devices]
    return lax.ppermute(block, axis, route)


def rms_scale(values, scale_gain):
    return (
        values * lax.rsqrt(jnp.mean(values * values, axis=-1, keepdims=True) + EPSILON) * scale_gain
    )


def swiglu(gate_up):
    half_width = gate_up.shape[-1] // 2
    return jax.nn.silu(gate_up[:, :half_width]) * gate_up[:, half_width:]


def exchange(block, axis, bit):
    route = [(i, i ^ (1 << bit)) for i in range(lax.axis_size(axis))]
    return lax.ppermute(block, axis, route)


def axis_bits(axis):
    return lax.axis_size(axis).bit_length() - 1


def bit_orders():
    dp_bits = [("dp", bit) for bit in range(axis_bits("dp"))]
    seq_bits = [("seq", bit) for bit in range(axis_bits("seq"))]
    first, rest = dp_bits[:1], dp_bits[1:]
    inner = rest[:1] + seq_bits[:1]
    outer = rest[1:] + seq_bits[1:]
    return first + inner + outer, first + inner[::-1] + outer


def scatter_sum(part, order):
    dp_bits, seq_bits = axis_bits("dp"), axis_bits("seq")
    dims = [("dp", bit) for bit in reversed(range(dp_bits))] + [("seq", bit) for bit in reversed(range(seq_bits))]
    rows = part.shape[0] >> len(dims)
    part = part.reshape((2,) * len(dims) + (rows, part.shape[1]))
    for axis, bit in order:
        place = dims.index((axis, bit))
        dims.pop(place)
        mine = (lax.axis_index(axis) >> bit) & 1
        sent = lax.dynamic_index_in_dim(part, 1 - mine, place, keepdims=False)
        kept = lax.dynamic_index_in_dim(part, mine, place, keepdims=False)
        got = exchange(sent.astype(jnp.bfloat16), axis, bit)
        part = kept.astype(jnp.float32) + got.astype(jnp.float32)
    return part


def scatter_halves(part):
    half = part.shape[1] // 2
    orders = bit_orders()
    return jnp.concatenate(
        [scatter_sum(part[:, :half], orders[0]), scatter_sum(part[:, half:], orders[1])], axis=1
    )


def total_sum(block):
    for axis in ("dp", "seq"):
        for bit in range(axis_bits(axis)):
            block = block + exchange(block, axis, bit)
    return block


def gate_vectors(seg_now, seg_prev, gates_raw, decay_log):
    length = gates_raw.shape[0]
    chunks = length // GROUP
    beta = jax.nn.sigmoid(gates_raw[:, : NH * H]).reshape(chunks, GROUP, NH, H)
    rate = -jnp.exp(decay_log) * jax.nn.softplus(gates_raw[:, NH * H :])
    lower = jnp.tril(jnp.ones((GROUP, GROUP), jnp.float32))
    total = jnp.einsum("ts,csh->cth", lower, rate.reshape(chunks, GROUP, H), precision=HIGHEST)
    seg = seg_now.reshape(chunks, GROUP)
    before = jnp.concatenate([seg_prev.reshape(1), seg[:-1, -1]])
    scale = jnp.exp(total) * (seg == before[:, None]).astype(jnp.float32)[:, :, None]
    tail = jnp.exp(total[:, -1:, :] - total) * (seg == seg[:, -1:]).astype(jnp.float32)[:, :, None]

    def both(values):
        moved = jnp.moveaxis(values, 2, 0)
        return jnp.concatenate([moved, moved], axis=-1)

    beta_rows = beta.transpose(3, 0, 2, 1).reshape(H, chunks, SPAN)
    seg_rows = jnp.broadcast_to(jnp.concatenate([seg, seg], axis=1).astype(jnp.float32), (H, chunks, SPAN))
    none = jnp.zeros((H, chunks, SPAN), jnp.float32)
    return jnp.stack([both(total), beta_rows, seg_rows, both(scale), both(tail), none, none, none], axis=2)


def head_spec(shape):
    rank = len(shape)
    return pl.BlockSpec((1,) + shape, lambda head: (head,) + (0,) * rank)


def column_spec(rows, first):
    return pl.BlockSpec((rows, DK), lambda head: (0, first + head))


def whole_spec(shape):
    rank = len(shape)
    return pl.BlockSpec(shape, lambda head: (0,) * rank)


def per_head(shape, dtype=jnp.float32):
    return jax.ShapeDtypeStruct((H,) + shape, dtype)


def call(kernel, out_shape, in_specs, out_specs, scratch, flops, bytes_accessed):
    return pl.pallas_call(
        kernel,
        grid=(H,),
        out_shape=out_shape,
        in_specs=in_specs,
        out_specs=out_specs,
        scratch_shapes=scratch,
        compiler_params=pltpu.CompilerParams(
            dimension_semantics=("arbitrary",), vmem_limit_bytes=LIMIT
        ),
        cost_estimate=pl.CostEstimate(flops=flops, bytes_accessed=bytes_accessed, transcendentals=0),
    )


def conv_specs(length):
    return (
        [column_spec(length, H * part) for part in range(1 + 2 * NH)]
        + [column_spec(8, H * part) for part in range(1 + 2 * NH)] * 2
        + [whole_spec((3, length, DK))]
    )


def forward_call(projected, border, taps, masks, vec, start):
    length = projected.shape[0]
    chunks = length // GROUP
    square = (chunks, SPAN, DK)
    outs = [
        (square, jnp.float32),
        (square, jnp.float32),
        (square, jnp.float32),
        (square, jnp.float32),
        (square, jnp.float32),
        ((chunks, GROUP, DK), jnp.float32),
        ((chunks, GROUP, DV), jnp.float32),
        ((DV, DK), jnp.float32),
    ]
    parts = 1 + 2 * NH
    return call(
        forward_kernel,
        [per_head(*out) for out in outs],
        conv_specs(length) + [head_spec((chunks, 8, SPAN)), head_spec((DV, DK))],
        [head_spec(out[0]) for out in outs],
        [
            pltpu.VMEM((length + 8, DK), jnp.float32),
            pltpu.VMEM((length, DK), jnp.float32),
            pltpu.VMEM((NH, length, DK), jnp.float32),
            pltpu.VMEM((NH, length, DK), jnp.float32),
        ],
        H * chunks * 20 * 2 * SPAN**3 * 4,
        H * chunks * 8 * SPAN * DK * 4,
    )(*[projected] * parts, *[border] * parts, *[taps] * parts, masks, vec, start)


def chain_call(vec, transfer, start):
    chunks = transfer.shape[1]
    return call(
        chain_kernel,
        per_head((DV, DK)),
        [head_spec((chunks, 8, SPAN)), head_spec((chunks, SPAN, DK)), head_spec((DV, DK))],
        head_spec((DV, DK)),
        [],
        H * chunks * 2 * SPAN**3,
        H * chunks * SPAN * DK * 4,
    )(vec, transfer, start)


def readout_call(vec, key_part, value_part, transfer, inject, out_keys, out_values, entry, projected, gain):
    length = projected.shape[0]
    chunks = length // GROUP
    square = head_spec((chunks, SPAN, DK))
    half = head_spec((chunks, GROUP, DK))
    return call(
        readout_kernel,
        [
            jax.ShapeDtypeStruct((length, H * DV), jnp.bfloat16),
            jax.ShapeDtypeStruct((length, H * DV), jnp.float32),
            per_head((chunks, SPAN, DK)),
            per_head((chunks, SPAN, DK)),
        ],
        [
            head_spec((chunks, 8, SPAN)), square, square, square, square, half, half,
            head_spec((DV, DK)), column_spec(length, (1 + 2 * NH) * H), whole_spec((8, DV)),
        ],
        [column_spec(length, 0), column_spec(length, 0), square, square],
        [],
        H * chunks * 4 * 2 * SPAN**3 * 4,
        H * chunks * 8 * SPAN * DK * 4,
    )(vec, key_part, value_part, transfer, inject, out_keys, out_values, entry, projected, gain)


def readout_back_call(vec, transfer, out_keys, mixed, projected, gain, d_gated, start):
    length = projected.shape[0]
    chunks = length // GROUP
    square = head_spec((chunks, SPAN, DK))
    return call(
        readout_back_kernel,
        [
            jax.ShapeDtypeStruct((length, H * DV), jnp.float32),
            jax.ShapeDtypeStruct((length, H * DV), jnp.bfloat16),
            per_head((chunks, SPAN, DK)),
            per_head((DV, DK)),
            per_head((8, DV)),
        ],
        [
            head_spec((chunks, 8, SPAN)), square, head_spec((chunks, GROUP, DK)),
            column_spec(length, 0), column_spec(length, (1 + 2 * NH) * H), whole_spec((8, DV)),
            column_spec(length, 0), head_spec((DV, DK)),
        ],
        [column_spec(length, 0), column_spec(length, 0), square, head_spec((DV, DK)), head_spec((8, DV))],
        [],
        H * chunks * 4 * 2 * SPAN**3 * 4,
        H * chunks * 8 * SPAN * DK * 4,
    )(vec, transfer, out_keys, mixed, projected, gain, d_gated, start)


def backward_call(projected, border, taps, masks, vec, transfer, inverse, solved, entries, d_mixed, local, exit_grad):
    length = projected.shape[0]
    chunks = length // GROUP
    parts = 1 + 2 * NH
    square = head_spec((chunks, SPAN, DK))
    outs = (
        [jax.ShapeDtypeStruct((length, H * DK), jnp.bfloat16)] * parts
        + [jax.ShapeDtypeStruct((16, H * DK), jnp.float32)] * parts
        + [jax.ShapeDtypeStruct((8, H * DK), jnp.float32)] * parts
        + [per_head((chunks, 8, SPAN))]
    )
    out_specs = (
        [column_spec(length, 0)] * parts
        + [column_spec(16, 0)] * parts
        + [column_spec(8, 0)] * parts
        + [head_spec((chunks, 8, SPAN))]
    )
    tall = pltpu.VMEM((parts, length, DK), jnp.float32)
    return call(
        backward_kernel,
        outs,
        conv_specs(length)
        + [head_spec((chunks, 8, SPAN)), square, square, square, square, column_spec(length, 0), square, head_spec((DV, DK))],
        out_specs,
        [
            pltpu.VMEM((parts, length + 8, DK), jnp.float32),
            tall,
            pltpu.VMEM((length, DK), jnp.float32),
            pltpu.VMEM((NH, length, DK), jnp.float32),
            pltpu.VMEM((NH, length, DK), jnp.float32),
            pltpu.VMEM((1 + NH, length, DK), jnp.float32),
            tall,
            pltpu.VMEM((length + 16, DK), jnp.float32),
        ],
        H * chunks * 14 * 2 * SPAN**3 * 4,
        H * chunks * 16 * SPAN * DK * 4,
    )(*[projected] * parts, *[border] * parts, *[taps] * parts, masks, vec, transfer, inverse, solved, entries, d_mixed, local, exit_grad)


def gather(block, dim=0):
    return lax.all_gather(block, ("dp", "seq"), axis=dim, tiled=True)


def on_device(
    block_input, doc_starts, norm_in, w_mix, w_small, conv_w, decay_log, norm_out,
    w_out, norm_mlp, w_gu, w_down, cotangent,
):
    row_count, seg_len, width = block_input.shape
    tap_count = conv_w.shape[0]
    key_width = H * DK
    parts = 1 + 2 * NH
    seqs = lax.axis_size("seq")
    residual_in = block_input.astype(jnp.float32).reshape(seg_len, width)
    smalls, rows = w_small.shape[1], w_mix.shape[0]
    fast = lax.axis_size("dp") == 4 * ZS and seqs == 2 and rows % 16 == 0
    if fast:
        small = jnp.concatenate(
            [w_small, norm_in[:, None], norm_mlp[:, None], conv_w.reshape(tap_count, rows, -1).transpose(1, 2, 0).reshape(rows, -1)], axis=1
        )
        small = jnp.concatenate([small, jnp.zeros((rows, DK - small.shape[1]), small.dtype)], axis=1)
        mix_all, out_all, down_own, small_pack, normed_low, normed_t, channels, gate, gates_raw, border, gains = gather_project_call(
            block_input.reshape(seg_len, width), small, w_mix, w_out, w_down
        )
        small_all = small_pack[:, :smalls]
        gates_raw = gates_raw[:, :smalls]
        norm_in_all, norm_mlp_all = gains[0], gains[1]
        per_row = conv_w.shape[1] // rows
        conv_all = small_pack[:, smalls + 2 : smalls + 2 + per_row * tap_count]
        conv_all = conv_all.reshape(-1, tap_count).transpose(1, 0)
        normed, norm_in_back = jax.vjp(rms_scale, residual_in, norm_in_all)
    else:
        mix_all, small_all, conv_all, out_all = gather(w_mix), gather(w_small), gather(conv_w, 1), gather(w_out)
        norm_in_all = gather(norm_in).astype(jnp.float32)
        norm_mlp_all = gather(norm_mlp).astype(jnp.float32)
        normed, norm_in_back = jax.vjp(rms_scale, residual_in, norm_in_all)
        normed_low = normed.astype(jnp.bfloat16)
        projected = jnp.dot(normed_low, mix_all, preferred_element_type=jnp.float32)
        gates_raw = jnp.dot(normed_low, small_all, preferred_element_type=jnp.float32)
    if fast:
        down_all = gather(down_own)
    else:
        gu_all, down_all = gather(w_gu), gather(w_down)
        border = from_behind(projected[seg_len - tap_count + 1 :, : parts * key_width], "seq", 1)
        border = jnp.concatenate([jnp.zeros((9 - tap_count, parts * key_width), jnp.float32), border], axis=0)
    positions = lax.axis_index("seq") * seg_len + jnp.arange(1 - tap_count, seg_len, dtype=jnp.int32)
    seg_ext = jnp.sum((positions[:, None] >= doc_starts[0][None, :]).astype(jnp.int32), axis=1)
    seg_ext = jnp.where(positions < 0, -1, seg_ext)
    seg_now = seg_ext[tap_count - 1 :]
    masks = jnp.stack(
        [seg_ext[tap_count - 1 - tap : tap_count - 1 - tap + seg_len] == seg_now for tap in range(1, tap_count)]
    ).astype(jnp.float32)
    masks = jnp.broadcast_to(masks[:, :, None], (tap_count - 1, seg_len, DK))
    if fast:
        masks = masks.astype(jnp.bfloat16)
    taps = jnp.concatenate([conv_all.astype(jnp.float32), jnp.zeros((8 - tap_count, parts * key_width), jnp.float32)], axis=0)
    vec, vec_back = jax.vjp(
        partial(gate_vectors, seg_now, seg_ext[tap_count - 2]), gates_raw, decay_log.astype(jnp.float32)
    )
    gain = jnp.broadcast_to(norm_out.astype(jnp.float32)[None, :], (8, DV))
    if fast:
        xt, out_keys, us, normed_out_low, mixed, gu_all = mixer_call(channels, gate, vec, masks, taps, border, gain, w_gu)
        gu_all = gu_all.reshape(width, -1)
    else:
        zero_state = jnp.zeros((H, DV, DK), jnp.float32)
        inverse, key_part, value_part, transfer, inject, out_keys, out_values, final_state = forward_call(
            projected, border, taps, masks, vec, zero_state
        )
        entry = zero_state
        device_transfer = None
        if seqs > 2:
            eye = jnp.broadcast_to(jnp.eye(DK, dtype=jnp.float32), (H, DK, DK))
            device_transfer = chain_call(vec, transfer, eye)
        for turn in range(seqs - 1):
            leaving = final_state
            if turn > 0:
                leaving = leaving + jnp.einsum("hvk,hkl->hvl", entry, device_transfer, precision=HIGHEST)
            entry = from_behind(leaving.astype(jnp.bfloat16), "seq", 1).astype(jnp.float32)
        normed_out_low, mixed, solved, entries = readout_call(
            vec, key_part, value_part, transfer, inject, out_keys, out_values, entry, projected, gain
        )
    if fast:
        mlp_gain = jnp.broadcast_to(norm_mlp_all[None, :], (8, width))
        backs = back_call(
            xt, out_keys, mixed, gate, channels, us, gu_all, down_all, vec, masks, taps, border, gain,
            out_all, mlp_gain,
            block_input.reshape(seg_len, width), normed_out_low, cotangent.reshape(seg_len, width), mix_all.reshape(STACK + (rows, -1)), normed_t,
        )
        d_projected, block_output, d_hidden, d_normed, gain_parts, d_vec, grad_conv, mlp_gain_parts = backs[:8]
        grad_gu, grad_down, grad_out, grad_mix = backs[8:]
        block_output = block_output.reshape(block_input.shape)
        d_hidden = d_hidden.reshape(seg_len, width)
        grad_norm_mlp = mlp_gain_parts[0]
        grad_down = grad_down.reshape(-1, width)[: w_down.shape[0]]
    else:
        hidden = residual_in + jnp.dot(normed_out_low, out_all, preferred_element_type=jnp.float32)
        mlp_in, norm_mlp_back = jax.vjp(rms_scale, hidden, norm_mlp_all)
        mlp_in_low = mlp_in.astype(jnp.bfloat16)
        gate_up = jnp.dot(mlp_in_low, gu_all, preferred_element_type=jnp.float32)
        activated, act_back = jax.vjp(swiglu, gate_up)
        activated_low = activated.astype(jnp.bfloat16)
        result = hidden + jnp.dot(activated_low, down_all, preferred_element_type=jnp.float32)
        block_output = result.astype(jnp.bfloat16).reshape(block_input.shape)

        d_result_low = cotangent.reshape(seg_len, width)
        d_result = d_result_low.astype(jnp.float32)
        grad_down = jnp.einsum("nf,nd->fd", activated_low, d_result_low, preferred_element_type=jnp.float32)
        d_activated = jnp.einsum("nd,fd->nf", d_result_low, down_all, preferred_element_type=jnp.float32)
        (d_gate_up,) = act_back(d_activated)
        d_gate_low = d_gate_up.astype(jnp.bfloat16)
        grad_gu = jnp.einsum("nd,nf->df", mlp_in_low, d_gate_low, preferred_element_type=jnp.float32)
        d_mlp_in = jnp.einsum("nf,df->nd", d_gate_low, gu_all, preferred_element_type=jnp.float32)
        d_hidden_norm, grad_norm_mlp = norm_mlp_back(d_mlp_in)
        d_hidden = d_result + d_hidden_norm
        d_mixer_low = d_hidden.astype(jnp.bfloat16)
        grad_out = jnp.einsum("nh,nd->hd", normed_out_low, d_mixer_low, preferred_element_type=jnp.float32)
        d_normed_out = jnp.einsum("nd,hd->nh", d_mixer_low, out_all, preferred_element_type=jnp.float32)
        grad_gu = scatter_halves(grad_gu.astype(jnp.bfloat16))
        grad_down = scatter_halves(grad_down.astype(jnp.bfloat16))
        grad_out = scatter_halves(grad_out.astype(jnp.bfloat16))
        d_mixed, d_out_gate, local, own_entry, gain_parts = readout_back_call(
            vec, transfer, out_keys, mixed, projected, gain, d_normed_out, zero_state
        )
        exit_grad = zero_state
        for turn in range(seqs - 1):
            leaving = own_entry
            if turn > 0:
                leaving = leaving + jnp.einsum("hvl,hkl->hvk", exit_grad, device_transfer, precision=HIGHEST)
            exit_grad = from_behind(leaving.astype(jnp.bfloat16), "seq", -1).astype(jnp.float32)
        backs = backward_call(
            projected, border, taps, masks, vec, transfer, inverse, solved, entries, d_mixed, local, exit_grad
        )
        d_columns, edges, tap_grads, d_vec = backs[:parts], backs[parts : 2 * parts], backs[2 * parts : 3 * parts], backs[-1]
        edge = jnp.concatenate(edges, axis=1)
        returned = from_behind(edge[9 - tap_count : 8].astype(jnp.bfloat16), "seq", -1).astype(jnp.float32)
        fixed = (edge[17 - tap_count :] + returned).astype(jnp.bfloat16)
        d_projected = jnp.concatenate(list(d_columns) + [d_out_gate], axis=1)
        d_projected = lax.dynamic_update_slice(d_projected, fixed, (seg_len - tap_count + 1, 0))
        grad_mix = jnp.einsum("nd,nc->dc", normed_low, d_projected, preferred_element_type=jnp.float32)
        grad_mix = scatter_halves(grad_mix.astype(jnp.bfloat16))
        grad_conv = jnp.concatenate(tap_grads, axis=1)
    grad_norm_out = jnp.sum(gain_parts[:, 0, :], axis=0)
    d_gates_raw, grad_decay = vec_back(d_vec)
    d_gates_low = d_gates_raw.astype(jnp.bfloat16)
    grad_small = jnp.einsum("nd,nc->dc", normed_low, d_gates_low, preferred_element_type=jnp.float32)
    if not fast:
        d_normed = jnp.einsum("nc,dc->nd", d_projected, mix_all, preferred_element_type=jnp.float32)
    d_normed = d_normed + jnp.einsum("nc,dc->nd", d_gates_low, small_all, preferred_element_type=jnp.float32)
    d_input_norm, grad_norm_in = norm_in_back(d_normed)
    input_grad = (d_hidden + d_input_norm).astype(jnp.bfloat16).reshape(block_input.shape)

    grad_conv = grad_conv[:tap_count]
    devices = lax.axis_size("dp") * seqs
    conv_rows = grad_conv.reshape(tap_count, devices, -1).transpose(1, 0, 2).reshape(width, -1)
    packed = jnp.concatenate([grad_small, grad_norm_in[:, None], grad_norm_mlp[:, None], conv_rows], axis=1)
    packed = jnp.concatenate([packed, jnp.zeros((width, 128 - packed.shape[1]), jnp.float32)], axis=1)
    if fast:
        sums = jnp.stack([grad_norm_out, jnp.pad(grad_decay, (0, DV - H))] + [jnp.zeros((DV,), jnp.float32)] * 6)
        packed, sums = total_call(packed.reshape(STACK + (rows, -1)), sums)
        grad_norm_out, grad_decay = sums[0], sums[1, :H]
    else:
        packed = scatter_sum(packed, bit_orders()[0])
        sums = total_sum(jnp.concatenate([grad_norm_out, grad_decay]))
        grad_norm_out, grad_decay = sums[:DV], sums[DV:]
    smalls = grad_small.shape[1]
    grad_small = packed[:, :smalls]
    grad_norm_in, grad_norm_mlp = packed[:, smalls], packed[:, smalls + 1]
    grad_conv = packed[:, smalls + 2 : smalls + 2 + conv_rows.shape[1]].reshape(tap_count, -1)
    return (
        block_output, input_grad, grad_norm_in, grad_mix, grad_small, grad_conv, grad_decay,
        grad_norm_out, grad_out, grad_norm_mlp, grad_gu, grad_down,
    )


def solution(mesh):
    sharded = ("dp", "seq")
    in_specs = (
        P("dp", "seq", None), P("dp", None), P(sharded), P(sharded, None), P(sharded, None),
        P(None, sharded), P(), P(), P(sharded, None), P(sharded), P(sharded, None),
        P(sharded, None), P("dp", "seq", None),
    )
    out_specs = (
        P("dp", "seq", None), P("dp", "seq", None), P(sharded), P(sharded, None), P(sharded, None),
        P(None, sharded), P(), P(), P(sharded, None), P(sharded), P(sharded, None), P(sharded, None),
    )
    return jax.shard_map(
        on_device, mesh=mesh, in_specs=in_specs, out_specs=out_specs, check_vma=False
    )
```
